32 devices in a mesh: dp: 4 (over y, core), seq: 8 (over z, x).
Axes of the slice: x: 2, y: 2, z: 4, core: 2. Of those that a mesh axis runs over, the one named last changes fastest.
Arguments:
- hidden: bfloat16 [8, 512, 2048], P('dp', 'seq'), may hold values from -6 to 6
- segments: int32 [8, 512], P('dp', 'seq'), may hold values from 0 to 3, never falling along the last dimension, each value on 1 to 256 neighbouring positions
- in_weight: bfloat16 [2048, 8512], P(('dp', 'seq')), may hold values from -0.125 to 0.125
- conv_weight: float32 [4352, 4], replicated, may hold values from -3 to 3
- conv_bias: float32 [4352], replicated, may hold values from -2 to 2
- dt_bias: float32 [64], replicated, may hold values from -6 to -2
- a_log: float32 [64], replicated, may hold values from 0 to 2.8
- d_skip: float32 [64], replicated, may hold values from 0.5 to 1.5
- norm_gain: float32 [2048], replicated, may hold values from 0.5 to 1.5
- gate_gain: float32 [4096], replicated, may hold values from 0.5 to 1.5
- out_weight: bfloat16 [4096, 2048], P(('dp', 'seq')), may hold values from -0.09375 to 0.09375
- cotangent: bfloat16 [8, 512, 2048], P('dp', 'seq'), may hold values from -6 to 6
Outputs:
- result: bfloat16 [8, 512, 2048], P('dp', 'seq')
- d_hidden: bfloat16 [8, 512, 2048], P('dp', 'seq')
- grad_in_weight: float32 [2048, 8512], P(('dp', 'seq'))
- grad_conv_weight: float32 [4352, 4], replicated
- grad_conv_bias: float32 [4352], replicated
- grad_dt_bias: float32 [64], replicated
- grad_a_log: float32 [64], replicated
- grad_d_skip: float32 [64], replicated
- grad_norm_gain: float32 [2048], replicated
- grad_gate_gain: float32 [4096], replicated
- grad_out_weight: float32 [4096, 2048], P(('dp', 'seq'))
The draws below stay inside these ranges and needn't reach their ends.
Inputs may be any that keep to these rules, and one draw needn't show every extreme that they name: `segments`: within a sequence the document numbers start at 0, never fall and rise by at most one from a token to the next; every document has 1 to 256 tokens and one has exactly 256.
All inputs are finite; a program needn't handle non-finite values.
Results may differ from the reference program's by a relative error of at most 0.012.
The reference program's roundings to bfloat16 on the way count: a program that leaves them out, or rounds other values in their place, can miss the bound.
Values may be sent and summed in bfloat16 or wider, within the bound.
A program may use at most 320 MiB of HBM per device.

```python
import math
import jax
import jax.numpy as jnp
import numpy as np
from jax import lax

D = 2048
HEADS = 64
HDIM = 64
NST = 128
GROUP = 256
CONV = 4
DI = 4096
NPROJ = 8512
CONVCH = 4352
L = 512
SEQS = 8
DOCS = 4
DOC_MOST = 256


def level_of(key, shape, split, smallest, top_value):
    loudness = 1.0
    for axis_at, parts in split:
        steps = jax.random.uniform(jax.random.fold_in(jax.random.fold_in(key, 6), axis_at), (parts,), jnp.float32, smallest / len(split), top_value / len(split))
        loudness = loudness * jnp.repeat(jnp.exp(steps), shape[axis_at] // parts).reshape((-1,) + (1,) * (len(shape) - 1 - axis_at))
    return loudness


def profile(amount, total, reach, slope):
    weights = [(1 << 20) // math.isqrt(grade ** slope) + 1 for grade in range(2, amount + 1)]
    spare, counts = total - reach - (amount - 1), [1] * (amount - 1)
    while spare > 0:
        free = [i for i in range(amount - 1) if counts[i] < reach]
        mass, left = sum([weights[i] for i in free]), spare
        for i in free:
            addition = min(reach - counts[i], max(1, left * weights[i] // mass), spare)
            counts[i] = counts[i] + addition
            spare = spare - addition
    return np.array([reach] + counts)


def ragged_sizes(rng, count, total, reach, lean):
    if count == 2:
        one = jax.random.randint(rng, (), max(1, total - reach), min(reach, total - 1) + 1)
        return jnp.stack([one, total - one])
    lengths = jnp.asarray(profile(count, total, reach, lean), jnp.int32)
    twos = (count - 1) // 2
    source_of, taker = lengths[1:1 + 2 * twos:2], lengths[2:2 + 2 * twos:2]
    margin = jnp.minimum(source_of - 1, reach - taker)
    passed = jax.random.randint(jax.random.fold_in(rng, 1), (twos,), 0, 1 << 20) % (margin + 1)
    lengths = lengths.at[1:1 + 2 * twos:2].set(source_of - passed).at[2:2 + 2 * twos:2].set(taker + passed)
    return lengths[jax.random.permutation(jax.random.fold_in(rng, 2), count)]


def noise(key, shape, scale, reach, shards=(), kind=jnp.bfloat16):
    drawn = jax.random.normal(key, shape, jnp.float32) * scale
    if len(shards) > 0:
        drawn = level_of(key, shape, shards, -0.22, 0.18) * drawn
    return jnp.clip(drawn, min=-reach, max=reach).astype(kind)


def setup_inputs(seed: int = 0) -> dict:
    key_of = jax.random.split(jax.random.key(seed), 13)
    return {
        "hidden": noise(key_of[0], (SEQS, L, D), 1.0, 6.0, ((0, 4), (1, 8))),
        "segments": jax.vmap(lambda own: jnp.searchsorted(jnp.cumsum(ragged_sizes(own, DOCS, L, DOC_MOST, 1)), jnp.arange(L), side="right"))(jax.random.split(key_of[1], SEQS)).reshape((SEQS, L)).astype(jnp.int32),
        "in_weight": noise(key_of[2], (D, NPROJ), D ** -0.5, 0.125, ((0, 32),)),
        "conv_weight": noise(key_of[3], (CONVCH, CONV), 0.5, 3.0, (), jnp.float32),
        "conv_bias": noise(key_of[4], (CONVCH,), 0.3, 2.0, (), jnp.float32),
        "dt_bias": jnp.clip(jax.random.uniform(key_of[5], (HEADS,), jnp.float32, -6.0, -2.0), -6.0, -2.0),
        "a_log": jnp.clip(jax.random.uniform(key_of[6], (HEADS,), jnp.float32, 0.0, 2.8), 0.0, 2.8),
        "d_skip": jnp.clip(jax.random.uniform(key_of[7], (HEADS,), jnp.float32, 0.5, 1.5), 0.5, 1.5),
        "norm_gain": jnp.clip(1.0 + 0.1 * jax.random.normal(key_of[8], (D,), jnp.float32), 0.5, 1.5),
        "gate_gain": jnp.clip(1.0 + 0.1 * jax.random.normal(key_of[9], (DI,), jnp.float32), 0.5, 1.5),
        "out_weight": noise(key_of[10], (DI, D), DI ** -0.5, 0.09375, ((0, 32),)),
        "cotangent": noise(key_of[11], (SEQS, L, D), 1.0, 6.0, ((0, 4), (1, 8))),
    }


@jax.custom_vjp
def low(v):
    return lax.optimization_barrier(v.astype(jnp.bfloat16)).astype(jnp.float32)

@jax.custom_vjp
def low_back(v):
    return v

def low_keep(v):
    return (low(v), None)

def low_pass(kept, grad):
    return (grad,)

def back_keep(v):
    return (v, None)

def back_low(kept, grad):
    return (low(grad),)
low.defvjp(low_keep, low_pass)
low_back.defvjp(back_keep, back_low)

def pre_norm(hidden_f, gain_vec):
    return hidden_f * lax.rsqrt(lax.optimization_barrier(jnp.mean(hidden_f * hidden_f, axis=-1, keepdims=True)) + 1e-05) * gain_vec

def gate_norm(y_values, gate_values, gain_vec):
    product = y_values * jax.nn.silu(gate_values)
    return product * lax.rsqrt(lax.optimization_barrier(jnp.mean(product * product, axis=-1, keepdims=True)) + 1e-05) * gain_vec

def conv_reset(signal, kernel, offset, seg_ids):
    tap_count = kernel.shape[1]
    summed = offset[None, :] + kernel[None, :, tap_count - 1] * signal
    for lag_steps in range(1, tap_count):
        shifted = jnp.pad(signal, ((lag_steps, 0), (0, 0)))[:-lag_steps]
        earlier = jnp.pad(seg_ids, (lag_steps, 0), constant_values=-1)[:-lag_steps]
        matches = (earlier == seg_ids).astype(jnp.float32)
        summed = summed + kernel[None, :, tap_count - 1 - lag_steps] * shifted * matches[:, None]
    return summed

def state_scan(values, deltas, rates, b_mat, c_mat, seg_ids):
    length, head_count, head_width = values.shape
    block_count = length // GROUP
    log_decay = deltas * rates[None, :]
    pieces = (values.reshape(block_count, GROUP, head_count, head_width), deltas.reshape(block_count, GROUP, head_count), log_decay.reshape(block_count, GROUP, head_count), b_mat.reshape(block_count, GROUP, b_mat.shape[-1]), c_mat.reshape(block_count, GROUP, c_mat.shape[-1]), seg_ids.reshape(block_count, GROUP))
    position = lax.broadcasted_iota(jnp.int32, (GROUP, GROUP), 0)
    source = lax.broadcasted_iota(jnp.int32, (GROUP, GROUP), 1)

    def advance(carry, piece):
        memory, ending = carry
        block_vals, block_dt, block_log, b_block, c_block, seg_block = piece
        cumulative = jnp.cumsum(block_log, axis=0).T
        causal = (source <= position) & (seg_block[:, None] == seg_block[None, :])
        spread = cumulative[:, :, None] - cumulative[:, None, :]
        decays = jnp.where(causal[None], jnp.exp(jnp.where(causal[None], spread, 0.0)), 0.0)
        inner_prod = jnp.dot(c_block, b_block.T, precision=lax.Precision.HIGHEST)
        scores = inner_prod[None] * decays * block_dt.T[:, None, :]
        output = jnp.einsum('hij,jhp->ihp', scores, block_vals, precision=lax.Precision.HIGHEST)
        follows = (seg_block == ending).astype(jnp.float32)
        carried = jnp.einsum('in,hpn->ihp', c_block, memory, precision=lax.Precision.HIGHEST)
        output = output + (jnp.exp(cumulative).T * follows[:, None])[:, :, None] * carried
        last_seg = seg_block[-1]
        weights = jnp.exp(cumulative[:, -1:] - cumulative) * (seg_block == last_seg).astype(jnp.float32)[None, :] * block_dt.T
        keep_on = jnp.exp(cumulative[:, -1]) * (last_seg == ending).astype(jnp.float32)
        memory = memory * keep_on[:, None, None] + jnp.einsum('hj,jhp,jn->hpn', weights, block_vals, b_block, precision=lax.Precision.HIGHEST)
        return ((memory, last_seg), output)
    initial = (jnp.zeros((head_count, head_width, b_mat.shape[-1]), jnp.float32), jnp.array(-1, jnp.int32))
    unused, outputs = lax.scan(jax.checkpoint(advance), initial, pieces)
    return outputs.reshape(length, head_count, head_width)

def mixer(x_values, step_raw, bc_values, seg_ids, kernel_x, offset_x, kernel_bc, offset_bc, dt_shift, decay_log, skip_gain):
    x_conv = jax.nn.silu(conv_reset(x_values, kernel_x, offset_x, seg_ids))
    bc_conv = jax.nn.silu(conv_reset(bc_values, kernel_bc, offset_bc, seg_ids))
    step_sizes = jax.nn.softplus(step_raw + dt_shift[None, :])
    rates = -jnp.exp(decay_log)
    length = x_values.shape[0]
    head_count = step_raw.shape[1]
    shaped = x_conv.reshape(length, head_count, HDIM)
    mixed = state_scan(shaped, step_sizes, rates, bc_conv[:, :NST], bc_conv[:, NST:], seg_ids) + skip_gain[None, :, None] * shaped
    return mixed.reshape(length, head_count * HDIM)

def forward(hidden_row, seg_row, in_weight, conv_weight, conv_bias, dt_bias, a_log, d_skip, norm_gain, gate_gain, out_weight):
    normed = low(pre_norm(hidden_row, norm_gain))
    project = low_back(jnp.dot(normed, in_weight, precision=lax.Precision.HIGHEST))
    gate_part = project[:, :DI]
    x_part = low(project[:, DI:2 * DI])
    bc_part = low(project[:, 2 * DI:2 * DI + 2 * NST])
    step_part = low(project[:, 2 * DI + 2 * NST:])
    mixed = low_back(low(mixer(x_part, step_part, bc_part, seg_row, conv_weight[:DI], conv_bias[:DI], conv_weight[DI:], conv_bias[DI:], dt_bias, a_log, d_skip)))
    gated = low(gate_norm(mixed, gate_part, gate_gain))
    return hidden_row + jnp.dot(gated, out_weight, precision=lax.Precision.HIGHEST)

def reference(hidden, segments, in_weight, conv_weight, conv_bias, dt_bias, a_log, d_skip, norm_gain, gate_gain, out_weight, cotangent):
    params = (in_weight.astype(jnp.float32), conv_weight, conv_bias, dt_bias, a_log, d_skip, norm_gain, gate_gain, out_weight.astype(jnp.float32))

    def one_sequence(totals, item):
        hidden_row, seg_row, cot_row = item

        def local_forward(row_input, *param_list):
            return forward(row_input, seg_row, *param_list)
        value, pullback = jax.vjp(local_forward, hidden_row.astype(jnp.float32), *params)
        grads = pullback(cot_row.astype(jnp.float32))
        totals = tuple((older + newer for older, newer in zip(totals, grads[1:])))
        return (totals, (value.astype(jnp.bfloat16), grads[0].astype(jnp.bfloat16)))
    zero_grads = tuple((jnp.zeros_like(param) for param in params))
    totals, outputs = lax.scan(one_sequence, zero_grads, (hidden, segments, cotangent))
    return (outputs[0], outputs[1], totals[0], totals[1], totals[2], totals[3], totals[4], totals[5], totals[6], totals[7], totals[8])
```

```python
import jax
import jax.numpy as jnp
from jax import lax
from jax.sharding import PartitionSpec as P

HEADS = 64
HDIM = 64
NST = 128
GROUP = 256
DI = 4096


def pre_norm(hidden_f, gain_vec):
    return (
        hidden_f
        * lax.rsqrt(jnp.mean(hidden_f * hidden_f, axis=-1, keepdims=True) + 1e-05)
        * gain_vec
    )


def gate_norm(y_values, gate_values, gain_vec):
    product = y_values * jax.nn.silu(gate_values)
    return (
        product * lax.rsqrt(jnp.mean(product * product, axis=-1, keepdims=True) + 1e-05) * gain_vec
    )


def conv_reset(signal, kernel, offset, seg_ids):
    tap_count = kernel.shape[1]
    summed = offset[None, :] + kernel[None, :, tap_count - 1] * signal
    for lag_steps in range(1, tap_count):
        shifted = jnp.pad(signal, ((lag_steps, 0), (0, 0)))[:-lag_steps]
        earlier = jnp.pad(seg_ids, (lag_steps, 0), constant_values=-1)[:-lag_steps]
        matches = (earlier == seg_ids).astype(jnp.float32)
        summed = summed + kernel[None, :, tap_count - 1 - lag_steps] * shifted * matches[:, None]
    return summed


def state_scan(values, deltas, rates, b_mat, c_mat, seg_ids):
    length, head_count, head_width = values.shape
    block_count = length // GROUP
    log_decay = deltas * rates[None, :]
    pieces = (
        values.reshape(block_count, GROUP, head_count, head_width),
        deltas.reshape(block_count, GROUP, head_count),
        log_decay.reshape(block_count, GROUP, head_count),
        b_mat.reshape(block_count, GROUP, b_mat.shape[-1]),
        c_mat.reshape(block_count, GROUP, c_mat.shape[-1]),
        seg_ids.reshape(block_count, GROUP),
    )
    position = lax.broadcasted_iota(jnp.int32, (GROUP, GROUP), 0)
    source = lax.broadcasted_iota(jnp.int32, (GROUP, GROUP), 1)

    def advance(carry, piece):
        memory, ending = carry
        block_vals, block_dt, block_log, b_block, c_block, seg_block = piece
        cumulative = jnp.cumsum(block_log, axis=0).T
        causal = (source <= position) & (seg_block[:, None] == seg_block[None, :])
        spread = cumulative[:, :, None] - cumulative[:, None, :]
        decays = jnp.where(causal[None], jnp.exp(jnp.where(causal[None], spread, 0.0)), 0.0)
        inner_prod = jnp.dot(c_block, b_block.T, precision=lax.Precision.HIGHEST)
        scores = inner_prod[None] * decays * block_dt.T[:, None, :]
        output = jnp.einsum("hij,jhp->ihp", scores, block_vals, precision=lax.Precision.HIGHEST)
        follows = (seg_block == ending).astype(jnp.float32)
        carried = jnp.einsum("in,hpn->ihp", c_block, memory, precision=lax.Precision.HIGHEST)
        output = output + (jnp.exp(cumulative).T * follows[:, None])[:, :, None] * carried
        last_seg = seg_block[-1]
        weights = (
            jnp.exp(cumulative[:, -1:] - cumulative)
            * (seg_block == last_seg).astype(jnp.float32)[None, :]
            * block_dt.T
        )
        keep_on = jnp.exp(cumulative[:, -1]) * (last_seg == ending).astype(jnp.float32)
        memory = memory * keep_on[:, None, None] + jnp.einsum(
            "hj,jhp,jn->hpn", weights, block_vals, b_block, precision=lax.Precision.HIGHEST
        )
        return ((memory, last_seg), output)

    initial = (
        jnp.zeros((head_count, head_width, b_mat.shape[-1]), jnp.float32),
        jnp.array(-1, jnp.int32),
    )
    unused, outputs = lax.scan(jax.checkpoint(advance), initial, pieces)
    return outputs.reshape(length, head_count, head_width)


def mixer(
    x_values,
    step_raw,
    bc_values,
    seg_ids,
    kernel_x,
    offset_x,
    kernel_bc,
    offset_bc,
    dt_shift,
    decay_log,
    skip_gain,
):
    x_conv = jax.nn.silu(conv_reset(x_values, kernel_x, offset_x, seg_ids))
    bc_conv = jax.nn.silu(conv_reset(bc_values, kernel_bc, offset_bc, seg_ids))
    step_sizes = jax.nn.softplus(step_raw + dt_shift[None, :])
    rates = -jnp.exp(decay_log)
    length = x_values.shape[0]
    head_count = step_raw.shape[1]
    shaped = x_conv.reshape(length, head_count, HDIM)
    mixed = (
        state_scan(shaped, step_sizes, rates, bc_conv[:, :NST], bc_conv[:, NST:], seg_ids)
        + skip_gain[None, :, None] * shaped
    )
    return mixed.reshape(length, head_count * HDIM)


def general_plan(
    hidden,
    segments,
    in_weight,
    conv_weight,
    conv_bias,
    dt_bias,
    a_log,
    d_skip,
    norm_gain,
    gate_gain,
    out_weight,
    cotangent,
):
    full_in, full_out = (
        lax.all_gather(in_weight, ("dp", "seq"), axis=0, tiled=True),
        lax.all_gather(out_weight, ("dp", "seq"), axis=0, tiled=True),
    )
    hidden_f = hidden.astype(jnp.float32)
    normed_f, pull_pre = jax.vjp(pre_norm, hidden_f, norm_gain)
    normed = normed_f.astype(jnp.bfloat16)
    project = jnp.einsum("mtd,df->mtf", normed, full_in, preferred_element_type=jnp.float32)
    gate_part = project[:, :, :DI]
    x_part = project[:, :, DI : 2 * DI].astype(jnp.bfloat16)
    bc_part = project[:, :, 2 * DI : 2 * DI + 2 * NST].astype(jnp.bfloat16)
    step_part = project[:, :, 2 * DI + 2 * NST :].astype(jnp.bfloat16)
    x_heads, step_heads = (
        lax.all_to_all(x_part, "seq", split_axis=2, concat_axis=1, tiled=True),
        lax.all_to_all(step_part, "seq", split_axis=2, concat_axis=1, tiled=True),
    )
    bc_full = lax.all_gather(bc_part, "seq", axis=1, tiled=True)
    seg_full = lax.all_gather(segments, "seq", axis=1, tiled=True)
    seq_rank = lax.axis_index("seq")
    head_local = step_heads.shape[2]
    chan_local = x_heads.shape[2]
    kernel_x = lax.dynamic_slice_in_dim(conv_weight, seq_rank * chan_local, chan_local, 0)
    offset_x = lax.dynamic_slice_in_dim(conv_bias, seq_rank * chan_local, chan_local, 0)
    shift_local = lax.dynamic_slice_in_dim(dt_bias, seq_rank * head_local, head_local, 0)
    decay_local = lax.dynamic_slice_in_dim(a_log, seq_rank * head_local, head_local, 0)
    skip_local = lax.dynamic_slice_in_dim(d_skip, seq_rank * head_local, head_local, 0)
    local_params = (
        kernel_x,
        offset_x,
        conv_weight[DI:],
        conv_bias[DI:],
        shift_local,
        decay_local,
        skip_local,
    )

    def head_mixer(x_values, step_raw, bc_values, params_in):

        def single_seq(x_one, step_one, bc_one, seg_one):
            return mixer(x_one, step_one, bc_one, seg_one, *params_in)

        return jax.vmap(single_seq)(x_values, step_raw, bc_values, seg_full)

    mixed, pull_mix = jax.vjp(
        head_mixer,
        x_heads.astype(jnp.float32),
        step_heads.astype(jnp.float32),
        bc_full.astype(jnp.float32),
        local_params,
    )
    y_tokens = lax.all_to_all(
        mixed.astype(jnp.bfloat16), "seq", split_axis=1, concat_axis=2, tiled=True
    )
    gated_f, pull_gate = jax.vjp(gate_norm, y_tokens.astype(jnp.float32), gate_part, gate_gain)
    gated = gated_f.astype(jnp.bfloat16)
    branch_out = jnp.einsum("mtf,fd->mtd", gated, full_out, preferred_element_type=jnp.float32)
    result = (hidden_f + branch_out).astype(jnp.bfloat16)
    d_gated = jnp.einsum("mtd,fd->mtf", cotangent, full_out, preferred_element_type=jnp.float32)
    d_mixed, d_gate_part, d_gate_gain = pull_gate(d_gated)
    d_heads = lax.all_to_all(
        d_mixed.astype(jnp.bfloat16), "seq", split_axis=2, concat_axis=1, tiled=True
    )
    d_x_heads, d_step_heads, d_bc_full, d_params = pull_mix(d_heads.astype(jnp.float32))
    d_x_part, d_step_part = (
        lax.all_to_all(
            d_x_heads.astype(jnp.bfloat16), "seq", split_axis=1, concat_axis=2, tiled=True
        ),
        lax.all_to_all(
            d_step_heads.astype(jnp.bfloat16), "seq", split_axis=1, concat_axis=2, tiled=True
        ),
    )
    d_bc_part = lax.psum_scatter(
        d_bc_full.astype(jnp.bfloat16), "seq", scatter_dimension=1, tiled=True
    )
    d_project = jnp.concatenate(
        [d_gate_part.astype(jnp.bfloat16), d_x_part, d_bc_part, d_step_part], axis=2
    )
    d_normed = jnp.einsum("mtf,df->mtd", d_project, full_in, preferred_element_type=jnp.float32)
    d_hidden_f, d_norm_gain = pull_pre(d_normed)
    d_hidden = (cotangent.astype(jnp.float32) + d_hidden_f).astype(jnp.bfloat16)
    in_rows = in_weight.shape[0]
    out_rows = out_weight.shape[0]
    column_ranges = ((0, DI), (DI, d_project.shape[2]))
    in_pieces = [jnp.zeros((in_rows, upper - lower), jnp.float32) for lower, upper in column_ranges]
    grad_out = jnp.zeros(out_weight.shape, jnp.float32)
    for batch_index in range(hidden.shape[0]):
        for range_index in range(len(column_ranges)):
            lower, upper = column_ranges[range_index]

            def in_term(
                start,
                count,
                normed_one=normed[batch_index],
                d_one=d_project[batch_index, :, lower:upper],
            ):
                return lax.dot_general(
                    normed_one, d_one, (((0,), (0,)), ((), ())), preferred_element_type=jnp.float32
                )

            in_pieces[range_index] = in_pieces[range_index] + lax.psum_scatter(
                in_term(jnp.int32(0), in_rows * lax.axis_size(("dp", "seq"))),
                ("dp", "seq"),
                scatter_dimension=0,
                tiled=True,
            )

        def out_term(start, count, gated_one=gated[batch_index], cot_one=cotangent[batch_index]):
            return lax.dot_general(
                gated_one, cot_one, (((0,), (0,)), ((), ())), preferred_element_type=jnp.float32
            )

        grad_out = grad_out + lax.psum_scatter(
            out_term(jnp.int32(0), out_rows * lax.axis_size(("dp", "seq"))),
            ("dp", "seq"),
            scatter_dimension=0,
            tiled=True,
        )
    grad_in = jnp.concatenate(in_pieces, axis=1)
    d_kernel_x, d_offset_x, d_kernel_bc, d_offset_bc, d_shift, d_decay, d_skip_part = d_params
    tap_count = conv_weight.shape[1]
    grad_conv_w = jnp.concatenate(
        [
            lax.dynamic_update_slice_in_dim(
                jnp.zeros((DI, tap_count), jnp.float32), d_kernel_x, seq_rank * chan_local, 0
            ),
            d_kernel_bc,
        ],
        axis=0,
    )
    grad_conv_b = jnp.concatenate(
        [
            lax.dynamic_update_slice_in_dim(
                jnp.zeros((DI,), jnp.float32), d_offset_x, seq_rank * chan_local, 0
            ),
            d_offset_bc,
        ],
        axis=0,
    )
    grad_shift = lax.dynamic_update_slice_in_dim(
        jnp.zeros((HEADS,), jnp.float32), d_shift, seq_rank * head_local, 0
    )
    grad_decay = lax.dynamic_update_slice_in_dim(
        jnp.zeros((HEADS,), jnp.float32), d_decay, seq_rank * head_local, 0
    )
    grad_skip = lax.dynamic_update_slice_in_dim(
        jnp.zeros((HEADS,), jnp.float32), d_skip_part, seq_rank * head_local, 0
    )
    totals = lax.psum(
        (grad_conv_w, grad_conv_b, grad_shift, grad_decay, grad_skip, d_norm_gain, d_gate_gain),
        ("dp", "seq"),
    )
    return (
        result,
        d_hidden,
        grad_in,
        totals[0],
        totals[1],
        totals[2],
        totals[3],
        totals[4],
        totals[5],
        totals[6],
        grad_out,
    )


def head_plan(
    hidden,
    segments,
    in_weight,
    conv_weight,
    conv_bias,
    dt_bias,
    a_log,
    d_skip,
    norm_gain,
    gate_gain,
    out_weight,
    cotangent,
):
    f32, bf16 = jnp.float32, jnp.bfloat16
    n_dp, n_seq = lax.axis_size("dp"), lax.axis_size("seq")
    seq_rank = lax.axis_index("seq")
    n_own, shard_len, width = hidden.shape
    length = shard_len * n_seq
    rows = out_weight.shape[0]
    in_rows = in_weight.shape[0]
    chan = rows * n_dp
    h_own = chan // HDIM
    hidden_f = hidden.astype(f32)
    inv = lax.rsqrt(jnp.mean(hidden_f * hidden_f, axis=-1, keepdims=True) + 1e-05)
    normed = (hidden_f * inv * norm_gain).astype(bf16)
    normed_all = lax.all_gather(normed, "seq", axis=1, tiled=True).reshape(n_own * length, width)
    wide = in_weight[:, : 2 * DI].reshape(in_rows, 2, n_dp, n_seq, rows)
    wide = lax.all_to_all(wide, "seq", split_axis=3, concat_axis=0, tiled=True)
    wide = wide.reshape(n_seq * in_rows, 2 * chan)
    tail = lax.all_gather(in_weight[:, 2 * DI :], "seq", axis=0, tiled=True)
    w_in = lax.all_gather(jnp.concatenate([wide, tail], axis=1), "dp", axis=0, tiled=True)
    w_out = lax.all_gather(out_weight, "dp", axis=0, tiled=True)
    cot_all = lax.all_gather(cotangent, "seq", axis=1, tiled=True).reshape(n_own * length, width)
    seg_all = lax.all_gather(segments, "seq", axis=1, tiled=True)

    def own_chan(vec):
        return lax.dynamic_index_in_dim(
            vec.reshape((n_dp, n_seq, rows) + vec.shape[1:]), seq_rank, 1, keepdims=False
        ).reshape((chan,) + vec.shape[1:])

    heads_row = rows // HDIM

    def own_head(vec):
        return lax.dynamic_index_in_dim(
            vec.reshape((n_dp, n_seq, heads_row) + vec.shape[1:]), seq_rank, 1, keepdims=False
        ).reshape((h_own,) + vec.shape[1:])

    def spread_chan(vec):
        blank = jnp.zeros((n_dp, n_seq, rows) + vec.shape[1:], f32)
        piece = vec.reshape((n_dp, 1, rows) + vec.shape[1:])
        return lax.dynamic_update_slice_in_dim(blank, piece, seq_rank, 1).reshape(
            (DI,) + vec.shape[1:]
        )

    def spread_head(vec):
        blank = jnp.zeros((n_dp, n_seq, heads_row) + vec.shape[1:], f32)
        piece = vec.reshape((n_dp, 1, heads_row) + vec.shape[1:])
        return lax.dynamic_update_slice_in_dim(blank, piece, seq_rank, 1).reshape(
            (HEADS,) + vec.shape[1:]
        )

    project = jnp.dot(normed_all, w_in, preferred_element_type=f32)
    z = project[:, :chan]
    x_raw = project[:, chan : 2 * chan].astype(bf16)
    bc_raw = project[:, 2 * chan : 2 * chan + 2 * NST].astype(bf16)
    dt_all = project[:, 2 * chan + 2 * NST :].astype(bf16)
    dt_raw = own_head(dt_all.T).T
    local_params = (
        own_chan(conv_weight[:DI]),
        own_chan(conv_bias[:DI]),
        conv_weight[DI:],
        conv_bias[DI:],
        own_head(dt_bias),
        own_head(a_log),
        own_head(d_skip),
    )

    def head_mixer(x_values, step_raw, bc_values, params_in):
        def single_seq(x_one, step_one, bc_one, seg_one):
            return mixer(x_one, step_one, bc_one, seg_one, *params_in)

        return jax.vmap(single_seq)(x_values, step_raw, bc_values, seg_all)

    def by_seq(v):
        return v.reshape(n_own, length, v.shape[-1]).astype(f32)

    mixed, pull_mix = jax.vjp(
        head_mixer, by_seq(x_raw), by_seq(dt_raw), by_seq(bc_raw), local_params
    )
    y = mixed.reshape(n_own * length, chan).astype(bf16).astype(f32)
    gain = own_chan(gate_gain)
    sig = jax.nn.sigmoid(z)
    act = z * sig
    g = y * act
    d_gated = lax.dot_general(
        cot_all, w_out, (((1,), (1,)), ((), ())), preferred_element_type=f32
    )
    u = d_gated * gain
    sums = lax.psum(jnp.stack([jnp.sum(g * g, axis=1), jnp.sum(u * g, axis=1)]), "seq")
    r = lax.rsqrt(sums[0] / DI + 1e-05)[:, None]
    fall = (r * r * r) * (sums[1] / DI)[:, None]
    gr = g * r
    gated = (gr * gain).astype(bf16)
    part = jnp.dot(gated, w_out, preferred_element_type=f32).astype(bf16)
    branch = lax.psum_scatter(
        part.reshape(n_own, length, width), "seq", scatter_dimension=1, tiled=True
    )
    result = (hidden_f + branch.astype(f32)).astype(bf16)
    d_g = r * u - fall * g
    d_y = (d_g * act).astype(bf16)
    d_z = d_g * y * (sig * (1.0 + z * (1.0 - sig)))
    d_gate_gain = jnp.sum(d_gated * gr, axis=0)
    grad_out = jnp.einsum("tf,td->fd", gated, cot_all, preferred_element_type=f32)
    grad_out = lax.psum_scatter(grad_out, "dp", scatter_dimension=0, tiled=True)
    d_x, d_dt, d_bc, d_params = pull_mix(by_seq(d_y))
    d_project = jnp.concatenate(
        [
            d_z,
            d_x.reshape(n_own * length, chan),
            d_bc.reshape(n_own * length, 2 * NST),
            spread_head(d_dt.reshape(n_own * length, h_own).T).T,
        ],
        axis=1,
    ).astype(bf16)
    d_normed = lax.dot_general(
        d_project, w_in, (((1,), (1,)), ((), ())), preferred_element_type=f32
    ).astype(bf16)
    d_normed = lax.psum_scatter(
        d_normed.reshape(n_own, length, width), "seq", scatter_dimension=1, tiled=True
    ).astype(f32)
    grad_in = jnp.einsum("td,tf->df", normed_all, d_project, preferred_element_type=f32)
    grad_in = lax.psum_scatter(grad_in, "dp", scatter_dimension=0, tiled=True)
    grad_wide = grad_in[:, : 2 * chan].reshape(n_seq, in_rows, 2, n_dp, 1, rows)
    grad_wide = lax.all_to_all(grad_wide, "seq", split_axis=0, concat_axis=4, tiled=True)
    grad_wide = grad_wide.reshape(in_rows, 2 * DI)
    grad_tail = lax.psum_scatter(grad_in[:, 2 * chan :], "seq", scatter_dimension=0, tiled=True)
    grad_in = jnp.concatenate([grad_wide, grad_tail], axis=1)
    dn = d_normed * norm_gain
    along = jnp.mean(dn * hidden_f, axis=-1, keepdims=True)
    d_hidden = (
        cotangent.astype(f32) + inv * dn - (inv * inv * inv) * along * hidden_f
    ).astype(bf16)
    d_norm_gain = jnp.sum(d_normed * hidden_f * inv, axis=(0, 1))
    d_kernel_x, d_offset_x, d_kernel_bc, d_offset_bc, d_shift, d_decay, d_skip_part = d_params
    totals = lax.psum(
        (
            jnp.concatenate([spread_chan(d_kernel_x), d_kernel_bc], axis=0),
            jnp.concatenate([spread_chan(d_offset_x), d_offset_bc], axis=0),
            spread_head(d_shift),
            spread_head(d_decay),
            spread_head(d_skip_part),
            d_norm_gain,
            spread_chan(d_gate_gain),
        ),
        ("dp", "seq"),
    )
    return (result, d_hidden, grad_in) + tuple(totals) + (grad_out,)


def solution(mesh):
    whole_heads = (DI // mesh.size) % HDIM == 0
    shards = head_plan if whole_heads else general_plan
    placed = (
        P("dp", "seq", None),
        P("dp", "seq"),
        P(("dp", "seq"), None),
        P(),
        P(),
        P(),
        P(),
        P(),
        P(),
        P(),
        P(("dp", "seq"), None),
        P("dp", "seq", None),
    )
    return jax.shard_map(
        shards,
        mesh=mesh,
        in_specs=placed,
        out_specs=(
            P("dp", "seq", None),
            P("dp", "seq", None),
            P(("dp", "seq"), None),
            P(),
            P(),
            P(),
            P(),
            P(),
            P(),
            P(),
            P(("dp", "seq"), None),
        ),
        check_vma=False,
    )
```

```python
import functools

import jax
import jax.numpy as jnp
from jax import lax
from jax.experimental import pallas as pl
from jax.experimental.pallas import tpu as pltpu
from jax.sharding import PartitionSpec as P

HEADS = 64
HDIM = 64
NST = 128
GROUP = 256
CONV = 4
DI = 4096


def pre_norm(hidden_f, gain_vec):
    return (
        hidden_f
        * lax.rsqrt(jnp.mean(hidden_f * hidden_f, axis=-1, keepdims=True) + 1e-05)
        * gain_vec
    )


def gate_norm(y_values, gate_values, gain_vec):
    product = y_values * jax.nn.silu(gate_values)
    return (
        product * lax.rsqrt(jnp.mean(product * product, axis=-1, keepdims=True) + 1e-05) * gain_vec
    )


def conv_reset(signal, kernel, offset, seg_ids):
    tap_count = kernel.shape[1]
    summed = offset[None, :] + kernel[None, :, tap_count - 1] * signal
    for lag_steps in range(1, tap_count):
        shifted = jnp.pad(signal, ((lag_steps, 0), (0, 0)))[:-lag_steps]
        earlier = jnp.pad(seg_ids, (lag_steps, 0), constant_values=-1)[:-lag_steps]
        matches = (earlier == seg_ids).astype(jnp.float32)
        summed = summed + kernel[None, :, tap_count - 1 - lag_steps] * shifted * matches[:, None]
    return summed


def state_scan(values, deltas, rates, b_mat, c_mat, seg_ids):
    length, head_count, head_width = values.shape
    block_count = length // GROUP
    log_decay = deltas * rates[None, :]
    pieces = (
        values.reshape(block_count, GROUP, head_count, head_width),
        deltas.reshape(block_count, GROUP, head_count),
        log_decay.reshape(block_count, GROUP, head_count),
        b_mat.reshape(block_count, GROUP, b_mat.shape[-1]),
        c_mat.reshape(block_count, GROUP, c_mat.shape[-1]),
        seg_ids.reshape(block_count, GROUP),
    )
    position = lax.broadcasted_iota(jnp.int32, (GROUP, GROUP), 0)
    source = lax.broadcasted_iota(jnp.int32, (GROUP, GROUP), 1)

    def advance(carry, piece):
        memory, ending = carry
        block_vals, block_dt, block_log, b_block, c_block, seg_block = piece
        cumulative = jnp.cumsum(block_log, axis=0).T
        causal = (source <= position) & (seg_block[:, None] == seg_block[None, :])
        spread = cumulative[:, :, None] - cumulative[:, None, :]
        decays = jnp.where(causal[None], jnp.exp(jnp.where(causal[None], spread, 0.0)), 0.0)
        inner_prod = jnp.dot(c_block, b_block.T, precision=lax.Precision.HIGHEST)
        scores = inner_prod[None] * decays * block_dt.T[:, None, :]
        output = jnp.einsum("hij,jhp->ihp", scores, block_vals, precision=lax.Precision.HIGHEST)
        follows = (seg_block == ending).astype(jnp.float32)
        carried = jnp.einsum("in,hpn->ihp", c_block, memory, precision=lax.Precision.HIGHEST)
        output = output + (jnp.exp(cumulative).T * follows[:, None])[:, :, None] * carried
        last_seg = seg_block[-1]
        weights = (
            jnp.exp(cumulative[:, -1:] - cumulative)
            * (seg_block == last_seg).astype(jnp.float32)[None, :]
            * block_dt.T
        )
        keep_on = jnp.exp(cumulative[:, -1]) * (last_seg == ending).astype(jnp.float32)
        memory = memory * keep_on[:, None, None] + jnp.einsum(
            "hj,jhp,jn->hpn", weights, block_vals, b_block, precision=lax.Precision.HIGHEST
        )
        return ((memory, last_seg), output)

    initial = (
        jnp.zeros((head_count, head_width, b_mat.shape[-1]), jnp.float32),
        jnp.array(-1, jnp.int32),
    )
    unused, outputs = lax.scan(jax.checkpoint(advance), initial, pieces)
    return outputs.reshape(length, head_count, head_width)


def mixer(
    x_values,
    step_raw,
    bc_values,
    seg_ids,
    kernel_x,
    offset_x,
    kernel_bc,
    offset_bc,
    dt_shift,
    decay_log,
    skip_gain,
):
    x_conv = jax.nn.silu(conv_reset(x_values, kernel_x, offset_x, seg_ids))
    bc_conv = jax.nn.silu(conv_reset(bc_values, kernel_bc, offset_bc, seg_ids))
    step_sizes = jax.nn.softplus(step_raw + dt_shift[None, :])
    rates = -jnp.exp(decay_log)
    length = x_values.shape[0]
    head_count = step_raw.shape[1]
    shaped = x_conv.reshape(length, head_count, HDIM)
    mixed = (
        state_scan(shaped, step_sizes, rates, bc_conv[:, :NST], bc_conv[:, NST:], seg_ids)
        + skip_gain[None, :, None] * shaped
    )
    return mixed.reshape(length, head_count * HDIM)


def general_plan(
    hidden,
    segments,
    in_weight,
    conv_weight,
    conv_bias,
    dt_bias,
    a_log,
    d_skip,
    norm_gain,
    gate_gain,
    out_weight,
    cotangent,
):
    full_in, full_out = (
        lax.all_gather(in_weight, ("dp", "seq"), axis=0, tiled=True),
        lax.all_gather(out_weight, ("dp", "seq"), axis=0, tiled=True),
    )
    hidden_f = hidden.astype(jnp.float32)
    normed_f, pull_pre = jax.vjp(pre_norm, hidden_f, norm_gain)
    normed = normed_f.astype(jnp.bfloat16)
    project = jnp.einsum("mtd,df->mtf", normed, full_in, preferred_element_type=jnp.float32)
    gate_part = project[:, :, :DI]
    x_part = project[:, :, DI : 2 * DI].astype(jnp.bfloat16)
    bc_part = project[:, :, 2 * DI : 2 * DI + 2 * NST].astype(jnp.bfloat16)
    step_part = project[:, :, 2 * DI + 2 * NST :].astype(jnp.bfloat16)
    x_heads, step_heads = (
        lax.all_to_all(x_part, "seq", split_axis=2, concat_axis=1, tiled=True),
        lax.all_to_all(step_part, "seq", split_axis=2, concat_axis=1, tiled=True),
    )
    bc_full = lax.all_gather(bc_part, "seq", axis=1, tiled=True)
    seg_full = lax.all_gather(segments, "seq", axis=1, tiled=True)
    seq_rank = lax.axis_index("seq")
    head_local = step_heads.shape[2]
    chan_local = x_heads.shape[2]
    kernel_x = lax.dynamic_slice_in_dim(conv_weight, seq_rank * chan_local, chan_local, 0)
    offset_x = lax.dynamic_slice_in_dim(conv_bias, seq_rank * chan_local, chan_local, 0)
    shift_local = lax.dynamic_slice_in_dim(dt_bias, seq_rank * head_local, head_local, 0)
    decay_local = lax.dynamic_slice_in_dim(a_log, seq_rank * head_local, head_local, 0)
    skip_local = lax.dynamic_slice_in_dim(d_skip, seq_rank * head_local, head_local, 0)
    local_params = (
        kernel_x,
        offset_x,
        conv_weight[DI:],
        conv_bias[DI:],
        shift_local,
        decay_local,
        skip_local,
    )

    def head_mixer(x_values, step_raw, bc_values, params_in):

        def single_seq(x_one, step_one, bc_one, seg_one):
            return mixer(x_one, step_one, bc_one, seg_one, *params_in)

        return jax.vmap(single_seq)(x_values, step_raw, bc_values, seg_full)

    mixed, pull_mix = jax.vjp(
        head_mixer,
        x_heads.astype(jnp.float32),
        step_heads.astype(jnp.float32),
        bc_full.astype(jnp.float32),
        local_params,
    )
    y_tokens = lax.all_to_all(
        mixed.astype(jnp.bfloat16), "seq", split_axis=1, concat_axis=2, tiled=True
    )
    gated_f, pull_gate = jax.vjp(gate_norm, y_tokens.astype(jnp.float32), gate_part, gate_gain)
    gated = gated_f.astype(jnp.bfloat16)
    branch_out = jnp.einsum("mtf,fd->mtd", gated, full_out, preferred_element_type=jnp.float32)
    result = (hidden_f + branch_out).astype(jnp.bfloat16)
    d_gated = jnp.einsum("mtd,fd->mtf", cotangent, full_out, preferred_element_type=jnp.float32)
    d_mixed, d_gate_part, d_gate_gain = pull_gate(d_gated)
    d_heads = lax.all_to_all(
        d_mixed.astype(jnp.bfloat16), "seq", split_axis=2, concat_axis=1, tiled=True
    )
    d_x_heads, d_step_heads, d_bc_full, d_params = pull_mix(d_heads.astype(jnp.float32))
    d_x_part, d_step_part = (
        lax.all_to_all(
            d_x_heads.astype(jnp.bfloat16), "seq", split_axis=1, concat_axis=2, tiled=True
        ),
        lax.all_to_all(
            d_step_heads.astype(jnp.bfloat16), "seq", split_axis=1, concat_axis=2, tiled=True
        ),
    )
    d_bc_part = lax.psum_scatter(
        d_bc_full.astype(jnp.bfloat16), "seq", scatter_dimension=1, tiled=True
    )
    d_project = jnp.concatenate(
        [d_gate_part.astype(jnp.bfloat16), d_x_part, d_bc_part, d_step_part], axis=2
    )
    d_normed = jnp.einsum("mtf,df->mtd", d_project, full_in, preferred_element_type=jnp.float32)
    d_hidden_f, d_norm_gain = pull_pre(d_normed)
    d_hidden = (cotangent.astype(jnp.float32) + d_hidden_f).astype(jnp.bfloat16)
    in_rows = in_weight.shape[0]
    out_rows = out_weight.shape[0]
    column_ranges = ((0, DI), (DI, d_project.shape[2]))
    in_pieces = [jnp.zeros((in_rows, upper - lower), jnp.float32) for lower, upper in column_ranges]
    grad_out = jnp.zeros(out_weight.shape, jnp.float32)
    for batch_index in range(hidden.shape[0]):
        for range_index in range(len(column_ranges)):
            lower, upper = column_ranges[range_index]

            def in_term(
                start,
                count,
                normed_one=normed[batch_index],
                d_one=d_project[batch_index, :, lower:upper],
            ):
                return lax.dot_general(
                    normed_one, d_one, (((0,), (0,)), ((), ())), preferred_element_type=jnp.float32
                )

            in_pieces[range_index] = in_pieces[range_index] + lax.psum_scatter(
                in_term(jnp.int32(0), in_rows * lax.axis_size(("dp", "seq"))),
                ("dp", "seq"),
                scatter_dimension=0,
                tiled=True,
            )

        def out_term(start, count, gated_one=gated[batch_index], cot_one=cotangent[batch_index]):
            return lax.dot_general(
                gated_one, cot_one, (((0,), (0,)), ((), ())), preferred_element_type=jnp.float32
            )

        grad_out = grad_out + lax.psum_scatter(
            out_term(jnp.int32(0), out_rows * lax.axis_size(("dp", "seq"))),
            ("dp", "seq"),
            scatter_dimension=0,
            tiled=True,
        )
    grad_in = jnp.concatenate(in_pieces, axis=1)
    d_kernel_x, d_offset_x, d_kernel_bc, d_offset_bc, d_shift, d_decay, d_skip_part = d_params
    tap_count = conv_weight.shape[1]
    grad_conv_w = jnp.concatenate(
        [
            lax.dynamic_update_slice_in_dim(
                jnp.zeros((DI, tap_count), jnp.float32), d_kernel_x, seq_rank * chan_local, 0
            ),
            d_kernel_bc,
        ],
        axis=0,
    )
    grad_conv_b = jnp.concatenate(
        [
            lax.dynamic_update_slice_in_dim(
                jnp.zeros((DI,), jnp.float32), d_offset_x, seq_rank * chan_local, 0
            ),
            d_offset_bc,
        ],
        axis=0,
    )
    grad_shift = lax.dynamic_update_slice_in_dim(
        jnp.zeros((HEADS,), jnp.float32), d_shift, seq_rank * head_local, 0
    )
    grad_decay = lax.dynamic_update_slice_in_dim(
        jnp.zeros((HEADS,), jnp.float32), d_decay, seq_rank * head_local, 0
    )
    grad_skip = lax.dynamic_update_slice_in_dim(
        jnp.zeros((HEADS,), jnp.float32), d_skip_part, seq_rank * head_local, 0
    )
    totals = lax.psum(
        (grad_conv_w, grad_conv_b, grad_shift, grad_decay, grad_skip, d_norm_gain, d_gate_gain),
        ("dp", "seq"),
    )
    return (
        result,
        d_hidden,
        grad_in,
        totals[0],
        totals[1],
        totals[2],
        totals[3],
        totals[4],
        totals[5],
        totals[6],
        grad_out,
    )


LOG2E = 1.4426950408889634
TILE = 128
FAR = -1e30


def shift_rows(v, lag):
    return v if lag == 0 else pltpu.roll(v, lag % v.shape[0], axis=0)


def conv_silu(sig, taps, offset, keep):
    total = offset + taps[CONV - 1 : CONV] * sig
    for lag in range(1, CONV):
        total = total + taps[CONV - 1 - lag : CONV - lag] * (shift_rows(sig, lag) * keep[lag])
    gate = jax.nn.sigmoid(total)
    return total, gate, total * gate


def conv_back(d_out, total, gate, sig, taps, keep):
    d_total = d_out * (gate * (1.0 + total * (1.0 - gate)))
    d_sig = taps[CONV - 1 : CONV] * d_total
    tap_rows = [jnp.sum(d_total * sig, axis=0, keepdims=True)]
    for lag in range(1, CONV):
        kept = d_total * keep[lag]
        d_sig = d_sig + taps[CONV - 1 - lag : CONV - lag] * shift_rows(kept, -lag)
        tap_rows.append(jnp.sum(kept * shift_rows(sig, lag), axis=0, keepdims=True))
    return d_sig, tap_rows[::-1], jnp.sum(d_total, axis=0, keepdims=True)


def keep_masks(seg_col):
    length = seg_col.shape[0]
    row = lax.broadcasted_iota(jnp.int32, (length, 1), 0)
    masks = [None]
    for lag in range(1, CONV):
        same = (pltpu.roll(seg_col, lag, axis=0) == seg_col) & (row >= lag)
        masks.append(same.astype(jnp.float32))
    return masks


def lane_sums(v, reverse):
    length = v.shape[1]
    lane = lax.broadcasted_iota(jnp.int32, v.shape, 1)
    step = 1
    while step < length:
        if reverse:
            v = v + jnp.where(lane < length - step, pltpu.roll(v, length - step, axis=1), 0.0)
        else:
            v = v + jnp.where(lane >= step, pltpu.roll(v, step, axis=1), 0.0)
        step *= 2
    return v


def step_sizes_of(dt_all, head_rows, h_own, n_seq, heads_row):
    rank = lax.axis_index("seq")
    all_heads = dt_all.shape[1]
    lane = lax.broadcasted_iota(jnp.int32, (all_heads, 128), 1)
    row = lax.broadcasted_iota(jnp.int32, (all_heads, 128), 0)
    head = ((lane // heads_row) * n_seq + rank) * heads_row + lane % heads_row
    pick = ((row == head) & (lane < h_own)).astype(jnp.bfloat16)
    raw = jnp.dot(dt_all, pick, preferred_element_type=jnp.float32)
    shifted = raw + head_rows[0:1]
    dt = jnp.maximum(shifted, 0.0) + jnp.log1p(jnp.exp(-jnp.abs(shifted)))
    return shifted, dt


def head_prep(dt_all, head_rows, h_own, n_seq, heads_row, dt_cols, cum_cols, cum_rows):
    shifted, dt = step_sizes_of(dt_all, head_rows, h_own, n_seq, heads_row)
    rates = -jnp.exp(head_rows[1:2])
    step_log = dt * (rates * LOG2E)
    across = jnp.transpose(step_log)
    cum_t = lane_sums(across[:h_own], False)
    pad = jnp.zeros((128 - h_own, cum_t.shape[1]), jnp.float32)
    cum = jnp.transpose(jnp.concatenate([cum_t, pad], axis=0))
    for k in range(h_own):
        dt_cols[k] = dt[:, k : k + 1]
        cum_cols[k] = cum[:, k : k + 1]
        cum_rows[k] = cum_t[k : k + 1, :]
    return shifted, dt


def pair_wide(cols, pair):
    length = cols.shape[1]
    lane = lax.broadcasted_iota(jnp.int32, (length, 128), 1)
    return jnp.where(lane < HDIM, cols[2 * pair], cols[2 * pair + 1])


def scan_forward(h_own, n_seq, heads_row, x_ref, bc_ref, dt_ref, segc_ref, segr_ref, wx_ref, wbc_ref,
                 head_ref, y_ref, inner_ref, dt_cols, cum_cols, cum_rows, inner_prod, bias):
    pair = pl.program_id(1)
    length = x_ref.shape[0]
    seg_col = segc_ref[0]
    keep = keep_masks(seg_col)

    @pl.when(pair == 0)
    def prepare():
        head_prep(dt_ref[...], head_ref[...], h_own, n_seq, heads_row, dt_cols, cum_cols, cum_rows)
        _, _, bc = conv_silu(bc_ref[...].astype(jnp.float32), wbc_ref[0:CONV], wbc_ref[CONV : CONV + 1], keep)
        inner_prod[...] = lax.dot_general(
            bc[:, NST:], bc[:, :NST], (((1,), (1,)), ((), ())),
            precision=lax.Precision.HIGHEST, preferred_element_type=jnp.float32,
        )
        at = lax.broadcasted_iota(jnp.int32, (length, length), 0)
        source = lax.broadcasted_iota(jnp.int32, (length, length), 1)
        bias[...] = jnp.where((source <= at) & (seg_col == segr_ref[0]), 0.0, FAR)

    _, _, xc = conv_silu(x_ref[...].astype(jnp.float32), wx_ref[0:CONV], wx_ref[CONV : CONV + 1], keep)
    moved = (xc * pair_wide(dt_cols, pair)).astype(jnp.bfloat16)
    skip = wx_ref[CONV + 1 : CONV + 2]
    first = lax.broadcasted_iota(jnp.int32, (TILE, 128), 1) < HDIM
    for block in range(length // TILE):
        rows, wide = slice(block * TILE, (block + 1) * TILE), (block + 1) * TILE
        halves = []
        for half in range(2):
            head = 2 * pair + half
            decay = jnp.exp2(cum_cols[head, rows] - cum_rows[head, :, :wide] + bias[rows, :wide])
            scores = (inner_prod[rows, :wide] * decay).astype(jnp.bfloat16)
            halves.append(jnp.dot(scores, moved[:wide], preferred_element_type=jnp.float32))
        inner = jnp.where(first, halves[0], halves[1])
        inner_ref[rows] = inner
        y_ref[rows] = (inner + skip * xc[rows]).astype(jnp.bfloat16)


def scan_backward(h_own, n_seq, heads_row, x_ref, bc_ref, dt_ref, segc_ref, segr_ref, wx_ref, wbc_ref,
                  head_ref, dy_ref, inner_ref, dx_ref, dbc_ref, ddt_ref, gx_ref, gbc_ref, gh_ref,
                  dt_cols, cum_cols, cum_rows, inner_prod, bias, d_inner, d_cum, d_dt):
    pair = pl.program_id(1)
    n_pair = pl.num_programs(1)
    length = x_ref.shape[0]
    seg_col = segc_ref[0]
    keep = keep_masks(seg_col)
    f32, bf16 = jnp.float32, jnp.bfloat16

    @pl.when(pair == 0)
    def prepare():
        head_prep(dt_ref[...], head_ref[...], h_own, n_seq, heads_row, dt_cols, cum_cols, cum_rows)
        _, _, bc = conv_silu(bc_ref[...].astype(f32), wbc_ref[0:CONV], wbc_ref[CONV : CONV + 1], keep)
        inner_prod[...] = lax.dot_general(
            bc[:, :NST], bc[:, NST:], (((1,), (1,)), ((), ())),
            precision=lax.Precision.HIGHEST, preferred_element_type=f32,
        )
        source = lax.broadcasted_iota(jnp.int32, (length, length), 0)
        at = lax.broadcasted_iota(jnp.int32, (length, length), 1)
        bias[...] = jnp.where((source <= at) & (seg_col == segr_ref[0]), 0.0, FAR)
        d_inner[...] = jnp.zeros((length, length), f32)
        d_cum[...] = jnp.zeros((length, 128), f32)
        d_dt[...] = jnp.zeros((length, 128), f32)

    x_in = x_ref[...].astype(f32)
    taps = wx_ref[0:CONV]
    total, gate, xc = conv_silu(x_in, taps, wx_ref[CONV : CONV + 1], keep)
    dt_wide = pair_wide(dt_cols, pair)
    moved = (xc * dt_wide).astype(bf16)
    skip = wx_ref[CONV + 1 : CONV + 2]
    dy = dy_ref[...]
    first = lax.broadcasted_iota(jnp.int32, (TILE, 128), 1) < HDIM
    pieces = []
    for block in range(length // TILE):
        rows, later = slice(block * TILE, (block + 1) * TILE), slice(block * TILE, length)
        halves = []
        for half in range(2):
            head = 2 * pair + half
            decay = jnp.exp2(cum_rows[head, :, later] - cum_cols[head, rows] + bias[rows, later])
            scores = (inner_prod[rows, later] * decay).astype(bf16)
            halves.append(jnp.dot(scores, dy[later], preferred_element_type=f32))
            mine = jnp.where(first if half == 0 else ~first, moved[rows].astype(f32), 0.0).astype(bf16)
            d_scores = lax.dot_general(
                mine, dy[later], (((1,), (1,)), ((), ())), preferred_element_type=f32
            )
            d_inner[rows, later] += d_scores * decay
        pieces.append(jnp.where(first, halves[0], halves[1]))
    d_moved = jnp.concatenate(pieces, axis=0)
    dy_f = dy.astype(f32)
    change = dy_f * inner_ref[...] - moved.astype(f32) * d_moved
    direct = d_moved * xc
    lane = lax.broadcasted_iota(jnp.int32, (length, 128), 1)
    low = lane < HDIM
    for half in range(2):
        mine = low if half == 0 else ~low
        place = lane == 2 * pair + half
        d_cum[...] += jnp.where(place, jnp.sum(jnp.where(mine, change, 0.0), axis=1, keepdims=True), 0.0)
        d_dt[...] += jnp.where(place, jnp.sum(jnp.where(mine, direct, 0.0), axis=1, keepdims=True), 0.0)
    d_xc = d_moved * dt_wide + skip * dy_f
    d_x, tap_rows, d_offset = conv_back(d_xc, total, gate, x_in, taps, keep)
    dx_ref[...] = d_x.astype(bf16)
    d_skip = jnp.sum(dy_f * xc, axis=0, keepdims=True)
    blank = jnp.zeros((2, 128), f32)
    gx_ref[0] = jnp.concatenate(tap_rows + [d_offset, d_skip, blank], axis=0)

    @pl.when(pair == n_pair - 1)
    def finish():
        bc_in = bc_ref[...].astype(f32)
        taps_bc = wbc_ref[0:CONV]
        total_bc, gate_bc, bc = conv_silu(bc_in, taps_bc, wbc_ref[CONV : CONV + 1], keep)
        d_in = d_inner[...]
        d_b = jnp.dot(d_in, bc[:, NST:], precision=lax.Precision.HIGHEST, preferred_element_type=f32)
        d_c = lax.dot_general(
            d_in, bc[:, :NST], (((0,), (0,)), ((), ())),
            precision=lax.Precision.HIGHEST, preferred_element_type=f32,
        )
        d_bc, rows_bc, offset_bc = conv_back(
            jnp.concatenate([d_b, d_c], axis=1), total_bc, gate_bc, bc_in, taps_bc, keep
        )
        dbc_ref[...] = d_bc.astype(bf16)
        gbc_ref[0] = jnp.concatenate(rows_bc + [offset_bc, jnp.zeros((3, 2 * NST), f32)], axis=0)
        shifted, dt = step_sizes_of(dt_ref[...], head_ref[...], h_own, n_seq, heads_row)
        rates = -jnp.exp(head_ref[1:2])
        across = jnp.transpose(d_cum[...])
        d_log_t = lane_sums(across[:h_own], True)
        pad = jnp.zeros((128 - h_own, length), f32)
        d_log = jnp.transpose(jnp.concatenate([d_log_t, pad], axis=0))
        d_raw = (d_log * rates + d_dt[...]) * jax.nn.sigmoid(shifted)
        ddt_ref[...] = d_raw
        gh_ref[0] = jnp.concatenate(
            [
                jnp.sum(d_raw, axis=0, keepdims=True),
                jnp.sum(d_log * dt, axis=0, keepdims=True) * rates,
                jnp.zeros((6, 128), f32),
            ],
            axis=0,
        )


def scan_specs(length, all_heads):
    return [
        pl.BlockSpec((length, 128), lambda q, p: (q, p)),
        pl.BlockSpec((length, 2 * NST), lambda q, p: (q, 0)),
        pl.BlockSpec((length, all_heads), lambda q, p: (q, 0)),
        pl.BlockSpec((1, length, 1), lambda q, p: (q, 0, 0)),
        pl.BlockSpec((1, 1, length), lambda q, p: (q, 0, 0)),
        pl.BlockSpec((8, 128), lambda q, p: (0, p)),
        pl.BlockSpec((8, 2 * NST), lambda q, p: (0, 0)),
        pl.BlockSpec((8, 128), lambda q, p: (0, 0)),
    ]


def scan_scratch(length, h_own):
    f32 = jnp.float32
    return [
        pltpu.VMEM((h_own, length, 1), f32),
        pltpu.VMEM((h_own, length, 1), f32),
        pltpu.VMEM((h_own, 1, length), f32),
        pltpu.VMEM((length, length), f32),
        pltpu.VMEM((length, length), f32),
    ]


def run_forward(n_own, h_own, n_seq, heads_row, operands):
    tokens, chan = operands[0].shape
    length = tokens // n_own
    pair_block = pl.BlockSpec((length, 128), lambda q, p: (q, p))
    return pl.pallas_call(
        functools.partial(scan_forward, h_own, n_seq, heads_row),
        grid=(n_own, chan // 128),
        in_specs=scan_specs(length, operands[2].shape[1]),
        out_specs=[pair_block, pair_block],
        out_shape=[
            jax.ShapeDtypeStruct((tokens, chan), jnp.bfloat16),
            jax.ShapeDtypeStruct((tokens, chan), jnp.float32),
        ],
        scratch_shapes=scan_scratch(length, h_own),
        compiler_params=pltpu.CompilerParams(vmem_limit_bytes=48 << 20),
        name="scan_forward",
    )(*operands)


def run_backward(n_own, h_own, n_seq, heads_row, operands, d_y, inner):
    f32 = jnp.float32
    tokens, chan = operands[0].shape
    length = tokens // n_own
    pair_block = pl.BlockSpec((length, 128), lambda q, p: (q, p))
    return pl.pallas_call(
        functools.partial(scan_backward, h_own, n_seq, heads_row),
        grid=(n_own, chan // 128),
        in_specs=scan_specs(length, operands[2].shape[1]) + [pair_block, pair_block],
        out_specs=[
            pair_block,
            pl.BlockSpec((length, 2 * NST), lambda q, p: (q, 0)),
            pl.BlockSpec((length, 128), lambda q, p: (q, 0)),
            pl.BlockSpec((1, 8, 128), lambda q, p: (q, 0, p)),
            pl.BlockSpec((1, 8, 2 * NST), lambda q, p: (q, 0, 0)),
            pl.BlockSpec((1, 8, 128), lambda q, p: (q, 0, 0)),
        ],
        out_shape=[
            jax.ShapeDtypeStruct((tokens, chan), jnp.bfloat16),
            jax.ShapeDtypeStruct((tokens, 2 * NST), jnp.bfloat16),
            jax.ShapeDtypeStruct((tokens, 128), f32),
            jax.ShapeDtypeStruct((n_own, 8, chan), f32),
            jax.ShapeDtypeStruct((n_own, 8, 2 * NST), f32),
            jax.ShapeDtypeStruct((n_own, 8, 128), f32),
        ],
        scratch_shapes=scan_scratch(length, h_own)
        + [
            pltpu.VMEM((length, length), f32),
            pltpu.VMEM((length, 128), f32),
            pltpu.VMEM((length, 128), f32),
        ],
        compiler_params=pltpu.CompilerParams(vmem_limit_bytes=56 << 20),
        name="scan_backward",
    )(*operands, d_y, inner)


def head_plan(
    hidden,
    segments,
    in_weight,
    conv_weight,
    conv_bias,
    dt_bias,
    a_log,
    d_skip,
    norm_gain,
    gate_gain,
    out_weight,
    cotangent,
):
    f32, bf16 = jnp.float32, jnp.bfloat16
    n_dp, n_seq = lax.axis_size("dp"), lax.axis_size("seq")
    seq_rank = lax.axis_index("seq")
    n_own, shard_len, width = hidden.shape
    length = shard_len * n_seq
    rows = out_weight.shape[0]
    in_rows = in_weight.shape[0]
    chan = rows * n_dp
    h_own = chan // HDIM
    hidden_f = hidden.astype(f32)
    inv = lax.rsqrt(jnp.mean(hidden_f * hidden_f, axis=-1, keepdims=True) + 1e-05)
    normed = (hidden_f * inv * norm_gain).astype(bf16)
    normed_all = lax.all_gather(normed, "seq", axis=1, tiled=True).reshape(n_own * length, width)
    wide = in_weight[:, : 2 * DI].reshape(in_rows, 2, n_dp, n_seq, rows)
    wide = lax.all_to_all(wide, "seq", split_axis=3, concat_axis=0, tiled=True)
    wide = wide.reshape(n_seq * in_rows, 2 * chan)
    tail = lax.all_gather(in_weight[:, 2 * DI :], "seq", axis=0, tiled=True)
    w_in = lax.all_gather(jnp.concatenate([wide, tail], axis=1), "dp", axis=0, tiled=True)
    w_out = lax.all_gather(out_weight, "dp", axis=0, tiled=True)
    cot_all = lax.all_gather(cotangent, "seq", axis=1, tiled=True).reshape(n_own * length, width)
    seg_all = lax.all_gather(segments, "seq", axis=1, tiled=True)

    def own_chan(vec):
        return lax.dynamic_index_in_dim(
            vec.reshape((n_dp, n_seq, rows) + vec.shape[1:]), seq_rank, 1, keepdims=False
        ).reshape((chan,) + vec.shape[1:])

    heads_row = rows // HDIM

    def own_head(vec):
        return lax.dynamic_index_in_dim(
            vec.reshape((n_dp, n_seq, heads_row) + vec.shape[1:]), seq_rank, 1, keepdims=False
        ).reshape((h_own,) + vec.shape[1:])

    def spread_chan(vec):
        blank = jnp.zeros((n_dp, n_seq, rows) + vec.shape[1:], f32)
        piece = vec.reshape((n_dp, 1, rows) + vec.shape[1:])
        return lax.dynamic_update_slice_in_dim(blank, piece, seq_rank, 1).reshape(
            (DI,) + vec.shape[1:]
        )

    def spread_head(vec):
        blank = jnp.zeros((n_dp, n_seq, heads_row) + vec.shape[1:], f32)
        piece = vec.reshape((n_dp, 1, heads_row) + vec.shape[1:])
        return lax.dynamic_update_slice_in_dim(blank, piece, seq_rank, 1).reshape(
            (HEADS,) + vec.shape[1:]
        )

    project = jnp.dot(normed_all, w_in, preferred_element_type=f32)
    z = project[:, :chan]
    x_raw = project[:, chan : 2 * chan].astype(bf16)
    bc_raw = project[:, 2 * chan : 2 * chan + 2 * NST].astype(bf16)
    dt_all = project[:, 2 * chan + 2 * NST :].astype(bf16)
    wx = jnp.concatenate(
        [
            own_chan(conv_weight[:DI]).T,
            own_chan(conv_bias[:DI])[None],
            jnp.repeat(own_head(d_skip), HDIM)[None],
            jnp.zeros((2, chan), f32),
        ],
        axis=0,
    )
    wbc = jnp.concatenate(
        [conv_weight[DI:].T, conv_bias[DI:][None], jnp.zeros((3, 2 * NST), f32)], axis=0
    )
    head_vals = jnp.pad(jnp.stack([own_head(dt_bias), own_head(a_log)]), ((0, 6), (0, 128 - h_own)))
    operands = (x_raw, bc_raw, dt_all, seg_all[:, :, None], seg_all[:, None, :], wx, wbc, head_vals)
    y, inner = run_forward(n_own, h_own, n_seq, heads_row, operands)
    y = y.astype(f32)
    gain = own_chan(gate_gain)
    sig = jax.nn.sigmoid(z)
    act = z * sig
    g = y * act
    d_gated = lax.dot_general(
        cot_all, w_out, (((1,), (1,)), ((), ())), preferred_element_type=f32
    )
    u = d_gated * gain
    sums = lax.psum(jnp.stack([jnp.sum(g * g, axis=1), jnp.sum(u * g, axis=1)]), "seq")
    r = lax.rsqrt(sums[0] / DI + 1e-05)[:, None]
    fall = (r * r * r) * (sums[1] / DI)[:, None]
    gr = g * r
    gated = (gr * gain).astype(bf16)
    part = jnp.dot(gated, w_out, preferred_element_type=f32).astype(bf16)
    branch = lax.psum_scatter(
        part.reshape(n_own, length, width), "seq", scatter_dimension=1, tiled=True
    )
    result = (hidden_f + branch.astype(f32)).astype(bf16)
    d_g = r * u - fall * g
    d_y = (d_g * act).astype(bf16)
    d_z = d_g * y * (sig * (1.0 + z * (1.0 - sig)))
    d_gate_gain = jnp.sum(d_gated * gr, axis=0)
    grad_out = jnp.einsum("tf,td->fd", gated, cot_all, preferred_element_type=f32)
    grad_out = lax.psum_scatter(grad_out, "dp", scatter_dimension=0, tiled=True)
    d_x, d_bc, d_dt, g_x, g_bc, g_head = run_backward(
        n_own, h_own, n_seq, heads_row, operands, d_y, inner
    )
    g_x, g_bc, g_head = jnp.sum(g_x, 0), jnp.sum(g_bc, 0), jnp.sum(g_head, 0)
    d_project = jnp.concatenate(
        [
            d_z.astype(bf16),
            d_x,
            d_bc,
            spread_head(d_dt[:, :h_own].T).T.astype(bf16),
        ],
        axis=1,
    )
    d_normed = lax.dot_general(
        d_project, w_in, (((1,), (1,)), ((), ())), preferred_element_type=f32
    ).astype(bf16)
    d_normed = lax.psum_scatter(
        d_normed.reshape(n_own, length, width), "seq", scatter_dimension=1, tiled=True
    ).astype(f32)
    grad_in = jnp.einsum("td,tf->df", normed_all, d_project, preferred_element_type=f32)
    grad_in = lax.psum_scatter(grad_in, "dp", scatter_dimension=0, tiled=True)
    grad_wide = grad_in[:, : 2 * chan].reshape(n_seq, in_rows, 2, n_dp, 1, rows)
    grad_wide = lax.all_to_all(grad_wide, "seq", split_axis=0, concat_axis=4, tiled=True)
    grad_wide = grad_wide.reshape(in_rows, 2 * DI)
    grad_tail = lax.psum_scatter(grad_in[:, 2 * chan :], "seq", scatter_dimension=0, tiled=True)
    grad_in = jnp.concatenate([grad_wide, grad_tail], axis=1)
    dn = d_normed * norm_gain
    along = jnp.mean(dn * hidden_f, axis=-1, keepdims=True)
    d_hidden = (
        cotangent.astype(f32) + inv * dn - (inv * inv * inv) * along * hidden_f
    ).astype(bf16)
    d_norm_gain = jnp.sum(d_normed * hidden_f * inv, axis=(0, 1))
    totals = lax.psum(
        (
            jnp.concatenate([spread_chan(g_x[:CONV].T), g_bc[:CONV].T], axis=0),
            jnp.concatenate([spread_chan(g_x[CONV]), g_bc[CONV]], axis=0),
            spread_head(g_head[0, :h_own]),
            spread_head(g_head[1, :h_own]),
            spread_head(jnp.sum(g_x[CONV + 1].reshape(h_own, HDIM), axis=1)),
            d_norm_gain,
            spread_chan(d_gate_gain),
        ),
        ("dp", "seq"),
    )
    return (result, d_hidden, grad_in) + tuple(totals) + (grad_out,)


def solution(mesh):
    whole_heads = (DI // mesh.size) % HDIM == 0
    shards = head_plan if whole_heads else general_plan
    placed = (
        P("dp", "seq", None),
        P("dp", "seq"),
        P(("dp", "seq"), None),
        P(),
        P(),
        P(),
        P(),
        P(),
        P(),
        P(),
        P(("dp", "seq"), None),
        P("dp", "seq", None),
    )
    return jax.shard_map(
        shards,
        mesh=mesh,
        in_specs=placed,
        out_specs=(
            P("dp", "seq", None),
            P("dp", "seq", None),
            P(("dp", "seq"), None),
            P(),
            P(),
            P(),
            P(),
            P(),
            P(),
            P(),
            P(("dp", "seq"), None),
        ),
        check_vma=False,
    )
```

```python
import functools

import jax
import jax.numpy as jnp
from jax import lax
from jax.experimental import pallas as pl
from jax.experimental.pallas import tpu as pltpu
from jax.sharding import PartitionSpec as P

HEADS = 64
HDIM = 64
NST = 128
GROUP = 256
CONV = 4
DI = 4096


def pre_norm(hidden_f, gain_vec):
    return (
        hidden_f
        * lax.rsqrt(jnp.mean(hidden_f * hidden_f, axis=-1, keepdims=True) + 1e-05)
        * gain_vec
    )


def gate_norm(y_values, gate_values, gain_vec):
    product = y_values * jax.nn.silu(gate_values)
    return (
        product * lax.rsqrt(jnp.mean(product * product, axis=-1, keepdims=True) + 1e-05) * gain_vec
    )


def conv_reset(signal, kernel, offset, seg_ids):
    tap_count = kernel.shape[1]
    summed = offset[None, :] + kernel[None, :, tap_count - 1] * signal
    for lag_steps in range(1, tap_count):
        shifted = jnp.pad(signal, ((lag_steps, 0), (0, 0)))[:-lag_steps]
        earlier = jnp.pad(seg_ids, (lag_steps, 0), constant_values=-1)[:-lag_steps]
        matches = (earlier == seg_ids).astype(jnp.float32)
        summed = summed + kernel[None, :, tap_count - 1 - lag_steps] * shifted * matches[:, None]
    return summed


def state_scan(values, deltas, rates, b_mat, c_mat, seg_ids):
    length, head_count, head_width = values.shape
    block_count = length // GROUP
    log_decay = deltas * rates[None, :]
    pieces = (
        values.reshape(block_count, GROUP, head_count, head_width),
        deltas.reshape(block_count, GROUP, head_count),
        log_decay.reshape(block_count, GROUP, head_count),
        b_mat.reshape(block_count, GROUP, b_mat.shape[-1]),
        c_mat.reshape(block_count, GROUP, c_mat.shape[-1]),
        seg_ids.reshape(block_count, GROUP),
    )
    position = lax.broadcasted_iota(jnp.int32, (GROUP, GROUP), 0)
    source = lax.broadcasted_iota(jnp.int32, (GROUP, GROUP), 1)

    def advance(carry, piece):
        memory, ending = carry
        block_vals, block_dt, block_log, b_block, c_block, seg_block = piece
        cumulative = jnp.cumsum(block_log, axis=0).T
        causal = (source <= position) & (seg_block[:, None] == seg_block[None, :])
        spread = cumulative[:, :, None] - cumulative[:, None, :]
        decays = jnp.where(causal[None], jnp.exp(jnp.where(causal[None], spread, 0.0)), 0.0)
        inner_prod = jnp.dot(c_block, b_block.T, precision=lax.Precision.HIGHEST)
        scores = inner_prod[None] * decays * block_dt.T[:, None, :]
        output = jnp.einsum("hij,jhp->ihp", scores, block_vals, precision=lax.Precision.HIGHEST)
        follows = (seg_block == ending).astype(jnp.float32)
        carried = jnp.einsum("in,hpn->ihp", c_block, memory, precision=lax.Precision.HIGHEST)
        output = output + (jnp.exp(cumulative).T * follows[:, None])[:, :, None] * carried
        last_seg = seg_block[-1]
        weights = (
            jnp.exp(cumulative[:, -1:] - cumulative)
            * (seg_block == last_seg).astype(jnp.float32)[None, :]
            * block_dt.T
        )
        keep_on = jnp.exp(cumulative[:, -1]) * (last_seg == ending).astype(jnp.float32)
        memory = memory * keep_on[:, None, None] + jnp.einsum(
            "hj,jhp,jn->hpn", weights, block_vals, b_block, precision=lax.Precision.HIGHEST
        )
        return ((memory, last_seg), output)

    initial = (
        jnp.zeros((head_count, head_width, b_mat.shape[-1]), jnp.float32),
        jnp.array(-1, jnp.int32),
    )
    unused, outputs = lax.scan(jax.checkpoint(advance), initial, pieces)
    return outputs.reshape(length, head_count, head_width)


def mixer(
    x_values,
    step_raw,
    bc_values,
    seg_ids,
    kernel_x,
    offset_x,
    kernel_bc,
    offset_bc,
    dt_shift,
    decay_log,
    skip_gain,
):
    x_conv = jax.nn.silu(conv_reset(x_values, kernel_x, offset_x, seg_ids))
    bc_conv = jax.nn.silu(conv_reset(bc_values, kernel_bc, offset_bc, seg_ids))
    step_sizes = jax.nn.softplus(step_raw + dt_shift[None, :])
    rates = -jnp.exp(decay_log)
    length = x_values.shape[0]
    head_count = step_raw.shape[1]
    shaped = x_conv.reshape(length, head_count, HDIM)
    mixed = (
        state_scan(shaped, step_sizes, rates, bc_conv[:, :NST], bc_conv[:, NST:], seg_ids)
        + skip_gain[None, :, None] * shaped
    )
    return mixed.reshape(length, head_count * HDIM)


def general_plan(
    hidden,
    segments,
    in_weight,
    conv_weight,
    conv_bias,
    dt_bias,
    a_log,
    d_skip,
    norm_gain,
    gate_gain,
    out_weight,
    cotangent,
):
    full_in, full_out = (
        lax.all_gather(in_weight, ("dp", "seq"), axis=0, tiled=True),
        lax.all_gather(out_weight, ("dp", "seq"), axis=0, tiled=True),
    )
    hidden_f = hidden.astype(jnp.float32)
    normed_f, pull_pre = jax.vjp(pre_norm, hidden_f, norm_gain)
    normed = normed_f.astype(jnp.bfloat16)
    project = jnp.einsum("mtd,df->mtf", normed, full_in, preferred_element_type=jnp.float32)
    gate_part = project[:, :, :DI]
    x_part = project[:, :, DI : 2 * DI].astype(jnp.bfloat16)
    bc_part = project[:, :, 2 * DI : 2 * DI + 2 * NST].astype(jnp.bfloat16)
    step_part = project[:, :, 2 * DI + 2 * NST :].astype(jnp.bfloat16)
    x_heads, step_heads = (
        lax.all_to_all(x_part, "seq", split_axis=2, concat_axis=1, tiled=True),
        lax.all_to_all(step_part, "seq", split_axis=2, concat_axis=1, tiled=True),
    )
    bc_full = lax.all_gather(bc_part, "seq", axis=1, tiled=True)
    seg_full = lax.all_gather(segments, "seq", axis=1, tiled=True)
    seq_rank = lax.axis_index("seq")
    head_local = step_heads.shape[2]
    chan_local = x_heads.shape[2]
    kernel_x = lax.dynamic_slice_in_dim(conv_weight, seq_rank * chan_local, chan_local, 0)
    offset_x = lax.dynamic_slice_in_dim(conv_bias, seq_rank * chan_local, chan_local, 0)
    shift_local = lax.dynamic_slice_in_dim(dt_bias, seq_rank * head_local, head_local, 0)
    decay_local = lax.dynamic_slice_in_dim(a_log, seq_rank * head_local, head_local, 0)
    skip_local = lax.dynamic_slice_in_dim(d_skip, seq_rank * head_local, head_local, 0)
    local_params = (
        kernel_x,
        offset_x,
        conv_weight[DI:],
        conv_bias[DI:],
        shift_local,
        decay_local,
        skip_local,
    )

    def head_mixer(x_values, step_raw, bc_values, params_in):

        def single_seq(x_one, step_one, bc_one, seg_one):
            return mixer(x_one, step_one, bc_one, seg_one, *params_in)

        return jax.vmap(single_seq)(x_values, step_raw, bc_values, seg_full)

    mixed, pull_mix = jax.vjp(
        head_mixer,
        x_heads.astype(jnp.float32),
        step_heads.astype(jnp.float32),
        bc_full.astype(jnp.float32),
        local_params,
    )
    y_tokens = lax.all_to_all(
        mixed.astype(jnp.bfloat16), "seq", split_axis=1, concat_axis=2, tiled=True
    )
    gated_f, pull_gate = jax.vjp(gate_norm, y_tokens.astype(jnp.float32), gate_part, gate_gain)
    gated = gated_f.astype(jnp.bfloat16)
    branch_out = jnp.einsum("mtf,fd->mtd", gated, full_out, preferred_element_type=jnp.float32)
    result = (hidden_f + branch_out).astype(jnp.bfloat16)
    d_gated = jnp.einsum("mtd,fd->mtf", cotangent, full_out, preferred_element_type=jnp.float32)
    d_mixed, d_gate_part, d_gate_gain = pull_gate(d_gated)
    d_heads = lax.all_to_all(
        d_mixed.astype(jnp.bfloat16), "seq", split_axis=2, concat_axis=1, tiled=True
    )
    d_x_heads, d_step_heads, d_bc_full, d_params = pull_mix(d_heads.astype(jnp.float32))
    d_x_part, d_step_part = (
        lax.all_to_all(
            d_x_heads.astype(jnp.bfloat16), "seq", split_axis=1, concat_axis=2, tiled=True
        ),
        lax.all_to_all(
            d_step_heads.astype(jnp.bfloat16), "seq", split_axis=1, concat_axis=2, tiled=True
        ),
    )
    d_bc_part = lax.psum_scatter(
        d_bc_full.astype(jnp.bfloat16), "seq", scatter_dimension=1, tiled=True
    )
    d_project = jnp.concatenate(
        [d_gate_part.astype(jnp.bfloat16), d_x_part, d_bc_part, d_step_part], axis=2
    )
    d_normed = jnp.einsum("mtf,df->mtd", d_project, full_in, preferred_element_type=jnp.float32)
    d_hidden_f, d_norm_gain = pull_pre(d_normed)
    d_hidden = (cotangent.astype(jnp.float32) + d_hidden_f).astype(jnp.bfloat16)
    in_rows = in_weight.shape[0]
    out_rows = out_weight.shape[0]
    column_ranges = ((0, DI), (DI, d_project.shape[2]))
    in_pieces = [jnp.zeros((in_rows, upper - lower), jnp.float32) for lower, upper in column_ranges]
    grad_out = jnp.zeros(out_weight.shape, jnp.float32)
    for batch_index in range(hidden.shape[0]):
        for range_index in range(len(column_ranges)):
            lower, upper = column_ranges[range_index]

            def in_term(
                start,
                count,
                normed_one=normed[batch_index],
                d_one=d_project[batch_index, :, lower:upper],
            ):
                return lax.dot_general(
                    normed_one, d_one, (((0,), (0,)), ((), ())), preferred_element_type=jnp.float32
                )

            in_pieces[range_index] = in_pieces[range_index] + lax.psum_scatter(
                in_term(jnp.int32(0), in_rows * lax.axis_size(("dp", "seq"))),
                ("dp", "seq"),
                scatter_dimension=0,
                tiled=True,
            )

        def out_term(start, count, gated_one=gated[batch_index], cot_one=cotangent[batch_index]):
            return lax.dot_general(
                gated_one, cot_one, (((0,), (0,)), ((), ())), preferred_element_type=jnp.float32
            )

        grad_out = grad_out + lax.psum_scatter(
            out_term(jnp.int32(0), out_rows * lax.axis_size(("dp", "seq"))),
            ("dp", "seq"),
            scatter_dimension=0,
            tiled=True,
        )
    grad_in = jnp.concatenate(in_pieces, axis=1)
    d_kernel_x, d_offset_x, d_kernel_bc, d_offset_bc, d_shift, d_decay, d_skip_part = d_params
    tap_count = conv_weight.shape[1]
    grad_conv_w = jnp.concatenate(
        [
            lax.dynamic_update_slice_in_dim(
                jnp.zeros((DI, tap_count), jnp.float32), d_kernel_x, seq_rank * chan_local, 0
            ),
            d_kernel_bc,
        ],
        axis=0,
    )
    grad_conv_b = jnp.concatenate(
        [
            lax.dynamic_update_slice_in_dim(
                jnp.zeros((DI,), jnp.float32), d_offset_x, seq_rank * chan_local, 0
            ),
            d_offset_bc,
        ],
        axis=0,
    )
    grad_shift = lax.dynamic_update_slice_in_dim(
        jnp.zeros((HEADS,), jnp.float32), d_shift, seq_rank * head_local, 0
    )
    grad_decay = lax.dynamic_update_slice_in_dim(
        jnp.zeros((HEADS,), jnp.float32), d_decay, seq_rank * head_local, 0
    )
    grad_skip = lax.dynamic_update_slice_in_dim(
        jnp.zeros((HEADS,), jnp.float32), d_skip_part, seq_rank * head_local, 0
    )
    totals = lax.psum(
        (grad_conv_w, grad_conv_b, grad_shift, grad_decay, grad_skip, d_norm_gain, d_gate_gain),
        ("dp", "seq"),
    )
    return (
        result,
        d_hidden,
        grad_in,
        totals[0],
        totals[1],
        totals[2],
        totals[3],
        totals[4],
        totals[5],
        totals[6],
        grad_out,
    )


LOG2E = 1.4426950408889634
TILE = 128
FAR = -1e30


def shift_rows(v, lag):
    return v if lag == 0 else pltpu.roll(v, lag % v.shape[0], axis=0)


def conv_silu(sig, taps, offset, keep):
    total = offset + taps[CONV - 1 : CONV] * sig
    for lag in range(1, CONV):
        total = total + taps[CONV - 1 - lag : CONV - lag] * (shift_rows(sig, lag) * keep[lag])
    gate = jax.nn.sigmoid(total)
    return total, gate, total * gate


def conv_back(d_out, total, gate, sig, taps, keep):
    d_total = d_out * (gate * (1.0 + total * (1.0 - gate)))
    d_sig = taps[CONV - 1 : CONV] * d_total
    tap_rows = [jnp.sum(d_total * sig, axis=0, keepdims=True)]
    for lag in range(1, CONV):
        kept = d_total * keep[lag]
        d_sig = d_sig + taps[CONV - 1 - lag : CONV - lag] * shift_rows(kept, -lag)
        tap_rows.append(jnp.sum(kept * shift_rows(sig, lag), axis=0, keepdims=True))
    return d_sig, tap_rows[::-1], jnp.sum(d_total, axis=0, keepdims=True)


def keep_masks(seg_col):
    length = seg_col.shape[0]
    row = lax.broadcasted_iota(jnp.int32, (length, 1), 0)
    masks = [None]
    for lag in range(1, CONV):
        same = (pltpu.roll(seg_col, lag, axis=0) == seg_col) & (row >= lag)
        masks.append(same.astype(jnp.float32))
    return masks


def lane_sums(v, reverse):
    length = v.shape[1]
    lane = lax.broadcasted_iota(jnp.int32, v.shape, 1)
    step = 1
    while step < length:
        if reverse:
            v = v + jnp.where(lane < length - step, pltpu.roll(v, length - step, axis=1), 0.0)
        else:
            v = v + jnp.where(lane >= step, pltpu.roll(v, step, axis=1), 0.0)
        step *= 2
    return v


def step_sizes_of(dt_all, head_rows, h_own, n_seq, heads_row):
    rank = lax.axis_index("seq")
    all_heads = dt_all.shape[1]
    lane = lax.broadcasted_iota(jnp.int32, (all_heads, 128), 1)
    row = lax.broadcasted_iota(jnp.int32, (all_heads, 128), 0)
    head = ((lane // heads_row) * n_seq + rank) * heads_row + lane % heads_row
    pick = ((row == head) & (lane < h_own)).astype(jnp.bfloat16)
    raw = jnp.dot(dt_all, pick, preferred_element_type=jnp.float32)
    shifted = raw + head_rows[0:1]
    dt = jnp.maximum(shifted, 0.0) + jnp.log1p(jnp.exp(-jnp.abs(shifted)))
    return shifted, dt


def head_prep(dt_all, head_rows, h_own, n_seq, heads_row, dt_cols, cum_cols, cum_rows):
    shifted, dt = step_sizes_of(dt_all, head_rows, h_own, n_seq, heads_row)
    rates = -jnp.exp(head_rows[1:2])
    step_log = dt * (rates * LOG2E)
    across = jnp.transpose(step_log)
    cum_t = lane_sums(across[:h_own], False)
    pad = jnp.zeros((128 - h_own, cum_t.shape[1]), jnp.float32)
    cum = jnp.transpose(jnp.concatenate([cum_t, pad], axis=0))
    for k in range(h_own):
        dt_cols[k] = dt[:, k : k + 1]
        cum_cols[k] = cum[:, k : k + 1]
        cum_rows[k] = cum_t[k : k + 1, :]
    return shifted, dt


def pair_wide(cols, pair):
    length = cols.shape[1]
    lane = lax.broadcasted_iota(jnp.int32, (length, 128), 1)
    return jnp.where(lane < HDIM, cols[2 * pair], cols[2 * pair + 1])


def scan_forward(h_own, n_seq, heads_row, x_ref, bc_ref, dt_ref, segc_ref, segr_ref, wx_ref, wbc_ref,
                 head_ref, y_ref, inner_ref, dt_cols, cum_cols, cum_rows, inner_prod, bias):
    pair = pl.program_id(1)
    length = x_ref.shape[0]
    seg_col = segc_ref[0]
    keep = keep_masks(seg_col)

    @pl.when(pair == 0)
    def prepare():
        head_prep(dt_ref[...], head_ref[...], h_own, n_seq, heads_row, dt_cols, cum_cols, cum_rows)
        _, _, bc = conv_silu(bc_ref[...].astype(jnp.float32), wbc_ref[0:CONV], wbc_ref[CONV : CONV + 1], keep)
        inner_prod[...] = lax.dot_general(
            bc[:, NST:], bc[:, :NST], (((1,), (1,)), ((), ())),
            precision=lax.Precision.HIGHEST, preferred_element_type=jnp.float32,
        )
        at = lax.broadcasted_iota(jnp.int32, (length, length), 0)
        source = lax.broadcasted_iota(jnp.int32, (length, length), 1)
        bias[...] = jnp.where((source <= at) & (seg_col == segr_ref[0]), 0.0, FAR)

    _, _, xc = conv_silu(x_ref[...].astype(jnp.float32), wx_ref[0:CONV], wx_ref[CONV : CONV + 1], keep)
    moved = (xc * pair_wide(dt_cols, pair)).astype(jnp.bfloat16)
    skip = wx_ref[CONV + 1 : CONV + 2]
    first = lax.broadcasted_iota(jnp.int32, (TILE, 128), 1) < HDIM
    for block in range(length // TILE):
        rows, wide = slice(block * TILE, (block + 1) * TILE), (block + 1) * TILE
        halves = []
        for half in range(2):
            head = 2 * pair + half
            decay = jnp.exp2(cum_cols[head, rows] - cum_rows[head, :, :wide] + bias[rows, :wide])
            scores = (inner_prod[rows, :wide] * decay).astype(jnp.bfloat16)
            halves.append(jnp.dot(scores, moved[:wide], preferred_element_type=jnp.float32))
        inner = jnp.where(first, halves[0], halves[1])
        inner_ref[rows] = inner
        y_ref[rows] = (inner + skip * xc[rows]).astype(jnp.bfloat16)


def scan_backward(h_own, n_seq, heads_row, x_ref, bc_ref, dt_ref, segc_ref, segr_ref, wx_ref, wbc_ref,
                  head_ref, dy_ref, inner_ref, dx_ref, dbc_ref, ddt_ref, gx_ref, gbc_ref, gh_ref,
                  dt_cols, cum_cols, cum_rows, inner_prod, bias, d_inner, d_cum, d_dt):
    pair = pl.program_id(1)
    n_pair = pl.num_programs(1)
    length = x_ref.shape[0]
    seg_col = segc_ref[0]
    keep = keep_masks(seg_col)
    f32, bf16 = jnp.float32, jnp.bfloat16

    @pl.when(pair == 0)
    def prepare():
        head_prep(dt_ref[...], head_ref[...], h_own, n_seq, heads_row, dt_cols, cum_cols, cum_rows)
        _, _, bc = conv_silu(bc_ref[...].astype(f32), wbc_ref[0:CONV], wbc_ref[CONV : CONV + 1], keep)
        inner_prod[...] = lax.dot_general(
            bc[:, :NST], bc[:, NST:], (((1,), (1,)), ((), ())),
            precision=lax.Precision.HIGHEST, preferred_element_type=f32,
        )
        source = lax.broadcasted_iota(jnp.int32, (length, length), 0)
        at = lax.broadcasted_iota(jnp.int32, (length, length), 1)
        bias[...] = jnp.where((source <= at) & (seg_col == segr_ref[0]), 0.0, FAR)
        d_inner[...] = jnp.zeros((length, length), f32)
        d_cum[...] = jnp.zeros((length, 128), f32)
        d_dt[...] = jnp.zeros((length, 128), f32)

    x_in = x_ref[...].astype(f32)
    taps = wx_ref[0:CONV]
    total, gate, xc = conv_silu(x_in, taps, wx_ref[CONV : CONV + 1], keep)
    dt_wide = pair_wide(dt_cols, pair)
    moved = (xc * dt_wide).astype(bf16)
    skip = wx_ref[CONV + 1 : CONV + 2]
    dy = dy_ref[...]
    first = lax.broadcasted_iota(jnp.int32, (TILE, 128), 1) < HDIM
    pieces = []
    for block in range(length // TILE):
        rows, later = slice(block * TILE, (block + 1) * TILE), slice(block * TILE, length)
        halves = []
        for half in range(2):
            head = 2 * pair + half
            decay = jnp.exp2(cum_rows[head, :, later] - cum_cols[head, rows] + bias[rows, later])
            scores = (inner_prod[rows, later] * decay).astype(bf16)
            halves.append(jnp.dot(scores, dy[later], preferred_element_type=f32))
            mine = jnp.where(first if half == 0 else ~first, moved[rows].astype(f32), 0.0).astype(bf16)
            d_scores = lax.dot_general(
                mine, dy[later], (((1,), (1,)), ((), ())), preferred_element_type=f32
            )
            d_inner[rows, later] += d_scores * decay
        pieces.append(jnp.where(first, halves[0], halves[1]))
    d_moved = jnp.concatenate(pieces, axis=0)
    dy_f = dy.astype(f32)
    change = dy_f * inner_ref[...] - moved.astype(f32) * d_moved
    direct = d_moved * xc
    lane = lax.broadcasted_iota(jnp.int32, (length, 128), 1)
    low = lane < HDIM
    for half in range(2):
        mine = low if half == 0 else ~low
        place = lane == 2 * pair + half
        d_cum[...] += jnp.where(place, jnp.sum(jnp.where(mine, change, 0.0), axis=1, keepdims=True), 0.0)
        d_dt[...] += jnp.where(place, jnp.sum(jnp.where(mine, direct, 0.0), axis=1, keepdims=True), 0.0)
    d_xc = d_moved * dt_wide + skip * dy_f
    d_x, tap_rows, d_offset = conv_back(d_xc, total, gate, x_in, taps, keep)
    dx_ref[...] = d_x.astype(bf16)
    d_skip = jnp.sum(dy_f * xc, axis=0, keepdims=True)
    blank = jnp.zeros((2, 128), f32)
    gx_ref[0] = jnp.concatenate(tap_rows + [d_offset, d_skip, blank], axis=0)

    @pl.when(pair == n_pair - 1)
    def finish():
        bc_in = bc_ref[...].astype(f32)
        taps_bc = wbc_ref[0:CONV]
        total_bc, gate_bc, bc = conv_silu(bc_in, taps_bc, wbc_ref[CONV : CONV + 1], keep)
        d_in = d_inner[...]
        d_b = jnp.dot(d_in, bc[:, NST:], precision=lax.Precision.HIGHEST, preferred_element_type=f32)
        d_c = lax.dot_general(
            d_in, bc[:, :NST], (((0,), (0,)), ((), ())),
            precision=lax.Precision.HIGHEST, preferred_element_type=f32,
        )
        d_bc, rows_bc, offset_bc = conv_back(
            jnp.concatenate([d_b, d_c], axis=1), total_bc, gate_bc, bc_in, taps_bc, keep
        )
        dbc_ref[...] = d_bc.astype(bf16)
        gbc_ref[0] = jnp.concatenate(rows_bc + [offset_bc, jnp.zeros((3, 2 * NST), f32)], axis=0)
        shifted, dt = step_sizes_of(dt_ref[...], head_ref[...], h_own, n_seq, heads_row)
        rates = -jnp.exp(head_ref[1:2])
        across = jnp.transpose(d_cum[...])
        d_log_t = lane_sums(across[:h_own], True)
        pad = jnp.zeros((128 - h_own, length), f32)
        d_log = jnp.transpose(jnp.concatenate([d_log_t, pad], axis=0))
        d_raw = (d_log * rates + d_dt[...]) * jax.nn.sigmoid(shifted)
        ddt_ref[...] = d_raw
        gh_ref[0] = jnp.concatenate(
            [
                jnp.sum(d_raw, axis=0, keepdims=True),
                jnp.sum(d_log * dt, axis=0, keepdims=True) * rates,
                jnp.zeros((6, 128), f32),
            ],
            axis=0,
        )


def scan_specs(length, all_heads):
    return [
        pl.BlockSpec((length, 128), lambda q, p: (q, p)),
        pl.BlockSpec((length, 2 * NST), lambda q, p: (q, 0)),
        pl.BlockSpec((length, all_heads), lambda q, p: (q, 0)),
        pl.BlockSpec((1, length, 1), lambda q, p: (q, 0, 0)),
        pl.BlockSpec((1, 1, length), lambda q, p: (q, 0, 0)),
        pl.BlockSpec((8, 128), lambda q, p: (0, p)),
        pl.BlockSpec((8, 2 * NST), lambda q, p: (0, 0)),
        pl.BlockSpec((8, 128), lambda q, p: (0, 0)),
    ]


def scan_scratch(length, h_own):
    f32 = jnp.float32
    return [
        pltpu.VMEM((h_own, length, 1), f32),
        pltpu.VMEM((h_own, length, 1), f32),
        pltpu.VMEM((h_own, 1, length), f32),
        pltpu.VMEM((length, length), f32),
        pltpu.VMEM((length, length), f32),
    ]


def run_forward(n_own, h_own, n_seq, heads_row, operands):
    tokens, chan = operands[0].shape
    length = tokens // n_own
    pair_block = pl.BlockSpec((length, 128), lambda q, p: (q, p))
    return pl.pallas_call(
        functools.partial(scan_forward, h_own, n_seq, heads_row),
        grid=(n_own, chan // 128),
        in_specs=scan_specs(length, operands[2].shape[1]),
        out_specs=[pair_block, pair_block],
        out_shape=[
            jax.ShapeDtypeStruct((tokens, chan), jnp.bfloat16),
            jax.ShapeDtypeStruct((tokens, chan), jnp.float32),
        ],
        scratch_shapes=scan_scratch(length, h_own),
        compiler_params=pltpu.CompilerParams(vmem_limit_bytes=48 << 20),
        name="scan_forward",
    )(*operands)


def run_backward(n_own, h_own, n_seq, heads_row, operands, d_y, inner):
    f32 = jnp.float32
    tokens, chan = operands[0].shape
    length = tokens // n_own
    pair_block = pl.BlockSpec((length, 128), lambda q, p: (q, p))
    return pl.pallas_call(
        functools.partial(scan_backward, h_own, n_seq, heads_row),
        grid=(n_own, chan // 128),
        in_specs=scan_specs(length, operands[2].shape[1]) + [pair_block, pair_block],
        out_specs=[
            pair_block,
            pl.BlockSpec((length, 2 * NST), lambda q, p: (q, 0)),
            pl.BlockSpec((length, 128), lambda q, p: (q, 0)),
            pl.BlockSpec((1, 8, 128), lambda q, p: (q, 0, p)),
            pl.BlockSpec((1, 8, 2 * NST), lambda q, p: (q, 0, 0)),
            pl.BlockSpec((1, 8, 128), lambda q, p: (q, 0, 0)),
        ],
        out_shape=[
            jax.ShapeDtypeStruct((tokens, chan), jnp.bfloat16),
            jax.ShapeDtypeStruct((tokens, 2 * NST), jnp.bfloat16),
            jax.ShapeDtypeStruct((tokens, 128), f32),
            jax.ShapeDtypeStruct((n_own, 8, chan), f32),
            jax.ShapeDtypeStruct((n_own, 8, 2 * NST), f32),
            jax.ShapeDtypeStruct((n_own, 8, 128), f32),
        ],
        scratch_shapes=scan_scratch(length, h_own)
        + [
            pltpu.VMEM((length, length), f32),
            pltpu.VMEM((length, 128), f32),
            pltpu.VMEM((length, 128), f32),
        ],
        compiler_params=pltpu.CompilerParams(vmem_limit_bytes=56 << 20),
        name="scan_backward",
    )(*operands, d_y, inner)


MESH = pl.DeviceIdType.MESH
WIDE = 8


def place():
    dp, s = lax.axis_index("dp"), lax.axis_index("seq")
    z, x = s // 2, s % 2
    y, core = dp // 2, dp % 2
    return dp, s, z, x, s + 1 - 2 * x, dp + 2 - 4 * y, dp + 1 - 2 * core


def greet(peers):
    barrier = pltpu.get_barrier_semaphore()
    for device in peers:
        pl.semaphore_signal(barrier, inc=1, device_id=device, device_id_type=MESH)
    pl.semaphore_wait(barrier, len(peers))


def remote(src, dst, send, recv, device):
    return pltpu.make_async_remote_copy(
        src_ref=src, dst_ref=dst, send_sem=send, recv_sem=recv, device_id=device, device_id_type=MESH
    )


class TokenGather:
    def __init__(self, own, full, send, recv, where):
        self.own, self.full, self.send, self.recv = own, full, send, recv
        self.dp, self.s, self.z, self.x, self.x_peer, _, _ = where
        self.span = own.shape[1]

    def part(self, shard, q):
        return self.full.at[q, pl.ds(pl.multiple_of(shard * self.span, self.span), self.span)]

    def copy(self, shard_z, way, q, mine):
        shard = shard_z * 2 + self.x
        target = (self.s + 2, self.s - 2, self.x_peer)[way]
        src = self.own.at[q] if mine else self.part(shard, q)
        return remote(
            src, self.part(shard, q), self.send.at[way, shard_z, q], self.recv.at[shard, q], (self.dp, target)
        )

    def arrived(self, shard, q):
        part = self.part(shard, q)
        remote(part, part, self.send.at[0, 0, q], self.recv.at[shard, q], (self.dp, self.x_peer)).wait_recv()

    def start(self, q):
        @pl.when(self.z < 3)
        def up():
            self.copy(self.z, 0, q, True).start()

        @pl.when(self.z > 0)
        def down():
            self.copy(self.z, 1, q, True).start()

        self.copy(self.z, 2, q, True).start()

    def step(self, hop, q):
        @pl.when(self.z >= hop)
        def from_below():
            shard_z = self.z - hop
            self.arrived(shard_z * 2 + self.x, q)

            @pl.when(self.z < 3)
            def up():
                self.copy(shard_z, 0, q, False).start()

            self.copy(shard_z, 2, q, False).start()

        @pl.when(self.z + hop <= 3)
        def from_above():
            shard_z = self.z + hop
            self.arrived(shard_z * 2 + self.x, q)

            @pl.when(self.z > 0)
            def down():
                self.copy(shard_z, 1, q, False).start()

            self.copy(shard_z, 2, q, False).start()

    def finish(self, q):
        for shard_z in range(4):
            self.arrived(shard_z * 2 + 1 - self.x, q)
        for shard_z in range(4):
            self.copy(shard_z, 2, q, False).wait_send()

            @pl.when((self.z < 3) & (self.z >= shard_z))
            def up():
                self.copy(shard_z, 0, q, False).wait_send()

            @pl.when((self.z > 0) & (self.z <= shard_z))
            def down():
                self.copy(shard_z, 1, q, False).wait_send()


def gather_kernel(normed, cot, in_w, out_w, seg, n_all, c_all, w_in, w_out, seg_all,
                  n_send, n_recv, c_send, c_recv, wide_send, tail_send, wide_recv, tail_recv,
                  y_send, core_send, cross_send, block_recv, out_send, out_recv, seg_send, seg_recv, local):
    where = place()
    dp, s, z, x, x_peer, y_peer, core_peer = where
    peers = [(dp, (s + k) % 8) for k in range(1, 8)] + [(y_peer, s), (core_peer, s)]
    greet(peers)
    in_rows, rows = in_w.shape[0], out_w.shape[0]
    chan = w_out.shape[0]
    tail = in_w.shape[1] - 2 * DI

    def block(d, shard, lo=0, size=None):
        size = w_in.shape[1] if size is None else size
        at = pl.multiple_of((d * 8 + shard) * in_rows, in_rows)
        return w_in.at[pl.ds(at, in_rows), pl.ds(lo, size)]

    def wide_src(piece, target):
        at = pl.multiple_of((piece * 8 + target) * rows, rows)
        return in_w.at[:, pl.ds(at, rows)]

    tail_src = in_w.at[:, pl.ds(2 * DI, tail)]

    def push(k, _):
        target = (s + k) % 8
        remote(seg, seg_all.at[s], seg_send.at[k], seg_recv.at[s], (dp, target)).start()
        for piece in range(WIDE):
            remote(
                wide_src(piece, target), block(dp, s, piece * rows, rows), wide_send.at[k], wide_recv.at[s],
                (dp, target),
            ).start()
        remote(tail_src, block(dp, s, 2 * chan, tail), tail_send.at[k], tail_recv.at[s], (dp, target)).start()
        return 0

    lax.fori_loop(1, 8, push, 0)
    tokens = TokenGather(normed, n_all, n_send, n_recv, where)
    cots = TokenGather(cot, c_all, c_send, c_recv, where)
    for q in range(2):
        tokens.start(q)
    own_copies = []
    for piece in range(WIDE):
        own_copies.append(pltpu.make_async_copy(wide_src(piece, s), block(dp, s, piece * rows, rows), local.at[piece]))
    own_copies.append(pltpu.make_async_copy(tail_src, block(dp, s, 2 * chan, tail), local.at[8]))
    later_copies = [
        pltpu.make_async_copy(out_w, w_out.at[pl.ds(pl.multiple_of(dp * rows, rows), rows)], local.at[9]),
        pltpu.make_async_copy(seg, seg_all.at[s], local.at[10]),
    ]
    for q in range(2):
        later_copies.append(pltpu.make_async_copy(normed.at[q], tokens.part(s, q), local.at[11 + q]))
        later_copies.append(pltpu.make_async_copy(cot.at[q], cots.part(s, q), local.at[13 + q]))
    for copy in own_copies + later_copies:
        copy.start()
    for copy in own_copies:
        copy.wait()

    def spread(shard, shard_sem):
        remote(block(dp, shard), block(dp, shard), y_send.at[shard_sem], block_recv.at[dp, shard], (y_peer, s)).start()
        remote(
            block(dp, shard), block(dp, shard), core_send.at[shard_sem], block_recv.at[dp, shard], (core_peer, s)
        ).start()

    spread(s, 0)
    out_block = w_out.at[pl.ds(pl.multiple_of(dp * rows, rows), rows)]

    def forward(k, _):
        source = (s + 8 - k) % 8
        remote(
            block(dp, source, 0, 2 * chan), block(dp, source, 0, 2 * chan), wide_send.at[k], wide_recv.at[source],
            (dp, x_peer),
        ).wait_recv()
        remote(
            block(dp, source, 2 * chan, tail), block(dp, source, 2 * chan, tail), tail_send.at[k],
            tail_recv.at[source], (dp, x_peer),
        ).wait_recv()
        spread(source, k)
        return 0

    def cross(k, _):
        source = (s + 8 - k) % 8
        there = block(y_peer, source)
        copy = remote(there, there, cross_send.at[k], block_recv.at[y_peer, source], (core_peer, s))
        copy.wait_recv()
        copy.start()
        return 0

    tokens.step(1, 0)
    lax.fori_loop(1, 4, forward, 0)
    tokens.step(1, 1)
    lax.fori_loop(4, 8, forward, 0)
    tokens.step(2, 0)
    lax.fori_loop(0, 4, cross, 0)
    tokens.step(2, 1)
    lax.fori_loop(4, 8, cross, 0)
    tokens.step(3, 0)
    tokens.step(3, 1)
    for q in range(2):
        cots.start(q)

    def out_part(d):
        return w_out.at[pl.ds(pl.multiple_of(d * rows, rows), rows)]

    remote(out_w, out_part(dp), out_send.at[0], out_recv.at[dp], (y_peer, s)).start()
    remote(out_w, out_part(dp), out_send.at[1], out_recv.at[dp], (core_peer, s)).start()
    for hop in range(1, 4):
        for q in range(2):
            cots.step(hop, q)
    out_cross = remote(out_part(y_peer), out_part(y_peer), out_send.at[2], out_recv.at[y_peer], (core_peer, s))
    out_cross.wait_recv()
    out_cross.start()
    for q in range(2):
        tokens.finish(q)
        cots.finish(q)
    for copy in later_copies:
        copy.wait()

    def settle(k, _):
        shard = (s + 8 - k) % 8
        for d in (core_peer, core_peer + y_peer - dp):
            there = block(d, shard)
            remote(there, there, core_send.at[k], block_recv.at[d, shard], (core_peer, s)).wait_recv()
        there = block(dp, shard)
        remote(there, there, y_send.at[k], block_recv.at[dp, shard], (y_peer, s)).wait_send()
        remote(there, there, core_send.at[k], block_recv.at[dp, shard], (core_peer, s)).wait_send()
        remote(there, there, cross_send.at[k], block_recv.at[dp, shard], (core_peer, s)).wait_send()
        return 0

    lax.fori_loop(0, 8, settle, 0)

    def settle_push(k, _):
        source = (s + 8 - k) % 8
        remote(seg, seg_all.at[source], seg_send.at[k], seg_recv.at[source], (dp, x_peer)).wait_recv()
        remote(seg, seg_all.at[source], seg_send.at[k], seg_recv.at[source], (dp, x_peer)).wait_send()
        remote(
            block(dp, source, 0, 2 * chan), block(dp, source, 0, 2 * chan), wide_send.at[k], wide_recv.at[source],
            (dp, x_peer),
        ).wait_send()
        remote(
            block(dp, source, 2 * chan, tail), block(dp, source, 2 * chan, tail), tail_send.at[k],
            tail_recv.at[source], (dp, x_peer),
        ).wait_send()
        return 0

    lax.fori_loop(1, 8, settle_push, 0)
    for d in (core_peer, core_peer + y_peer - dp):
        remote(out_part(d), out_part(d), out_send.at[0], out_recv.at[d], (core_peer, s)).wait_recv()
    for k in range(3):
        remote(out_w, out_part(dp), out_send.at[k], out_recv.at[dp], (core_peer, s)).wait_send()


def run_gather(normed, cot, in_w, out_w, seg):
    bf16 = jnp.bfloat16
    n_own, span, width = normed.shape
    in_rows, rows = in_w.shape[0], out_w.shape[0]
    chan = 4 * rows
    columns = 2 * chan + in_w.shape[1] - 2 * DI
    sem = pltpu.SemaphoreType.DMA
    return pl.pallas_call(
        gather_kernel,
        in_specs=[pl.BlockSpec(memory_space=pl.ANY)] * 5,
        out_specs=[pl.BlockSpec(memory_space=pl.ANY)] * 5,
        out_shape=[
            jax.ShapeDtypeStruct((n_own, 8 * span, width), bf16),
            jax.ShapeDtypeStruct((n_own, 8 * span, width), bf16),
            jax.ShapeDtypeStruct((32 * in_rows, columns), bf16),
            jax.ShapeDtypeStruct((chan, width), bf16),
            jax.ShapeDtypeStruct((8, 8, 128), jnp.float32),
        ],
        scratch_shapes=[
            sem((3, 4, 2)), sem((8, 2)), sem((3, 4, 2)), sem((8, 2)),
            sem((8,)), sem((8,)), sem((8,)), sem((8,)),
            sem((8,)), sem((8,)), sem((8,)), sem((4, 8)), sem((3,)), sem((4,)), sem((8,)), sem((8,)), sem((15,)),
        ],
        compiler_params=pltpu.CompilerParams(collective_id=0, has_side_effects=True),
        name="gather",
    )(normed, cot, in_w, out_w, seg)


def head_plan(
    hidden,
    segments,
    in_weight,
    conv_weight,
    conv_bias,
    dt_bias,
    a_log,
    d_skip,
    norm_gain,
    gate_gain,
    out_weight,
    cotangent,
):
    f32, bf16 = jnp.float32, jnp.bfloat16
    n_dp, n_seq = lax.axis_size("dp"), lax.axis_size("seq")
    seq_rank = lax.axis_index("seq")
    n_own, shard_len, width = hidden.shape
    length = shard_len * n_seq
    rows = out_weight.shape[0]
    in_rows = in_weight.shape[0]
    chan = rows * n_dp
    h_own = chan // HDIM
    hidden_f = hidden.astype(f32)
    inv = lax.rsqrt(jnp.mean(hidden_f * hidden_f, axis=-1, keepdims=True) + 1e-05)
    normed = (hidden_f * inv * norm_gain).astype(bf16)
    seg_tile = jnp.pad(segments.astype(f32), ((0, 8 - n_own), (0, 128 - shard_len)))
    normed_all, cot_all, w_in, w_out, seg_all = run_gather(
        normed, cotangent, in_weight, out_weight, seg_tile
    )
    normed_all = normed_all.reshape(n_own * length, width)
    cot_all = cot_all.reshape(n_own * length, width)
    seg_all = seg_all[:, :n_own, :shard_len].swapaxes(0, 1).reshape(n_own, length)

    def own_chan(vec):
        return lax.dynamic_index_in_dim(
            vec.reshape((n_dp, n_seq, rows) + vec.shape[1:]), seq_rank, 1, keepdims=False
        ).reshape((chan,) + vec.shape[1:])

    heads_row = rows // HDIM

    def own_head(vec):
        return lax.dynamic_index_in_dim(
            vec.reshape((n_dp, n_seq, heads_row) + vec.shape[1:]), seq_rank, 1, keepdims=False
        ).reshape((h_own,) + vec.shape[1:])

    def spread_chan(vec):
        blank = jnp.zeros((n_dp, n_seq, rows) + vec.shape[1:], f32)
        piece = vec.reshape((n_dp, 1, rows) + vec.shape[1:])
        return lax.dynamic_update_slice_in_dim(blank, piece, seq_rank, 1).reshape(
            (DI,) + vec.shape[1:]
        )

    def spread_head(vec):
        blank = jnp.zeros((n_dp, n_seq, heads_row) + vec.shape[1:], f32)
        piece = vec.reshape((n_dp, 1, heads_row) + vec.shape[1:])
        return lax.dynamic_update_slice_in_dim(blank, piece, seq_rank, 1).reshape(
            (HEADS,) + vec.shape[1:]
        )

    project = jnp.dot(normed_all, w_in, preferred_element_type=f32)
    z = project[:, :chan]
    x_raw = project[:, chan : 2 * chan].astype(bf16)
    bc_raw = project[:, 2 * chan : 2 * chan + 2 * NST].astype(bf16)
    dt_all = project[:, 2 * chan + 2 * NST :].astype(bf16)
    wx = jnp.concatenate(
        [
            own_chan(conv_weight[:DI]).T,
            own_chan(conv_bias[:DI])[None],
            jnp.repeat(own_head(d_skip), HDIM)[None],
            jnp.zeros((2, chan), f32),
        ],
        axis=0,
    )
    wbc = jnp.concatenate(
        [conv_weight[DI:].T, conv_bias[DI:][None], jnp.zeros((3, 2 * NST), f32)], axis=0
    )
    head_vals = jnp.pad(jnp.stack([own_head(dt_bias), own_head(a_log)]), ((0, 6), (0, 128 - h_own)))
    operands = (x_raw, bc_raw, dt_all, seg_all[:, :, None], seg_all[:, None, :], wx, wbc, head_vals)
    y, inner = run_forward(n_own, h_own, n_seq, heads_row, operands)
    y = y.astype(f32)
    gain = own_chan(gate_gain)
    sig = jax.nn.sigmoid(z)
    act = z * sig
    g = y * act
    d_gated = lax.dot_general(
        cot_all, w_out, (((1,), (1,)), ((), ())), preferred_element_type=f32
    )
    u = d_gated * gain
    sums = lax.psum(jnp.stack([jnp.sum(g * g, axis=1), jnp.sum(u * g, axis=1)]), "seq")
    r = lax.rsqrt(sums[0] / DI + 1e-05)[:, None]
    fall = (r * r * r) * (sums[1] / DI)[:, None]
    gr = g * r
    gated = (gr * gain).astype(bf16)
    part = jnp.dot(gated, w_out, preferred_element_type=f32).astype(bf16)
    branch = lax.psum_scatter(
        part.reshape(n_own, length, width), "seq", scatter_dimension=1, tiled=True
    )
    result = (hidden_f + branch.astype(f32)).astype(bf16)
    d_g = r * u - fall * g
    d_y = (d_g * act).astype(bf16)
    d_z = d_g * y * (sig * (1.0 + z * (1.0 - sig)))
    d_gate_gain = jnp.sum(d_gated * gr, axis=0)
    grad_out = jnp.einsum("tf,td->fd", gated, cot_all, preferred_element_type=f32)
    grad_out = lax.psum_scatter(grad_out, "dp", scatter_dimension=0, tiled=True)
    d_x, d_bc, d_dt, g_x, g_bc, g_head = run_backward(
        n_own, h_own, n_seq, heads_row, operands, d_y, inner
    )
    g_x, g_bc, g_head = jnp.sum(g_x, 0), jnp.sum(g_bc, 0), jnp.sum(g_head, 0)
    d_project = jnp.concatenate(
        [
            d_z.astype(bf16),
            d_x,
            d_bc,
            spread_head(d_dt[:, :h_own].T).T.astype(bf16),
        ],
        axis=1,
    )
    d_normed = lax.dot_general(
        d_project, w_in, (((1,), (1,)), ((), ())), preferred_element_type=f32
    ).astype(bf16)
    d_normed = lax.psum_scatter(
        d_normed.reshape(n_own, length, width), "seq", scatter_dimension=1, tiled=True
    ).astype(f32)
    grad_in = jnp.einsum("td,tf->df", normed_all, d_project, preferred_element_type=f32)
    grad_in = lax.psum_scatter(grad_in, "dp", scatter_dimension=0, tiled=True)
    grad_wide = grad_in[:, : 2 * chan].reshape(n_seq, in_rows, 2, n_dp, 1, rows)
    grad_wide = lax.all_to_all(grad_wide, "seq", split_axis=0, concat_axis=4, tiled=True)
    grad_wide = grad_wide.reshape(in_rows, 2 * DI)
    grad_tail = lax.psum_scatter(grad_in[:, 2 * chan :], "seq", scatter_dimension=0, tiled=True)
    grad_in = jnp.concatenate([grad_wide, grad_tail], axis=1)
    dn = d_normed * norm_gain
    along = jnp.mean(dn * hidden_f, axis=-1, keepdims=True)
    d_hidden = (
        cotangent.astype(f32) + inv * dn - (inv * inv * inv) * along * hidden_f
    ).astype(bf16)
    d_norm_gain = jnp.sum(d_normed * hidden_f * inv, axis=(0, 1))
    totals = lax.psum(
        (
            jnp.concatenate([spread_chan(g_x[:CONV].T), g_bc[:CONV].T], axis=0),
            jnp.concatenate([spread_chan(g_x[CONV]), g_bc[CONV]], axis=0),
            spread_head(g_head[0, :h_own]),
            spread_head(g_head[1, :h_own]),
            spread_head(jnp.sum(g_x[CONV + 1].reshape(h_own, HDIM), axis=1)),
            d_norm_gain,
            spread_chan(d_gate_gain),
        ),
        ("dp", "seq"),
    )
    return (result, d_hidden, grad_in) + tuple(totals) + (grad_out,)


def solution(mesh):
    whole_heads = mesh.shape["dp"] == 4 and mesh.shape["seq"] == 8
    shards = head_plan if whole_heads else general_plan
    placed = (
        P("dp", "seq", None),
        P("dp", "seq"),
        P(("dp", "seq"), None),
        P(),
        P(),
        P(),
        P(),
        P(),
        P(),
        P(),
        P(("dp", "seq"), None),
        P("dp", "seq", None),
    )
    return jax.shard_map(
        shards,
        mesh=mesh,
        in_specs=placed,
        out_specs=(
            P("dp", "seq", None),
            P("dp", "seq", None),
            P(("dp", "seq"), None),
            P(),
            P(),
            P(),
            P(),
            P(),
            P(),
            P(),
            P(("dp", "seq"), None),
        ),
        check_vma=False,
    )
```

```python
import functools

import jax
import jax.numpy as jnp
from jax import lax
from jax.experimental import pallas as pl
from jax.experimental.pallas import tpu as pltpu
from jax.sharding import PartitionSpec as P

HEADS = 64
HDIM = 64
NST = 128
GROUP = 256
CONV = 4
DI = 4096


def pre_norm(hidden_f, gain_vec):
    return (
        hidden_f
        * lax.rsqrt(jnp.mean(hidden_f * hidden_f, axis=-1, keepdims=True) + 1e-05)
        * gain_vec
    )


def gate_norm(y_values, gate_values, gain_vec):
    product = y_values * jax.nn.silu(gate_values)
    return (
        product * lax.rsqrt(jnp.mean(product * product, axis=-1, keepdims=True) + 1e-05) * gain_vec
    )


def conv_reset(signal, kernel, offset, seg_ids):
    tap_count = kernel.shape[1]
    summed = offset[None, :] + kernel[None, :, tap_count - 1] * signal
    for lag_steps in range(1, tap_count):
        shifted = jnp.pad(signal, ((lag_steps, 0), (0, 0)))[:-lag_steps]
        earlier = jnp.pad(seg_ids, (lag_steps, 0), constant_values=-1)[:-lag_steps]
        matches = (earlier == seg_ids).astype(jnp.float32)
        summed = summed + kernel[None, :, tap_count - 1 - lag_steps] * shifted * matches[:, None]
    return summed


def state_scan(values, deltas, rates, b_mat, c_mat, seg_ids):
    length, head_count, head_width = values.shape
    block_count = length // GROUP
    log_decay = deltas * rates[None, :]
    pieces = (
        values.reshape(block_count, GROUP, head_count, head_width),
        deltas.reshape(block_count, GROUP, head_count),
        log_decay.reshape(block_count, GROUP, head_count),
        b_mat.reshape(block_count, GROUP, b_mat.shape[-1]),
        c_mat.reshape(block_count, GROUP, c_mat.shape[-1]),
        seg_ids.reshape(block_count, GROUP),
    )
    position = lax.broadcasted_iota(jnp.int32, (GROUP, GROUP), 0)
    source = lax.broadcasted_iota(jnp.int32, (GROUP, GROUP), 1)

    def advance(carry, piece):
        memory, ending = carry
        block_vals, block_dt, block_log, b_block, c_block, seg_block = piece
        cumulative = jnp.cumsum(block_log, axis=0).T
        causal = (source <= position) & (seg_block[:, None] == seg_block[None, :])
        spread = cumulative[:, :, None] - cumulative[:, None, :]
        decays = jnp.where(causal[None], jnp.exp(jnp.where(causal[None], spread, 0.0)), 0.0)
        inner_prod = jnp.dot(c_block, b_block.T, precision=lax.Precision.HIGHEST)
        scores = inner_prod[None] * decays * block_dt.T[:, None, :]
        output = jnp.einsum("hij,jhp->ihp", scores, block_vals, precision=lax.Precision.HIGHEST)
        follows = (seg_block == ending).astype(jnp.float32)
        carried = jnp.einsum("in,hpn->ihp", c_block, memory, precision=lax.Precision.HIGHEST)
        output = output + (jnp.exp(cumulative).T * follows[:, None])[:, :, None] * carried
        last_seg = seg_block[-1]
        weights = (
            jnp.exp(cumulative[:, -1:] - cumulative)
            * (seg_block == last_seg).astype(jnp.float32)[None, :]
            * block_dt.T
        )
        keep_on = jnp.exp(cumulative[:, -1]) * (last_seg == ending).astype(jnp.float32)
        memory = memory * keep_on[:, None, None] + jnp.einsum(
            "hj,jhp,jn->hpn", weights, block_vals, b_block, precision=lax.Precision.HIGHEST
        )
        return ((memory, last_seg), output)

    initial = (
        jnp.zeros((head_count, head_width, b_mat.shape[-1]), jnp.float32),
        jnp.array(-1, jnp.int32),
    )
    unused, outputs = lax.scan(jax.checkpoint(advance), initial, pieces)
    return outputs.reshape(length, head_count, head_width)


def mixer(
    x_values,
    step_raw,
    bc_values,
    seg_ids,
    kernel_x,
    offset_x,
    kernel_bc,
    offset_bc,
    dt_shift,
    decay_log,
    skip_gain,
):
    x_conv = jax.nn.silu(conv_reset(x_values, kernel_x, offset_x, seg_ids))
    bc_conv = jax.nn.silu(conv_reset(bc_values, kernel_bc, offset_bc, seg_ids))
    step_sizes = jax.nn.softplus(step_raw + dt_shift[None, :])
    rates = -jnp.exp(decay_log)
    length = x_values.shape[0]
    head_count = step_raw.shape[1]
    shaped = x_conv.reshape(length, head_count, HDIM)
    mixed = (
        state_scan(shaped, step_sizes, rates, bc_conv[:, :NST], bc_conv[:, NST:], seg_ids)
        + skip_gain[None, :, None] * shaped
    )
    return mixed.reshape(length, head_count * HDIM)


def general_plan(
    hidden,
    segments,
    in_weight,
    conv_weight,
    conv_bias,
    dt_bias,
    a_log,
    d_skip,
    norm_gain,
    gate_gain,
    out_weight,
    cotangent,
):
    full_in, full_out = (
        lax.all_gather(in_weight, ("dp", "seq"), axis=0, tiled=True),
        lax.all_gather(out_weight, ("dp", "seq"), axis=0, tiled=True),
    )
    hidden_f = hidden.astype(jnp.float32)
    normed_f, pull_pre = jax.vjp(pre_norm, hidden_f, norm_gain)
    normed = normed_f.astype(jnp.bfloat16)
    project = jnp.einsum("mtd,df->mtf", normed, full_in, preferred_element_type=jnp.float32)
    gate_part = project[:, :, :DI]
    x_part = project[:, :, DI : 2 * DI].astype(jnp.bfloat16)
    bc_part = project[:, :, 2 * DI : 2 * DI + 2 * NST].astype(jnp.bfloat16)
    step_part = project[:, :, 2 * DI + 2 * NST :].astype(jnp.bfloat16)
    x_heads, step_heads = (
        lax.all_to_all(x_part, "seq", split_axis=2, concat_axis=1, tiled=True),
        lax.all_to_all(step_part, "seq", split_axis=2, concat_axis=1, tiled=True),
    )
    bc_full = lax.all_gather(bc_part, "seq", axis=1, tiled=True)
    seg_full = lax.all_gather(segments, "seq", axis=1, tiled=True)
    seq_rank = lax.axis_index("seq")
    head_local = step_heads.shape[2]
    chan_local = x_heads.shape[2]
    kernel_x = lax.dynamic_slice_in_dim(conv_weight, seq_rank * chan_local, chan_local, 0)
    offset_x = lax.dynamic_slice_in_dim(conv_bias, seq_rank * chan_local, chan_local, 0)
    shift_local = lax.dynamic_slice_in_dim(dt_bias, seq_rank * head_local, head_local, 0)
    decay_local = lax.dynamic_slice_in_dim(a_log, seq_rank * head_local, head_local, 0)
    skip_local = lax.dynamic_slice_in_dim(d_skip, seq_rank * head_local, head_local, 0)
    local_params = (
        kernel_x,
        offset_x,
        conv_weight[DI:],
        conv_bias[DI:],
        shift_local,
        decay_local,
        skip_local,
    )

    def head_mixer(x_values, step_raw, bc_values, params_in):

        def single_seq(x_one, step_one, bc_one, seg_one):
            return mixer(x_one, step_one, bc_one, seg_one, *params_in)

        return jax.vmap(single_seq)(x_values, step_raw, bc_values, seg_full)

    mixed, pull_mix = jax.vjp(
        head_mixer,
        x_heads.astype(jnp.float32),
        step_heads.astype(jnp.float32),
        bc_full.astype(jnp.float32),
        local_params,
    )
    y_tokens = lax.all_to_all(
        mixed.astype(jnp.bfloat16), "seq", split_axis=1, concat_axis=2, tiled=True
    )
    gated_f, pull_gate = jax.vjp(gate_norm, y_tokens.astype(jnp.float32), gate_part, gate_gain)
    gated = gated_f.astype(jnp.bfloat16)
    branch_out = jnp.einsum("mtf,fd->mtd", gated, full_out, preferred_element_type=jnp.float32)
    result = (hidden_f + branch_out).astype(jnp.bfloat16)
    d_gated = jnp.einsum("mtd,fd->mtf", cotangent, full_out, preferred_element_type=jnp.float32)
    d_mixed, d_gate_part, d_gate_gain = pull_gate(d_gated)
    d_heads = lax.all_to_all(
        d_mixed.astype(jnp.bfloat16), "seq", split_axis=2, concat_axis=1, tiled=True
    )
    d_x_heads, d_step_heads, d_bc_full, d_params = pull_mix(d_heads.astype(jnp.float32))
    d_x_part, d_step_part = (
        lax.all_to_all(
            d_x_heads.astype(jnp.bfloat16), "seq", split_axis=1, concat_axis=2, tiled=True
        ),
        lax.all_to_all(
            d_step_heads.astype(jnp.bfloat16), "seq", split_axis=1, concat_axis=2, tiled=True
        ),
    )
    d_bc_part = lax.psum_scatter(
        d_bc_full.astype(jnp.bfloat16), "seq", scatter_dimension=1, tiled=True
    )
    d_project = jnp.concatenate(
        [d_gate_part.astype(jnp.bfloat16), d_x_part, d_bc_part, d_step_part], axis=2
    )
    d_normed = jnp.einsum("mtf,df->mtd", d_project, full_in, preferred_element_type=jnp.float32)
    d_hidden_f, d_norm_gain = pull_pre(d_normed)
    d_hidden = (cotangent.astype(jnp.float32) + d_hidden_f).astype(jnp.bfloat16)
    in_rows = in_weight.shape[0]
    out_rows = out_weight.shape[0]
    column_ranges = ((0, DI), (DI, d_project.shape[2]))
    in_pieces = [jnp.zeros((in_rows, upper - lower), jnp.float32) for lower, upper in column_ranges]
    grad_out = jnp.zeros(out_weight.shape, jnp.float32)
    for batch_index in range(hidden.shape[0]):
        for range_index in range(len(column_ranges)):
            lower, upper = column_ranges[range_index]

            def in_term(
                start,
                count,
                normed_one=normed[batch_index],
                d_one=d_project[batch_index, :, lower:upper],
            ):
                return lax.dot_general(
                    normed_one, d_one, (((0,), (0,)), ((), ())), preferred_element_type=jnp.float32
                )

            in_pieces[range_index] = in_pieces[range_index] + lax.psum_scatter(
                in_term(jnp.int32(0), in_rows * lax.axis_size(("dp", "seq"))),
                ("dp", "seq"),
                scatter_dimension=0,
                tiled=True,
            )

        def out_term(start, count, gated_one=gated[batch_index], cot_one=cotangent[batch_index]):
            return lax.dot_general(
                gated_one, cot_one, (((0,), (0,)), ((), ())), preferred_element_type=jnp.float32
            )

        grad_out = grad_out + lax.psum_scatter(
            out_term(jnp.int32(0), out_rows * lax.axis_size(("dp", "seq"))),
            ("dp", "seq"),
            scatter_dimension=0,
            tiled=True,
        )
    grad_in = jnp.concatenate(in_pieces, axis=1)
    d_kernel_x, d_offset_x, d_kernel_bc, d_offset_bc, d_shift, d_decay, d_skip_part = d_params
    tap_count = conv_weight.shape[1]
    grad_conv_w = jnp.concatenate(
        [
            lax.dynamic_update_slice_in_dim(
                jnp.zeros((DI, tap_count), jnp.float32), d_kernel_x, seq_rank * chan_local, 0
            ),
            d_kernel_bc,
        ],
        axis=0,
    )
    grad_conv_b = jnp.concatenate(
        [
            lax.dynamic_update_slice_in_dim(
                jnp.zeros((DI,), jnp.float32), d_offset_x, seq_rank * chan_local, 0
            ),
            d_offset_bc,
        ],
        axis=0,
    )
    grad_shift = lax.dynamic_update_slice_in_dim(
        jnp.zeros((HEADS,), jnp.float32), d_shift, seq_rank * head_local, 0
    )
    grad_decay = lax.dynamic_update_slice_in_dim(
        jnp.zeros((HEADS,), jnp.float32), d_decay, seq_rank * head_local, 0
    )
    grad_skip = lax.dynamic_update_slice_in_dim(
        jnp.zeros((HEADS,), jnp.float32), d_skip_part, seq_rank * head_local, 0
    )
    totals = lax.psum(
        (grad_conv_w, grad_conv_b, grad_shift, grad_decay, grad_skip, d_norm_gain, d_gate_gain),
        ("dp", "seq"),
    )
    return (
        result,
        d_hidden,
        grad_in,
        totals[0],
        totals[1],
        totals[2],
        totals[3],
        totals[4],
        totals[5],
        totals[6],
        grad_out,
    )


LOG2E = 1.4426950408889634
TILE = 128
FAR = -1e30


def shift_rows(v, lag):
    return v if lag == 0 else pltpu.roll(v, lag % v.shape[0], axis=0)


def conv_silu(sig, taps, offset, keep):
    total = offset + taps[CONV - 1 : CONV] * sig
    for lag in range(1, CONV):
        total = total + taps[CONV - 1 - lag : CONV - lag] * (shift_rows(sig, lag) * keep[lag])
    gate = jax.nn.sigmoid(total)
    return total, gate, total * gate


def conv_back(d_out, total, gate, sig, taps, keep):
    d_total = d_out * (gate * (1.0 + total * (1.0 - gate)))
    d_sig = taps[CONV - 1 : CONV] * d_total
    tap_rows = [jnp.sum(d_total * sig, axis=0, keepdims=True)]
    for lag in range(1, CONV):
        kept = d_total * keep[lag]
        d_sig = d_sig + taps[CONV - 1 - lag : CONV - lag] * shift_rows(kept, -lag)
        tap_rows.append(jnp.sum(kept * shift_rows(sig, lag), axis=0, keepdims=True))
    return d_sig, tap_rows[::-1], jnp.sum(d_total, axis=0, keepdims=True)


def keep_masks(seg_col):
    length = seg_col.shape[0]
    row = lax.broadcasted_iota(jnp.int32, (length, 1), 0)
    masks = [None]
    for lag in range(1, CONV):
        same = (pltpu.roll(seg_col, lag, axis=0) == seg_col) & (row >= lag)
        masks.append(same.astype(jnp.float32))
    return masks


def lane_sums(v, reverse):
    length = v.shape[1]
    lane = lax.broadcasted_iota(jnp.int32, v.shape, 1)
    step = 1
    while step < length:
        if reverse:
            v = v + jnp.where(lane < length - step, pltpu.roll(v, length - step, axis=1), 0.0)
        else:
            v = v + jnp.where(lane >= step, pltpu.roll(v, step, axis=1), 0.0)
        step *= 2
    return v


def step_sizes_of(dt_all, head_rows, h_own, n_seq, heads_row):
    rank = lax.axis_index("seq")
    all_heads = dt_all.shape[1]
    lane = lax.broadcasted_iota(jnp.int32, (all_heads, 128), 1)
    row = lax.broadcasted_iota(jnp.int32, (all_heads, 128), 0)
    head = ((lane // heads_row) * n_seq + rank) * heads_row + lane % heads_row
    pick = ((row == head) & (lane < h_own)).astype(jnp.bfloat16)
    raw = jnp.dot(dt_all, pick, preferred_element_type=jnp.float32)
    shifted = raw + head_rows[0:1]
    dt = jnp.maximum(shifted, 0.0) + jnp.log1p(jnp.exp(-jnp.abs(shifted)))
    return shifted, dt


def head_prep(dt_all, head_rows, h_own, n_seq, heads_row, dt_cols, cum_cols, cum_rows):
    shifted, dt = step_sizes_of(dt_all, head_rows, h_own, n_seq, heads_row)
    rates = -jnp.exp(head_rows[1:2])
    step_log = dt * (rates * LOG2E)
    across = jnp.transpose(step_log)
    cum_t = lane_sums(across[:h_own], False)
    pad = jnp.zeros((128 - h_own, cum_t.shape[1]), jnp.float32)
    cum = jnp.transpose(jnp.concatenate([cum_t, pad], axis=0))
    for k in range(h_own):
        dt_cols[k] = dt[:, k : k + 1]
        cum_cols[k] = cum[:, k : k + 1]
        cum_rows[k] = cum_t[k : k + 1, :]
    return shifted, dt


def pair_wide(cols, pair):
    length = cols.shape[1]
    lane = lax.broadcasted_iota(jnp.int32, (length, 128), 1)
    return jnp.where(lane < HDIM, cols[2 * pair], cols[2 * pair + 1])


def scan_forward(h_own, n_seq, heads_row, x_ref, bc_ref, dt_ref, segc_ref, segr_ref, wx_ref, wbc_ref,
                 head_ref, y_ref, inner_ref, dt_cols, cum_cols, cum_rows, inner_prod, bias):
    pair = pl.program_id(1)
    length = x_ref.shape[0]
    seg_col = segc_ref[0]
    keep = keep_masks(seg_col)

    @pl.when(pair == 0)
    def prepare():
        head_prep(dt_ref[...], head_ref[...], h_own, n_seq, heads_row, dt_cols, cum_cols, cum_rows)
        _, _, bc = conv_silu(bc_ref[...].astype(jnp.float32), wbc_ref[0:CONV], wbc_ref[CONV : CONV + 1], keep)
        inner_prod[...] = lax.dot_general(
            bc[:, NST:], bc[:, :NST], (((1,), (1,)), ((), ())),
            precision=lax.Precision.HIGHEST, preferred_element_type=jnp.float32,
        )
        at = lax.broadcasted_iota(jnp.int32, (length, length), 0)
        source = lax.broadcasted_iota(jnp.int32, (length, length), 1)
        bias[...] = jnp.where((source <= at) & (seg_col == segr_ref[0]), 0.0, FAR)

    _, _, xc = conv_silu(x_ref[...].astype(jnp.float32), wx_ref[0:CONV], wx_ref[CONV : CONV + 1], keep)
    moved = (xc * pair_wide(dt_cols, pair)).astype(jnp.bfloat16)
    skip = wx_ref[CONV + 1 : CONV + 2]
    first = lax.broadcasted_iota(jnp.int32, (TILE, 128), 1) < HDIM
    for block in range(length // TILE):
        rows, wide = slice(block * TILE, (block + 1) * TILE), (block + 1) * TILE
        halves = []
        for half in range(2):
            head = 2 * pair + half
            decay = jnp.exp2(cum_cols[head, rows] - cum_rows[head, :, :wide] + bias[rows, :wide])
            scores = (inner_prod[rows, :wide] * decay).astype(jnp.bfloat16)
            halves.append(jnp.dot(scores, moved[:wide], preferred_element_type=jnp.float32))
        inner = jnp.where(first, halves[0], halves[1])
        inner_ref[rows] = inner
        y_ref[rows] = (inner + skip * xc[rows]).astype(jnp.bfloat16)


def scan_backward(h_own, n_seq, heads_row, x_ref, bc_ref, dt_ref, segc_ref, segr_ref, wx_ref, wbc_ref,
                  head_ref, dy_ref, inner_ref, dx_ref, dbc_ref, ddt_ref, gx_ref, gbc_ref, gh_ref,
                  dt_cols, cum_cols, cum_rows, inner_prod, bias, d_inner, d_cum, d_dt):
    pair = pl.program_id(1)
    n_pair = pl.num_programs(1)
    length = x_ref.shape[0]
    seg_col = segc_ref[0]
    keep = keep_masks(seg_col)
    f32, bf16 = jnp.float32, jnp.bfloat16

    @pl.when(pair == 0)
    def prepare():
        head_prep(dt_ref[...], head_ref[...], h_own, n_seq, heads_row, dt_cols, cum_cols, cum_rows)
        _, _, bc = conv_silu(bc_ref[...].astype(f32), wbc_ref[0:CONV], wbc_ref[CONV : CONV + 1], keep)
        inner_prod[...] = lax.dot_general(
            bc[:, :NST], bc[:, NST:], (((1,), (1,)), ((), ())),
            precision=lax.Precision.HIGHEST, preferred_element_type=f32,
        )
        source = lax.broadcasted_iota(jnp.int32, (length, length), 0)
        at = lax.broadcasted_iota(jnp.int32, (length, length), 1)
        bias[...] = jnp.where((source <= at) & (seg_col == segr_ref[0]), 0.0, FAR)
        d_inner[...] = jnp.zeros((length, length), f32)
        d_cum[...] = jnp.zeros((length, 128), f32)
        d_dt[...] = jnp.zeros((length, 128), f32)

    x_in = x_ref[...].astype(f32)
    taps = wx_ref[0:CONV]
    total, gate, xc = conv_silu(x_in, taps, wx_ref[CONV : CONV + 1], keep)
    dt_wide = pair_wide(dt_cols, pair)
    moved = (xc * dt_wide).astype(bf16)
    skip = wx_ref[CONV + 1 : CONV + 2]
    dy = dy_ref[...]
    first = lax.broadcasted_iota(jnp.int32, (TILE, 128), 1) < HDIM
    pieces = []
    for block in range(length // TILE):
        rows, later = slice(block * TILE, (block + 1) * TILE), slice(block * TILE, length)
        halves = []
        for half in range(2):
            head = 2 * pair + half
            decay = jnp.exp2(cum_rows[head, :, later] - cum_cols[head, rows] + bias[rows, later])
            scores = (inner_prod[rows, later] * decay).astype(bf16)
            halves.append(jnp.dot(scores, dy[later], preferred_element_type=f32))
            mine = jnp.where(first if half == 0 else ~first, moved[rows].astype(f32), 0.0).astype(bf16)
            d_scores = lax.dot_general(
                mine, dy[later], (((1,), (1,)), ((), ())), preferred_element_type=f32
            )
            d_inner[rows, later] += d_scores * decay
        pieces.append(jnp.where(first, halves[0], halves[1]))
    d_moved = jnp.concatenate(pieces, axis=0)
    dy_f = dy.astype(f32)
    change = dy_f * inner_ref[...] - moved.astype(f32) * d_moved
    direct = d_moved * xc
    lane = lax.broadcasted_iota(jnp.int32, (length, 128), 1)
    low = lane < HDIM
    for half in range(2):
        mine = low if half == 0 else ~low
        place = lane == 2 * pair + half
        d_cum[...] += jnp.where(place, jnp.sum(jnp.where(mine, change, 0.0), axis=1, keepdims=True), 0.0)
        d_dt[...] += jnp.where(place, jnp.sum(jnp.where(mine, direct, 0.0), axis=1, keepdims=True), 0.0)
    d_xc = d_moved * dt_wide + skip * dy_f
    d_x, tap_rows, d_offset = conv_back(d_xc, total, gate, x_in, taps, keep)
    dx_ref[...] = d_x.astype(bf16)
    d_skip = jnp.sum(dy_f * xc, axis=0, keepdims=True)
    blank = jnp.zeros((2, 128), f32)
    gx_ref[0] = jnp.concatenate(tap_rows + [d_offset, d_skip, blank], axis=0)

    @pl.when(pair == n_pair - 1)
    def finish():
        bc_in = bc_ref[...].astype(f32)
        taps_bc = wbc_ref[0:CONV]
        total_bc, gate_bc, bc = conv_silu(bc_in, taps_bc, wbc_ref[CONV : CONV + 1], keep)
        d_in = d_inner[...]
        d_b = jnp.dot(d_in, bc[:, NST:], precision=lax.Precision.HIGHEST, preferred_element_type=f32)
        d_c = lax.dot_general(
            d_in, bc[:, :NST], (((0,), (0,)), ((), ())),
            precision=lax.Precision.HIGHEST, preferred_element_type=f32,
        )
        d_bc, rows_bc, offset_bc = conv_back(
            jnp.concatenate([d_b, d_c], axis=1), total_bc, gate_bc, bc_in, taps_bc, keep
        )
        dbc_ref[...] = d_bc.astype(bf16)
        gbc_ref[0] = jnp.concatenate(rows_bc + [offset_bc, jnp.zeros((3, 2 * NST), f32)], axis=0)
        shifted, dt = step_sizes_of(dt_ref[...], head_ref[...], h_own, n_seq, heads_row)
        rates = -jnp.exp(head_ref[1:2])
        across = jnp.transpose(d_cum[...])
        d_log_t = lane_sums(across[:h_own], True)
        pad = jnp.zeros((128 - h_own, length), f32)
        d_log = jnp.transpose(jnp.concatenate([d_log_t, pad], axis=0))
        d_raw = (d_log * rates + d_dt[...]) * jax.nn.sigmoid(shifted)
        ddt_ref[...] = d_raw
        gh_ref[0] = jnp.concatenate(
            [
                jnp.sum(d_raw, axis=0, keepdims=True),
                jnp.sum(d_log * dt, axis=0, keepdims=True) * rates,
                jnp.zeros((6, 128), f32),
            ],
            axis=0,
        )


def scan_specs(length, all_heads):
    return [
        pl.BlockSpec((length, 128), lambda q, p: (q, p)),
        pl.BlockSpec((length, 2 * NST), lambda q, p: (q, 0)),
        pl.BlockSpec((length, all_heads), lambda q, p: (q, 0)),
        pl.BlockSpec((1, length, 1), lambda q, p: (q, 0, 0)),
        pl.BlockSpec((1, 1, length), lambda q, p: (q, 0, 0)),
        pl.BlockSpec((8, 128), lambda q, p: (0, p)),
        pl.BlockSpec((8, 2 * NST), lambda q, p: (0, 0)),
        pl.BlockSpec((8, 128), lambda q, p: (0, 0)),
    ]


def scan_scratch(length, h_own):
    f32 = jnp.float32
    return [
        pltpu.VMEM((h_own, length, 1), f32),
        pltpu.VMEM((h_own, length, 1), f32),
        pltpu.VMEM((h_own, 1, length), f32),
        pltpu.VMEM((length, length), f32),
        pltpu.VMEM((length, length), f32),
    ]


def run_forward(n_own, h_own, n_seq, heads_row, operands):
    tokens, chan = operands[0].shape
    length = tokens // n_own
    pair_block = pl.BlockSpec((length, 128), lambda q, p: (q, p))
    return pl.pallas_call(
        functools.partial(scan_forward, h_own, n_seq, heads_row),
        grid=(n_own, chan // 128),
        in_specs=scan_specs(length, operands[2].shape[1]),
        out_specs=[pair_block, pair_block],
        out_shape=[
            jax.ShapeDtypeStruct((tokens, chan), jnp.bfloat16),
            jax.ShapeDtypeStruct((tokens, chan), jnp.float32),
        ],
        scratch_shapes=scan_scratch(length, h_own),
        compiler_params=pltpu.CompilerParams(vmem_limit_bytes=48 << 20),
        name="scan_forward",
    )(*operands)


def run_backward(n_own, h_own, n_seq, heads_row, operands, d_y, inner):
    f32 = jnp.float32
    tokens, chan = operands[0].shape
    length = tokens // n_own
    pair_block = pl.BlockSpec((length, 128), lambda q, p: (q, p))
    return pl.pallas_call(
        functools.partial(scan_backward, h_own, n_seq, heads_row),
        grid=(n_own, chan // 128),
        in_specs=scan_specs(length, operands[2].shape[1]) + [pair_block, pair_block],
        out_specs=[
            pair_block,
            pl.BlockSpec((length, 2 * NST), lambda q, p: (q, 0)),
            pl.BlockSpec((length, 128), lambda q, p: (q, 0)),
            pl.BlockSpec((1, 8, 128), lambda q, p: (q, 0, p)),
            pl.BlockSpec((1, 8, 2 * NST), lambda q, p: (q, 0, 0)),
            pl.BlockSpec((1, 8, 128), lambda q, p: (q, 0, 0)),
        ],
        out_shape=[
            jax.ShapeDtypeStruct((tokens, chan), jnp.bfloat16),
            jax.ShapeDtypeStruct((tokens, 2 * NST), jnp.bfloat16),
            jax.ShapeDtypeStruct((tokens, 128), f32),
            jax.ShapeDtypeStruct((n_own, 8, chan), f32),
            jax.ShapeDtypeStruct((n_own, 8, 2 * NST), f32),
            jax.ShapeDtypeStruct((n_own, 8, 128), f32),
        ],
        scratch_shapes=scan_scratch(length, h_own)
        + [
            pltpu.VMEM((length, length), f32),
            pltpu.VMEM((length, 128), f32),
            pltpu.VMEM((length, 128), f32),
        ],
        compiler_params=pltpu.CompilerParams(vmem_limit_bytes=56 << 20),
        name="scan_backward",
    )(*operands, d_y, inner)


MESH = pl.DeviceIdType.MESH
WIDE = 8


def place():
    dp, s = lax.axis_index("dp"), lax.axis_index("seq")
    z, x = s // 2, s % 2
    y, core = dp // 2, dp % 2
    return dp, s, z, x, s + 1 - 2 * x, dp + 2 - 4 * y, dp + 1 - 2 * core


def greet(peers):
    barrier = pltpu.get_barrier_semaphore()
    for device in peers:
        pl.semaphore_signal(barrier, inc=1, device_id=device, device_id_type=MESH)
    pl.semaphore_wait(barrier, len(peers))


def remote(src, dst, send, recv, device):
    return pltpu.make_async_remote_copy(
        src_ref=src, dst_ref=dst, send_sem=send, recv_sem=recv, device_id=device, device_id_type=MESH
    )


class TokenGather:
    def __init__(self, own, full, send, recv, where):
        self.own, self.full, self.send, self.recv = own, full, send, recv
        self.dp, self.s, self.z, self.x, self.x_peer, _, _ = where
        self.span = own.shape[1]

    def part(self, shard, q):
        return self.full.at[q, pl.ds(pl.multiple_of(shard * self.span, self.span), self.span)]

    def copy(self, shard_z, way, q, mine):
        shard = shard_z * 2 + self.x
        target = (self.s + 2, self.s - 2, self.x_peer)[way]
        src = self.own.at[q] if mine else self.part(shard, q)
        return remote(
            src, self.part(shard, q), self.send.at[way, shard_z, q], self.recv.at[shard, q], (self.dp, target)
        )

    def arrived(self, shard, q):
        part = self.part(shard, q)
        remote(part, part, self.send.at[0, 0, q], self.recv.at[shard, q], (self.dp, self.x_peer)).wait_recv()

    def start(self, q):
        @pl.when(self.z < 3)
        def up():
            self.copy(self.z, 0, q, True).start()

        @pl.when(self.z > 0)
        def down():
            self.copy(self.z, 1, q, True).start()

        self.copy(self.z, 2, q, True).start()

    def step(self, hop, q):
        @pl.when(self.z >= hop)
        def from_below():
            shard_z = self.z - hop
            self.arrived(shard_z * 2 + self.x, q)

            @pl.when(self.z < 3)
            def up():
                self.copy(shard_z, 0, q, False).start()

            self.copy(shard_z, 2, q, False).start()

        @pl.when(self.z + hop <= 3)
        def from_above():
            shard_z = self.z + hop
            self.arrived(shard_z * 2 + self.x, q)

            @pl.when(self.z > 0)
            def down():
                self.copy(shard_z, 1, q, False).start()

            self.copy(shard_z, 2, q, False).start()

    def finish(self, q):
        for shard_z in range(4):
            self.arrived(shard_z * 2 + 1 - self.x, q)
        for shard_z in range(4):
            self.copy(shard_z, 2, q, False).wait_send()

            @pl.when((self.z < 3) & (self.z >= shard_z))
            def up():
                self.copy(shard_z, 0, q, False).wait_send()

            @pl.when((self.z > 0) & (self.z <= shard_z))
            def down():
                self.copy(shard_z, 1, q, False).wait_send()


def gather_kernel(normed, cot, in_w, in_tail, out_w, seg, n_all, c_all, w_in, w_out, seg_all,
                  n_send, n_recv, c_send, c_recv, wide_send, tail_send, wide_recv, tail_recv,
                  y_send, core_send, cross_send, block_recv, out_send, out_recv, seg_send, seg_recv, local):
    where = place()
    dp, s, z, x, x_peer, y_peer, core_peer = where
    peers = [(dp, (s + k) % 8) for k in range(1, 8)] + [(y_peer, s), (core_peer, s)]
    greet(peers)
    in_rows, rows = in_w.shape[0], out_w.shape[0]
    chan = w_out.shape[0]
    tail = in_tail.shape[1]

    def block(d, shard, lo=0, size=None):
        size = w_in.shape[1] if size is None else size
        at = pl.multiple_of((d * 8 + shard) * in_rows, in_rows)
        return w_in.at[pl.ds(at, in_rows), pl.ds(lo, size)]

    def wide_src(piece, target):
        at = pl.multiple_of((piece * 8 + target) * rows, rows)
        return in_w.at[:, pl.ds(at, rows)]


    def push(k, _):
        target = (s + k) % 8
        remote(seg, seg_all.at[s], seg_send.at[k], seg_recv.at[s], (dp, target)).start()
        for piece in range(WIDE):
            remote(
                wide_src(piece, target), block(dp, s, piece * rows, rows), wide_send.at[k], wide_recv.at[s],
                (dp, target),
            ).start()
        remote(in_tail, block(dp, s, 2 * chan, tail), tail_send.at[k], tail_recv.at[s], (dp, target)).start()
        return 0

    lax.fori_loop(1, 8, push, 0)
    tokens = TokenGather(normed, n_all, n_send, n_recv, where)
    cots = TokenGather(cot, c_all, c_send, c_recv, where)
    for q in range(2):
        tokens.start(q)
    own_copies = []
    for piece in range(WIDE):
        own_copies.append(pltpu.make_async_copy(wide_src(piece, s), block(dp, s, piece * rows, rows), local.at[piece]))
    own_copies.append(pltpu.make_async_copy(in_tail, block(dp, s, 2 * chan, tail), local.at[8]))
    later_copies = [
        pltpu.make_async_copy(out_w, w_out.at[pl.ds(pl.multiple_of(dp * rows, rows), rows)], local.at[9]),
        pltpu.make_async_copy(seg, seg_all.at[s], local.at[10]),
    ]
    for q in range(2):
        later_copies.append(pltpu.make_async_copy(normed.at[q], tokens.part(s, q), local.at[11 + q]))
        later_copies.append(pltpu.make_async_copy(cot.at[q], cots.part(s, q), local.at[13 + q]))
    for copy in own_copies + later_copies:
        copy.start()
    for copy in own_copies:
        copy.wait()

    def spread(shard, shard_sem):
        remote(block(dp, shard), block(dp, shard), y_send.at[shard_sem], block_recv.at[dp, shard], (y_peer, s)).start()
        remote(
            block(dp, shard), block(dp, shard), core_send.at[shard_sem], block_recv.at[dp, shard], (core_peer, s)
        ).start()

    spread(s, 0)
    out_block = w_out.at[pl.ds(pl.multiple_of(dp * rows, rows), rows)]

    def forward(k, _):
        source = (s + 8 - k) % 8
        remote(
            block(dp, source, 0, 2 * chan), block(dp, source, 0, 2 * chan), wide_send.at[k], wide_recv.at[source],
            (dp, x_peer),
        ).wait_recv()
        remote(
            block(dp, source, 2 * chan, tail), block(dp, source, 2 * chan, tail), tail_send.at[k],
            tail_recv.at[source], (dp, x_peer),
        ).wait_recv()
        spread(source, k)
        return 0

    def cross(k, _):
        source = (s + 8 - k) % 8
        there = block(y_peer, source)
        copy = remote(there, there, cross_send.at[k], block_recv.at[y_peer, source], (core_peer, s))
        copy.wait_recv()
        copy.start()
        return 0

    tokens.step(1, 0)
    lax.fori_loop(1, 4, forward, 0)
    tokens.step(1, 1)
    lax.fori_loop(4, 8, forward, 0)
    tokens.step(2, 0)
    lax.fori_loop(0, 4, cross, 0)
    tokens.step(2, 1)
    lax.fori_loop(4, 8, cross, 0)
    tokens.step(3, 0)
    tokens.step(3, 1)
    for q in range(2):
        cots.start(q)

    def out_part(d):
        return w_out.at[pl.ds(pl.multiple_of(d * rows, rows), rows)]

    remote(out_w, out_part(dp), out_send.at[0], out_recv.at[dp], (y_peer, s)).start()
    remote(out_w, out_part(dp), out_send.at[1], out_recv.at[dp], (core_peer, s)).start()
    for hop in range(1, 4):
        for q in range(2):
            cots.step(hop, q)
    out_cross = remote(out_part(y_peer), out_part(y_peer), out_send.at[2], out_recv.at[y_peer], (core_peer, s))
    out_cross.wait_recv()
    out_cross.start()
    for q in range(2):
        tokens.finish(q)
        cots.finish(q)
    for copy in later_copies:
        copy.wait()

    def settle(k, _):
        shard = (s + 8 - k) % 8
        for d in (core_peer, core_peer + y_peer - dp):
            there = block(d, shard)
            remote(there, there, core_send.at[k], block_recv.at[d, shard], (core_peer, s)).wait_recv()
        there = block(dp, shard)
        remote(there, there, y_send.at[k], block_recv.at[dp, shard], (y_peer, s)).wait_send()
        remote(there, there, core_send.at[k], block_recv.at[dp, shard], (core_peer, s)).wait_send()
        remote(there, there, cross_send.at[k], block_recv.at[dp, shard], (core_peer, s)).wait_send()
        return 0

    lax.fori_loop(0, 8, settle, 0)

    def settle_push(k, _):
        source = (s + 8 - k) % 8
        remote(seg, seg_all.at[source], seg_send.at[k], seg_recv.at[source], (dp, x_peer)).wait_recv()
        remote(seg, seg_all.at[source], seg_send.at[k], seg_recv.at[source], (dp, x_peer)).wait_send()
        remote(
            block(dp, source, 0, 2 * chan), block(dp, source, 0, 2 * chan), wide_send.at[k], wide_recv.at[source],
            (dp, x_peer),
        ).wait_send()
        remote(
            block(dp, source, 2 * chan, tail), block(dp, source, 2 * chan, tail), tail_send.at[k],
            tail_recv.at[source], (dp, x_peer),
        ).wait_send()
        return 0

    lax.fori_loop(1, 8, settle_push, 0)
    for d in (core_peer, core_peer + y_peer - dp):
        remote(out_part(d), out_part(d), out_send.at[0], out_recv.at[d], (core_peer, s)).wait_recv()
    for k in range(3):
        remote(out_w, out_part(dp), out_send.at[k], out_recv.at[dp], (core_peer, s)).wait_send()


def run_gather(normed, cot, in_w, in_tail, out_w, seg):
    bf16 = jnp.bfloat16
    n_own, span, width = normed.shape
    in_rows, rows = in_w.shape[0], out_w.shape[0]
    chan = 4 * rows
    columns = 2 * chan + in_tail.shape[1]
    sem = pltpu.SemaphoreType.DMA
    return pl.pallas_call(
        gather_kernel,
        in_specs=[pl.BlockSpec(memory_space=pl.ANY)] * 6,
        out_specs=[pl.BlockSpec(memory_space=pl.ANY)] * 5,
        out_shape=[
            jax.ShapeDtypeStruct((n_own, 8 * span, width), bf16),
            jax.ShapeDtypeStruct((n_own, 8 * span, width), bf16),
            jax.ShapeDtypeStruct((32 * in_rows, columns), bf16),
            jax.ShapeDtypeStruct((chan, width), bf16),
            jax.ShapeDtypeStruct((8, 8, 128), jnp.float32),
        ],
        scratch_shapes=[
            sem((3, 4, 2)), sem((8, 2)), sem((3, 4, 2)), sem((8, 2)),
            sem((8,)), sem((8,)), sem((8,)), sem((8,)),
            sem((8,)), sem((8,)), sem((8,)), sem((4, 8)), sem((3,)), sem((4,)), sem((8,)), sem((8,)), sem((15,)),
        ],
        compiler_params=pltpu.CompilerParams(collective_id=0, has_side_effects=True),
        name="gather",
    )(normed, cot, in_w, in_tail, out_w, seg)


class TokenReduce:
    def __init__(self, part, from_x, from_near, from_far, x_sems, near_sems, far_sems, where, span):
        self.part, self.from_x, self.from_near, self.from_far = part, from_x, from_near, from_far
        self.x_sems, self.near_sems, self.far_sems, self.span = x_sems, near_sems, far_sems, span
        self.dp, self.s, self.z, self.x, self.x_peer, _, _ = where
        self.near = self.s + 2 - 4 * (self.z % 2)
        self.far = self.s + 4 - 8 * (self.z // 2)

    def rows(self, shard, q):
        return self.part.at[q, pl.ds(pl.multiple_of(shard * self.span, self.span), self.span)]

    def x_copy(self, shard_z, q):
        return remote(
            self.rows(shard_z * 2 + 1 - self.x, q), self.from_x.at[shard_z, q],
            self.x_sems.at[0, shard_z, q], self.x_sems.at[1, shard_z, q], (self.dp, self.x_peer),
        )

    def near_copy(self, high, q):
        shard = (high * 2 + 1 - self.z % 2) * 2 + self.x
        return remote(
            self.rows(shard, q), self.from_near.at[high, q],
            self.near_sems.at[0, high, q], self.near_sems.at[1, high, q], (self.dp, self.near),
        )

    def far_copy(self, q):
        shard = ((1 - self.z // 2) * 2 + self.z % 2) * 2 + self.x
        return remote(
            self.rows(shard, q), self.from_far.at[q], self.far_sems.at[0, q], self.far_sems.at[1, q],
            (self.dp, self.far),
        )

    def start(self, q):
        for high in range(2):
            for low in range(2):
                shard_z = (1 - self.z // 2 + high) % 2 * 2 + (1 - self.z % 2 + low) % 2
                self.x_copy(shard_z, q).start()

    def add(self, shard, q, other):
        rows = self.rows(shard, q)
        rows[...] = (rows[...].astype(jnp.float32) + other[...].astype(jnp.float32)).astype(jnp.bfloat16)

    def step_near(self, q):
        for turn in range(2):
            high = (1 - self.z // 2 + turn) % 2
            shard_z = high * 2 + 1 - self.z % 2
            self.x_copy(shard_z, q).wait_recv()
            self.add(shard_z * 2 + self.x, q, self.from_x.at[shard_z, q])
            self.near_copy(high, q).start()
        for turn in range(2):
            high = (1 - self.z // 2 + turn) % 2
            shard_z = high * 2 + self.z % 2
            self.x_copy(shard_z, q).wait_recv()
            self.add(shard_z * 2 + self.x, q, self.from_x.at[shard_z, q])

    def step_far(self, q):
        high = 1 - self.z // 2
        self.near_copy(high, q).wait_recv()
        self.add((high * 2 + self.z % 2) * 2 + self.x, q, self.from_near.at[high, q])
        self.far_copy(q).start()

    def total(self, q):
        high = self.z // 2
        self.near_copy(high, q).wait_recv()
        self.far_copy(q).wait_recv()
        f32 = jnp.float32
        return (
            self.rows(self.s, q)[...].astype(f32)
            + self.from_near[high, q].astype(f32)
            + self.from_far[q].astype(f32)
        )

    def settle(self):
        for q in range(2):
            for shard_z in range(4):
                self.x_copy(shard_z, q).wait_send()
            for high in range(2):
                self.near_copy(high, q).wait_send()
            self.far_copy(q).wait_send()


def finish_kernel(gated, w_out, d_z, d_x, d_bc, d_dt, w_in, cot_all, normed_all, hidden, cot, gain, small,
                  result, d_hidden, grad_in, grad_out, small_all, gain_sum,
                  gated_v, w_out_v, dp_v, w_in_v, tok_v,
                  part_r, rx, rn, rf, part_d, dx, dn, df,
                  core_out, core_in, keep, y_in, plane_in,
                  out_core, out_core_in, out_keep, out_y, out_y_in, small_v, small_in, gain_v, gain_in,
                  load, rxs, rns, rfs, dxs, dns, dfs, core_sems, y_sems, plane_sems, out_sems, out_y_sems,
                  small_sems, small_plane, gain_sems, gain_plane):
    f32, bf16 = jnp.float32, jnp.bfloat16
    where = place()
    dp, s, z, x, x_peer, y_peer, core_peer = where
    y, core = dp // 2, dp % 2
    n_own, span, width = hidden.shape
    length = 8 * span
    chan = w_out.shape[0]
    rows = chan // 4
    in_rows = grad_in.shape[0]
    columns = keep.shape[3]
    tail = columns - 2 * chan
    peers = [(dp, (s + k) % 8) for k in range(1, 8)] + [(y_peer, s), (core_peer, s)]
    loads = [
        pltpu.make_async_copy(gated, gated_v, load.at[0]),
        pltpu.make_async_copy(w_out, w_out_v, load.at[1]),
        pltpu.make_async_copy(d_z, dp_v.at[:, pl.ds(0, chan)], load.at[2]),
        pltpu.make_async_copy(d_x, dp_v.at[:, pl.ds(chan, chan)], load.at[3]),
        pltpu.make_async_copy(d_bc, dp_v.at[:, pl.ds(2 * chan, 2 * NST)], load.at[4]),
        pltpu.make_async_copy(d_dt, dp_v.at[:, pl.ds(2 * chan + 2 * NST, 128)], load.at[5]),
        pltpu.make_async_copy(w_in, w_in_v, load.at[6]),
        pltpu.make_async_copy(cot_all, tok_v, load.at[7]),
    ]
    for copy in loads:
        copy.start()
    greet(peers)
    small_v[0] = small[...]

    def small_copy(stage, device):
        return remote(small_v.at[stage], small_in.at[stage], small_sems.at[0, stage], small_sems.at[1, stage], device)

    small_core = small_copy(0, (core_peer, s))
    small_core.start()
    reduce_r = TokenReduce(part_r, rx, rn, rf, rxs, rns, rfs, where, span)
    reduce_d = TokenReduce(part_d, dx, dn, df, dxs, dns, dfs, where, span)
    loads[0].wait()
    loads[1].wait()
    step = 512
    for q in range(2):

        @pl.loop(0, width // step)
        def forward(n):
            cols = pl.ds(pl.multiple_of(n * step, step), step)
            part_r[q, :, cols] = jnp.dot(
                gated_v[q * length : (q + 1) * length], w_out_v[:, cols], preferred_element_type=f32
            ).astype(bf16)

        reduce_r.start(q)
    for copy in loads[2:7]:
        copy.wait()
    for q in range(2):

        @pl.loop(0, width // step)
        def backward(n):
            cols = pl.ds(pl.multiple_of(n * step, step), step)
            part_d[q, :, cols] = lax.dot_general(
                dp_v[q * length : (q + 1) * length], w_in_v[cols], (((1,), (1,)), ((), ())),
                preferred_element_type=f32,
            ).astype(bf16)

        reduce_d.start(q)

    small_core.wait_recv()
    small_v[1] = small_v[0] + small_in[0]
    small_y = small_copy(1, (y_peer, s))
    small_y.start()
    loads[7].wait()

    def out_term(d, n):
        lanes = pl.ds(pl.multiple_of(d * rows, rows), rows)
        return lax.dot_general(
            gated_v[:, lanes], tok_v[:, n * step : (n + 1) * step], (((0,), (0,)), ((), ())),
            preferred_element_type=f32,
        )

    def out_core_copy(yy):
        return remote(out_core.at[yy], out_core_in.at[yy], out_sems.at[0, yy], out_sems.at[1, yy], (core_peer, s))

    for yy in range(2):
        for n in range(width // step):
            out_core[yy, :, n * step : (n + 1) * step] = out_term(yy * 2 + 1 - core, n).astype(bf16)
        out_core_copy(yy).start()
    for yy in range(2):
        for n in range(width // step):
            out_keep[yy, :, n * step : (n + 1) * step] = out_term(yy * 2 + core, n)
    norm_load = pltpu.make_async_copy(normed_all, tok_v, load.at[8])
    norm_load.start()
    reduce_r.step_near(0)
    out_core_copy(1 - y).wait_recv()
    out_y[...] = (out_keep[1 - y] + out_core_in[1 - y].astype(f32)).astype(bf16)
    out_y_copy = remote(out_y, out_y_in, out_y_sems.at[0], out_y_sems.at[1], (y_peer, s))
    out_y_copy.start()
    small_y.wait_recv()
    small_all[s] = small_v[1] + small_in[1]

    def small_push(k):
        return remote(
            small_all.at[s], small_all.at[s], small_plane.at[0, k], small_plane.at[1, s], (dp, (s + k) % 8)
        )

    for k in range(1, 8):
        small_push(k).start()
    norm_load.wait()

    def in_term(d, m, lo, size):
        lanes = pl.ds(pl.multiple_of(d * 8 * in_rows + m * 2 * in_rows, 2 * in_rows), 2 * in_rows)
        return lax.dot_general(
            tok_v[:, lanes], dp_v[:, lo : lo + size], (((0,), (0,)), ((), ())), preferred_element_type=f32
        )

    pieces = ((0, chan, chan), (chan, chan, chan), (2 * chan, tail, 2 * NST + 128))

    def core_copy(m, yy):
        return remote(core_out.at[m, yy], core_in.at[m, yy], core_sems.at[0, m, yy], core_sems.at[1, m, yy], (core_peer, s))

    def y_copy(m):
        return remote(keep.at[m, 1 - y], y_in.at[m], y_sems.at[0, m], y_sems.at[1, m], (y_peer, s))

    def in_compute(m):
        for yy in range(2):
            for lo, size, span_in in pieces:
                core_out[m, yy, :, lo : lo + size] = in_term(yy * 2 + 1 - core, m, lo, span_in)[:, :size].astype(bf16)
            core_copy(m, yy).start()
        for yy in range(2):
            for lo, size, span_in in pieces:
                keep[m, yy, :, lo : lo + size] = in_term(yy * 2 + core, m, lo, span_in)[:, :size].astype(bf16)

    def in_core(m):
        for yy in range(2):
            core_copy(m, yy).wait_recv()
            keep[m, yy] = (keep[m, yy].astype(f32) + core_in[m, yy].astype(f32)).astype(bf16)
        y_copy(m).start()

    def plane_copy(m, half):
        target = 2 * m + half
        return remote(
            keep.at[m, y, pl.ds(half * in_rows, in_rows)], plane_in.at[s],
            plane_sems.at[0, target], plane_sems.at[1, s], (dp, target),
        )

    def in_plane(m):
        y_copy(m).wait_recv()
        keep[m, y] = (keep[m, y].astype(f32) + y_in[m].astype(f32)).astype(bf16)
        for half in range(2):

            @pl.when(s != 2 * m + half)
            def away():
                plane_copy(m, half).start()

            @pl.when(s == 2 * m + half)
            def here():
                plane_in[s] = keep[m, y, half * in_rows : (half + 1) * in_rows]

    in_compute(0)
    in_compute(1)
    in_core(0)
    reduce_r.step_near(1)
    in_compute(2)
    in_core(1)
    reduce_r.step_far(0)
    in_compute(3)
    in_core(2)
    in_plane(0)
    in_core(3)
    reduce_r.step_far(1)
    in_plane(1)
    reduce_d.step_near(0)
    in_plane(2)
    hidden_f = [hidden[q].astype(f32) for q in range(2)]
    for q in range(2):
        result[q] = (hidden[q].astype(f32) + reduce_r.total(q)).astype(bf16)
    in_plane(3)
    reduce_d.step_far(0)
    out_y_copy.wait_recv()
    out_core_copy(y).wait_recv()
    grad_out[...] = out_keep[y] + out_core_in[y].astype(f32) + out_y_in[...].astype(f32)
    reduce_d.step_near(1)
    reduce_d.step_far(1)
    gain_row = gain[...]
    gain_part = None
    for q in range(2):
        d_normed = reduce_d.total(q)
        h = hidden[q].astype(f32)
        inv = lax.rsqrt(jnp.mean(h * h, axis=-1, keepdims=True) + 1e-05)
        scaled = d_normed * gain_row
        along = jnp.mean(scaled * h, axis=-1, keepdims=True)
        d_hidden[q] = (cot[q].astype(f32) + inv * scaled - (inv * inv * inv) * along * h).astype(bf16)
        term = jnp.sum(d_normed * h * inv, axis=0, keepdims=True)
        gain_part = term if q == 0 else gain_part + term
    folded = width // 8
    gain_v[0] = jnp.concatenate([gain_part[:, k * folded : (k + 1) * folded] for k in range(8)], axis=0)

    def gain_copy(stage, device):
        return remote(gain_v.at[stage], gain_in.at[stage], gain_sems.at[0, stage], gain_sems.at[1, stage], device)

    gain_core = gain_copy(0, (core_peer, s))
    gain_core.start()
    for k in range(1, 8):
        source = (s + 8 - k) % 8
        remote(plane_in.at[source], plane_in.at[source], plane_sems.at[0, source], plane_sems.at[1, source], (dp, x_peer)).wait_recv()
    gain_core.wait_recv()
    gain_v[1] = gain_v[0] + gain_in[0]
    gain_y = gain_copy(1, (y_peer, s))
    gain_y.start()
    tail_sum = None
    for source in range(8):
        for piece in range(WIDE):
            at = (piece * 8 + source) * rows
            grad_in[:, at : at + rows] = plane_in[source, :, piece * rows : (piece + 1) * rows].astype(f32)
        term = plane_in[source, :, 2 * chan :].astype(f32)
        tail_sum = term if source == 0 else tail_sum + term
    grad_in[:, 2 * DI :] = tail_sum
    gain_y.wait_recv()
    gain_v[2 + s] = gain_v[1] + gain_in[1]

    def gain_push(k):
        return remote(gain_v.at[2 + s], gain_v.at[2 + s], gain_plane.at[0, k], gain_plane.at[1, s], (dp, (s + k) % 8))

    for k in range(1, 8):
        gain_push(k).start()
    reduce_r.settle()
    reduce_d.settle()
    small_core.wait_send()
    small_y.wait_send()
    out_y_copy.wait_send()
    for yy in range(2):
        out_core_copy(yy).wait_send()
    for m in range(4):
        for yy in range(2):
            core_copy(m, yy).wait_send()
        y_copy(m).wait_send()
        for half in range(2):

            @pl.when(s != 2 * m + half)
            def sent():
                plane_copy(m, half).wait_send()

    for k in range(1, 8):
        source = (s + 8 - k) % 8
        remote(
            small_all.at[source], small_all.at[source], small_plane.at[0, k], small_plane.at[1, source], (dp, x_peer)
        ).wait_recv()
        small_push(k).wait_send()
        remote(
            gain_v.at[2 + source], gain_v.at[2 + source], gain_plane.at[0, k], gain_plane.at[1, source], (dp, x_peer)
        ).wait_recv()
        gain_push(k).wait_send()
    gain_core.wait_send()
    gain_y.wait_send()
    gain_total = gain_v[2]
    for source in range(1, 8):
        gain_total = gain_total + gain_v[2 + source]
    gain_sum[...] = gain_total


def run_finish(gated, w_out, d_z, d_x, d_bc, d_dt, w_in, cot_all, normed_all, hidden, cot, gain, small, in_rows):
    f32, bf16 = jnp.float32, jnp.bfloat16
    n_own, span, width = hidden.shape
    tokens, chan = gated.shape
    length, rows = 8 * span, chan // 4
    columns = 2 * chan + 2 * NST + HEADS
    vmem = pltpu.VMEM
    anywhere, inside = pl.BlockSpec(memory_space=pl.ANY), pl.BlockSpec(memory_space=vmem)
    sem = pltpu.SemaphoreType.DMA
    tokens_like = [
        vmem((n_own, length, width), bf16), vmem((4, n_own, span, width), bf16),
        vmem((2, n_own, span, width), bf16), vmem((n_own, span, width), bf16),
    ]
    return pl.pallas_call(
        finish_kernel,
        in_specs=[anywhere] * 9 + [inside] * 4,
        out_specs=[inside] * 6,
        out_shape=[
            jax.ShapeDtypeStruct(hidden.shape, bf16),
            jax.ShapeDtypeStruct(hidden.shape, bf16),
            jax.ShapeDtypeStruct((in_rows, 2 * DI + columns - 2 * chan), f32),
            jax.ShapeDtypeStruct((rows, width), f32),
            jax.ShapeDtypeStruct((8,) + small.shape, f32),
            jax.ShapeDtypeStruct((8, width // 8), f32),
        ],
        scratch_shapes=[
            vmem((tokens, chan), bf16), vmem((chan, width), bf16),
            vmem((tokens, 2 * chan + 2 * NST + 128), bf16), vmem((width, 2 * chan + 2 * NST + 128), bf16),
            vmem((tokens, width), bf16),
        ]
        + tokens_like + tokens_like
        + [
            vmem((4, 2, 2 * in_rows, columns), bf16), vmem((4, 2, 2 * in_rows, columns), bf16),
            vmem((4, 2, 2 * in_rows, columns), bf16), vmem((4, 2 * in_rows, columns), bf16),
            vmem((8, in_rows, columns), bf16),
            vmem((2, rows, width), bf16), vmem((2, rows, width), bf16), vmem((2, rows, width), f32),
            vmem((rows, width), bf16), vmem((rows, width), bf16),
            vmem((2,) + small.shape, f32), vmem((2,) + small.shape, f32),
            vmem((10, 8, width // 8), f32), vmem((2, 8, width // 8), f32),
            sem((9,)), sem((2, 4, 2)), sem((2, 2, 2)), sem((2, 2)), sem((2, 4, 2)), sem((2, 2, 2)), sem((2, 2)),
            sem((2, 4, 2)), sem((2, 4)), sem((2, 8)), sem((2, 2)), sem((2,)),
            sem((2, 2)), sem((2, 8)), sem((2, 2)), sem((2, 8)),
        ],
        compiler_params=pltpu.CompilerParams(
            collective_id=1, has_side_effects=True, vmem_limit_bytes=60 << 20
        ),
        name="finish",
    )(gated, w_out, d_z, d_x, d_bc, d_dt, w_in, cot_all, normed_all, hidden, cot, gain, small)


def head_plan(
    hidden,
    segments,
    in_weight,
    conv_weight,
    conv_bias,
    dt_bias,
    a_log,
    d_skip,
    norm_gain,
    gate_gain,
    out_weight,
    cotangent,
):
    f32, bf16 = jnp.float32, jnp.bfloat16
    n_dp, n_seq = lax.axis_size("dp"), lax.axis_size("seq")
    seq_rank = lax.axis_index("seq")
    n_own, shard_len, width = hidden.shape
    length = shard_len * n_seq
    rows = out_weight.shape[0]
    in_rows = in_weight.shape[0]
    chan = rows * n_dp
    h_own = chan // HDIM
    hidden_f = hidden.astype(f32)
    inv = lax.rsqrt(jnp.mean(hidden_f * hidden_f, axis=-1, keepdims=True) + 1e-05)
    normed = (hidden_f * inv * norm_gain).astype(bf16)
    seg_tile = jnp.pad(segments.astype(f32), ((0, 8 - n_own), (0, 128 - shard_len)))
    in_tail = jnp.pad(in_weight[:, 2 * DI :], ((0, 0), (0, 128 - HEADS)))
    normed_all, cot_all, w_in, w_out, seg_all = run_gather(
        normed, cotangent, in_weight, in_tail, out_weight, seg_tile
    )
    normed_all = normed_all.reshape(n_own * length, width)
    cot_all = cot_all.reshape(n_own * length, width)
    seg_all = seg_all[:, :n_own, :shard_len].swapaxes(0, 1).reshape(n_own, length)

    def own_chan(vec):
        return lax.dynamic_index_in_dim(
            vec.reshape((n_dp, n_seq, rows) + vec.shape[1:]), seq_rank, 1, keepdims=False
        ).reshape((chan,) + vec.shape[1:])

    heads_row = rows // HDIM

    def own_head(vec):
        return lax.dynamic_index_in_dim(
            vec.reshape((n_dp, n_seq, heads_row) + vec.shape[1:]), seq_rank, 1, keepdims=False
        ).reshape((h_own,) + vec.shape[1:])

    def spread_chan(vec):
        blank = jnp.zeros((n_dp, n_seq, rows) + vec.shape[1:], f32)
        piece = vec.reshape((n_dp, 1, rows) + vec.shape[1:])
        return lax.dynamic_update_slice_in_dim(blank, piece, seq_rank, 1).reshape(
            (DI,) + vec.shape[1:]
        )

    def spread_head(vec):
        blank = jnp.zeros((n_dp, n_seq, heads_row) + vec.shape[1:], f32)
        piece = vec.reshape((n_dp, 1, heads_row) + vec.shape[1:])
        return lax.dynamic_update_slice_in_dim(blank, piece, seq_rank, 1).reshape(
            (HEADS,) + vec.shape[1:]
        )

    project = jnp.dot(normed_all, w_in, preferred_element_type=f32)
    z = project[:, :chan]
    x_raw = project[:, chan : 2 * chan].astype(bf16)
    bc_raw = project[:, 2 * chan : 2 * chan + 2 * NST].astype(bf16)
    dt_all = project[:, 2 * chan + 2 * NST : 2 * chan + 2 * NST + HEADS].astype(bf16)
    wx = jnp.concatenate(
        [
            own_chan(conv_weight[:DI]).T,
            own_chan(conv_bias[:DI])[None],
            jnp.repeat(own_head(d_skip), HDIM)[None],
            jnp.zeros((2, chan), f32),
        ],
        axis=0,
    )
    wbc = jnp.concatenate(
        [conv_weight[DI:].T, conv_bias[DI:][None], jnp.zeros((3, 2 * NST), f32)], axis=0
    )
    head_vals = jnp.pad(jnp.stack([own_head(dt_bias), own_head(a_log)]), ((0, 6), (0, 128 - h_own)))
    operands = (x_raw, bc_raw, dt_all, seg_all[:, :, None], seg_all[:, None, :], wx, wbc, head_vals)
    y, inner = run_forward(n_own, h_own, n_seq, heads_row, operands)
    y = y.astype(f32)
    gain = own_chan(gate_gain)
    sig = jax.nn.sigmoid(z)
    act = z * sig
    g = y * act
    d_gated = lax.dot_general(
        cot_all, w_out, (((1,), (1,)), ((), ())), preferred_element_type=f32
    )
    u = d_gated * gain
    sums = lax.psum(jnp.stack([jnp.sum(g * g, axis=1), jnp.sum(u * g, axis=1)]), "seq")
    r = lax.rsqrt(sums[0] / DI + 1e-05)[:, None]
    fall = (r * r * r) * (sums[1] / DI)[:, None]
    gr = g * r
    gated = (gr * gain).astype(bf16)
    d_g = r * u - fall * g
    d_y = (d_g * act).astype(bf16)
    d_z = d_g * y * (sig * (1.0 + z * (1.0 - sig)))
    d_gate_gain = jnp.sum(d_gated * gr, axis=0)
    d_x, d_bc, d_dt, g_x, g_bc, g_head = run_backward(
        n_own, h_own, n_seq, heads_row, operands, d_y, inner
    )
    g_x, g_bc, g_head = jnp.sum(g_x, 0), jnp.sum(g_bc, 0), jnp.sum(g_head, 0)
    g_x = jnp.concatenate([g_x[: CONV + 2], d_gate_gain[None], g_x[CONV + 3 :]], axis=0)
    small = jnp.concatenate([g_x, g_bc, g_head], axis=1)
    d_dt = jnp.pad(spread_head(d_dt[:, :h_own].T).T, ((0, 0), (0, 128 - HEADS))).astype(bf16)
    result, d_hidden, grad_in, grad_out, small_all, gain_sum = run_finish(
        gated, w_out, d_z.astype(bf16), d_x, d_bc, d_dt, w_in, cot_all, normed_all,
        hidden, cotangent, norm_gain[None], small, in_rows,
    )
    over_chan = small_all[:, :, :chan].reshape(n_seq, 8, n_dp, rows)
    over_chan = over_chan.transpose(1, 2, 0, 3).reshape(8, DI)
    over_bc = jnp.sum(small_all[:, :, chan : chan + 2 * NST], axis=0)
    over_head = small_all[:, :2, chan + 2 * NST : chan + 2 * NST + h_own]
    over_head = over_head.reshape(n_seq, 2, n_dp, heads_row).transpose(1, 2, 0, 3).reshape(2, HEADS)
    grad_skip = jnp.sum(over_chan[CONV + 1].reshape(HEADS, HDIM), axis=1)
    return (
        result,
        d_hidden,
        grad_in,
        jnp.concatenate([over_chan[:CONV], over_bc[:CONV]], axis=1).T,
        jnp.concatenate([over_chan[CONV], over_bc[CONV]], axis=0),
        over_head[0],
        over_head[1],
        grad_skip,
        gain_sum.reshape(width),
        over_chan[CONV + 2],
        grad_out,
    )


def solution(mesh):
    whole_heads = mesh.shape["dp"] == 4 and mesh.shape["seq"] == 8
    shards = head_plan if whole_heads else general_plan
    placed = (
        P("dp", "seq", None),
        P("dp", "seq"),
        P(("dp", "seq"), None),
        P(),
        P(),
        P(),
        P(),
        P(),
        P(),
        P(),
        P(("dp", "seq"), None),
        P("dp", "seq", None),
    )
    return jax.shard_map(
        shards,
        mesh=mesh,
        in_specs=placed,
        out_specs=(
            P("dp", "seq", None),
            P("dp", "seq", None),
            P(("dp", "seq"), None),
            P(),
            P(),
            P(),
            P(),
            P(),
            P(),
            P(),
            P(("dp", "seq"), None),
        ),
        check_vma=False,
    )
```

```python
import functools

import jax
import jax.numpy as jnp
from jax import lax
from jax.experimental import pallas as pl
from jax.experimental.pallas import tpu as pltpu
from jax.sharding import PartitionSpec as P

HEADS = 64
HDIM = 64
NST = 128
GROUP = 256
CONV = 4
DI = 4096


def pre_norm(hidden_f, gain_vec):
    return (
        hidden_f
        * lax.rsqrt(jnp.mean(hidden_f * hidden_f, axis=-1, keepdims=True) + 1e-05)
        * gain_vec
    )


def gate_norm(y_values, gate_values, gain_vec):
    product = y_values * jax.nn.silu(gate_values)
    return (
        product * lax.rsqrt(jnp.mean(product * product, axis=-1, keepdims=True) + 1e-05) * gain_vec
    )


def conv_reset(signal, kernel, offset, seg_ids):
    tap_count = kernel.shape[1]
    summed = offset[None, :] + kernel[None, :, tap_count - 1] * signal
    for lag_steps in range(1, tap_count):
        shifted = jnp.pad(signal, ((lag_steps, 0), (0, 0)))[:-lag_steps]
        earlier = jnp.pad(seg_ids, (lag_steps, 0), constant_values=-1)[:-lag_steps]
        matches = (earlier == seg_ids).astype(jnp.float32)
        summed = summed + kernel[None, :, tap_count - 1 - lag_steps] * shifted * matches[:, None]
    return summed


def state_scan(values, deltas, rates, b_mat, c_mat, seg_ids):
    length, head_count, head_width = values.shape
    block_count = length // GROUP
    log_decay = deltas * rates[None, :]
    pieces = (
        values.reshape(block_count, GROUP, head_count, head_width),
        deltas.reshape(block_count, GROUP, head_count),
        log_decay.reshape(block_count, GROUP, head_count),
        b_mat.reshape(block_count, GROUP, b_mat.shape[-1]),
        c_mat.reshape(block_count, GROUP, c_mat.shape[-1]),
        seg_ids.reshape(block_count, GROUP),
    )
    position = lax.broadcasted_iota(jnp.int32, (GROUP, GROUP), 0)
    source = lax.broadcasted_iota(jnp.int32, (GROUP, GROUP), 1)

    def advance(carry, piece):
        memory, ending = carry
        block_vals, block_dt, block_log, b_block, c_block, seg_block = piece
        cumulative = jnp.cumsum(block_log, axis=0).T
        causal = (source <= position) & (seg_block[:, None] == seg_block[None, :])
        spread = cumulative[:, :, None] - cumulative[:, None, :]
        decays = jnp.where(causal[None], jnp.exp(jnp.where(causal[None], spread, 0.0)), 0.0)
        inner_prod = jnp.dot(c_block, b_block.T, precision=lax.Precision.HIGHEST)
        scores = inner_prod[None] * decays * block_dt.T[:, None, :]
        output = jnp.einsum("hij,jhp->ihp", scores, block_vals, precision=lax.Precision.HIGHEST)
        follows = (seg_block == ending).astype(jnp.float32)
        carried = jnp.einsum("in,hpn->ihp", c_block, memory, precision=lax.Precision.HIGHEST)
        output = output + (jnp.exp(cumulative).T * follows[:, None])[:, :, None] * carried
        last_seg = seg_block[-1]
        weights = (
            jnp.exp(cumulative[:, -1:] - cumulative)
            * (seg_block == last_seg).astype(jnp.float32)[None, :]
            * block_dt.T
        )
        keep_on = jnp.exp(cumulative[:, -1]) * (last_seg == ending).astype(jnp.float32)
        memory = memory * keep_on[:, None, None] + jnp.einsum(
            "hj,jhp,jn->hpn", weights, block_vals, b_block, precision=lax.Precision.HIGHEST
        )
        return ((memory, last_seg), output)

    initial = (
        jnp.zeros((head_count, head_width, b_mat.shape[-1]), jnp.float32),
        jnp.array(-1, jnp.int32),
    )
    unused, outputs = lax.scan(jax.checkpoint(advance), initial, pieces)
    return outputs.reshape(length, head_count, head_width)


def mixer(
    x_values,
    step_raw,
    bc_values,
    seg_ids,
    kernel_x,
    offset_x,
    kernel_bc,
    offset_bc,
    dt_shift,
    decay_log,
    skip_gain,
):
    x_conv = jax.nn.silu(conv_reset(x_values, kernel_x, offset_x, seg_ids))
    bc_conv = jax.nn.silu(conv_reset(bc_values, kernel_bc, offset_bc, seg_ids))
    step_sizes = jax.nn.softplus(step_raw + dt_shift[None, :])
    rates = -jnp.exp(decay_log)
    length = x_values.shape[0]
    head_count = step_raw.shape[1]
    shaped = x_conv.reshape(length, head_count, HDIM)
    mixed = (
        state_scan(shaped, step_sizes, rates, bc_conv[:, :NST], bc_conv[:, NST:], seg_ids)
        + skip_gain[None, :, None] * shaped
    )
    return mixed.reshape(length, head_count * HDIM)


def general_plan(
    hidden,
    segments,
    in_weight,
    conv_weight,
    conv_bias,
    dt_bias,
    a_log,
    d_skip,
    norm_gain,
    gate_gain,
    out_weight,
    cotangent,
):
    full_in, full_out = (
        lax.all_gather(in_weight, ("dp", "seq"), axis=0, tiled=True),
        lax.all_gather(out_weight, ("dp", "seq"), axis=0, tiled=True),
    )
    hidden_f = hidden.astype(jnp.float32)
    normed_f, pull_pre = jax.vjp(pre_norm, hidden_f, norm_gain)
    normed = normed_f.astype(jnp.bfloat16)
    project = jnp.einsum("mtd,df->mtf", normed, full_in, preferred_element_type=jnp.float32)
    gate_part = project[:, :, :DI]
    x_part = project[:, :, DI : 2 * DI].astype(jnp.bfloat16)
    bc_part = project[:, :, 2 * DI : 2 * DI + 2 * NST].astype(jnp.bfloat16)
    step_part = project[:, :, 2 * DI + 2 * NST :].astype(jnp.bfloat16)
    x_heads, step_heads = (
        lax.all_to_all(x_part, "seq", split_axis=2, concat_axis=1, tiled=True),
        lax.all_to_all(step_part, "seq", split_axis=2, concat_axis=1, tiled=True),
    )
    bc_full = lax.all_gather(bc_part, "seq", axis=1, tiled=True)
    seg_full = lax.all_gather(segments, "seq", axis=1, tiled=True)
    seq_rank = lax.axis_index("seq")
    head_local = step_heads.shape[2]
    chan_local = x_heads.shape[2]
    kernel_x = lax.dynamic_slice_in_dim(conv_weight, seq_rank * chan_local, chan_local, 0)
    offset_x = lax.dynamic_slice_in_dim(conv_bias, seq_rank * chan_local, chan_local, 0)
    shift_local = lax.dynamic_slice_in_dim(dt_bias, seq_rank * head_local, head_local, 0)
    decay_local = lax.dynamic_slice_in_dim(a_log, seq_rank * head_local, head_local, 0)
    skip_local = lax.dynamic_slice_in_dim(d_skip, seq_rank * head_local, head_local, 0)
    local_params = (
        kernel_x,
        offset_x,
        conv_weight[DI:],
        conv_bias[DI:],
        shift_local,
        decay_local,
        skip_local,
    )

    def head_mixer(x_values, step_raw, bc_values, params_in):

        def single_seq(x_one, step_one, bc_one, seg_one):
            return mixer(x_one, step_one, bc_one, seg_one, *params_in)

        return jax.vmap(single_seq)(x_values, step_raw, bc_values, seg_full)

    mixed, pull_mix = jax.vjp(
        head_mixer,
        x_heads.astype(jnp.float32),
        step_heads.astype(jnp.float32),
        bc_full.astype(jnp.float32),
        local_params,
    )
    y_tokens = lax.all_to_all(
        mixed.astype(jnp.bfloat16), "seq", split_axis=1, concat_axis=2, tiled=True
    )
    gated_f, pull_gate = jax.vjp(gate_norm, y_tokens.astype(jnp.float32), gate_part, gate_gain)
    gated = gated_f.astype(jnp.bfloat16)
    branch_out = jnp.einsum("mtf,fd->mtd", gated, full_out, preferred_element_type=jnp.float32)
    result = (hidden_f + branch_out).astype(jnp.bfloat16)
    d_gated = jnp.einsum("mtd,fd->mtf", cotangent, full_out, preferred_element_type=jnp.float32)
    d_mixed, d_gate_part, d_gate_gain = pull_gate(d_gated)
    d_heads = lax.all_to_all(
        d_mixed.astype(jnp.bfloat16), "seq", split_axis=2, concat_axis=1, tiled=True
    )
    d_x_heads, d_step_heads, d_bc_full, d_params = pull_mix(d_heads.astype(jnp.float32))
    d_x_part, d_step_part = (
        lax.all_to_all(
            d_x_heads.astype(jnp.bfloat16), "seq", split_axis=1, concat_axis=2, tiled=True
        ),
        lax.all_to_all(
            d_step_heads.astype(jnp.bfloat16), "seq", split_axis=1, concat_axis=2, tiled=True
        ),
    )
    d_bc_part = lax.psum_scatter(
        d_bc_full.astype(jnp.bfloat16), "seq", scatter_dimension=1, tiled=True
    )
    d_project = jnp.concatenate(
        [d_gate_part.astype(jnp.bfloat16), d_x_part, d_bc_part, d_step_part], axis=2
    )
    d_normed = jnp.einsum("mtf,df->mtd", d_project, full_in, preferred_element_type=jnp.float32)
    d_hidden_f, d_norm_gain = pull_pre(d_normed)
    d_hidden = (cotangent.astype(jnp.float32) + d_hidden_f).astype(jnp.bfloat16)
    in_rows = in_weight.shape[0]
    out_rows = out_weight.shape[0]
    column_ranges = ((0, DI), (DI, d_project.shape[2]))
    in_pieces = [jnp.zeros((in_rows, upper - lower), jnp.float32) for lower, upper in column_ranges]
    grad_out = jnp.zeros(out_weight.shape, jnp.float32)
    for batch_index in range(hidden.shape[0]):
        for range_index in range(len(column_ranges)):
            lower, upper = column_ranges[range_index]

            def in_term(
                start,
                count,
                normed_one=normed[batch_index],
                d_one=d_project[batch_index, :, lower:upper],
            ):
                return lax.dot_general(
                    normed_one, d_one, (((0,), (0,)), ((), ())), preferred_element_type=jnp.float32
                )

            in_pieces[range_index] = in_pieces[range_index] + lax.psum_scatter(
                in_term(jnp.int32(0), in_rows * lax.axis_size(("dp", "seq"))),
                ("dp", "seq"),
                scatter_dimension=0,
                tiled=True,
            )

        def out_term(start, count, gated_one=gated[batch_index], cot_one=cotangent[batch_index]):
            return lax.dot_general(
                gated_one, cot_one, (((0,), (0,)), ((), ())), preferred_element_type=jnp.float32
            )

        grad_out = grad_out + lax.psum_scatter(
            out_term(jnp.int32(0), out_rows * lax.axis_size(("dp", "seq"))),
            ("dp", "seq"),
            scatter_dimension=0,
            tiled=True,
        )
    grad_in = jnp.concatenate(in_pieces, axis=1)
    d_kernel_x, d_offset_x, d_kernel_bc, d_offset_bc, d_shift, d_decay, d_skip_part = d_params
    tap_count = conv_weight.shape[1]
    grad_conv_w = jnp.concatenate(
        [
            lax.dynamic_update_slice_in_dim(
                jnp.zeros((DI, tap_count), jnp.float32), d_kernel_x, seq_rank * chan_local, 0
            ),
            d_kernel_bc,
        ],
        axis=0,
    )
    grad_conv_b = jnp.concatenate(
        [
            lax.dynamic_update_slice_in_dim(
                jnp.zeros((DI,), jnp.float32), d_offset_x, seq_rank * chan_local, 0
            ),
            d_offset_bc,
        ],
        axis=0,
    )
    grad_shift = lax.dynamic_update_slice_in_dim(
        jnp.zeros((HEADS,), jnp.float32), d_shift, seq_rank * head_local, 0
    )
    grad_decay = lax.dynamic_update_slice_in_dim(
        jnp.zeros((HEADS,), jnp.float32), d_decay, seq_rank * head_local, 0
    )
    grad_skip = lax.dynamic_update_slice_in_dim(
        jnp.zeros((HEADS,), jnp.float32), d_skip_part, seq_rank * head_local, 0
    )
    totals = lax.psum(
        (grad_conv_w, grad_conv_b, grad_shift, grad_decay, grad_skip, d_norm_gain, d_gate_gain),
        ("dp", "seq"),
    )
    return (
        result,
        d_hidden,
        grad_in,
        totals[0],
        totals[1],
        totals[2],
        totals[3],
        totals[4],
        totals[5],
        totals[6],
        grad_out,
    )


LOG2E = 1.4426950408889634
TILE = 128
FAR = -1e30


def shift_rows(v, lag):
    return v if lag == 0 else pltpu.roll(v, lag % v.shape[0], axis=0)


def conv_silu(sig, taps, offset, keep):
    total = offset + taps[CONV - 1 : CONV] * sig
    for lag in range(1, CONV):
        total = total + taps[CONV - 1 - lag : CONV - lag] * (shift_rows(sig, lag) * keep[lag])
    gate = jax.nn.sigmoid(total)
    return total, gate, total * gate


def conv_back(d_out, total, gate, sig, taps, keep):
    d_total = d_out * (gate * (1.0 + total * (1.0 - gate)))
    d_sig = taps[CONV - 1 : CONV] * d_total
    tap_rows = [jnp.sum(d_total * sig, axis=0, keepdims=True)]
    for lag in range(1, CONV):
        kept = d_total * keep[lag]
        d_sig = d_sig + taps[CONV - 1 - lag : CONV - lag] * shift_rows(kept, -lag)
        tap_rows.append(jnp.sum(kept * shift_rows(sig, lag), axis=0, keepdims=True))
    return d_sig, tap_rows[::-1], jnp.sum(d_total, axis=0, keepdims=True)


def keep_masks(seg_col):
    length = seg_col.shape[0]
    row = lax.broadcasted_iota(jnp.int32, (length, 1), 0)
    masks = [None]
    for lag in range(1, CONV):
        same = (pltpu.roll(seg_col, lag, axis=0) == seg_col) & (row >= lag)
        masks.append(same.astype(jnp.float32))
    return masks


def lane_sums(v, reverse):
    length = v.shape[1]
    lane = lax.broadcasted_iota(jnp.int32, v.shape, 1)
    step = 1
    while step < length:
        if reverse:
            v = v + jnp.where(lane < length - step, pltpu.roll(v, length - step, axis=1), 0.0)
        else:
            v = v + jnp.where(lane >= step, pltpu.roll(v, step, axis=1), 0.0)
        step *= 2
    return v


def step_sizes_of(dt_all, head_rows, h_own, n_seq, heads_row):
    rank = lax.axis_index("seq")
    all_heads = dt_all.shape[1]
    lane = lax.broadcasted_iota(jnp.int32, (all_heads, 128), 1)
    row = lax.broadcasted_iota(jnp.int32, (all_heads, 128), 0)
    head = ((lane // heads_row) * n_seq + rank) * heads_row + lane % heads_row
    pick = ((row == head) & (lane < h_own)).astype(jnp.bfloat16)
    raw = jnp.dot(dt_all, pick, preferred_element_type=jnp.float32)
    shifted = raw + head_rows[0:1]
    dt = jnp.maximum(shifted, 0.0) + jnp.log1p(jnp.exp(-jnp.abs(shifted)))
    return shifted, dt


def head_prep(dt_all, head_rows, h_own, n_seq, heads_row, dt_cols, cum_cols, cum_rows):
    shifted, dt = step_sizes_of(dt_all, head_rows, h_own, n_seq, heads_row)
    rates = -jnp.exp(head_rows[1:2])
    step_log = dt * (rates * LOG2E)
    across = jnp.transpose(step_log)
    cum_t = lane_sums(across[:h_own], False)
    pad = jnp.zeros((128 - h_own, cum_t.shape[1]), jnp.float32)
    cum = jnp.transpose(jnp.concatenate([cum_t, pad], axis=0))
    for k in range(h_own):
        dt_cols[k] = dt[:, k : k + 1]
        cum_cols[k] = cum[:, k : k + 1]
        cum_rows[k] = cum_t[k : k + 1, :]
    return shifted, dt


def pair_wide(cols, pair):
    length = cols.shape[1]
    lane = lax.broadcasted_iota(jnp.int32, (length, 128), 1)
    return jnp.where(lane < HDIM, cols[2 * pair], cols[2 * pair + 1])


def scan_backward(h_own, n_seq, heads_row, x_ref, bc_ref, dt_ref, segc_ref, segr_ref, wx_ref, wbc_ref,
                  head_ref, dy_ref, inner_ref, dx_ref, dbc_ref, ddt_ref, gx_ref, gbc_ref, gh_ref,
                  dt_cols, cum_cols, cum_rows, inner_prod, bias, d_inner, d_cum, d_dt):
    pair = pl.program_id(1)
    n_pair = pl.num_programs(1)
    length = x_ref.shape[0]
    seg_col = segc_ref[0]
    keep = keep_masks(seg_col)
    f32, bf16 = jnp.float32, jnp.bfloat16

    @pl.when(pair == 0)
    def prepare():
        head_prep(dt_ref[...], head_ref[...], h_own, n_seq, heads_row, dt_cols, cum_cols, cum_rows)
        _, _, bc = conv_silu(bc_ref[...].astype(f32), wbc_ref[0:CONV], wbc_ref[CONV : CONV + 1], keep)
        inner_prod[...] = lax.dot_general(
            bc[:, :NST], bc[:, NST:], (((1,), (1,)), ((), ())),
            precision=lax.Precision.HIGHEST, preferred_element_type=f32,
        )
        source = lax.broadcasted_iota(jnp.int32, (length, length), 0)
        at = lax.broadcasted_iota(jnp.int32, (length, length), 1)
        bias[...] = jnp.where((source <= at) & (seg_col == segr_ref[0]), 0.0, FAR)
        d_inner[...] = jnp.zeros((length, length), f32)
        d_cum[...] = jnp.zeros((length, 128), f32)
        d_dt[...] = jnp.zeros((length, 128), f32)

    x_in = x_ref[...].astype(f32)
    taps = wx_ref[0:CONV]
    total, gate, xc = conv_silu(x_in, taps, wx_ref[CONV : CONV + 1], keep)
    dt_wide = pair_wide(dt_cols, pair)
    moved = (xc * dt_wide).astype(bf16)
    skip = wx_ref[CONV + 1 : CONV + 2]
    dy = dy_ref[...]
    first = lax.broadcasted_iota(jnp.int32, (TILE, 128), 1) < HDIM
    pieces = []
    for block in range(length // TILE):
        rows, later = slice(block * TILE, (block + 1) * TILE), slice(block * TILE, length)
        halves = []
        for half in range(2):
            head = 2 * pair + half
            decay = jnp.exp2(cum_rows[head, :, later] - cum_cols[head, rows] + bias[rows, later])
            scores = (inner_prod[rows, later] * decay).astype(bf16)
            halves.append(jnp.dot(scores, dy[later], preferred_element_type=f32))
            mine = jnp.where(first if half == 0 else ~first, moved[rows].astype(f32), 0.0).astype(bf16)
            d_scores = lax.dot_general(
                mine, dy[later], (((1,), (1,)), ((), ())), preferred_element_type=f32
            )
            d_inner[rows, later] += d_scores * decay
        pieces.append(jnp.where(first, halves[0], halves[1]))
    d_moved = jnp.concatenate(pieces, axis=0)
    dy_f = dy.astype(f32)
    change = dy_f * inner_ref[...] - moved.astype(f32) * d_moved
    direct = d_moved * xc
    lane = lax.broadcasted_iota(jnp.int32, (length, 128), 1)
    low = lane < HDIM
    for half in range(2):
        mine = low if half == 0 else ~low
        place = lane == 2 * pair + half
        d_cum[...] += jnp.where(place, jnp.sum(jnp.where(mine, change, 0.0), axis=1, keepdims=True), 0.0)
        d_dt[...] += jnp.where(place, jnp.sum(jnp.where(mine, direct, 0.0), axis=1, keepdims=True), 0.0)
    d_xc = d_moved * dt_wide + skip * dy_f
    d_x, tap_rows, d_offset = conv_back(d_xc, total, gate, x_in, taps, keep)
    dx_ref[...] = d_x.astype(bf16)
    d_skip = jnp.sum(dy_f * xc, axis=0, keepdims=True)
    blank = jnp.zeros((2, 128), f32)
    gx_ref[0] = jnp.concatenate(tap_rows + [d_offset, d_skip, blank], axis=0)

    @pl.when(pair == n_pair - 1)
    def finish():
        bc_in = bc_ref[...].astype(f32)
        taps_bc = wbc_ref[0:CONV]
        total_bc, gate_bc, bc = conv_silu(bc_in, taps_bc, wbc_ref[CONV : CONV + 1], keep)
        d_in = d_inner[...]
        d_b = jnp.dot(d_in, bc[:, NST:], precision=lax.Precision.HIGHEST, preferred_element_type=f32)
        d_c = lax.dot_general(
            d_in, bc[:, :NST], (((0,), (0,)), ((), ())),
            precision=lax.Precision.HIGHEST, preferred_element_type=f32,
        )
        d_bc, rows_bc, offset_bc = conv_back(
            jnp.concatenate([d_b, d_c], axis=1), total_bc, gate_bc, bc_in, taps_bc, keep
        )
        dbc_ref[...] = d_bc.astype(bf16)
        gbc_ref[0] = jnp.concatenate(rows_bc + [offset_bc, jnp.zeros((3, 2 * NST), f32)], axis=0)
        shifted, dt = step_sizes_of(dt_ref[...], head_ref[...], h_own, n_seq, heads_row)
        rates = -jnp.exp(head_ref[1:2])
        across = jnp.transpose(d_cum[...])
        d_log_t = lane_sums(across[:h_own], True)
        pad = jnp.zeros((128 - h_own, length), f32)
        d_log = jnp.transpose(jnp.concatenate([d_log_t, pad], axis=0))
        d_raw = (d_log * rates + d_dt[...]) * jax.nn.sigmoid(shifted)
        ddt_ref[...] = d_raw
        gh_ref[0] = jnp.concatenate(
            [
                jnp.sum(d_raw, axis=0, keepdims=True),
                jnp.sum(d_log * dt, axis=0, keepdims=True) * rates,
                jnp.zeros((6, 128), f32),
            ],
            axis=0,
        )


def scan_specs(length, all_heads):
    return [
        pl.BlockSpec((length, 128), lambda q, p: (q, p)),
        pl.BlockSpec((length, 2 * NST), lambda q, p: (q, 0)),
        pl.BlockSpec((length, all_heads), lambda q, p: (q, 0)),
        pl.BlockSpec((1, length, 1), lambda q, p: (q, 0, 0)),
        pl.BlockSpec((1, 1, length), lambda q, p: (q, 0, 0)),
        pl.BlockSpec((8, 128), lambda q, p: (0, p)),
        pl.BlockSpec((8, 2 * NST), lambda q, p: (0, 0)),
        pl.BlockSpec((8, 128), lambda q, p: (0, 0)),
    ]


def scan_scratch(length, h_own):
    f32 = jnp.float32
    return [
        pltpu.VMEM((h_own, length, 1), f32),
        pltpu.VMEM((h_own, length, 1), f32),
        pltpu.VMEM((h_own, 1, length), f32),
        pltpu.VMEM((length, length), f32),
        pltpu.VMEM((length, length), f32),
    ]


def run_backward(n_own, h_own, n_seq, heads_row, operands, d_y, inner):
    f32 = jnp.float32
    tokens, chan = operands[0].shape
    length = tokens // n_own
    pair_block = pl.BlockSpec((length, 128), lambda q, p: (q, p))
    return pl.pallas_call(
        functools.partial(scan_backward, h_own, n_seq, heads_row),
        grid=(n_own, chan // 128),
        in_specs=scan_specs(length, operands[2].shape[1]) + [pair_block, pair_block],
        out_specs=[
            pair_block,
            pl.BlockSpec((length, 2 * NST), lambda q, p: (q, 0)),
            pl.BlockSpec((length, 128), lambda q, p: (q, 0)),
            pl.BlockSpec((1, 8, 128), lambda q, p: (q, 0, p)),
            pl.BlockSpec((1, 8, 2 * NST), lambda q, p: (q, 0, 0)),
            pl.BlockSpec((1, 8, 128), lambda q, p: (q, 0, 0)),
        ],
        out_shape=[
            jax.ShapeDtypeStruct((tokens, chan), jnp.bfloat16),
            jax.ShapeDtypeStruct((tokens, 2 * NST), jnp.bfloat16),
            jax.ShapeDtypeStruct((tokens, 128), f32),
            jax.ShapeDtypeStruct((n_own, 8, chan), f32),
            jax.ShapeDtypeStruct((n_own, 8, 2 * NST), f32),
            jax.ShapeDtypeStruct((n_own, 8, 128), f32),
        ],
        scratch_shapes=scan_scratch(length, h_own)
        + [
            pltpu.VMEM((length, length), f32),
            pltpu.VMEM((length, 128), f32),
            pltpu.VMEM((length, 128), f32),
        ],
        compiler_params=pltpu.CompilerParams(vmem_limit_bytes=56 << 20),
        name="scan_backward",
    )(*operands, d_y, inner)


MESH = pl.DeviceIdType.MESH
WIDE = 8


def place():
    dp, s = lax.axis_index("dp"), lax.axis_index("seq")
    z, x = s // 2, s % 2
    y, core = dp // 2, dp % 2
    return dp, s, z, x, s + 1 - 2 * x, dp + 2 - 4 * y, dp + 1 - 2 * core


def greet(peers):
    barrier = pltpu.get_barrier_semaphore()
    for device in peers:
        pl.semaphore_signal(barrier, inc=1, device_id=device, device_id_type=MESH)
    pl.semaphore_wait(barrier, len(peers))


def remote(src, dst, send, recv, device):
    return pltpu.make_async_remote_copy(
        src_ref=src, dst_ref=dst, send_sem=send, recv_sem=recv, device_id=device, device_id_type=MESH
    )


class TokenGather:
    def __init__(self, own, full, send, recv, where):
        self.own, self.full, self.send, self.recv = own, full, send, recv
        self.dp, self.s, self.z, self.x, self.x_peer, _, _ = where
        self.span = own.shape[1]

    def part(self, shard, q):
        return self.full.at[q, pl.ds(pl.multiple_of(shard * self.span, self.span), self.span)]

    def copy(self, shard_z, way, q, mine):
        shard = shard_z * 2 + self.x
        target = (self.s + 2, self.s - 2, self.x_peer)[way]
        src = self.own.at[q] if mine else self.part(shard, q)
        return remote(
            src, self.part(shard, q), self.send.at[way, shard_z, q], self.recv.at[shard, q], (self.dp, target)
        )

    def arrived(self, shard, q):
        part = self.part(shard, q)
        remote(part, part, self.send.at[0, 0, q], self.recv.at[shard, q], (self.dp, self.x_peer)).wait_recv()

    def start(self, q):
        @pl.when(self.z < 3)
        def up():
            self.copy(self.z, 0, q, True).start()

        @pl.when(self.z > 0)
        def down():
            self.copy(self.z, 1, q, True).start()

        self.copy(self.z, 2, q, True).start()

    def step(self, hop, q):
        @pl.when(self.z >= hop)
        def from_below():
            shard_z = self.z - hop
            self.arrived(shard_z * 2 + self.x, q)

            @pl.when(self.z < 3)
            def up():
                self.copy(shard_z, 0, q, False).start()

            self.copy(shard_z, 2, q, False).start()

        @pl.when(self.z + hop <= 3)
        def from_above():
            shard_z = self.z + hop
            self.arrived(shard_z * 2 + self.x, q)

            @pl.when(self.z > 0)
            def down():
                self.copy(shard_z, 1, q, False).start()

            self.copy(shard_z, 2, q, False).start()

    def arrive_x(self, q):
        for shard_z in range(4):
            self.arrived(shard_z * 2 + 1 - self.x, q)

    def settle(self, q):
        for shard_z in range(4):
            self.copy(shard_z, 2, q, False).wait_send()

            @pl.when((self.z < 3) & (self.z >= shard_z))
            def up():
                self.copy(shard_z, 0, q, False).wait_send()

            @pl.when((self.z > 0) & (self.z <= shard_z))
            def down():
                self.copy(shard_z, 1, q, False).wait_send()


def column_of(mat, index):
    return pltpu.roll(mat, (128 - index) % 128, axis=1)[:, :1]


def pair_lanes(mat, pair):
    lane = lax.broadcasted_iota(jnp.int32, (mat.shape[0], 128), 1)
    return jnp.where(lane < HDIM, column_of(mat, 2 * pair), column_of(mat, 2 * pair + 1))


def load_params(rank, conv_t, conv_b, dt_bias, a_log, d_skip, wx, wbc, heads):
    lane = lax.broadcasted_iota(jnp.int32, (1, 128), 1)
    bias_row, log_row = jnp.zeros((1, 128), jnp.float32), jnp.zeros((1, 128), jnp.float32)
    wx[...] = jnp.zeros(wx.shape, jnp.float32)
    wbc[...] = jnp.zeros(wbc.shape, jnp.float32)
    heads[...] = jnp.zeros(heads.shape, jnp.float32)
    for d in range(wx.shape[1] // 128):
        cols, own = pl.ds(pl.multiple_of((d * 8 + rank) * 128, 128), 128), slice(d * 128, (d + 1) * 128)
        head = (d * 8 + rank) * 2
        wx[0:CONV, own] = conv_t[:, cols]
        wx[CONV : CONV + 1, own] = conv_b[:, cols]
        wx[CONV + 1 : CONV + 2, own] = jnp.where(lane < HDIM, d_skip[head], d_skip[head + 1])
        for half in range(2):
            bias_row = jnp.where(lane == 2 * d + half, dt_bias[head + half], bias_row)
            log_row = jnp.where(lane == 2 * d + half, a_log[head + half], log_row)
    wbc[0:CONV] = conv_t[:, DI:]
    wbc[CONV : CONV + 1] = conv_b[:, DI:]
    heads[0:1] = bias_row
    heads[1:2] = log_row


def head_mats(dt_all, heads, h_own, dt_mat, cum_mat, cum_rows):
    shifted, dt = step_sizes_of(dt_all, heads, h_own, 8, 2)
    rates = -jnp.exp(heads[1:2])
    across = jnp.transpose(dt * (rates * LOG2E))
    cum_t = lane_sums(across[:h_own], False)
    pad = jnp.zeros((128 - h_own, cum_t.shape[1]), jnp.float32)
    dt_mat[...] = dt
    cum_mat[...] = jnp.transpose(jnp.concatenate([cum_t, pad], axis=0))
    for k in range(h_own):
        cum_rows[k] = cum_t[k : k + 1, :]


def forward_prepare(h_own, bc_ref, dt_ref, seg_col, seg_row, wbc, heads, dt_mat, cum_mat, cum_rows, inner_prod, bias):
    length = bc_ref.shape[0]
    keep = keep_masks(seg_col)
    head_mats(dt_ref[...], heads[...], h_own, dt_mat, cum_mat, cum_rows)
    _, _, bc = conv_silu(bc_ref[...].astype(jnp.float32), wbc[0:CONV], wbc[CONV : CONV + 1], keep)
    inner_prod[...] = lax.dot_general(
        bc[:, NST:], bc[:, :NST], (((1,), (1,)), ((), ())),
        precision=lax.Precision.HIGHEST, preferred_element_type=jnp.float32,
    )
    at = lax.broadcasted_iota(jnp.int32, (length, length), 0)
    source = lax.broadcasted_iota(jnp.int32, (length, length), 1)
    bias[...] = jnp.where((source <= at) & (seg_col == seg_row), 0.0, FAR)


def forward_pair(pair, x_ref, seg_col, wx_ref, y_ref, inner_ref, dt_mat, cum_mat, cum_rows, inner_prod, bias):
    length = x_ref.shape[0]
    keep = keep_masks(seg_col)
    _, _, xc = conv_silu(x_ref[...].astype(jnp.float32), wx_ref[0:CONV], wx_ref[CONV : CONV + 1], keep)
    moved = (xc * pair_lanes(dt_mat[...], pair)).astype(jnp.bfloat16)
    skip = wx_ref[CONV + 1 : CONV + 2]
    first = lax.broadcasted_iota(jnp.int32, (TILE, 128), 1) < HDIM
    cum = [column_of(cum_mat[...], 2 * pair + half) for half in range(2)]
    for block in range(length // TILE):
        rows, wide = slice(block * TILE, (block + 1) * TILE), (block + 1) * TILE
        halves = []
        for half in range(2):
            decay = jnp.exp2(cum[half][rows] - cum_rows[2 * pair + half, :, :wide] + bias[rows, :wide])
            scores = (inner_prod[rows, :wide] * decay).astype(jnp.bfloat16)
            halves.append(jnp.dot(scores, moved[:wide], preferred_element_type=jnp.float32))
        inner = jnp.where(first, halves[0], halves[1])
        inner_ref[rows] = inner
        y_ref[rows] = (inner + skip * xc[rows]).astype(jnp.bfloat16)


def ahead_kernel(hidden, cot, in_w, in_tail, out_w, seg, conv_t, conv_b, norm_gain, gate_gain, dt_bias, a_log, d_skip,
                 n_all, c_all, w_in, w_out, x_raw, bc_raw, dt_raw, inner, gated, d_y, d_z, seg_col, seg_row,
                 wx, wbc, heads, gain_back,
                 nrm, tok_v, w_in_v, w_out_v, z_v, y_v, dg, seg_all, dt_mat, cum_mat, cum_rows, inner_prod, bias,
                 sum_cols, sums,
                 n_send, n_recv, c_send, c_recv, wide_send, tail_send, wide_recv, tail_recv,
                 y_send, core_send, cross_send, block_recv, out_send, out_recv, seg_send, seg_recv, local, load,
                 sum_send, sum_recv):
    f32, bf16 = jnp.float32, jnp.bfloat16
    where = place()
    dp, s, z, x, x_peer, y_peer, core_peer = where
    peers = [(dp, (s + k) % 8) for k in range(1, 8)] + [(y_peer, s), (core_peer, s)]
    greet(peers)
    in_rows, rows = in_w.shape[0], out_w.shape[0]
    chan = w_out.shape[0]
    h_own = chan // HDIM
    tail = in_tail.shape[1]
    n_own, length, width = n_all.shape

    def block(d, shard, lo=0, size=None):
        size = w_in.shape[1] if size is None else size
        at = pl.multiple_of((d * 8 + shard) * in_rows, in_rows)
        return w_in.at[pl.ds(at, in_rows), pl.ds(lo, size)]

    def wide_src(piece, target):
        at = pl.multiple_of((piece * 8 + target) * rows, rows)
        return in_w.at[:, pl.ds(at, rows)]

    def push(k, _):
        target = (s + k) % 8
        remote(seg, seg_all.at[s], seg_send.at[k], seg_recv.at[s], (dp, target)).start()
        for piece in range(WIDE):
            remote(
                wide_src(piece, target), block(dp, s, piece * rows, rows), wide_send.at[k], wide_recv.at[s],
                (dp, target),
            ).start()
        remote(in_tail, block(dp, s, 2 * chan, tail), tail_send.at[k], tail_recv.at[s], (dp, target)).start()
        return 0

    lax.fori_loop(1, 8, push, 0)
    for q in range(n_own):
        h = hidden[q].astype(f32)
        inv = lax.rsqrt(jnp.mean(h * h, axis=-1, keepdims=True) + 1e-05)
        nrm[q] = (h * inv * norm_gain[...]).astype(bf16)
    tokens = TokenGather(nrm, n_all, n_send, n_recv, where)
    cots = TokenGather(cot, c_all, c_send, c_recv, where)
    tokens.start(0)
    own_copies = []
    for piece in range(WIDE):
        own_copies.append(pltpu.make_async_copy(wide_src(piece, s), block(dp, s, piece * rows, rows), local.at[piece]))
    own_copies.append(pltpu.make_async_copy(in_tail, block(dp, s, 2 * chan, tail), local.at[8]))
    token_copies, cot_copies = [], []
    out_copy = pltpu.make_async_copy(out_w, w_out.at[pl.ds(pl.multiple_of(dp * rows, rows), rows)], local.at[9])
    for q in range(n_own):
        token_copies.append(pltpu.make_async_copy(nrm.at[q], tokens.part(s, q), local.at[10 + q]))
        cot_copies.append(pltpu.make_async_copy(cot.at[q], cots.part(s, q), local.at[12 + q]))
    for copy in own_copies + token_copies + cot_copies + [out_copy]:
        copy.start()
    seg_all[s] = seg[...]
    for copy in own_copies:
        copy.wait()

    def spread(shard, k):
        there = block(dp, shard)
        remote(there, there, y_send.at[k], block_recv.at[dp, shard], (y_peer, s)).start()
        remote(there, there, core_send.at[k], block_recv.at[dp, shard], (core_peer, s)).start()

    spread(s, 0)
    load_params(s, conv_t, conv_b, dt_bias, a_log, d_skip, wx, wbc, heads)

    def wide_copy(source, k):
        there = block(dp, source, 0, 2 * chan)
        return remote(there, there, wide_send.at[k], wide_recv.at[source], (dp, x_peer))

    def tail_copy(source, k):
        there = block(dp, source, 2 * chan, tail)
        return remote(there, there, tail_send.at[k], tail_recv.at[source], (dp, x_peer))

    def forward(k, _):
        source = (s + 8 - k) % 8
        wide_copy(source, k).wait_recv()
        tail_copy(source, k).wait_recv()
        spread(source, k)
        return 0

    def cross(k, _):
        source = (s + 8 - k) % 8
        there = block(y_peer, source)
        copy = remote(there, there, cross_send.at[k], block_recv.at[y_peer, source], (core_peer, s))
        copy.wait_recv()
        copy.start()
        return 0

    def out_part(d):
        return w_out.at[pl.ds(pl.multiple_of(d * rows, rows), rows)]

    tokens.step(1, 0)
    tokens.start(1)
    lax.fori_loop(1, 4, forward, 0)
    tokens.step(2, 0)
    lax.fori_loop(4, 8, forward, 0)
    tokens.step(3, 0)
    tokens.step(1, 1)
    lax.fori_loop(0, 4, cross, 0)
    tokens.step(2, 1)
    lax.fori_loop(4, 8, cross, 0)
    tokens.step(3, 1)
    for q in range(n_own):
        cots.start(q)
    out_y = remote(out_w, out_part(dp), out_send.at[0], out_recv.at[dp], (y_peer, s))
    out_core = remote(out_w, out_part(dp), out_send.at[1], out_recv.at[dp], (core_peer, s))
    out_y.start()
    out_core.start()

    def arrive(k, _):
        source = (s + 8 - k) % 8
        for d in (core_peer, core_peer + y_peer - dp):
            there = block(d, source)
            remote(there, there, core_send.at[k], block_recv.at[d, source], (core_peer, s)).wait_recv()
        return 0

    lax.fori_loop(0, 8, arrive, 0)
    w_load = pltpu.make_async_copy(w_in, w_in_v, load.at[0])
    w_load.start()

    def segments_in(k, _):
        source = (s + 8 - k) % 8
        remote(seg, seg_all.at[source], seg_send.at[k], seg_recv.at[source], (dp, x_peer)).wait_recv()
        return 0

    lax.fori_loop(1, 8, segments_in, 0)
    lane = lax.broadcasted_iota(jnp.int32, (1, 128), 1)
    for q in range(n_own):
        pieces = [
            jnp.where(lane < 64, seg_all[2 * m, q : q + 1], pltpu.roll(seg_all[2 * m + 1, q : q + 1], 64, axis=1))
            for m in range(4)
        ]
        row = jnp.concatenate(pieces, axis=1)
        seg_row[q] = row
        seg_col[q] = jnp.transpose(jnp.broadcast_to(row, (128, length)))[:, :1]

    def project(q):
        at = slice(q * length, (q + 1) * length)
        half = chan // 2

        @pl.loop(0, 2)
        def gates(n):
            cols = pl.ds(pl.multiple_of(n * half, half), half)
            z_v[at, cols] = jnp.dot(tok_v[q], w_in_v[:, cols], preferred_element_type=f32)

        @pl.loop(0, 2)
        def values(n):
            cols = pl.ds(pl.multiple_of(n * half, half), half)
            from_cols = pl.ds(pl.multiple_of(chan + n * half, half), half)
            x_raw[at, cols] = jnp.dot(tok_v[q], w_in_v[:, from_cols], preferred_element_type=f32).astype(bf16)

        last = jnp.dot(tok_v[q], w_in_v[:, 2 * chan :], preferred_element_type=f32).astype(bf16)
        bc_raw[at] = last[:, : 2 * NST]
        dt_raw[at] = last[:, 2 * NST :]

    token_loads = [pltpu.make_async_copy(n_all.at[q], tok_v.at[q], load.at[1 + q]) for q in range(n_own)]
    for q in range(n_own):
        token_copies[q].wait()
        tokens.arrive_x(q)
        token_loads[q].start()
        if q == 0:
            w_load.wait()
        token_loads[q].wait()
        project(q)
        cots.step(1, q)

    for q in range(n_own):
        at = pl.ds(q * length, length)
        forward_prepare(
            h_own, bc_raw.at[at], dt_raw.at[at], seg_col[q], seg_row[q], wbc, heads,
            dt_mat, cum_mat, cum_rows, inner_prod, bias,
        )

        @pl.loop(0, chan // 128)
        def pairs(pair):
            cols = pl.ds(pl.multiple_of(pair * 128, 128), 128)
            forward_pair(
                pair, x_raw.at[at, cols], seg_col[q], wx.at[:, cols], y_v.at[at, cols], inner.at[at, cols],
                dt_mat, cum_mat, cum_rows, inner_prod, bias,
            )

            @pl.when(pair == 1)
            def hop():
                if q == 0:
                    cots.step(2, 0)
                else:
                    cots.step(3, 0)

            @pl.when(pair == 3)
            def hop_again():
                if q == 0:
                    cots.step(2, 1)
                else:
                    cots.step(3, 1)

    out_cross = remote(out_part(y_peer), out_part(y_peer), out_send.at[2], out_recv.at[y_peer], (core_peer, s))
    out_cross.wait_recv()
    out_cross.start()
    for d in (core_peer, core_peer + y_peer - dp):
        remote(out_part(d), out_part(d), out_send.at[0], out_recv.at[d], (core_peer, s)).wait_recv()
    out_copy.wait()
    out_load = pltpu.make_async_copy(w_out, w_out_v, load.at[3])
    out_load.start()
    gain = jnp.concatenate(
        [gate_gain[:, pl.ds(pl.multiple_of((d * 8 + s) * 128, 128), 128)] for d in range(chan // 128)], axis=1
    )
    lane_wide = lax.broadcasted_iota(jnp.int32, (TILE, 128), 1)

    def sum_copy(q, k):
        return remote(
            sums.at[q, s], sums.at[q, s], sum_send.at[q, k], sum_recv.at[q, s], (dp, (s + k) % 8)
        )

    cot_loads = [pltpu.make_async_copy(c_all.at[q], tok_v.at[q], load.at[4 + q]) for q in range(n_own)]
    for q in range(n_own):
        cot_copies[q].wait()
        cots.arrive_x(q)
        cot_loads[q].start()
        if q == 0:
            out_load.wait()
        cot_loads[q].wait()
        half = chan // 2

        @pl.loop(0, 2)
        def back(n):
            cols = pl.ds(pl.multiple_of(n * half, half), half)
            dg[q * length : (q + 1) * length, cols] = lax.dot_general(
                tok_v[q], w_out_v[cols], (((1,), (1,)), ((), ())), preferred_element_type=f32
            )

        @pl.loop(0, length // TILE)
        def reduce_rows(n):
            at = pl.ds(pl.multiple_of(q * length + n * TILE, TILE), TILE)
            zz = z_v[at]
            g = y_v[at].astype(f32) * (zz * jax.nn.sigmoid(zz))
            first = jnp.sum(g * g, axis=1, keepdims=True)
            second = jnp.sum(dg[at] * gain * g, axis=1, keepdims=True)
            sum_cols[pl.ds(pl.multiple_of(n * TILE, TILE), TILE)] = jnp.where(
                lane_wide == 0, first, jnp.where(lane_wide == 1, second, 0.0)
            )

        sums[q, s] = jnp.transpose(sum_cols[...])[:8]
        for k in range(1, 8):
            sum_copy(q, k).start()

    gain_back[...] = jnp.zeros(gain_back.shape, f32)
    for q in range(n_own):
        for k in range(1, 8):
            source = (s + 8 - k) % 8
            remote(
                sums.at[q, source], sums.at[q, source], sum_send.at[q, k], sum_recv.at[q, source], (dp, x_peer)
            ).wait_recv()
        total = sums[q, 0]
        for source in range(1, 8):
            total = total + sums[q, source]
        total = jnp.concatenate([total, jnp.zeros((120, length), f32)], axis=0)
        sum_cols[...] = jnp.transpose(total)

        @pl.loop(0, length // TILE)
        def gate_rows(n):
            at = pl.ds(pl.multiple_of(q * length + n * TILE, TILE), TILE)
            both = sum_cols[pl.ds(pl.multiple_of(n * TILE, TILE), TILE)]
            r = lax.rsqrt(both[:, 0:1] / DI + 1e-05)
            fall = (r * r * r) * (both[:, 1:2] / DI)
            zz = z_v[at]
            sig = jax.nn.sigmoid(zz)
            act = zz * sig
            yy = y_v[at].astype(f32)
            g = yy * act
            gr = g * r
            back = dg[at]
            d_g = r * (back * gain) - fall * g
            gated[at] = (gr * gain).astype(bf16)
            d_y[at] = (d_g * act).astype(bf16)
            d_z[at] = (d_g * yy * (sig * (1.0 + zz * (1.0 - sig)))).astype(bf16)
            gain_back[0:1] += jnp.sum(back * gr, axis=0, keepdims=True)

    for q in range(n_own):
        tokens.settle(q)
        cots.settle(q)
        for k in range(1, 8):
            sum_copy(q, k).wait_send()

    def settle(k, _):
        shard = (s + 8 - k) % 8
        there = block(dp, shard)
        remote(there, there, y_send.at[k], block_recv.at[dp, shard], (y_peer, s)).wait_send()
        remote(there, there, core_send.at[k], block_recv.at[dp, shard], (core_peer, s)).wait_send()
        remote(there, there, cross_send.at[k], block_recv.at[dp, shard], (core_peer, s)).wait_send()
        return 0

    lax.fori_loop(0, 8, settle, 0)

    def settle_push(k, _):
        source = (s + 8 - k) % 8
        remote(seg, seg_all.at[source], seg_send.at[k], seg_recv.at[source], (dp, x_peer)).wait_send()
        wide_copy(source, k).wait_send()
        tail_copy(source, k).wait_send()
        return 0

    lax.fori_loop(1, 8, settle_push, 0)
    out_y.wait_send()
    out_core.wait_send()
    out_cross.wait_send()


def run_ahead(hidden, cot, in_w, in_tail, out_w, seg, conv_t, conv_b, norm_gain, gate_gain, dt_bias, a_log, d_skip):
    f32, bf16 = jnp.float32, jnp.bfloat16
    n_own, span, width = hidden.shape
    in_rows, rows = in_w.shape[0], out_w.shape[0]
    chan, length = 4 * rows, 8 * span
    tokens, h_own = n_own * length, chan // HDIM
    columns = 2 * chan + in_tail.shape[1]
    sem, vmem = pltpu.SemaphoreType.DMA, pltpu.VMEM
    anywhere, inside = pl.BlockSpec(memory_space=pl.ANY), pl.BlockSpec(memory_space=vmem)
    scalars = pl.BlockSpec(memory_space=pltpu.SMEM)
    shape = jax.ShapeDtypeStruct
    return pl.pallas_call(
        ahead_kernel,
        in_specs=[inside] + [anywhere] * 4 + [inside] * 5 + [scalars] * 3,
        out_specs=[anywhere] * 4 + [inside] * 13,
        out_shape=[
            shape((n_own, length, width), bf16),
            shape((n_own, length, width), bf16),
            shape((32 * in_rows, columns), bf16),
            shape((chan, width), bf16),
            shape((tokens, chan), bf16),
            shape((tokens, 2 * NST), bf16),
            shape((tokens, 128), bf16),
            shape((tokens, chan), f32),
            shape((tokens, chan), bf16),
            shape((tokens, chan), bf16),
            shape((tokens, chan), bf16),
            shape((n_own, length, 1), f32),
            shape((n_own, 1, length), f32),
            shape((8, chan), f32),
            shape((8, 2 * NST), f32),
            shape((8, 128), f32),
            shape((8, chan), f32),
        ],
        scratch_shapes=[
            vmem((n_own, span, width), bf16),
            vmem((n_own, length, width), bf16),
            vmem((width, columns), bf16),
            vmem((chan, width), bf16),
            vmem((tokens, chan), f32),
            vmem((tokens, chan), bf16),
            vmem((tokens, chan), f32),
            vmem((8, 8, 128), f32),
            vmem((length, 128), f32),
            vmem((length, 128), f32),
            vmem((h_own, 1, length), f32),
            vmem((length, length), f32),
            vmem((length, length), f32),
            vmem((length, 128), f32),
            vmem((n_own, 8, 8, length), f32),
            sem((3, 4, 2)), sem((8, 2)), sem((3, 4, 2)), sem((8, 2)),
            sem((8,)), sem((8,)), sem((8,)), sem((8,)),
            sem((8,)), sem((8,)), sem((8,)), sem((4, 8)), sem((3,)), sem((4,)), sem((8,)), sem((8,)),
            sem((14,)), sem((6,)), sem((2, 8)), sem((2, 8)),
        ],
        compiler_params=pltpu.CompilerParams(collective_id=0, has_side_effects=True, vmem_limit_bytes=56 << 20),
        name="ahead",
    )(hidden, cot, in_w, in_tail, out_w, seg, conv_t, conv_b, norm_gain, gate_gain, dt_bias, a_log, d_skip)


class TokenReduce:
    def __init__(self, part, from_x, from_near, from_far, x_sems, near_sems, far_sems, where, span):
        self.part, self.from_x, self.from_near, self.from_far = part, from_x, from_near, from_far
        self.x_sems, self.near_sems, self.far_sems, self.span = x_sems, near_sems, far_sems, span
        self.dp, self.s, self.z, self.x, self.x_peer, _, _ = where
        self.near = self.s + 2 - 4 * (self.z % 2)
        self.far = self.s + 4 - 8 * (self.z // 2)

    def rows(self, shard, q):
        return self.part.at[q, pl.ds(pl.multiple_of(shard * self.span, self.span), self.span)]

    def x_copy(self, shard_z, q):
        return remote(
            self.rows(shard_z * 2 + 1 - self.x, q), self.from_x.at[shard_z, q],
            self.x_sems.at[0, shard_z, q], self.x_sems.at[1, shard_z, q], (self.dp, self.x_peer),
        )

    def near_copy(self, high, q):
        shard = (high * 2 + 1 - self.z % 2) * 2 + self.x
        return remote(
            self.rows(shard, q), self.from_near.at[high, q],
            self.near_sems.at[0, high, q], self.near_sems.at[1, high, q], (self.dp, self.near),
        )

    def far_copy(self, q):
        shard = ((1 - self.z // 2) * 2 + self.z % 2) * 2 + self.x
        return remote(
            self.rows(shard, q), self.from_far.at[q], self.far_sems.at[0, q], self.far_sems.at[1, q],
            (self.dp, self.far),
        )

    def start(self, q):
        for high in range(2):
            for low in range(2):
                shard_z = (1 - self.z // 2 + high) % 2 * 2 + (1 - self.z % 2 + low) % 2
                self.x_copy(shard_z, q).start()

    def add(self, shard, q, other):
        rows = self.rows(shard, q)
        rows[...] = (rows[...].astype(jnp.float32) + other[...].astype(jnp.float32)).astype(jnp.bfloat16)

    def step_near(self, q):
        for turn in range(2):
            high = (1 - self.z // 2 + turn) % 2
            shard_z = high * 2 + 1 - self.z % 2
            self.x_copy(shard_z, q).wait_recv()
            self.add(shard_z * 2 + self.x, q, self.from_x.at[shard_z, q])
            self.near_copy(high, q).start()
        for turn in range(2):
            high = (1 - self.z // 2 + turn) % 2
            shard_z = high * 2 + self.z % 2
            self.x_copy(shard_z, q).wait_recv()
            self.add(shard_z * 2 + self.x, q, self.from_x.at[shard_z, q])

    def step_far(self, q):
        high = 1 - self.z // 2
        self.near_copy(high, q).wait_recv()
        self.add((high * 2 + self.z % 2) * 2 + self.x, q, self.from_near.at[high, q])
        self.far_copy(q).start()

    def total(self, q):
        high = self.z // 2
        self.near_copy(high, q).wait_recv()
        self.far_copy(q).wait_recv()
        f32 = jnp.float32
        return (
            self.rows(self.s, q)[...].astype(f32)
            + self.from_near[high, q].astype(f32)
            + self.from_far[q].astype(f32)
        )

    def settle(self):
        for q in range(2):
            for shard_z in range(4):
                self.x_copy(shard_z, q).wait_send()
            for high in range(2):
                self.near_copy(high, q).wait_send()
            self.far_copy(q).wait_send()


def finish_kernel(gated, w_out, d_z, d_x, d_bc, d_dt, w_in, cot_all, normed_all, hidden, cot, gain, small,
                  result, d_hidden, grad_in, grad_out, small_all, gain_sum,
                  gated_v, w_out_v, dp_v, w_in_v, tok_v,
                  part_r, rx, rn, rf, part_d, dx, dn, df,
                  core_out, core_in, keep, y_in, plane_in,
                  out_core, out_core_in, out_keep, out_y, out_y_in, small_v, small_in, gain_v, gain_in,
                  load, rxs, rns, rfs, dxs, dns, dfs, core_sems, y_sems, plane_sems, out_sems, out_y_sems,
                  small_sems, small_plane, gain_sems, gain_plane):
    f32, bf16 = jnp.float32, jnp.bfloat16
    where = place()
    dp, s, z, x, x_peer, y_peer, core_peer = where
    y, core = dp // 2, dp % 2
    n_own, span, width = hidden.shape
    length = 8 * span
    chan = w_out.shape[0]
    rows = chan // 4
    in_rows = grad_in.shape[0]
    columns = keep.shape[3]
    tail = columns - 2 * chan
    peers = [(dp, (s + k) % 8) for k in range(1, 8)] + [(y_peer, s), (core_peer, s)]
    loads = [
        pltpu.make_async_copy(gated, gated_v, load.at[0]),
        pltpu.make_async_copy(w_out, w_out_v, load.at[1]),
        pltpu.make_async_copy(d_z, dp_v.at[:, pl.ds(0, chan)], load.at[2]),
        pltpu.make_async_copy(d_x, dp_v.at[:, pl.ds(chan, chan)], load.at[3]),
        pltpu.make_async_copy(d_bc, dp_v.at[:, pl.ds(2 * chan, 2 * NST)], load.at[4]),
        pltpu.make_async_copy(d_dt, dp_v.at[:, pl.ds(2 * chan + 2 * NST, 128)], load.at[5]),
        pltpu.make_async_copy(w_in, w_in_v, load.at[6]),
        pltpu.make_async_copy(cot_all, tok_v, load.at[7]),
    ]
    for copy in loads:
        copy.start()
    greet(peers)
    small_v[0] = small[...]

    def small_copy(stage, device):
        return remote(small_v.at[stage], small_in.at[stage], small_sems.at[0, stage], small_sems.at[1, stage], device)

    small_core = small_copy(0, (core_peer, s))
    small_core.start()
    reduce_r = TokenReduce(part_r, rx, rn, rf, rxs, rns, rfs, where, span)
    reduce_d = TokenReduce(part_d, dx, dn, df, dxs, dns, dfs, where, span)
    loads[0].wait()
    loads[1].wait()
    step = 512
    for q in range(2):

        @pl.loop(0, width // step)
        def forward(n):
            cols = pl.ds(pl.multiple_of(n * step, step), step)
            part_r[q, :, cols] = jnp.dot(
                gated_v[q * length : (q + 1) * length], w_out_v[:, cols], preferred_element_type=f32
            ).astype(bf16)

        reduce_r.start(q)
    for copy in loads[2:7]:
        copy.wait()
    for q in range(2):

        @pl.loop(0, width // step)
        def backward(n):
            cols = pl.ds(pl.multiple_of(n * step, step), step)
            part_d[q, :, cols] = lax.dot_general(
                dp_v[q * length : (q + 1) * length], w_in_v[cols], (((1,), (1,)), ((), ())),
                preferred_element_type=f32,
            ).astype(bf16)

        reduce_d.start(q)

    small_core.wait_recv()
    small_v[1] = small_v[0] + small_in[0]
    small_y = small_copy(1, (y_peer, s))
    small_y.start()
    loads[7].wait()

    def out_term(d, n):
        lanes = pl.ds(pl.multiple_of(d * rows, rows), rows)
        return lax.dot_general(
            gated_v[:, lanes], tok_v[:, n * step : (n + 1) * step], (((0,), (0,)), ((), ())),
            preferred_element_type=f32,
        )

    def out_core_copy(yy):
        return remote(out_core.at[yy], out_core_in.at[yy], out_sems.at[0, yy], out_sems.at[1, yy], (core_peer, s))

    for yy in range(2):
        for n in range(width // step):
            out_core[yy, :, n * step : (n + 1) * step] = out_term(yy * 2 + 1 - core, n).astype(bf16)
        out_core_copy(yy).start()
    for yy in range(2):
        for n in range(width // step):
            out_keep[yy, :, n * step : (n + 1) * step] = out_term(yy * 2 + core, n)
    norm_load = pltpu.make_async_copy(normed_all, tok_v, load.at[8])
    norm_load.start()
    reduce_r.step_near(0)
    out_core_copy(1 - y).wait_recv()
    out_y[...] = (out_keep[1 - y] + out_core_in[1 - y].astype(f32)).astype(bf16)
    out_y_copy = remote(out_y, out_y_in, out_y_sems.at[0], out_y_sems.at[1], (y_peer, s))
    out_y_copy.start()
    small_y.wait_recv()
    small_all[s] = small_v[1] + small_in[1]

    def small_push(k):
        return remote(
            small_all.at[s], small_all.at[s], small_plane.at[0, k], small_plane.at[1, s], (dp, (s + k) % 8)
        )

    for k in range(1, 8):
        small_push(k).start()
    norm_load.wait()

    def in_term(d, m, lo, size):
        lanes = pl.ds(pl.multiple_of(d * 8 * in_rows + m * 2 * in_rows, 2 * in_rows), 2 * in_rows)
        return lax.dot_general(
            tok_v[:, lanes], dp_v[:, lo : lo + size], (((0,), (0,)), ((), ())), preferred_element_type=f32
        )

    pieces = ((0, chan, chan), (chan, chan, chan), (2 * chan, tail, 2 * NST + 128))

    def core_copy(m, yy):
        return remote(core_out.at[m, yy], core_in.at[m, yy], core_sems.at[0, m, yy], core_sems.at[1, m, yy], (core_peer, s))

    def y_copy(m):
        return remote(keep.at[m, 1 - y], y_in.at[m], y_sems.at[0, m], y_sems.at[1, m], (y_peer, s))

    def in_compute(m):
        for yy in range(2):
            for lo, size, span_in in pieces:
                core_out[m, yy, :, lo : lo + size] = in_term(yy * 2 + 1 - core, m, lo, span_in)[:, :size].astype(bf16)
            core_copy(m, yy).start()
        for yy in range(2):
            for lo, size, span_in in pieces:
                keep[m, yy, :, lo : lo + size] = in_term(yy * 2 + core, m, lo, span_in)[:, :size].astype(bf16)

    def in_core(m):
        for yy in range(2):
            core_copy(m, yy).wait_recv()
            keep[m, yy] = (keep[m, yy].astype(f32) + core_in[m, yy].astype(f32)).astype(bf16)
        y_copy(m).start()

    def plane_copy(m, half):
        target = 2 * m + half
        return remote(
            keep.at[m, y, pl.ds(half * in_rows, in_rows)], plane_in.at[s],
            plane_sems.at[0, target], plane_sems.at[1, s], (dp, target),
        )

    def in_plane(m):
        y_copy(m).wait_recv()
        keep[m, y] = (keep[m, y].astype(f32) + y_in[m].astype(f32)).astype(bf16)
        for half in range(2):

            @pl.when(s != 2 * m + half)
            def away():
                plane_copy(m, half).start()

            @pl.when(s == 2 * m + half)
            def here():
                plane_in[s] = keep[m, y, half * in_rows : (half + 1) * in_rows]

    in_compute(0)
    in_compute(1)
    in_core(0)
    reduce_r.step_near(1)
    in_compute(2)
    in_core(1)
    reduce_r.step_far(0)
    in_compute(3)
    in_core(2)
    in_plane(0)
    in_core(3)
    reduce_r.step_far(1)
    in_plane(1)
    reduce_d.step_near(0)
    in_plane(2)
    hidden_f = [hidden[q].astype(f32) for q in range(2)]
    for q in range(2):
        result[q] = (hidden[q].astype(f32) + reduce_r.total(q)).astype(bf16)
    in_plane(3)
    reduce_d.step_far(0)
    out_y_copy.wait_recv()
    out_core_copy(y).wait_recv()
    grad_out[...] = out_keep[y] + out_core_in[y].astype(f32) + out_y_in[...].astype(f32)
    reduce_d.step_near(1)
    reduce_d.step_far(1)
    gain_row = gain[...]
    gain_part = None
    for q in range(2):
        d_normed = reduce_d.total(q)
        h = hidden[q].astype(f32)
        inv = lax.rsqrt(jnp.mean(h * h, axis=-1, keepdims=True) + 1e-05)
        scaled = d_normed * gain_row
        along = jnp.mean(scaled * h, axis=-1, keepdims=True)
        d_hidden[q] = (cot[q].astype(f32) + inv * scaled - (inv * inv * inv) * along * h).astype(bf16)
        term = jnp.sum(d_normed * h * inv, axis=0, keepdims=True)
        gain_part = term if q == 0 else gain_part + term
    folded = width // 8
    gain_v[0] = jnp.concatenate([gain_part[:, k * folded : (k + 1) * folded] for k in range(8)], axis=0)

    def gain_copy(stage, device):
        return remote(gain_v.at[stage], gain_in.at[stage], gain_sems.at[0, stage], gain_sems.at[1, stage], device)

    gain_core = gain_copy(0, (core_peer, s))
    gain_core.start()
    for k in range(1, 8):
        source = (s + 8 - k) % 8
        remote(plane_in.at[source], plane_in.at[source], plane_sems.at[0, source], plane_sems.at[1, source], (dp, x_peer)).wait_recv()
    gain_core.wait_recv()
    gain_v[1] = gain_v[0] + gain_in[0]
    gain_y = gain_copy(1, (y_peer, s))
    gain_y.start()
    tail_sum = None
    for source in range(8):
        for piece in range(WIDE):
            at = (piece * 8 + source) * rows
            grad_in[:, at : at + rows] = plane_in[source, :, piece * rows : (piece + 1) * rows].astype(f32)
        term = plane_in[source, :, 2 * chan :].astype(f32)
        tail_sum = term if source == 0 else tail_sum + term
    grad_in[:, 2 * DI :] = tail_sum
    gain_y.wait_recv()
    gain_v[2 + s] = gain_v[1] + gain_in[1]

    def gain_push(k):
        return remote(gain_v.at[2 + s], gain_v.at[2 + s], gain_plane.at[0, k], gain_plane.at[1, s], (dp, (s + k) % 8))

    for k in range(1, 8):
        gain_push(k).start()
    reduce_r.settle()
    reduce_d.settle()
    small_core.wait_send()
    small_y.wait_send()
    out_y_copy.wait_send()
    for yy in range(2):
        out_core_copy(yy).wait_send()
    for m in range(4):
        for yy in range(2):
            core_copy(m, yy).wait_send()
        y_copy(m).wait_send()
        for half in range(2):

            @pl.when(s != 2 * m + half)
            def sent():
                plane_copy(m, half).wait_send()

    for k in range(1, 8):
        source = (s + 8 - k) % 8
        remote(
            small_all.at[source], small_all.at[source], small_plane.at[0, k], small_plane.at[1, source], (dp, x_peer)
        ).wait_recv()
        small_push(k).wait_send()
        remote(
            gain_v.at[2 + source], gain_v.at[2 + source], gain_plane.at[0, k], gain_plane.at[1, source], (dp, x_peer)
        ).wait_recv()
        gain_push(k).wait_send()
    gain_core.wait_send()
    gain_y.wait_send()
    gain_total = gain_v[2]
    for source in range(1, 8):
        gain_total = gain_total + gain_v[2 + source]
    gain_sum[...] = gain_total


def run_finish(gated, w_out, d_z, d_x, d_bc, d_dt, w_in, cot_all, normed_all, hidden, cot, gain, small, in_rows):
    f32, bf16 = jnp.float32, jnp.bfloat16
    n_own, span, width = hidden.shape
    tokens, chan = gated.shape
    length, rows = 8 * span, chan // 4
    columns = 2 * chan + 2 * NST + HEADS
    vmem = pltpu.VMEM
    anywhere, inside = pl.BlockSpec(memory_space=pl.ANY), pl.BlockSpec(memory_space=vmem)
    sem = pltpu.SemaphoreType.DMA
    tokens_like = [
        vmem((n_own, length, width), bf16), vmem((4, n_own, span, width), bf16),
        vmem((2, n_own, span, width), bf16), vmem((n_own, span, width), bf16),
    ]
    return pl.pallas_call(
        finish_kernel,
        in_specs=[anywhere] * 9 + [inside] * 4,
        out_specs=[inside] * 6,
        out_shape=[
            jax.ShapeDtypeStruct(hidden.shape, bf16),
            jax.ShapeDtypeStruct(hidden.shape, bf16),
            jax.ShapeDtypeStruct((in_rows, 2 * DI + columns - 2 * chan), f32),
            jax.ShapeDtypeStruct((rows, width), f32),
            jax.ShapeDtypeStruct((8,) + small.shape, f32),
            jax.ShapeDtypeStruct((8, width // 8), f32),
        ],
        scratch_shapes=[
            vmem((tokens, chan), bf16), vmem((chan, width), bf16),
            vmem((tokens, 2 * chan + 2 * NST + 128), bf16), vmem((width, 2 * chan + 2 * NST + 128), bf16),
            vmem((tokens, width), bf16),
        ]
        + tokens_like + tokens_like
        + [
            vmem((4, 2, 2 * in_rows, columns), bf16), vmem((4, 2, 2 * in_rows, columns), bf16),
            vmem((4, 2, 2 * in_rows, columns), bf16), vmem((4, 2 * in_rows, columns), bf16),
            vmem((8, in_rows, columns), bf16),
            vmem((2, rows, width), bf16), vmem((2, rows, width), bf16), vmem((2, rows, width), f32),
            vmem((rows, width), bf16), vmem((rows, width), bf16),
            vmem((2,) + small.shape, f32), vmem((2,) + small.shape, f32),
            vmem((10, 8, width // 8), f32), vmem((2, 8, width // 8), f32),
            sem((9,)), sem((2, 4, 2)), sem((2, 2, 2)), sem((2, 2)), sem((2, 4, 2)), sem((2, 2, 2)), sem((2, 2)),
            sem((2, 4, 2)), sem((2, 4)), sem((2, 8)), sem((2, 2)), sem((2,)),
            sem((2, 2)), sem((2, 8)), sem((2, 2)), sem((2, 8)),
        ],
        compiler_params=pltpu.CompilerParams(
            collective_id=1, has_side_effects=True, vmem_limit_bytes=60 << 20
        ),
        name="finish",
    )(gated, w_out, d_z, d_x, d_bc, d_dt, w_in, cot_all, normed_all, hidden, cot, gain, small)


def head_plan(
    hidden,
    segments,
    in_weight,
    conv_weight,
    conv_bias,
    dt_bias,
    a_log,
    d_skip,
    norm_gain,
    gate_gain,
    out_weight,
    cotangent,
):
    f32, bf16 = jnp.float32, jnp.bfloat16
    n_dp, n_seq = lax.axis_size("dp"), lax.axis_size("seq")
    seq_rank = lax.axis_index("seq")
    n_own, shard_len, width = hidden.shape
    length = shard_len * n_seq
    rows = out_weight.shape[0]
    in_rows = in_weight.shape[0]
    chan = rows * n_dp
    h_own = chan // HDIM
    seg_tile = jnp.pad(segments.astype(f32), ((0, 8 - n_own), (0, 128 - shard_len)))
    in_tail = jnp.pad(in_weight[:, 2 * DI :], ((0, 0), (0, 128 - HEADS)))
    (n_all, cot_all, w_in, w_out, x_raw, bc_raw, dt_raw, inner, gated, d_y, d_z, seg_col, seg_row, wx, wbc, head_vals,
     gain_back) = run_ahead(
        hidden, cotangent, in_weight, in_tail, out_weight, seg_tile, conv_weight.T, conv_bias[None],
        norm_gain[None], gate_gain[None], dt_bias, a_log, d_skip,
    )
    normed_all = n_all.reshape(n_own * length, width)
    cot_all = cot_all.reshape(n_own * length, width)
    operands = (x_raw, bc_raw, dt_raw, seg_col, seg_row, wx, wbc, head_vals)

    def spread_head(vec):
        blank = jnp.zeros((n_dp, n_seq, heads_row) + vec.shape[1:], f32)
        piece = vec.reshape((n_dp, 1, heads_row) + vec.shape[1:])
        return lax.dynamic_update_slice_in_dim(blank, piece, seq_rank, 1).reshape(
            (HEADS,) + vec.shape[1:]
        )

    heads_row = rows // HDIM
    d_x, d_bc, d_dt, g_x, g_bc, g_head = run_backward(
        n_own, h_own, n_seq, heads_row, operands, d_y, inner
    )
    g_x, g_bc, g_head = jnp.sum(g_x, 0), jnp.sum(g_bc, 0), jnp.sum(g_head, 0)
    g_x = jnp.concatenate([g_x[: CONV + 2], gain_back[:1], g_x[CONV + 3 :]], axis=0)
    small = jnp.concatenate([g_x, g_bc, g_head], axis=1)
    d_dt = jnp.pad(spread_head(d_dt[:, :h_own].T).T, ((0, 0), (0, 128 - HEADS))).astype(bf16)
    result, d_hidden, grad_in, grad_out, small_all, gain_sum = run_finish(
        gated, w_out, d_z, d_x, d_bc, d_dt, w_in, cot_all, normed_all,
        hidden, cotangent, norm_gain[None], small, in_rows,
    )
    over_chan = small_all[:, :, :chan].reshape(n_seq, 8, n_dp, rows)
    over_chan = over_chan.transpose(1, 2, 0, 3).reshape(8, DI)
    over_bc = jnp.sum(small_all[:, :, chan : chan + 2 * NST], axis=0)
    over_head = small_all[:, :2, chan + 2 * NST : chan + 2 * NST + h_own]
    over_head = over_head.reshape(n_seq, 2, n_dp, heads_row).transpose(1, 2, 0, 3).reshape(2, HEADS)
    grad_skip = jnp.sum(over_chan[CONV + 1].reshape(HEADS, HDIM), axis=1)
    return (
        result,
        d_hidden,
        grad_in,
        jnp.concatenate([over_chan[:CONV], over_bc[:CONV]], axis=1).T,
        jnp.concatenate([over_chan[CONV], over_bc[CONV]], axis=0),
        over_head[0],
        over_head[1],
        grad_skip,
        gain_sum.reshape(width),
        over_chan[CONV + 2],
        grad_out,
    )


def solution(mesh):
    whole_heads = mesh.shape["dp"] == 4 and mesh.shape["seq"] == 8
    shards = head_plan if whole_heads else general_plan
    placed = (
        P("dp", "seq", None),
        P("dp", "seq"),
        P(("dp", "seq"), None),
        P(),
        P(),
        P(),
        P(),
        P(),
        P(),
        P(),
        P(("dp", "seq"), None),
        P("dp", "seq", None),
    )
    return jax.shard_map(
        shards,
        mesh=mesh,
        in_specs=placed,
        out_specs=(
            P("dp", "seq", None),
            P("dp", "seq", None),
            P(("dp", "seq"), None),
            P(),
            P(),
            P(),
            P(),
            P(),
            P(),
            P(),
            P(("dp", "seq"), None),
        ),
        check_vma=False,
    )
```

```python
import functools

import jax
import jax.numpy as jnp
from jax import lax
from jax.experimental import pallas as pl
from jax.experimental.pallas import tpu as pltpu
from jax.sharding import PartitionSpec as P

HEADS = 64
HDIM = 64
NST = 128
GROUP = 256
CONV = 4
DI = 4096


def pre_norm(hidden_f, gain_vec):
    return (
        hidden_f
        * lax.rsqrt(jnp.mean(hidden_f * hidden_f, axis=-1, keepdims=True) + 1e-05)
        * gain_vec
    )


def gate_norm(y_values, gate_values, gain_vec):
    product = y_values * jax.nn.silu(gate_values)
    return (
        product * lax.rsqrt(jnp.mean(product * product, axis=-1, keepdims=True) + 1e-05) * gain_vec
    )


def conv_reset(signal, kernel, offset, seg_ids):
    tap_count = kernel.shape[1]
    summed = offset[None, :] + kernel[None, :, tap_count - 1] * signal
    for lag_steps in range(1, tap_count):
        shifted = jnp.pad(signal, ((lag_steps, 0), (0, 0)))[:-lag_steps]
        earlier = jnp.pad(seg_ids, (lag_steps, 0), constant_values=-1)[:-lag_steps]
        matches = (earlier == seg_ids).astype(jnp.float32)
        summed = summed + kernel[None, :, tap_count - 1 - lag_steps] * shifted * matches[:, None]
    return summed


def state_scan(values, deltas, rates, b_mat, c_mat, seg_ids):
    length, head_count, head_width = values.shape
    block_count = length // GROUP
    log_decay = deltas * rates[None, :]
    pieces = (
        values.reshape(block_count, GROUP, head_count, head_width),
        deltas.reshape(block_count, GROUP, head_count),
        log_decay.reshape(block_count, GROUP, head_count),
        b_mat.reshape(block_count, GROUP, b_mat.shape[-1]),
        c_mat.reshape(block_count, GROUP, c_mat.shape[-1]),
        seg_ids.reshape(block_count, GROUP),
    )
    position = lax.broadcasted_iota(jnp.int32, (GROUP, GROUP), 0)
    source = lax.broadcasted_iota(jnp.int32, (GROUP, GROUP), 1)

    def advance(carry, piece):
        memory, ending = carry
        block_vals, block_dt, block_log, b_block, c_block, seg_block = piece
        cumulative = jnp.cumsum(block_log, axis=0).T
        causal = (source <= position) & (seg_block[:, None] == seg_block[None, :])
        spread = cumulative[:, :, None] - cumulative[:, None, :]
        decays = jnp.where(causal[None], jnp.exp(jnp.where(causal[None], spread, 0.0)), 0.0)
        inner_prod = jnp.dot(c_block, b_block.T, precision=lax.Precision.HIGHEST)
        scores = inner_prod[None] * decays * block_dt.T[:, None, :]
        output = jnp.einsum("hij,jhp->ihp", scores, block_vals, precision=lax.Precision.HIGHEST)
        follows = (seg_block == ending).astype(jnp.float32)
        carried = jnp.einsum("in,hpn->ihp", c_block, memory, precision=lax.Precision.HIGHEST)
        output = output + (jnp.exp(cumulative).T * follows[:, None])[:, :, None] * carried
        last_seg = seg_block[-1]
        weights = (
            jnp.exp(cumulative[:, -1:] - cumulative)
            * (seg_block == last_seg).astype(jnp.float32)[None, :]
            * block_dt.T
        )
        keep_on = jnp.exp(cumulative[:, -1]) * (last_seg == ending).astype(jnp.float32)
        memory = memory * keep_on[:, None, None] + jnp.einsum(
            "hj,jhp,jn->hpn", weights, block_vals, b_block, precision=lax.Precision.HIGHEST
        )
        return ((memory, last_seg), output)

    initial = (
        jnp.zeros((head_count, head_width, b_mat.shape[-1]), jnp.float32),
        jnp.array(-1, jnp.int32),
    )
    unused, outputs = lax.scan(jax.checkpoint(advance), initial, pieces)
    return outputs.reshape(length, head_count, head_width)


def mixer(
    x_values,
    step_raw,
    bc_values,
    seg_ids,
    kernel_x,
    offset_x,
    kernel_bc,
    offset_bc,
    dt_shift,
    decay_log,
    skip_gain,
):
    x_conv = jax.nn.silu(conv_reset(x_values, kernel_x, offset_x, seg_ids))
    bc_conv = jax.nn.silu(conv_reset(bc_values, kernel_bc, offset_bc, seg_ids))
    step_sizes = jax.nn.softplus(step_raw + dt_shift[None, :])
    rates = -jnp.exp(decay_log)
    length = x_values.shape[0]
    head_count = step_raw.shape[1]
    shaped = x_conv.reshape(length, head_count, HDIM)
    mixed = (
        state_scan(shaped, step_sizes, rates, bc_conv[:, :NST], bc_conv[:, NST:], seg_ids)
        + skip_gain[None, :, None] * shaped
    )
    return mixed.reshape(length, head_count * HDIM)


def general_plan(
    hidden,
    segments,
    in_weight,
    conv_weight,
    conv_bias,
    dt_bias,
    a_log,
    d_skip,
    norm_gain,
    gate_gain,
    out_weight,
    cotangent,
):
    full_in, full_out = (
        lax.all_gather(in_weight, ("dp", "seq"), axis=0, tiled=True),
        lax.all_gather(out_weight, ("dp", "seq"), axis=0, tiled=True),
    )
    hidden_f = hidden.astype(jnp.float32)
    normed_f, pull_pre = jax.vjp(pre_norm, hidden_f, norm_gain)
    normed = normed_f.astype(jnp.bfloat16)
    project = jnp.einsum("mtd,df->mtf", normed, full_in, preferred_element_type=jnp.float32)
    gate_part = project[:, :, :DI]
    x_part = project[:, :, DI : 2 * DI].astype(jnp.bfloat16)
    bc_part = project[:, :, 2 * DI : 2 * DI + 2 * NST].astype(jnp.bfloat16)
    step_part = project[:, :, 2 * DI + 2 * NST :].astype(jnp.bfloat16)
    x_heads, step_heads = (
        lax.all_to_all(x_part, "seq", split_axis=2, concat_axis=1, tiled=True),
        lax.all_to_all(step_part, "seq", split_axis=2, concat_axis=1, tiled=True),
    )
    bc_full = lax.all_gather(bc_part, "seq", axis=1, tiled=True)
    seg_full = lax.all_gather(segments, "seq", axis=1, tiled=True)
    seq_rank = lax.axis_index("seq")
    head_local = step_heads.shape[2]
    chan_local = x_heads.shape[2]
    kernel_x = lax.dynamic_slice_in_dim(conv_weight, seq_rank * chan_local, chan_local, 0)
    offset_x = lax.dynamic_slice_in_dim(conv_bias, seq_rank * chan_local, chan_local, 0)
    shift_local = lax.dynamic_slice_in_dim(dt_bias, seq_rank * head_local, head_local, 0)
    decay_local = lax.dynamic_slice_in_dim(a_log, seq_rank * head_local, head_local, 0)
    skip_local = lax.dynamic_slice_in_dim(d_skip, seq_rank * head_local, head_local, 0)
    local_params = (
        kernel_x,
        offset_x,
        conv_weight[DI:],
        conv_bias[DI:],
        shift_local,
        decay_local,
        skip_local,
    )

    def head_mixer(x_values, step_raw, bc_values, params_in):

        def single_seq(x_one, step_one, bc_one, seg_one):
            return mixer(x_one, step_one, bc_one, seg_one, *params_in)

        return jax.vmap(single_seq)(x_values, step_raw, bc_values, seg_full)

    mixed, pull_mix = jax.vjp(
        head_mixer,
        x_heads.astype(jnp.float32),
        step_heads.astype(jnp.float32),
        bc_full.astype(jnp.float32),
        local_params,
    )
    y_tokens = lax.all_to_all(
        mixed.astype(jnp.bfloat16), "seq", split_axis=1, concat_axis=2, tiled=True
    )
    gated_f, pull_gate = jax.vjp(gate_norm, y_tokens.astype(jnp.float32), gate_part, gate_gain)
    gated = gated_f.astype(jnp.bfloat16)
    branch_out = jnp.einsum("mtf,fd->mtd", gated, full_out, preferred_element_type=jnp.float32)
    result = (hidden_f + branch_out).astype(jnp.bfloat16)
    d_gated = jnp.einsum("mtd,fd->mtf", cotangent, full_out, preferred_element_type=jnp.float32)
    d_mixed, d_gate_part, d_gate_gain = pull_gate(d_gated)
    d_heads = lax.all_to_all(
        d_mixed.astype(jnp.bfloat16), "seq", split_axis=2, concat_axis=1, tiled=True
    )
    d_x_heads, d_step_heads, d_bc_full, d_params = pull_mix(d_heads.astype(jnp.float32))
    d_x_part, d_step_part = (
        lax.all_to_all(
            d_x_heads.astype(jnp.bfloat16), "seq", split_axis=1, concat_axis=2, tiled=True
        ),
        lax.all_to_all(
            d_step_heads.astype(jnp.bfloat16), "seq", split_axis=1, concat_axis=2, tiled=True
        ),
    )
    d_bc_part = lax.psum_scatter(
        d_bc_full.astype(jnp.bfloat16), "seq", scatter_dimension=1, tiled=True
    )
    d_project = jnp.concatenate(
        [d_gate_part.astype(jnp.bfloat16), d_x_part, d_bc_part, d_step_part], axis=2
    )
    d_normed = jnp.einsum("mtf,df->mtd", d_project, full_in, preferred_element_type=jnp.float32)
    d_hidden_f, d_norm_gain = pull_pre(d_normed)
    d_hidden = (cotangent.astype(jnp.float32) + d_hidden_f).astype(jnp.bfloat16)
    in_rows = in_weight.shape[0]
    out_rows = out_weight.shape[0]
    column_ranges = ((0, DI), (DI, d_project.shape[2]))
    in_pieces = [jnp.zeros((in_rows, upper - lower), jnp.float32) for lower, upper in column_ranges]
    grad_out = jnp.zeros(out_weight.shape, jnp.float32)
    for batch_index in range(hidden.shape[0]):
        for range_index in range(len(column_ranges)):
            lower, upper = column_ranges[range_index]

            def in_term(
                start,
                count,
                normed_one=normed[batch_index],
                d_one=d_project[batch_index, :, lower:upper],
            ):
                return lax.dot_general(
                    normed_one, d_one, (((0,), (0,)), ((), ())), preferred_element_type=jnp.float32
                )

            in_pieces[range_index] = in_pieces[range_index] + lax.psum_scatter(
                in_term(jnp.int32(0), in_rows * lax.axis_size(("dp", "seq"))),
                ("dp", "seq"),
                scatter_dimension=0,
                tiled=True,
            )

        def out_term(start, count, gated_one=gated[batch_index], cot_one=cotangent[batch_index]):
            return lax.dot_general(
                gated_one, cot_one, (((0,), (0,)), ((), ())), preferred_element_type=jnp.float32
            )

        grad_out = grad_out + lax.psum_scatter(
            out_term(jnp.int32(0), out_rows * lax.axis_size(("dp", "seq"))),
            ("dp", "seq"),
            scatter_dimension=0,
            tiled=True,
        )
    grad_in = jnp.concatenate(in_pieces, axis=1)
    d_kernel_x, d_offset_x, d_kernel_bc, d_offset_bc, d_shift, d_decay, d_skip_part = d_params
    tap_count = conv_weight.shape[1]
    grad_conv_w = jnp.concatenate(
        [
            lax.dynamic_update_slice_in_dim(
                jnp.zeros((DI, tap_count), jnp.float32), d_kernel_x, seq_rank * chan_local, 0
            ),
            d_kernel_bc,
        ],
        axis=0,
    )
    grad_conv_b = jnp.concatenate(
        [
            lax.dynamic_update_slice_in_dim(
                jnp.zeros((DI,), jnp.float32), d_offset_x, seq_rank * chan_local, 0
            ),
            d_offset_bc,
        ],
        axis=0,
    )
    grad_shift = lax.dynamic_update_slice_in_dim(
        jnp.zeros((HEADS,), jnp.float32), d_shift, seq_rank * head_local, 0
    )
    grad_decay = lax.dynamic_update_slice_in_dim(
        jnp.zeros((HEADS,), jnp.float32), d_decay, seq_rank * head_local, 0
    )
    grad_skip = lax.dynamic_update_slice_in_dim(
        jnp.zeros((HEADS,), jnp.float32), d_skip_part, seq_rank * head_local, 0
    )
    totals = lax.psum(
        (grad_conv_w, grad_conv_b, grad_shift, grad_decay, grad_skip, d_norm_gain, d_gate_gain),
        ("dp", "seq"),
    )
    return (
        result,
        d_hidden,
        grad_in,
        totals[0],
        totals[1],
        totals[2],
        totals[3],
        totals[4],
        totals[5],
        totals[6],
        grad_out,
    )


LOG2E = 1.4426950408889634
TILE = 128
FAR = -1e30


def shift_rows(v, lag):
    return v if lag == 0 else pltpu.roll(v, lag % v.shape[0], axis=0)


def conv_silu(sig, taps, offset, keep):
    total = offset + taps[CONV - 1 : CONV] * sig
    for lag in range(1, CONV):
        total = total + taps[CONV - 1 - lag : CONV - lag] * (shift_rows(sig, lag) * keep[lag])
    gate = jax.nn.sigmoid(total)
    return total, gate, total * gate


def conv_back(d_out, total, gate, sig, taps, keep):
    d_total = d_out * (gate * (1.0 + total * (1.0 - gate)))
    d_sig = taps[CONV - 1 : CONV] * d_total
    tap_rows = [jnp.sum(d_total * sig, axis=0, keepdims=True)]
    for lag in range(1, CONV):
        kept = d_total * keep[lag]
        d_sig = d_sig + taps[CONV - 1 - lag : CONV - lag] * shift_rows(kept, -lag)
        tap_rows.append(jnp.sum(kept * shift_rows(sig, lag), axis=0, keepdims=True))
    return d_sig, tap_rows[::-1], jnp.sum(d_total, axis=0, keepdims=True)


def keep_masks(seg_col):
    length = seg_col.shape[0]
    row = lax.broadcasted_iota(jnp.int32, (length, 1), 0)
    masks = [None]
    for lag in range(1, CONV):
        same = (pltpu.roll(seg_col, lag, axis=0) == seg_col) & (row >= lag)
        masks.append(same.astype(jnp.float32))
    return masks


def lane_sums(v, reverse):
    length = v.shape[1]
    lane = lax.broadcasted_iota(jnp.int32, v.shape, 1)
    step = 1
    while step < length:
        if reverse:
            v = v + jnp.where(lane < length - step, pltpu.roll(v, length - step, axis=1), 0.0)
        else:
            v = v + jnp.where(lane >= step, pltpu.roll(v, step, axis=1), 0.0)
        step *= 2
    return v


def step_sizes_of(dt_all, head_rows, h_own, n_seq, heads_row):
    rank = lax.axis_index("seq")
    all_heads = dt_all.shape[1]
    lane = lax.broadcasted_iota(jnp.int32, (all_heads, 128), 1)
    row = lax.broadcasted_iota(jnp.int32, (all_heads, 128), 0)
    head = ((lane // heads_row) * n_seq + rank) * heads_row + lane % heads_row
    pick = ((row == head) & (lane < h_own)).astype(jnp.bfloat16)
    raw = jnp.dot(dt_all, pick, preferred_element_type=jnp.float32)
    shifted = raw + head_rows[0:1]
    dt = jnp.maximum(shifted, 0.0) + jnp.log1p(jnp.exp(-jnp.abs(shifted)))
    return shifted, dt


MESH = pl.DeviceIdType.MESH
WIDE = 8


def place():
    dp, s = lax.axis_index("dp"), lax.axis_index("seq")
    z, x = s // 2, s % 2
    y, core = dp // 2, dp % 2
    return dp, s, z, x, s + 1 - 2 * x, dp + 2 - 4 * y, dp + 1 - 2 * core


def greet(peers):
    barrier = pltpu.get_barrier_semaphore()
    for device in peers:
        pl.semaphore_signal(barrier, inc=1, device_id=device, device_id_type=MESH)
    pl.semaphore_wait(barrier, len(peers))


def remote(src, dst, send, recv, device):
    return pltpu.make_async_remote_copy(
        src_ref=src, dst_ref=dst, send_sem=send, recv_sem=recv, device_id=device, device_id_type=MESH
    )


class TokenGather:
    def __init__(self, own, full, send, recv, where):
        self.own, self.full, self.send, self.recv = own, full, send, recv
        self.dp, self.s, self.z, self.x, self.x_peer, _, _ = where
        self.span = own.shape[1]

    def part(self, shard, q):
        return self.full.at[q, pl.ds(pl.multiple_of(shard * self.span, self.span), self.span)]

    def copy(self, shard_z, way, q, mine):
        shard = shard_z * 2 + self.x
        target = (self.s + 2, self.s - 2, self.x_peer)[way]
        src = self.own.at[q] if mine else self.part(shard, q)
        return remote(
            src, self.part(shard, q), self.send.at[way, shard_z, q], self.recv.at[shard, q], (self.dp, target)
        )

    def arrived(self, shard, q):
        part = self.part(shard, q)
        remote(part, part, self.send.at[0, 0, q], self.recv.at[shard, q], (self.dp, self.x_peer)).wait_recv()

    def start(self, q):
        @pl.when(self.z < 3)
        def up():
            self.copy(self.z, 0, q, True).start()

        @pl.when(self.z > 0)
        def down():
            self.copy(self.z, 1, q, True).start()

        self.copy(self.z, 2, q, True).start()

    def step(self, hop, q):
        @pl.when(self.z >= hop)
        def from_below():
            shard_z = self.z - hop
            self.arrived(shard_z * 2 + self.x, q)

            @pl.when(self.z < 3)
            def up():
                self.copy(shard_z, 0, q, False).start()

            self.copy(shard_z, 2, q, False).start()

        @pl.when(self.z + hop <= 3)
        def from_above():
            shard_z = self.z + hop
            self.arrived(shard_z * 2 + self.x, q)

            @pl.when(self.z > 0)
            def down():
                self.copy(shard_z, 1, q, False).start()

            self.copy(shard_z, 2, q, False).start()

    def arrive_x(self, q):
        for shard_z in range(4):
            self.arrived(shard_z * 2 + 1 - self.x, q)

    def settle(self, q):
        for shard_z in range(4):
            self.copy(shard_z, 2, q, False).wait_send()

            @pl.when((self.z < 3) & (self.z >= shard_z))
            def up():
                self.copy(shard_z, 0, q, False).wait_send()

            @pl.when((self.z > 0) & (self.z <= shard_z))
            def down():
                self.copy(shard_z, 1, q, False).wait_send()


def column_of(mat, index):
    return pltpu.roll(mat, (128 - index) % 128, axis=1)[:, :1]


def pair_lanes(mat, pair):
    lane = lax.broadcasted_iota(jnp.int32, (mat.shape[0], 128), 1)
    return jnp.where(lane < HDIM, column_of(mat, 2 * pair), column_of(mat, 2 * pair + 1))


def load_params(rank, conv_t, conv_b, dt_bias, a_log, d_skip, wx, wbc, heads):
    lane = lax.broadcasted_iota(jnp.int32, (1, 128), 1)
    bias_row, log_row = jnp.zeros((1, 128), jnp.float32), jnp.zeros((1, 128), jnp.float32)
    wx[...] = jnp.zeros(wx.shape, jnp.float32)
    wbc[...] = jnp.zeros(wbc.shape, jnp.float32)
    heads[...] = jnp.zeros(heads.shape, jnp.float32)
    for d in range(wx.shape[1] // 128):
        cols, own = pl.ds(pl.multiple_of((d * 8 + rank) * 128, 128), 128), slice(d * 128, (d + 1) * 128)
        head = (d * 8 + rank) * 2
        wx[0:CONV, own] = conv_t[:, cols]
        wx[CONV : CONV + 1, own] = conv_b[:, cols]
        wx[CONV + 1 : CONV + 2, own] = jnp.where(lane < HDIM, d_skip[head], d_skip[head + 1])
        for half in range(2):
            bias_row = jnp.where(lane == 2 * d + half, dt_bias[head + half], bias_row)
            log_row = jnp.where(lane == 2 * d + half, a_log[head + half], log_row)
    wbc[0:CONV] = conv_t[:, DI:]
    wbc[CONV : CONV + 1] = conv_b[:, DI:]
    heads[0:1] = bias_row
    heads[1:2] = log_row


def head_mats(dt_all, heads, h_own, dt_mat, cum_mat, cum_rows):
    shifted, dt = step_sizes_of(dt_all, heads, h_own, 8, 2)
    rates = -jnp.exp(heads[1:2])
    across = jnp.transpose(dt * (rates * LOG2E))
    cum_t = lane_sums(across[:h_own], False)
    pad = jnp.zeros((128 - h_own, cum_t.shape[1]), jnp.float32)
    dt_mat[...] = dt
    cum_mat[...] = jnp.transpose(jnp.concatenate([cum_t, pad], axis=0))
    for k in range(h_own):
        cum_rows[k] = cum_t[k : k + 1, :]


def mask_rows(bias, seg_col, seg_row, source_first):
    length = bias.shape[0]
    for block in range(length // TILE):
        rows = slice(block * TILE, (block + 1) * TILE)
        down = lax.broadcasted_iota(jnp.int32, (TILE, length), 0) + block * TILE
        over = lax.broadcasted_iota(jnp.int32, (TILE, length), 1)
        past = down <= over if source_first else over <= down
        bias[rows] = jnp.where(past & (seg_col[rows] == seg_row), 0.0, FAR)


def convolve_bc(bc_ref, wbc, keep):
    out = []
    for part in range(2):
        lanes = slice(part * NST, (part + 1) * NST)
        _, _, values = conv_silu(
            bc_ref[:, lanes].astype(jnp.float32), wbc[0:CONV, lanes], wbc[CONV : CONV + 1, lanes], keep
        )
        out.append(values.astype(jnp.bfloat16))
    return out


def forward_prepare(h_own, bc_ref, dt_ref, seg_col, seg_row, wbc, heads, dt_mat, cum_mat, cum_rows, inner_prod, bias):
    length = bc_ref.shape[0]
    keep = keep_masks(seg_col)
    head_mats(dt_ref[...], heads[...], h_own, dt_mat, cum_mat, cum_rows)
    bc = convolve_bc(bc_ref, wbc, keep)
    inner_prod[...] = lax.dot_general(bc[1], bc[0], (((1,), (1,)), ((), ())), preferred_element_type=jnp.float32)
    mask_rows(bias, seg_col, seg_row, False)


def forward_pair(pair, x_ref, seg_col, wx_ref, y_ref, inner_ref, dt_mat, cum_mat, cum_rows, inner_prod, bias):
    length = x_ref.shape[0]
    keep = keep_masks(seg_col)
    _, _, xc = conv_silu(x_ref[...].astype(jnp.float32), wx_ref[0:CONV], wx_ref[CONV : CONV + 1], keep)
    moved = (xc * pair_lanes(dt_mat[...], pair)).astype(jnp.bfloat16)
    skip = wx_ref[CONV + 1 : CONV + 2]
    first = lax.broadcasted_iota(jnp.int32, (TILE, 128), 1) < HDIM
    cum = [column_of(cum_mat[...], 2 * pair + half) for half in range(2)]
    for block in range(length // TILE):
        rows, wide = slice(block * TILE, (block + 1) * TILE), (block + 1) * TILE
        halves = []
        for half in range(2):
            decay = jnp.exp2(cum[half][rows] - cum_rows[2 * pair + half, :, :wide] + bias[rows, :wide])
            scores = (inner_prod[rows, :wide] * decay).astype(jnp.bfloat16)
            halves.append(jnp.dot(scores, moved[:wide], preferred_element_type=jnp.float32))
        inner = jnp.where(first, halves[0], halves[1])
        inner_ref[rows] = inner
        y_ref[rows] = (inner + skip * xc[rows]).astype(jnp.bfloat16)


def ahead_kernel(hidden, cot, in_w, in_tail, out_w, seg, conv_t, conv_b, norm_gain, gate_gain, dt_bias, a_log, d_skip,
                 n_all, c_all, w_in, w_out, x_raw, bc_raw, dt_raw, inner, gated, d_y, d_z, seg_col, seg_row,
                 wx, wbc, heads, gain_back,
                 nrm, tok_v, w_in_v, w_out_v, z_v, y_v, dg, seg_all, dt_mat, cum_mat, cum_rows, inner_prod, bias,
                 sum_cols, sums,
                 n_send, n_recv, c_send, c_recv, wide_send, tail_send, wide_recv, tail_recv,
                 y_send, core_send, cross_send, block_recv, out_send, out_recv, seg_send, seg_recv, local, load,
                 sum_send, sum_recv):
    f32, bf16 = jnp.float32, jnp.bfloat16
    where = place()
    dp, s, z, x, x_peer, y_peer, core_peer = where
    peers = [(dp, (s + k) % 8) for k in range(1, 8)] + [(y_peer, s), (core_peer, s)]
    greet(peers)
    in_rows, rows = in_w.shape[0], out_w.shape[0]
    chan = w_out.shape[0]
    h_own = chan // HDIM
    tail = in_tail.shape[1]
    n_own, length, width = n_all.shape

    def block(d, shard, lo=0, size=None):
        size = w_in.shape[1] if size is None else size
        at = pl.multiple_of((d * 8 + shard) * in_rows, in_rows)
        return w_in.at[pl.ds(at, in_rows), pl.ds(lo, size)]

    def wide_src(piece, target):
        at = pl.multiple_of((piece * 8 + target) * rows, rows)
        return in_w.at[:, pl.ds(at, rows)]

    def push(k, _):
        target = (s + k) % 8
        remote(seg, seg_all.at[s], seg_send.at[k], seg_recv.at[s], (dp, target)).start()
        for piece in range(WIDE):
            remote(
                wide_src(piece, target), block(dp, s, piece * rows, rows), wide_send.at[k], wide_recv.at[s],
                (dp, target),
            ).start()
        remote(in_tail, block(dp, s, 2 * chan, tail), tail_send.at[k], tail_recv.at[s], (dp, target)).start()
        return 0

    lax.fori_loop(1, 8, push, 0)
    for q in range(n_own):
        h = hidden[q].astype(f32)
        inv = lax.rsqrt(jnp.mean(h * h, axis=-1, keepdims=True) + 1e-05)
        nrm[q] = (h * inv * norm_gain[...]).astype(bf16)
    tokens = TokenGather(nrm, n_all, n_send, n_recv, where)
    cots = TokenGather(cot, c_all, c_send, c_recv, where)
    tokens.start(0)
    own_copies = []
    for piece in range(WIDE):
        own_copies.append(pltpu.make_async_copy(wide_src(piece, s), block(dp, s, piece * rows, rows), local.at[piece]))
    own_copies.append(pltpu.make_async_copy(in_tail, block(dp, s, 2 * chan, tail), local.at[8]))
    token_copies, cot_copies = [], []
    out_copy = pltpu.make_async_copy(out_w, w_out.at[pl.ds(pl.multiple_of(dp * rows, rows), rows)], local.at[9])
    for q in range(n_own):
        token_copies.append(pltpu.make_async_copy(nrm.at[q], tokens.part(s, q), local.at[10 + q]))
        cot_copies.append(pltpu.make_async_copy(cot.at[q], cots.part(s, q), local.at[12 + q]))
    for copy in own_copies + token_copies + cot_copies + [out_copy]:
        copy.start()
    seg_all[s] = seg[...]
    for copy in own_copies:
        copy.wait()

    def spread(shard, k):
        there = block(dp, shard)
        remote(there, there, y_send.at[k], block_recv.at[dp, shard], (y_peer, s)).start()
        remote(there, there, core_send.at[k], block_recv.at[dp, shard], (core_peer, s)).start()

    spread(s, 0)
    load_params(s, conv_t, conv_b, dt_bias, a_log, d_skip, wx, wbc, heads)

    def wide_copy(source, k):
        there = block(dp, source, 0, 2 * chan)
        return remote(there, there, wide_send.at[k], wide_recv.at[source], (dp, x_peer))

    def tail_copy(source, k):
        there = block(dp, source, 2 * chan, tail)
        return remote(there, there, tail_send.at[k], tail_recv.at[source], (dp, x_peer))

    def forward(k, _):
        source = (s + 8 - k) % 8
        wide_copy(source, k).wait_recv()
        tail_copy(source, k).wait_recv()
        spread(source, k)
        return 0

    def cross(k, _):
        source = (s + 8 - k) % 8
        there = block(y_peer, source)
        copy = remote(there, there, cross_send.at[k], block_recv.at[y_peer, source], (core_peer, s))
        copy.wait_recv()
        copy.start()
        return 0

    def out_part(d):
        return w_out.at[pl.ds(pl.multiple_of(d * rows, rows), rows)]

    tokens.step(1, 0)
    tokens.start(1)
    lax.fori_loop(1, 4, forward, 0)
    tokens.step(2, 0)
    lax.fori_loop(4, 8, forward, 0)
    tokens.step(3, 0)
    tokens.step(1, 1)
    lax.fori_loop(0, 4, cross, 0)
    tokens.step(2, 1)
    lax.fori_loop(4, 8, cross, 0)
    tokens.step(3, 1)
    for q in range(n_own):
        cots.start(q)
    out_y = remote(out_w, out_part(dp), out_send.at[0], out_recv.at[dp], (y_peer, s))
    out_core = remote(out_w, out_part(dp), out_send.at[1], out_recv.at[dp], (core_peer, s))
    out_y.start()
    out_core.start()

    def arrive(k, _):
        source = (s + 8 - k) % 8
        for d in (core_peer, core_peer + y_peer - dp):
            there = block(d, source)
            remote(there, there, core_send.at[k], block_recv.at[d, source], (core_peer, s)).wait_recv()
        return 0

    lax.fori_loop(0, 8, arrive, 0)
    w_load = pltpu.make_async_copy(w_in, w_in_v, load.at[0])
    w_load.start()

    def segments_in(k, _):
        source = (s + 8 - k) % 8
        remote(seg, seg_all.at[source], seg_send.at[k], seg_recv.at[source], (dp, x_peer)).wait_recv()
        return 0

    lax.fori_loop(1, 8, segments_in, 0)
    lane = lax.broadcasted_iota(jnp.int32, (1, 128), 1)
    for q in range(n_own):
        pieces = [
            jnp.where(lane < 64, seg_all[2 * m, q : q + 1], pltpu.roll(seg_all[2 * m + 1, q : q + 1], 64, axis=1))
            for m in range(4)
        ]
        row = jnp.concatenate(pieces, axis=1)
        seg_row[q] = row
        seg_col[q] = jnp.transpose(jnp.broadcast_to(row, (128, length)))[:, :1]

    def project(q):
        at = slice(q * length, (q + 1) * length)
        half = chan // 2

        @pl.loop(0, 2)
        def gates(n):
            cols = pl.ds(pl.multiple_of(n * half, half), half)
            z_v[at, cols] = jnp.dot(tok_v[q], w_in_v[:, cols], preferred_element_type=f32)

        @pl.loop(0, 2)
        def values(n):
            cols = pl.ds(pl.multiple_of(n * half, half), half)
            from_cols = pl.ds(pl.multiple_of(chan + n * half, half), half)
            x_raw[at, cols] = jnp.dot(tok_v[q], w_in_v[:, from_cols], preferred_element_type=f32).astype(bf16)

        last = jnp.dot(tok_v[q], w_in_v[:, 2 * chan :], preferred_element_type=f32).astype(bf16)
        bc_raw[at] = last[:, : 2 * NST]
        dt_raw[at] = last[:, 2 * NST :]

    token_loads = [pltpu.make_async_copy(n_all.at[q], tok_v.at[q], load.at[1 + q]) for q in range(n_own)]
    for q in range(n_own):
        token_copies[q].wait()
        tokens.arrive_x(q)
        token_loads[q].start()
        if q == 0:
            w_load.wait()
        token_loads[q].wait()
        project(q)
        cots.step(1, q)

    for q in range(n_own):
        at = pl.ds(q * length, length)
        forward_prepare(
            h_own, bc_raw.at[at], dt_raw.at[at], seg_col[q], seg_row[q], wbc, heads,
            dt_mat, cum_mat, cum_rows, inner_prod, bias,
        )

        @pl.loop(0, chan // 128)
        def pairs(pair):
            cols = pl.ds(pl.multiple_of(pair * 128, 128), 128)
            forward_pair(
                pair, x_raw.at[at, cols], seg_col[q], wx.at[:, cols], y_v.at[at, cols], inner.at[at, cols],
                dt_mat, cum_mat, cum_rows, inner_prod, bias,
            )

            @pl.when(pair == 1)
            def hop():
                if q == 0:
                    cots.step(2, 0)
                else:
                    cots.step(3, 0)

            @pl.when(pair == 3)
            def hop_again():
                if q == 0:
                    cots.step(2, 1)
                else:
                    cots.step(3, 1)

    out_cross = remote(out_part(y_peer), out_part(y_peer), out_send.at[2], out_recv.at[y_peer], (core_peer, s))
    out_cross.wait_recv()
    out_cross.start()
    for d in (core_peer, core_peer + y_peer - dp):
        remote(out_part(d), out_part(d), out_send.at[0], out_recv.at[d], (core_peer, s)).wait_recv()
    out_copy.wait()
    out_load = pltpu.make_async_copy(w_out, w_out_v, load.at[3])
    out_load.start()
    gain = jnp.concatenate(
        [gate_gain[:, pl.ds(pl.multiple_of((d * 8 + s) * 128, 128), 128)] for d in range(chan // 128)], axis=1
    )
    lane_wide = lax.broadcasted_iota(jnp.int32, (TILE, 128), 1)

    def sum_copy(q, k):
        return remote(
            sums.at[q, s], sums.at[q, s], sum_send.at[q, k], sum_recv.at[q, s], (dp, (s + k) % 8)
        )

    cot_loads = [pltpu.make_async_copy(c_all.at[q], tok_v.at[q], load.at[4 + q]) for q in range(n_own)]
    for q in range(n_own):
        cot_copies[q].wait()
        cots.arrive_x(q)
        cot_loads[q].start()
        if q == 0:
            out_load.wait()
        cot_loads[q].wait()
        half = chan // 2

        @pl.loop(0, 2)
        def back(n):
            cols = pl.ds(pl.multiple_of(n * half, half), half)
            dg[q * length : (q + 1) * length, cols] = lax.dot_general(
                tok_v[q], w_out_v[cols], (((1,), (1,)), ((), ())), preferred_element_type=f32
            )

        @pl.loop(0, length // TILE)
        def reduce_rows(n):
            at = pl.ds(pl.multiple_of(q * length + n * TILE, TILE), TILE)
            zz = z_v[at]
            g = y_v[at].astype(f32) * (zz * jax.nn.sigmoid(zz))
            first = jnp.sum(g * g, axis=1, keepdims=True)
            second = jnp.sum(dg[at] * gain * g, axis=1, keepdims=True)
            sum_cols[pl.ds(pl.multiple_of(n * TILE, TILE), TILE)] = jnp.where(
                lane_wide == 0, first, jnp.where(lane_wide == 1, second, 0.0)
            )

        sums[q, s] = jnp.transpose(sum_cols[...])[:8]
        for k in range(1, 8):
            sum_copy(q, k).start()

    gain_back[...] = jnp.zeros(gain_back.shape, f32)
    for q in range(n_own):
        for k in range(1, 8):
            source = (s + 8 - k) % 8
            remote(
                sums.at[q, source], sums.at[q, source], sum_send.at[q, k], sum_recv.at[q, source], (dp, x_peer)
            ).wait_recv()
        total = sums[q, 0]
        for source in range(1, 8):
            total = total + sums[q, source]
        total = jnp.concatenate([total, jnp.zeros((120, length), f32)], axis=0)
        sum_cols[...] = jnp.transpose(total)

        @pl.loop(0, length // TILE)
        def gate_rows(n):
            at = pl.ds(pl.multiple_of(q * length + n * TILE, TILE), TILE)
            both = sum_cols[pl.ds(pl.multiple_of(n * TILE, TILE), TILE)]
            r = lax.rsqrt(both[:, 0:1] / DI + 1e-05)
            fall = (r * r * r) * (both[:, 1:2] / DI)
            zz = z_v[at]
            sig = jax.nn.sigmoid(zz)
            act = zz * sig
            yy = y_v[at].astype(f32)
            g = yy * act
            gr = g * r
            back = dg[at]
            d_g = r * (back * gain) - fall * g
            gated[at] = (gr * gain).astype(bf16)
            d_y[at] = (d_g * act).astype(bf16)
            d_z[at] = (d_g * yy * (sig * (1.0 + zz * (1.0 - sig)))).astype(bf16)
            gain_back[0:1] += jnp.sum(back * gr, axis=0, keepdims=True)

    for q in range(n_own):
        tokens.settle(q)
        cots.settle(q)
        for k in range(1, 8):
            sum_copy(q, k).wait_send()

    def settle(k, _):
        shard = (s + 8 - k) % 8
        there = block(dp, shard)
        remote(there, there, y_send.at[k], block_recv.at[dp, shard], (y_peer, s)).wait_send()
        remote(there, there, core_send.at[k], block_recv.at[dp, shard], (core_peer, s)).wait_send()
        remote(there, there, cross_send.at[k], block_recv.at[dp, shard], (core_peer, s)).wait_send()
        return 0

    lax.fori_loop(0, 8, settle, 0)

    def settle_push(k, _):
        source = (s + 8 - k) % 8
        remote(seg, seg_all.at[source], seg_send.at[k], seg_recv.at[source], (dp, x_peer)).wait_send()
        wide_copy(source, k).wait_send()
        tail_copy(source, k).wait_send()
        return 0

    lax.fori_loop(1, 8, settle_push, 0)
    out_y.wait_send()
    out_core.wait_send()
    out_cross.wait_send()


def run_ahead(hidden, cot, in_w, in_tail, out_w, seg, conv_t, conv_b, norm_gain, gate_gain, dt_bias, a_log, d_skip):
    f32, bf16 = jnp.float32, jnp.bfloat16
    n_own, span, width = hidden.shape
    in_rows, rows = in_w.shape[0], out_w.shape[0]
    chan, length = 4 * rows, 8 * span
    tokens, h_own = n_own * length, chan // HDIM
    columns = 2 * chan + in_tail.shape[1]
    sem, vmem = pltpu.SemaphoreType.DMA, pltpu.VMEM
    anywhere, inside = pl.BlockSpec(memory_space=pl.ANY), pl.BlockSpec(memory_space=vmem)
    scalars = pl.BlockSpec(memory_space=pltpu.SMEM)
    shape = jax.ShapeDtypeStruct
    return pl.pallas_call(
        ahead_kernel,
        in_specs=[inside] + [anywhere] * 4 + [inside] * 5 + [scalars] * 3,
        out_specs=[anywhere] * 4 + [inside] * 13,
        out_shape=[
            shape((n_own, length, width), bf16),
            shape((n_own, length, width), bf16),
            shape((32 * in_rows, columns), bf16),
            shape((chan, width), bf16),
            shape((tokens, chan), bf16),
            shape((tokens, 2 * NST), bf16),
            shape((tokens, 128), bf16),
            shape((tokens, chan), f32),
            shape((tokens, chan), bf16),
            shape((tokens, chan), bf16),
            shape((tokens, chan), bf16),
            shape((n_own, length, 1), f32),
            shape((n_own, 1, length), f32),
            shape((8, chan), f32),
            shape((8, 2 * NST), f32),
            shape((8, 128), f32),
            shape((8, chan), f32),
        ],
        scratch_shapes=[
            vmem((n_own, span, width), bf16),
            vmem((n_own, length, width), bf16),
            vmem((width, columns), bf16),
            vmem((chan, width), bf16),
            vmem((tokens, chan), f32),
            vmem((tokens, chan), bf16),
            vmem((tokens, chan), f32),
            vmem((8, 8, 128), f32),
            vmem((length, 128), f32),
            vmem((length, 128), f32),
            vmem((h_own, 1, length), f32),
            vmem((length, length), f32),
            vmem((length, length), f32),
            vmem((length, 128), f32),
            vmem((n_own, 8, 8, length), f32),
            sem((3, 4, 2)), sem((8, 2)), sem((3, 4, 2)), sem((8, 2)),
            sem((8,)), sem((8,)), sem((8,)), sem((8,)),
            sem((8,)), sem((8,)), sem((8,)), sem((4, 8)), sem((3,)), sem((4,)), sem((8,)), sem((8,)),
            sem((14,)), sem((6,)), sem((2, 8)), sem((2, 8)),
        ],
        compiler_params=pltpu.CompilerParams(collective_id=0, has_side_effects=True, vmem_limit_bytes=56 << 20),
        name="ahead",
    )(hidden, cot, in_w, in_tail, out_w, seg, conv_t, conv_b, norm_gain, gate_gain, dt_bias, a_log, d_skip)


def backward_prepare(h_own, bc_ref, dt_ref, seg_col, seg_row, wbc, heads, dt_mat, cum_mat, cum_rows, inner_prod, bias,
                     d_inner, d_cum, d_dt):
    length = bc_ref.shape[0]
    keep = keep_masks(seg_col)
    head_mats(dt_ref[...], heads[...], h_own, dt_mat, cum_mat, cum_rows)
    bc = convolve_bc(bc_ref, wbc, keep)
    inner_prod[...] = lax.dot_general(bc[0], bc[1], (((1,), (1,)), ((), ())), preferred_element_type=jnp.float32)
    mask_rows(bias, seg_col, seg_row, True)
    d_inner[...] = jnp.zeros((length, length), jnp.float32)
    d_cum[...] = jnp.zeros((length, 128), jnp.float32)
    d_dt[...] = jnp.zeros((length, 128), jnp.float32)


def backward_pair(pair, x_ref, seg_col, wx_ref, dy_ref, inner_ref, dx_ref, gx_ref, dt_mat, cum_mat, cum_rows,
                  inner_prod, bias, d_inner, d_cum, d_dt):
    f32, bf16 = jnp.float32, jnp.bfloat16
    length = x_ref.shape[0]
    keep = keep_masks(seg_col)
    x_in = x_ref[...].astype(f32)
    taps = wx_ref[0:CONV]
    total, gate, xc = conv_silu(x_in, taps, wx_ref[CONV : CONV + 1], keep)
    dt_wide = pair_lanes(dt_mat[...], pair)
    moved = (xc * dt_wide).astype(bf16)
    skip = wx_ref[CONV + 1 : CONV + 2]
    dy = dy_ref[...]
    first = lax.broadcasted_iota(jnp.int32, (TILE, 128), 1) < HDIM
    cum = [column_of(cum_mat[...], 2 * pair + half) for half in range(2)]
    pieces = []
    for block in range(length // TILE):
        rows, later = slice(block * TILE, (block + 1) * TILE), slice(block * TILE, length)
        halves = []
        for half in range(2):
            decay = jnp.exp2(cum_rows[2 * pair + half, :, later] - cum[half][rows] + bias[rows, later])
            scores = (inner_prod[rows, later] * decay).astype(bf16)
            halves.append(jnp.dot(scores, dy[later], preferred_element_type=f32))
            mine = jnp.where(first if half == 0 else ~first, moved[rows].astype(f32), 0.0).astype(bf16)
            d_scores = lax.dot_general(mine, dy[later], (((1,), (1,)), ((), ())), preferred_element_type=f32)
            d_inner[rows, later] += d_scores * decay
        pieces.append(jnp.where(first, halves[0], halves[1]))
    d_moved = jnp.concatenate(pieces, axis=0)
    dy_f = dy.astype(f32)
    change = dy_f * inner_ref[...] - moved.astype(f32) * d_moved
    direct = d_moved * xc
    lane = lax.broadcasted_iota(jnp.int32, (length, 128), 1)
    low = lane < HDIM
    for half in range(2):
        mine = low if half == 0 else ~low
        spot = lane == 2 * pair + half
        d_cum[...] += jnp.where(spot, jnp.sum(jnp.where(mine, change, 0.0), axis=1, keepdims=True), 0.0)
        d_dt[...] += jnp.where(spot, jnp.sum(jnp.where(mine, direct, 0.0), axis=1, keepdims=True), 0.0)
    d_xc = d_moved * dt_wide + skip * dy_f
    d_x, tap_rows, d_offset = conv_back(d_xc, total, gate, x_in, taps, keep)
    dx_ref[...] = d_x.astype(bf16)
    d_skip = jnp.sum(dy_f * xc, axis=0, keepdims=True)
    gx_ref[...] += jnp.concatenate(tap_rows + [d_offset, d_skip, jnp.zeros((2, 128), f32)], axis=0)


def backward_finish(h_own, bc_ref, dt_ref, seg_col, wbc, heads, d_inner, d_cum, d_dt, dbc_ref, ddt_ref, gbc_ref, gh_ref):
    f32, bf16 = jnp.float32, jnp.bfloat16
    length = bc_ref.shape[0]
    keep = keep_masks(seg_col)
    bc = convolve_bc(bc_ref, wbc, keep)
    d_in = d_inner[...].astype(bf16)
    for part in range(2):
        lanes = slice(part * NST, (part + 1) * NST)
        side = 1 - part
        d_value = lax.dot_general(d_in, bc[side], (((side,), (0,)), ((), ())), preferred_element_type=f32)
        bc_in = bc_ref[:, lanes].astype(f32)
        taps = wbc[0:CONV, lanes]
        total, gate, _ = conv_silu(bc_in, taps, wbc[CONV : CONV + 1, lanes], keep)
        d_bc, tap_rows, offset = conv_back(d_value, total, gate, bc_in, taps, keep)
        dbc_ref[:, lanes] = d_bc.astype(bf16)
        gbc_ref[:, lanes] += jnp.concatenate(tap_rows + [offset, jnp.zeros((3, NST), f32)], axis=0)
    shifted, dt = step_sizes_of(dt_ref[...], heads[...], h_own, 8, 2)
    rates = -jnp.exp(heads[1:2])
    across = jnp.transpose(d_cum[...])
    d_log_t = lane_sums(across[:h_own], True)
    d_log = jnp.transpose(jnp.concatenate([d_log_t, jnp.zeros((128 - h_own, length), f32)], axis=0))
    d_raw = (d_log * rates + d_dt[...]) * jax.nn.sigmoid(shifted)
    rank = lax.axis_index("seq")
    row = lax.broadcasted_iota(jnp.int32, (128, 128), 0)
    head = ((row // 2) * 8 + rank) * 2 + row % 2
    pick = ((lax.broadcasted_iota(jnp.int32, (128, 128), 1) == head) & (row < h_own)).astype(bf16)
    ddt_ref[...] = jnp.dot(d_raw.astype(bf16), pick, preferred_element_type=f32).astype(bf16)
    gh_ref[...] += jnp.concatenate(
        [
            jnp.sum(d_raw, axis=0, keepdims=True),
            jnp.sum(d_log * dt, axis=0, keepdims=True) * rates,
            jnp.zeros((6, 128), f32),
        ],
        axis=0,
    )


class TokenReduce:
    def __init__(self, part, from_x, from_near, from_far, x_sems, near_sems, far_sems, where, span):
        self.part, self.from_x, self.from_near, self.from_far = part, from_x, from_near, from_far
        self.x_sems, self.near_sems, self.far_sems, self.span = x_sems, near_sems, far_sems, span
        self.dp, self.s, self.z, self.x, self.x_peer, _, _ = where
        self.near = self.s + 2 - 4 * (self.z % 2)
        self.far = self.s + 4 - 8 * (self.z // 2)

    def rows(self, shard, q):
        return self.part.at[q, pl.ds(pl.multiple_of(shard * self.span, self.span), self.span)]

    def x_copy(self, shard_z, q):
        return remote(
            self.rows(shard_z * 2 + 1 - self.x, q), self.from_x.at[shard_z, q],
            self.x_sems.at[0, shard_z, q], self.x_sems.at[1, shard_z, q], (self.dp, self.x_peer),
        )

    def near_copy(self, high, q):
        shard = (high * 2 + 1 - self.z % 2) * 2 + self.x
        return remote(
            self.rows(shard, q), self.from_near.at[high, q],
            self.near_sems.at[0, high, q], self.near_sems.at[1, high, q], (self.dp, self.near),
        )

    def far_copy(self, q):
        shard = ((1 - self.z // 2) * 2 + self.z % 2) * 2 + self.x
        return remote(
            self.rows(shard, q), self.from_far.at[q], self.far_sems.at[0, q], self.far_sems.at[1, q],
            (self.dp, self.far),
        )

    def start(self, q):
        for high in range(2):
            for low in range(2):
                shard_z = (1 - self.z // 2 + high) % 2 * 2 + (1 - self.z % 2 + low) % 2
                self.x_copy(shard_z, q).start()

    def add(self, shard, q, other):
        rows = self.rows(shard, q)
        rows[...] = (rows[...].astype(jnp.float32) + other[...].astype(jnp.float32)).astype(jnp.bfloat16)

    def step_near(self, q):
        for turn in range(2):
            high = (1 - self.z // 2 + turn) % 2
            shard_z = high * 2 + 1 - self.z % 2
            self.x_copy(shard_z, q).wait_recv()
            self.add(shard_z * 2 + self.x, q, self.from_x.at[shard_z, q])
            self.near_copy(high, q).start()
        for turn in range(2):
            high = (1 - self.z // 2 + turn) % 2
            shard_z = high * 2 + self.z % 2
            self.x_copy(shard_z, q).wait_recv()
            self.add(shard_z * 2 + self.x, q, self.from_x.at[shard_z, q])

    def step_far(self, q):
        high = 1 - self.z // 2
        self.near_copy(high, q).wait_recv()
        self.add((high * 2 + self.z % 2) * 2 + self.x, q, self.from_near.at[high, q])
        self.far_copy(q).start()

    def total(self, q):
        high = self.z // 2
        self.near_copy(high, q).wait_recv()
        self.far_copy(q).wait_recv()
        f32 = jnp.float32
        return (
            self.rows(self.s, q)[...].astype(f32)
            + self.from_near[high, q].astype(f32)
            + self.from_far[q].astype(f32)
        )

    def settle(self):
        for q in range(2):
            for shard_z in range(4):
                self.x_copy(shard_z, q).wait_send()
            for high in range(2):
                self.near_copy(high, q).wait_send()
            self.far_copy(q).wait_send()


def finish_kernel(gated, w_out, d_z, d_y, x_raw, inner, w_in, cot_all, normed_all,
                  bc_raw, dt_raw, seg_col, seg_row, wx, wbc, heads, gain_back, hidden, cot, gain,
                  result, d_hidden, grad_in, grad_out, small_all, gain_sum,
                  gated_v, w_out_v, dp_v, w_in_v, tok_v, inner_v, dy_v,
                  dt_mat, cum_mat, cum_rows, inner_prod, bias, d_inner, d_cum, d_dt,
                  part_r, rx, rn, rf, part_d, dx, dn, df,
                  core_out, core_in, keep, y_in, plane_in,
                  out_core_in, out_y, out_y_in, small_v, small_in, gain_v, gain_in,
                  load, rxs, rns, rfs, dxs, dns, dfs, core_sems, y_sems, plane_sems, out_sems, out_y_sems,
                  small_sems, small_plane, gain_sems, gain_plane):
    f32, bf16 = jnp.float32, jnp.bfloat16
    where = place()
    dp, s, z, x, x_peer, y_peer, core_peer = where
    y, core = dp // 2, dp % 2
    n_own, span, width = hidden.shape
    length = 8 * span
    chan = w_out.shape[0]
    rows = chan // 4
    in_rows = grad_in.shape[0]
    columns = keep.shape[3]
    tail = columns - 2 * chan
    peers = [(dp, (s + k) % 8) for k in range(1, 8)] + [(y_peer, s), (core_peer, s)]
    h_own = chan // HDIM

    def scan_loads(q):
        at = pl.ds(q * length, length)
        return [
            pltpu.make_async_copy(inner.at[at], inner_v, load.at[3]),
            pltpu.make_async_copy(d_y.at[at], dy_v, load.at[4]),
        ]

    loads = [
        pltpu.make_async_copy(gated, gated_v, load.at[0]),
        pltpu.make_async_copy(w_out, w_out_v, load.at[1]),
        pltpu.make_async_copy(cot_all, tok_v, load.at[7]),
        pltpu.make_async_copy(w_in, w_in_v, load.at[6]),
        pltpu.make_async_copy(d_z, dp_v.at[:, pl.ds(0, chan)], load.at[5]),
        pltpu.make_async_copy(x_raw, dp_v.at[:, pl.ds(chan, chan)], load.at[2]),
    ]
    first_scan = scan_loads(0)
    for copy in loads[:3] + first_scan + loads[3:]:
        copy.start()
    greet(peers)
    small_v[0] = jnp.zeros(small_v.shape[1:], f32)

    def small_copy(stage, device):
        return remote(small_v.at[stage], small_in.at[stage], small_sems.at[0, stage], small_sems.at[1, stage], device)

    reduce_r = TokenReduce(part_r, rx, rn, rf, rxs, rns, rfs, where, span)
    reduce_d = TokenReduce(part_d, dx, dn, df, dxs, dns, dfs, where, span)
    loads[0].wait()
    loads[1].wait()
    step = 512
    for q in range(2):

        @pl.loop(0, width // 256)
        def forward(n):
            cols = pl.ds(pl.multiple_of(n * 256, 256), 256)
            part_r[q, :, cols] = jnp.dot(
                gated_v[q * length : (q + 1) * length], w_out_v[:, cols], preferred_element_type=f32
            ).astype(bf16)

        reduce_r.start(q)
    loads[2].wait()

    def out_term(d, n):
        lanes = pl.ds(pl.multiple_of(d * rows, rows), rows)
        return lax.dot_general(
            gated_v[:, lanes], tok_v[:, n * step : (n + 1) * step], (((0,), (0,)), ((), ())),
            preferred_element_type=f32,
        )

    def out_core_copy(yy):
        return remote(w_out_v.at[pl.ds(yy * rows, rows)], out_core_in.at[yy], out_sems.at[0, yy], out_sems.at[1, yy], (core_peer, s))

    for yy in range(2):
        for n in range(width // step):
            w_out_v[yy * rows : (yy + 1) * rows, n * step : (n + 1) * step] = out_term(yy * 2 + 1 - core, n).astype(bf16)
        out_core_copy(yy).start()
    for n in range(width // step):
        out_y[:, n * step : (n + 1) * step] = out_term((1 - y) * 2 + core, n).astype(bf16)
    for n in range(width // step):
        grad_out[:, n * step : (n + 1) * step] = out_term(y * 2 + core, n)
    norm_load = pltpu.make_async_copy(normed_all, tok_v, load.at[8])
    norm_load.start()
    out_y_copy = remote(out_y, out_y_in, out_y_sems.at[0], out_y_sems.at[1], (y_peer, s))
    for q in range(2):
        at = pl.ds(q * length, length)
        scan_in = first_scan if q == 0 else scan_loads(1)
        if q == 1:
            for copy in scan_in:
                copy.start()
        backward_prepare(
            h_own, bc_raw.at[at], dt_raw.at[at], seg_col[q], seg_row[q], wbc, heads,
            dt_mat, cum_mat, cum_rows, inner_prod, bias, d_inner, d_cum, d_dt,
        )
        for copy in scan_in:
            copy.wait()
        if q == 0:
            loads[5].wait()

        @pl.loop(0, chan // 128)
        def pairs(pair):
            cols = pl.ds(pl.multiple_of(pair * 128, 128), 128)
            x_cols = pl.ds(pl.multiple_of(chan + pair * 128, 128), 128)
            backward_pair(
                pair, dp_v.at[at, x_cols], seg_col[q], wx.at[:, cols], dy_v.at[:, cols], inner_v.at[:, cols],
                dp_v.at[at, x_cols], small_v.at[0, :, cols], dt_mat, cum_mat, cum_rows,
                inner_prod, bias, d_inner, d_cum, d_dt,
            )
            if q == 1:

                @pl.when(pair == 1)
                def forward_far():
                    reduce_r.step_far(0)

        backward_finish(
            h_own, bc_raw.at[at], dt_raw.at[at], seg_col[q], wbc, heads, d_inner, d_cum, d_dt,
            dp_v.at[at, pl.ds(2 * chan, 2 * NST)], dp_v.at[at, pl.ds(2 * chan + 2 * NST, 128)],
            small_v.at[0, :, pl.ds(chan, 2 * NST)], small_v.at[0, :, pl.ds(chan + 2 * NST, 128)],
        )
        if q == 0:
            loads[3].wait()
            loads[4].wait()

        @pl.loop(0, width // 256)
        def backward(n):
            cols = pl.ds(pl.multiple_of(n * 256, 256), 256)
            part_d[q, :, cols] = lax.dot_general(
                dp_v[q * length : (q + 1) * length], w_in_v[cols], (((1,), (1,)), ((), ())),
                preferred_element_type=f32,
            ).astype(bf16)

        reduce_d.start(q)
        if q == 0:
            reduce_r.step_near(0)
            out_core_copy(1 - y).wait_recv()
            out_y[...] = (out_y[...].astype(f32) + out_core_in[1 - y].astype(f32)).astype(bf16)
            out_y_copy.start()

    small_v[0, CONV + 2 : CONV + 3, :chan] = gain_back[0:1]
    small_core = small_copy(0, (core_peer, s))
    small_core.start()

    def small_push(k):
        return remote(
            small_all.at[s], small_all.at[s], small_plane.at[0, k], small_plane.at[1, s], (dp, (s + k) % 8)
        )

    norm_load.wait()

    def in_term(d, m, lo, size):
        lanes = pl.ds(pl.multiple_of(d * 8 * in_rows + m * 2 * in_rows, 2 * in_rows), 2 * in_rows)
        return lax.dot_general(
            tok_v[:, lanes], dp_v[:, lo : lo + size], (((0,), (0,)), ((), ())), preferred_element_type=f32
        )

    pieces = ((0, chan, chan), (chan, chan, chan), (2 * chan, tail, 2 * NST + 128))

    def core_copy(m, yy):
        return remote(core_out.at[m % 2, yy], core_in.at[m, yy], core_sems.at[0, m, yy], core_sems.at[1, m, yy], (core_peer, s))

    def y_copy(m):
        return remote(keep.at[m, 1 - y], y_in.at[m], y_sems.at[0, m], y_sems.at[1, m], (y_peer, s))

    def in_compute(m):
        for yy in range(2):
            if m >= 2:
                core_copy(m - 2, yy).wait_send()
            for lo, size, span_in in pieces:
                core_out[m % 2, yy, :, lo : lo + size] = in_term(yy * 2 + 1 - core, m, lo, span_in)[:, :size].astype(bf16)
            core_copy(m, yy).start()
        for yy in range(2):
            for lo, size, span_in in pieces:
                keep[m, yy, :, lo : lo + size] = in_term(yy * 2 + core, m, lo, span_in)[:, :size].astype(bf16)

    def in_core(m):
        for yy in range(2):
            core_copy(m, yy).wait_recv()
            keep[m, yy] = (keep[m, yy].astype(f32) + core_in[m, yy].astype(f32)).astype(bf16)
        y_copy(m).start()

    def plane_copy(m, half):
        target = 2 * m + half
        return remote(
            keep.at[m, y, pl.ds(half * in_rows, in_rows)], plane_in.at[s],
            plane_sems.at[0, target], plane_sems.at[1, s], (dp, target),
        )

    def in_plane(m):
        y_copy(m).wait_recv()
        keep[m, y] = (keep[m, y].astype(f32) + y_in[m].astype(f32)).astype(bf16)
        for half in range(2):

            @pl.when(s != 2 * m + half)
            def away():
                plane_copy(m, half).start()

            @pl.when(s == 2 * m + half)
            def here():
                plane_in[s] = keep[m, y, half * in_rows : (half + 1) * in_rows]

    in_compute(0)
    small_core.wait_recv()
    small_v[1] = small_v[0] + small_in[0]
    small_y = small_copy(1, (y_peer, s))
    small_y.start()
    in_compute(1)
    in_core(0)
    reduce_r.step_near(1)
    in_compute(2)
    in_core(1)
    small_y.wait_recv()
    small_all[s] = small_v[1] + small_in[1]
    for k in range(1, 8):
        small_push(k).start()
    in_plane(0)
    in_compute(3)
    in_core(2)
    in_core(3)
    reduce_r.step_far(1)
    in_plane(1)
    reduce_d.step_near(0)
    in_plane(2)
    for q in range(2):
        result[q] = (hidden[q].astype(f32) + reduce_r.total(q)).astype(bf16)
    in_plane(3)
    reduce_d.step_far(0)
    out_y_copy.wait_recv()
    out_core_copy(y).wait_recv()
    grad_out[...] = grad_out[...] + out_core_in[y].astype(f32) + out_y_in[...].astype(f32)
    reduce_d.step_near(1)
    reduce_d.step_far(1)
    gain_row = gain[...]
    gain_part = None
    for q in range(2):
        d_normed = reduce_d.total(q)
        h = hidden[q].astype(f32)
        inv = lax.rsqrt(jnp.mean(h * h, axis=-1, keepdims=True) + 1e-05)
        scaled = d_normed * gain_row
        along = jnp.mean(scaled * h, axis=-1, keepdims=True)
        d_hidden[q] = (cot[q].astype(f32) + inv * scaled - (inv * inv * inv) * along * h).astype(bf16)
        term = jnp.sum(d_normed * h * inv, axis=0, keepdims=True)
        gain_part = term if q == 0 else gain_part + term
    folded = width // 8
    gain_v[0] = jnp.concatenate([gain_part[:, k * folded : (k + 1) * folded] for k in range(8)], axis=0)

    def gain_copy(stage, device):
        return remote(gain_v.at[stage], gain_in.at[stage], gain_sems.at[0, stage], gain_sems.at[1, stage], device)

    gain_core = gain_copy(0, (core_peer, s))
    gain_core.start()
    for k in range(1, 8):
        source = (s + 8 - k) % 8
        remote(plane_in.at[source], plane_in.at[source], plane_sems.at[0, source], plane_sems.at[1, source], (dp, x_peer)).wait_recv()
    gain_core.wait_recv()
    gain_v[1] = gain_v[0] + gain_in[0]
    gain_y = gain_copy(1, (y_peer, s))
    gain_y.start()
    tail_sum = None
    for source in range(8):
        for piece in range(WIDE):
            at = (piece * 8 + source) * rows
            grad_in[:, at : at + rows] = plane_in[source, :, piece * rows : (piece + 1) * rows].astype(f32)
        term = plane_in[source, :, 2 * chan :].astype(f32)
        tail_sum = term if source == 0 else tail_sum + term
    grad_in[:, 2 * DI :] = tail_sum
    gain_y.wait_recv()
    gain_v[2 + s] = gain_v[1] + gain_in[1]

    def gain_push(k):
        return remote(gain_v.at[2 + s], gain_v.at[2 + s], gain_plane.at[0, k], gain_plane.at[1, s], (dp, (s + k) % 8))

    for k in range(1, 8):
        gain_push(k).start()
    reduce_r.settle()
    reduce_d.settle()
    small_core.wait_send()
    small_y.wait_send()
    out_y_copy.wait_send()
    for yy in range(2):
        out_core_copy(yy).wait_send()
    for m in range(4):
        for yy in range(2 if m >= 2 else 0):
            core_copy(m, yy).wait_send()
        y_copy(m).wait_send()
        for half in range(2):

            @pl.when(s != 2 * m + half)
            def sent():
                plane_copy(m, half).wait_send()

    for k in range(1, 8):
        source = (s + 8 - k) % 8
        remote(
            small_all.at[source], small_all.at[source], small_plane.at[0, k], small_plane.at[1, source], (dp, x_peer)
        ).wait_recv()
        small_push(k).wait_send()
        remote(
            gain_v.at[2 + source], gain_v.at[2 + source], gain_plane.at[0, k], gain_plane.at[1, source], (dp, x_peer)
        ).wait_recv()
        gain_push(k).wait_send()
    gain_core.wait_send()
    gain_y.wait_send()
    gain_total = gain_v[2]
    for source in range(1, 8):
        gain_total = gain_total + gain_v[2 + source]
    gain_sum[...] = gain_total


def run_finish(gated, w_out, d_z, d_y, x_raw, inner, w_in, cot_all, normed_all,
               bc_raw, dt_raw, seg_col, seg_row, wx, wbc, heads, gain_back, hidden, cot, gain, in_rows):
    f32, bf16 = jnp.float32, jnp.bfloat16
    n_own, span, width = hidden.shape
    tokens, chan = gated.shape
    length, rows = 8 * span, chan // 4
    columns = 2 * chan + 2 * NST + HEADS
    small = (8, chan + 2 * NST + 128)
    vmem = pltpu.VMEM
    anywhere, inside = pl.BlockSpec(memory_space=pl.ANY), pl.BlockSpec(memory_space=vmem)
    sem = pltpu.SemaphoreType.DMA
    tokens_like = [
        vmem((n_own, length, width), bf16), vmem((4, n_own, span, width), bf16),
        vmem((2, n_own, span, width), bf16), vmem((n_own, span, width), bf16),
    ]
    return pl.pallas_call(
        finish_kernel,
        in_specs=[anywhere] * 9 + [inside] * 11,
        out_specs=[inside] * 6,
        out_shape=[
            jax.ShapeDtypeStruct(hidden.shape, bf16),
            jax.ShapeDtypeStruct(hidden.shape, bf16),
            jax.ShapeDtypeStruct((in_rows, 2 * DI + columns - 2 * chan), f32),
            jax.ShapeDtypeStruct((rows, width), f32),
            jax.ShapeDtypeStruct((8,) + small, f32),
            jax.ShapeDtypeStruct((8, width // 8), f32),
        ],
        scratch_shapes=[
            vmem((tokens, chan), bf16), vmem((chan, width), bf16),
            vmem((tokens, 2 * chan + 2 * NST + 128), bf16), vmem((width, 2 * chan + 2 * NST + 128), bf16),
            vmem((tokens, width), bf16),
            vmem((length, chan), f32), vmem((length, chan), bf16),
            vmem((length, 128), f32), vmem((length, 128), f32), vmem((chan // HDIM, 1, length), f32),
            vmem((length, length), f32), vmem((length, length), f32), vmem((length, length), f32),
            vmem((length, 128), f32), vmem((length, 128), f32),
        ]
        + tokens_like + tokens_like
        + [
            vmem((2, 2, 2 * in_rows, columns), bf16), vmem((4, 2, 2 * in_rows, columns), bf16),
            vmem((4, 2, 2 * in_rows, columns), bf16), vmem((4, 2 * in_rows, columns), bf16),
            vmem((8, in_rows, columns), bf16),
            vmem((2, rows, width), bf16),
            vmem((rows, width), bf16), vmem((rows, width), bf16),
            vmem((2,) + small, f32), vmem((2,) + small, f32),
            vmem((10, 8, width // 8), f32), vmem((2, 8, width // 8), f32),
            sem((9,)), sem((2, 4, 2)), sem((2, 2, 2)), sem((2, 2)), sem((2, 4, 2)), sem((2, 2, 2)), sem((2, 2)),
            sem((2, 4, 2)), sem((2, 4)), sem((2, 8)), sem((2, 2)), sem((2,)),
            sem((2, 2)), sem((2, 8)), sem((2, 2)), sem((2, 8)),
        ],
        compiler_params=pltpu.CompilerParams(
            collective_id=1, has_side_effects=True, vmem_limit_bytes=63 << 20
        ),
        name="finish",
    )(
        gated, w_out, d_z, d_y, x_raw, inner, w_in, cot_all, normed_all,
        bc_raw, dt_raw, seg_col, seg_row, wx, wbc, heads, gain_back, hidden, cot, gain,
    )


def head_plan(
    hidden,
    segments,
    in_weight,
    conv_weight,
    conv_bias,
    dt_bias,
    a_log,
    d_skip,
    norm_gain,
    gate_gain,
    out_weight,
    cotangent,
):
    f32, bf16 = jnp.float32, jnp.bfloat16
    n_dp, n_seq = lax.axis_size("dp"), lax.axis_size("seq")
    seq_rank = lax.axis_index("seq")
    n_own, shard_len, width = hidden.shape
    length = shard_len * n_seq
    rows = out_weight.shape[0]
    in_rows = in_weight.shape[0]
    chan = rows * n_dp
    h_own = chan // HDIM
    seg_tile = jnp.pad(segments.astype(f32), ((0, 8 - n_own), (0, 128 - shard_len)))
    in_tail = jnp.pad(in_weight[:, 2 * DI :], ((0, 0), (0, 128 - HEADS)))
    (n_all, cot_all, w_in, w_out, x_raw, bc_raw, dt_raw, inner, gated, d_y, d_z, seg_col, seg_row, wx, wbc, head_vals,
     gain_back) = run_ahead(
        hidden, cotangent, in_weight, in_tail, out_weight, seg_tile, conv_weight.T, conv_bias[None],
        norm_gain[None], gate_gain[None], dt_bias, a_log, d_skip,
    )
    normed_all = n_all.reshape(n_own * length, width)
    cot_all = cot_all.reshape(n_own * length, width)
    result, d_hidden, grad_in, grad_out, small_all, gain_sum = run_finish(
        gated, w_out, d_z, d_y, x_raw, inner, w_in, cot_all, normed_all,
        bc_raw, dt_raw, seg_col, seg_row, wx, wbc, head_vals, gain_back, hidden, cotangent, norm_gain[None], in_rows,
    )
    heads_row = rows // HDIM
    over_chan = small_all[:, :, :chan].reshape(n_seq, 8, n_dp, rows)
    over_chan = over_chan.transpose(1, 2, 0, 3).reshape(8, DI)
    over_bc = jnp.sum(small_all[:, :, chan : chan + 2 * NST], axis=0)
    over_head = small_all[:, :2, chan + 2 * NST : chan + 2 * NST + h_own]
    over_head = over_head.reshape(n_seq, 2, n_dp, heads_row).transpose(1, 2, 0, 3).reshape(2, HEADS)
    grad_skip = jnp.sum(over_chan[CONV + 1].reshape(HEADS, HDIM), axis=1)
    return (
        result,
        d_hidden,
        grad_in,
        jnp.concatenate([over_chan[:CONV], over_bc[:CONV]], axis=1).T,
        jnp.concatenate([over_chan[CONV], over_bc[CONV]], axis=0),
        over_head[0],
        over_head[1],
        grad_skip,
        gain_sum.reshape(width),
        over_chan[CONV + 2],
        grad_out,
    )


def solution(mesh):
    whole_heads = mesh.shape["dp"] == 4 and mesh.shape["seq"] == 8
    shards = head_plan if whole_heads else general_plan
    placed = (
        P("dp", "seq", None),
        P("dp", "seq"),
        P(("dp", "seq"), None),
        P(),
        P(),
        P(),
        P(),
        P(),
        P(),
        P(),
        P(("dp", "seq"), None),
        P("dp", "seq", None),
    )
    return jax.shard_map(
        shards,
        mesh=mesh,
        in_specs=placed,
        out_specs=(
            P("dp", "seq", None),
            P("dp", "seq", None),
            P(("dp", "seq"), None),
            P(),
            P(),
            P(),
            P(),
            P(),
            P(),
            P(),
            P(("dp", "seq"), None),
        ),
        check_vma=False,
    )
```

```python
import functools

import jax
import jax.numpy as jnp
from jax import lax
from jax.experimental import pallas as pl
from jax.experimental.pallas import tpu as pltpu
from jax.sharding import PartitionSpec as P

HEADS = 64
HDIM = 64
NST = 128
GROUP = 256
CONV = 4
DI = 4096


def pre_norm(hidden_f, gain_vec):
    return (
        hidden_f
        * lax.rsqrt(jnp.mean(hidden_f * hidden_f, axis=-1, keepdims=True) + 1e-05)
        * gain_vec
    )


def gate_norm(y_values, gate_values, gain_vec):
    product = y_values * jax.nn.silu(gate_values)
    return (
        product * lax.rsqrt(jnp.mean(product * product, axis=-1, keepdims=True) + 1e-05) * gain_vec
    )


def conv_reset(signal, kernel, offset, seg_ids):
    tap_count = kernel.shape[1]
    summed = offset[None, :] + kernel[None, :, tap_count - 1] * signal
    for lag_steps in range(1, tap_count):
        shifted = jnp.pad(signal, ((lag_steps, 0), (0, 0)))[:-lag_steps]
        earlier = jnp.pad(seg_ids, (lag_steps, 0), constant_values=-1)[:-lag_steps]
        matches = (earlier == seg_ids).astype(jnp.float32)
        summed = summed + kernel[None, :, tap_count - 1 - lag_steps] * shifted * matches[:, None]
    return summed


def state_scan(values, deltas, rates, b_mat, c_mat, seg_ids):
    length, head_count, head_width = values.shape
    block_count = length // GROUP
    log_decay = deltas * rates[None, :]
    pieces = (
        values.reshape(block_count, GROUP, head_count, head_width),
        deltas.reshape(block_count, GROUP, head_count),
        log_decay.reshape(block_count, GROUP, head_count),
        b_mat.reshape(block_count, GROUP, b_mat.shape[-1]),
        c_mat.reshape(block_count, GROUP, c_mat.shape[-1]),
        seg_ids.reshape(block_count, GROUP),
    )
    position = lax.broadcasted_iota(jnp.int32, (GROUP, GROUP), 0)
    source = lax.broadcasted_iota(jnp.int32, (GROUP, GROUP), 1)

    def advance(carry, piece):
        memory, ending = carry
        block_vals, block_dt, block_log, b_block, c_block, seg_block = piece
        cumulative = jnp.cumsum(block_log, axis=0).T
        causal = (source <= position) & (seg_block[:, None] == seg_block[None, :])
        spread = cumulative[:, :, None] - cumulative[:, None, :]
        decays = jnp.where(causal[None], jnp.exp(jnp.where(causal[None], spread, 0.0)), 0.0)
        inner_prod = jnp.dot(c_block, b_block.T, precision=lax.Precision.HIGHEST)
        scores = inner_prod[None] * decays * block_dt.T[:, None, :]
        output = jnp.einsum("hij,jhp->ihp", scores, block_vals, precision=lax.Precision.HIGHEST)
        follows = (seg_block == ending).astype(jnp.float32)
        carried = jnp.einsum("in,hpn->ihp", c_block, memory, precision=lax.Precision.HIGHEST)
        output = output + (jnp.exp(cumulative).T * follows[:, None])[:, :, None] * carried
        last_seg = seg_block[-1]
        weights = (
            jnp.exp(cumulative[:, -1:] - cumulative)
            * (seg_block == last_seg).astype(jnp.float32)[None, :]
            * block_dt.T
        )
        keep_on = jnp.exp(cumulative[:, -1]) * (last_seg == ending).astype(jnp.float32)
        memory = memory * keep_on[:, None, None] + jnp.einsum(
            "hj,jhp,jn->hpn", weights, block_vals, b_block, precision=lax.Precision.HIGHEST
        )
        return ((memory, last_seg), output)

    initial = (
        jnp.zeros((head_count, head_width, b_mat.shape[-1]), jnp.float32),
        jnp.array(-1, jnp.int32),
    )
    unused, outputs = lax.scan(jax.checkpoint(advance), initial, pieces)
    return outputs.reshape(length, head_count, head_width)


def mixer(
    x_values,
    step_raw,
    bc_values,
    seg_ids,
    kernel_x,
    offset_x,
    kernel_bc,
    offset_bc,
    dt_shift,
    decay_log,
    skip_gain,
):
    x_conv = jax.nn.silu(conv_reset(x_values, kernel_x, offset_x, seg_ids))
    bc_conv = jax.nn.silu(conv_reset(bc_values, kernel_bc, offset_bc, seg_ids))
    step_sizes = jax.nn.softplus(step_raw + dt_shift[None, :])
    rates = -jnp.exp(decay_log)
    length = x_values.shape[0]
    head_count = step_raw.shape[1]
    shaped = x_conv.reshape(length, head_count, HDIM)
    mixed = (
        state_scan(shaped, step_sizes, rates, bc_conv[:, :NST], bc_conv[:, NST:], seg_ids)
        + skip_gain[None, :, None] * shaped
    )
    return mixed.reshape(length, head_count * HDIM)


def general_plan(
    hidden,
    segments,
    in_weight,
    conv_weight,
    conv_bias,
    dt_bias,
    a_log,
    d_skip,
    norm_gain,
    gate_gain,
    out_weight,
    cotangent,
):
    full_in, full_out = (
        lax.all_gather(in_weight, ("dp", "seq"), axis=0, tiled=True),
        lax.all_gather(out_weight, ("dp", "seq"), axis=0, tiled=True),
    )
    hidden_f = hidden.astype(jnp.float32)
    normed_f, pull_pre = jax.vjp(pre_norm, hidden_f, norm_gain)
    normed = normed_f.astype(jnp.bfloat16)
    project = jnp.einsum("mtd,df->mtf", normed, full_in, preferred_element_type=jnp.float32)
    gate_part = project[:, :, :DI]
    x_part = project[:, :, DI : 2 * DI].astype(jnp.bfloat16)
    bc_part = project[:, :, 2 * DI : 2 * DI + 2 * NST].astype(jnp.bfloat16)
    step_part = project[:, :, 2 * DI + 2 * NST :].astype(jnp.bfloat16)
    x_heads, step_heads = (
        lax.all_to_all(x_part, "seq", split_axis=2, concat_axis=1, tiled=True),
        lax.all_to_all(step_part, "seq", split_axis=2, concat_axis=1, tiled=True),
    )
    bc_full = lax.all_gather(bc_part, "seq", axis=1, tiled=True)
    seg_full = lax.all_gather(segments, "seq", axis=1, tiled=True)
    seq_rank = lax.axis_index("seq")
    head_local = step_heads.shape[2]
    chan_local = x_heads.shape[2]
    kernel_x = lax.dynamic_slice_in_dim(conv_weight, seq_rank * chan_local, chan_local, 0)
    offset_x = lax.dynamic_slice_in_dim(conv_bias, seq_rank * chan_local, chan_local, 0)
    shift_local = lax.dynamic_slice_in_dim(dt_bias, seq_rank * head_local, head_local, 0)
    decay_local = lax.dynamic_slice_in_dim(a_log, seq_rank * head_local, head_local, 0)
    skip_local = lax.dynamic_slice_in_dim(d_skip, seq_rank * head_local, head_local, 0)
    local_params = (
        kernel_x,
        offset_x,
        conv_weight[DI:],
        conv_bias[DI:],
        shift_local,
        decay_local,
        skip_local,
    )

    def head_mixer(x_values, step_raw, bc_values, params_in):

        def single_seq(x_one, step_one, bc_one, seg_one):
            return mixer(x_one, step_one, bc_one, seg_one, *params_in)

        return jax.vmap(single_seq)(x_values, step_raw, bc_values, seg_full)

    mixed, pull_mix = jax.vjp(
        head_mixer,
        x_heads.astype(jnp.float32),
        step_heads.astype(jnp.float32),
        bc_full.astype(jnp.float32),
        local_params,
    )
    y_tokens = lax.all_to_all(
        mixed.astype(jnp.bfloat16), "seq", split_axis=1, concat_axis=2, tiled=True
    )
    gated_f, pull_gate = jax.vjp(gate_norm, y_tokens.astype(jnp.float32), gate_part, gate_gain)
    gated = gated_f.astype(jnp.bfloat16)
    branch_out = jnp.einsum("mtf,fd->mtd", gated, full_out, preferred_element_type=jnp.float32)
    result = (hidden_f + branch_out).astype(jnp.bfloat16)
    d_gated = jnp.einsum("mtd,fd->mtf", cotangent, full_out, preferred_element_type=jnp.float32)
    d_mixed, d_gate_part, d_gate_gain = pull_gate(d_gated)
    d_heads = lax.all_to_all(
        d_mixed.astype(jnp.bfloat16), "seq", split_axis=2, concat_axis=1, tiled=True
    )
    d_x_heads, d_step_heads, d_bc_full, d_params = pull_mix(d_heads.astype(jnp.float32))
    d_x_part, d_step_part = (
        lax.all_to_all(
            d_x_heads.astype(jnp.bfloat16), "seq", split_axis=1, concat_axis=2, tiled=True
        ),
        lax.all_to_all(
            d_step_heads.astype(jnp.bfloat16), "seq", split_axis=1, concat_axis=2, tiled=True
        ),
    )
    d_bc_part = lax.psum_scatter(
        d_bc_full.astype(jnp.bfloat16), "seq", scatter_dimension=1, tiled=True
    )
    d_project = jnp.concatenate(
        [d_gate_part.astype(jnp.bfloat16), d_x_part, d_bc_part, d_step_part], axis=2
    )
    d_normed = jnp.einsum("mtf,df->mtd", d_project, full_in, preferred_element_type=jnp.float32)
    d_hidden_f, d_norm_gain = pull_pre(d_normed)
    d_hidden = (cotangent.astype(jnp.float32) + d_hidden_f).astype(jnp.bfloat16)
    in_rows = in_weight.shape[0]
    out_rows = out_weight.shape[0]
    column_ranges = ((0, DI), (DI, d_project.shape[2]))
    in_pieces = [jnp.zeros((in_rows, upper - lower), jnp.float32) for lower, upper in column_ranges]
    grad_out = jnp.zeros(out_weight.shape, jnp.float32)
    for batch_index in range(hidden.shape[0]):
        for range_index in range(len(column_ranges)):
            lower, upper = column_ranges[range_index]

            def in_term(
                start,
                count,
                normed_one=normed[batch_index],
                d_one=d_project[batch_index, :, lower:upper],
            ):
                return lax.dot_general(
                    normed_one, d_one, (((0,), (0,)), ((), ())), preferred_element_type=jnp.float32
                )

            in_pieces[range_index] = in_pieces[range_index] + lax.psum_scatter(
                in_term(jnp.int32(0), in_rows * lax.axis_size(("dp", "seq"))),
                ("dp", "seq"),
                scatter_dimension=0,
                tiled=True,
            )

        def out_term(start, count, gated_one=gated[batch_index], cot_one=cotangent[batch_index]):
            return lax.dot_general(
                gated_one, cot_one, (((0,), (0,)), ((), ())), preferred_element_type=jnp.float32
            )

        grad_out = grad_out + lax.psum_scatter(
            out_term(jnp.int32(0), out_rows * lax.axis_size(("dp", "seq"))),
            ("dp", "seq"),
            scatter_dimension=0,
            tiled=True,
        )
    grad_in = jnp.concatenate(in_pieces, axis=1)
    d_kernel_x, d_offset_x, d_kernel_bc, d_offset_bc, d_shift, d_decay, d_skip_part = d_params
    tap_count = conv_weight.shape[1]
    grad_conv_w = jnp.concatenate(
        [
            lax.dynamic_update_slice_in_dim(
                jnp.zeros((DI, tap_count), jnp.float32), d_kernel_x, seq_rank * chan_local, 0
            ),
            d_kernel_bc,
        ],
        axis=0,
    )
    grad_conv_b = jnp.concatenate(
        [
            lax.dynamic_update_slice_in_dim(
                jnp.zeros((DI,), jnp.float32), d_offset_x, seq_rank * chan_local, 0
            ),
            d_offset_bc,
        ],
        axis=0,
    )
    grad_shift = lax.dynamic_update_slice_in_dim(
        jnp.zeros((HEADS,), jnp.float32), d_shift, seq_rank * head_local, 0
    )
    grad_decay = lax.dynamic_update_slice_in_dim(
        jnp.zeros((HEADS,), jnp.float32), d_decay, seq_rank * head_local, 0
    )
    grad_skip = lax.dynamic_update_slice_in_dim(
        jnp.zeros((HEADS,), jnp.float32), d_skip_part, seq_rank * head_local, 0
    )
    totals = lax.psum(
        (grad_conv_w, grad_conv_b, grad_shift, grad_decay, grad_skip, d_norm_gain, d_gate_gain),
        ("dp", "seq"),
    )
    return (
        result,
        d_hidden,
        grad_in,
        totals[0],
        totals[1],
        totals[2],
        totals[3],
        totals[4],
        totals[5],
        totals[6],
        grad_out,
    )


LOG2E = 1.4426950408889634
TILE = 128
FAR = -1e30


def shift_rows(v, lag):
    return v if lag == 0 else pltpu.roll(v, lag % v.shape[0], axis=0)


def conv_silu(sig, taps, offset, keep):
    total = offset + taps[CONV - 1 : CONV] * sig
    for lag in range(1, CONV):
        total = total + taps[CONV - 1 - lag : CONV - lag] * (shift_rows(sig, lag) * keep[lag])
    gate = jax.nn.sigmoid(total)
    return total, gate, total * gate


def conv_back(d_out, total, gate, sig, taps, keep):
    d_total = d_out * (gate * (1.0 + total * (1.0 - gate)))
    d_sig = taps[CONV - 1 : CONV] * d_total
    tap_rows = [jnp.sum(d_total * sig, axis=0, keepdims=True)]
    for lag in range(1, CONV):
        kept = d_total * keep[lag]
        d_sig = d_sig + taps[CONV - 1 - lag : CONV - lag] * shift_rows(kept, -lag)
        tap_rows.append(jnp.sum(kept * shift_rows(sig, lag), axis=0, keepdims=True))
    return d_sig, tap_rows[::-1], jnp.sum(d_total, axis=0, keepdims=True)


def keep_masks(seg_col):
    length = seg_col.shape[0]
    row = lax.broadcasted_iota(jnp.int32, (length, 1), 0)
    masks = [None]
    for lag in range(1, CONV):
        same = (pltpu.roll(seg_col, lag, axis=0) == seg_col) & (row >= lag)
        masks.append(same.astype(jnp.float32))
    return masks


def lane_sums(v, reverse):
    length = v.shape[1]
    lane = lax.broadcasted_iota(jnp.int32, v.shape, 1)
    step = 1
    while step < length:
        if reverse:
            v = v + jnp.where(lane < length - step, pltpu.roll(v, length - step, axis=1), 0.0)
        else:
            v = v + jnp.where(lane >= step, pltpu.roll(v, step, axis=1), 0.0)
        step *= 2
    return v


def step_sizes_of(dt_all, head_rows, h_own, n_seq, heads_row):
    rank = lax.axis_index("seq")
    all_heads = dt_all.shape[1]
    lane = lax.broadcasted_iota(jnp.int32, (all_heads, 128), 1)
    row = lax.broadcasted_iota(jnp.int32, (all_heads, 128), 0)
    head = ((lane // heads_row) * n_seq + rank) * heads_row + lane % heads_row
    pick = ((row == head) & (lane < h_own)).astype(jnp.bfloat16)
    raw = jnp.dot(dt_all, pick, preferred_element_type=jnp.float32)
    shifted = raw + head_rows[0:1]
    dt = jnp.maximum(shifted, 0.0) + jnp.log1p(jnp.exp(-jnp.abs(shifted)))
    return shifted, dt


MESH = pl.DeviceIdType.MESH
WIDE = 8


def place():
    dp, s = lax.axis_index("dp"), lax.axis_index("seq")
    z, x = s // 2, s % 2
    y, core = dp // 2, dp % 2
    return dp, s, z, x, s + 1 - 2 * x, dp + 2 - 4 * y, dp + 1 - 2 * core


def greet(peers):
    barrier = pltpu.get_barrier_semaphore()
    for device in peers:
        pl.semaphore_signal(barrier, inc=1, device_id=device, device_id_type=MESH)


def greeted(peers):
    pl.semaphore_wait(pltpu.get_barrier_semaphore(), len(peers))


def remote(src, dst, send, recv, device):
    return pltpu.make_async_remote_copy(
        src_ref=src, dst_ref=dst, send_sem=send, recv_sem=recv, device_id=device, device_id_type=MESH
    )


class TokenGather:
    def __init__(self, full, send, recv, where):
        self.full, self.send, self.recv = full, send, recv
        self.dp, self.s, self.z, self.x, self.x_peer, _, _ = where
        self.span = full.shape[1] // 8

    def part(self, shard, q):
        return self.full.at[q, pl.ds(pl.multiple_of(shard * self.span, self.span), self.span)]

    def copy(self, shard_z, way, q):
        shard = shard_z * 2 + self.x
        target = (self.s + 2, self.s - 2, self.x_peer)[way]
        part = self.part(shard, q)
        return remote(part, part, self.send.at[way, shard_z, q], self.recv.at[shard, q], (self.dp, target))

    def arrived(self, shard, q):
        part = self.part(shard, q)
        remote(part, part, self.send.at[0, 0, q], self.recv.at[shard, q], (self.dp, self.x_peer)).wait_recv()

    def start(self, q):
        @pl.when(self.z < 3)
        def up():
            self.copy(self.z, 0, q).start()

        @pl.when(self.z > 0)
        def down():
            self.copy(self.z, 1, q).start()

        self.copy(self.z, 2, q).start()

    def step(self, hop, q):
        @pl.when(self.z >= hop)
        def from_below():
            shard_z = self.z - hop
            self.arrived(shard_z * 2 + self.x, q)

            @pl.when(self.z < 3)
            def up():
                self.copy(shard_z, 0, q).start()

            self.copy(shard_z, 2, q).start()

        @pl.when(self.z + hop <= 3)
        def from_above():
            shard_z = self.z + hop
            self.arrived(shard_z * 2 + self.x, q)

            @pl.when(self.z > 0)
            def down():
                self.copy(shard_z, 1, q).start()

            self.copy(shard_z, 2, q).start()

    def arrive_x(self, q):
        for shard_z in range(4):
            self.arrived(shard_z * 2 + 1 - self.x, q)

    def settle(self, q):
        for shard_z in range(4):
            self.copy(shard_z, 2, q).wait_send()

            @pl.when((self.z < 3) & (self.z >= shard_z))
            def up():
                self.copy(shard_z, 0, q).wait_send()

            @pl.when((self.z > 0) & (self.z <= shard_z))
            def down():
                self.copy(shard_z, 1, q).wait_send()


def column_of(mat, index):
    return pltpu.roll(mat, (128 - index) % 128, axis=1)[:, :1]


def pair_lanes(mat, pair):
    lane = lax.broadcasted_iota(jnp.int32, (mat.shape[0], 128), 1)
    return jnp.where(lane < HDIM, column_of(mat, 2 * pair), column_of(mat, 2 * pair + 1))


def load_params(rank, conv_t, conv_b, dt_bias, a_log, d_skip, wx, wbc, heads):
    lane = lax.broadcasted_iota(jnp.int32, (1, 128), 1)
    bias_row, log_row = jnp.zeros((1, 128), jnp.float32), jnp.zeros((1, 128), jnp.float32)
    wx[...] = jnp.zeros(wx.shape, jnp.float32)
    wbc[...] = jnp.zeros(wbc.shape, jnp.float32)
    heads[...] = jnp.zeros(heads.shape, jnp.float32)
    for d in range(wx.shape[1] // 128):
        cols, own = pl.ds(pl.multiple_of((d * 8 + rank) * 128, 128), 128), slice(d * 128, (d + 1) * 128)
        head = (d * 8 + rank) * 2
        wx[0:CONV, own] = conv_t[:, cols]
        wx[CONV : CONV + 1, own] = conv_b[cols].reshape(1, 128)
        wx[CONV + 1 : CONV + 2, own] = jnp.where(lane < HDIM, d_skip[head], d_skip[head + 1])
        for half in range(2):
            bias_row = jnp.where(lane == 2 * d + half, dt_bias[head + half], bias_row)
            log_row = jnp.where(lane == 2 * d + half, a_log[head + half], log_row)
    wbc[0:CONV] = conv_t[:, DI:]
    wbc[CONV : CONV + 1] = conv_b[pl.ds(DI, 2 * NST)].reshape(1, 2 * NST)
    heads[0:1] = bias_row
    heads[1:2] = log_row


def head_mats(dt_all, heads, h_own, dt_mat, cum_mat, cum_rows):
    shifted, dt = step_sizes_of(dt_all, heads, h_own, 8, 2)
    rates = -jnp.exp(heads[1:2])
    across = jnp.transpose(dt * (rates * LOG2E))
    cum_t = lane_sums(across[:h_own], False)
    pad = jnp.zeros((128 - h_own, cum_t.shape[1]), jnp.float32)
    dt_mat[...] = dt
    cum_mat[...] = jnp.transpose(jnp.concatenate([cum_t, pad], axis=0))
    for k in range(h_own):
        cum_rows[k] = cum_t[k : k + 1, :]


def mask_rows(bias, seg_col, seg_row, source_first):
    length = bias.shape[0]
    for block in range(length // TILE):
        rows = slice(block * TILE, (block + 1) * TILE)
        down = lax.broadcasted_iota(jnp.int32, (TILE, length), 0) + block * TILE
        over = lax.broadcasted_iota(jnp.int32, (TILE, length), 1)
        past = down <= over if source_first else over <= down
        bias[rows] = jnp.where(past & (seg_col[rows] == seg_row), 0.0, FAR)


def convolve_bc(bc_ref, wbc, keep):
    out = []
    for part in range(2):
        lanes = slice(part * NST, (part + 1) * NST)
        _, _, values = conv_silu(
            bc_ref[:, lanes].astype(jnp.float32), wbc[0:CONV, lanes], wbc[CONV : CONV + 1, lanes], keep
        )
        out.append(values.astype(jnp.bfloat16))
    return out


def forward_prepare(h_own, bc_ref, dt_ref, seg_col, seg_row, wbc, heads, dt_mat, cum_mat, cum_rows, inner_prod, bias):
    length = bc_ref.shape[0]
    keep = keep_masks(seg_col)
    head_mats(dt_ref[...], heads[...], h_own, dt_mat, cum_mat, cum_rows)
    bc = convolve_bc(bc_ref, wbc, keep)
    inner_prod[...] = lax.dot_general(bc[1], bc[0], (((1,), (1,)), ((), ())), preferred_element_type=jnp.float32)
    mask_rows(bias, seg_col, seg_row, False)


def forward_pair(pair, x_ref, seg_col, wx_ref, y_ref, inner_ref, dt_mat, cum_mat, cum_rows, inner_prod, bias):
    length = x_ref.shape[0]
    keep = keep_masks(seg_col)
    _, _, xc = conv_silu(x_ref[...].astype(jnp.float32), wx_ref[0:CONV], wx_ref[CONV : CONV + 1], keep)
    moved = (xc * pair_lanes(dt_mat[...], pair)).astype(jnp.bfloat16)
    skip = wx_ref[CONV + 1 : CONV + 2]
    first = lax.broadcasted_iota(jnp.int32, (TILE, 128), 1) < HDIM
    cum = [column_of(cum_mat[...], 2 * pair + half) for half in range(2)]
    for block in range(length // TILE):
        rows, wide = slice(block * TILE, (block + 1) * TILE), (block + 1) * TILE
        halves = []
        for half in range(2):
            decay = jnp.exp2(cum[half][rows] - cum_rows[2 * pair + half, :, :wide] + bias[rows, :wide])
            scores = (inner_prod[rows, :wide] * decay).astype(jnp.bfloat16)
            halves.append(jnp.dot(scores, moved[:wide], preferred_element_type=jnp.float32))
        inner = jnp.where(first, halves[0], halves[1])
        inner_ref[rows] = inner
        y_ref[rows] = (inner + skip * xc[rows]).astype(jnp.bfloat16)


def ahead_kernel(hidden, cot, in_w, out_w, seg_in, conv_t, conv_b, norm_gain, gate_gain, dt_bias, a_log, d_skip,
                 n_all, c_all, w_in, w_out, x_raw, bc_raw, dt_raw, inner, gated, d_y, d_z, seg_col, seg_row,
                 wx, wbc, heads, gain_back,
                 seg, in_tail, tok_v, cot_v, w_in_v, w_out_v, z_v, y_v, dg, seg_all, dt_mat, cum_mat, cum_rows, inner_prod, bias,
                 sum_cols, sums,
                 n_send, n_recv, c_send, c_recv, wide_send, tail_send, wide_recv, tail_recv,
                 y_send, core_send, cross_send, block_recv, out_send, out_recv, seg_send, seg_recv, store,
                 sum_send, sum_recv):
    f32, bf16 = jnp.float32, jnp.bfloat16
    where = place()
    dp, s, z, x, x_peer, y_peer, core_peer = where
    peers = [(dp, (s + k) % 8) for k in range(1, 8)] + [(y_peer, s), (core_peer, s)]
    greet(peers)
    in_rows, rows = in_w.shape[0], out_w.shape[0]
    chan = w_out.shape[0]
    h_own = chan // HDIM
    tail = in_tail.shape[1]
    n_own, length, width = n_all.shape
    in_tail[...] = jnp.zeros(in_tail.shape, bf16)
    in_tail[:, : in_w.shape[1] - 2 * DI] = in_w[:, 2 * DI :]
    seg[...] = jnp.zeros(seg.shape, f32)
    seg[:n_own, : seg_in.shape[1]] = seg_in[...].astype(f32)

    def block(d, shard, lo=0, size=None):
        size = w_in_v.shape[1] if size is None else size
        at = pl.multiple_of((d * 8 + shard) * in_rows, in_rows)
        return w_in_v.at[pl.ds(at, in_rows), pl.ds(lo, size)]

    def wide_src(piece, target):
        at = pl.multiple_of((piece * 8 + target) * rows, rows)
        return in_w.at[:, pl.ds(at, rows)]

    def push(k, _):
        target = (s + k) % 8
        remote(seg, seg_all.at[s], seg_send.at[k], seg_recv.at[s], (dp, target)).start()
        for piece in range(WIDE):
            remote(
                wide_src(piece, target), block(dp, s, piece * rows, rows), wide_send.at[k], wide_recv.at[s],
                (dp, target),
            ).start()
        remote(in_tail, block(dp, s, 2 * chan, tail), tail_send.at[k], tail_recv.at[s], (dp, target)).start()
        return 0

    span = hidden.shape[1]
    own_tokens = pl.ds(pl.multiple_of(s * span, span), span)
    for q in range(n_own):
        h = hidden[q].astype(f32)
        inv = lax.rsqrt(jnp.mean(h * h, axis=-1, keepdims=True) + 1e-05)
        tok_v[q, own_tokens] = (h * inv * norm_gain[...]).astype(bf16)
    tokens = TokenGather(tok_v, n_send, n_recv, where)
    cots = TokenGather(cot_v, c_send, c_recv, where)
    seg_all[s] = seg[...]
    own_rows = pl.ds(pl.multiple_of((dp * 8 + s) * in_rows, in_rows), in_rows)
    for piece in range(WIDE):
        at = pl.multiple_of((piece * 8 + s) * rows, rows)
        w_in_v[own_rows, piece * rows : (piece + 1) * rows] = in_w[:, pl.ds(at, rows)]
    w_in_v[own_rows, 2 * chan :] = in_tail[...]

    def out_part(d):
        return w_out_v.at[pl.ds(pl.multiple_of(d * rows, rows), rows)]

    w_out_v[pl.ds(pl.multiple_of(dp * rows, rows), rows)] = out_w[...]
    out_y = remote(out_part(dp), out_part(dp), out_send.at[0], out_recv.at[dp], (y_peer, s))
    out_core = remote(out_part(dp), out_part(dp), out_send.at[1], out_recv.at[dp], (core_peer, s))
    for q in range(n_own):
        cot_v[q, own_tokens] = cot[q]
    greeted(peers)
    tokens.start(0)
    tokens.start(1)
    out_y.start()
    out_core.start()
    lax.fori_loop(1, 8, push, 0)

    def spread(shard, k):
        there = block(dp, shard)
        remote(there, there, y_send.at[k], block_recv.at[dp, shard], (y_peer, s)).start()
        remote(there, there, core_send.at[k], block_recv.at[dp, shard], (core_peer, s)).start()

    spread(s, 0)
    load_params(s, conv_t, conv_b, dt_bias, a_log, d_skip, wx, wbc, heads)

    def wide_copy(source, k):
        there = block(dp, source, 0, 2 * chan)
        return remote(there, there, wide_send.at[k], wide_recv.at[source], (dp, x_peer))

    def tail_copy(source, k):
        there = block(dp, source, 2 * chan, tail)
        return remote(there, there, tail_send.at[k], tail_recv.at[source], (dp, x_peer))

    def forward(k, _):
        source = (s + 8 - k) % 8
        wide_copy(source, k).wait_recv()
        tail_copy(source, k).wait_recv()
        spread(source, k)
        return 0

    def cross(k, _):
        source = (s + 8 - k) % 8
        there = block(y_peer, source)
        copy = remote(there, there, cross_send.at[k], block_recv.at[y_peer, source], (core_peer, s))
        copy.wait_recv()
        copy.start()
        return 0

    tokens.step(1, 0)
    tokens.step(1, 1)
    cots.start(0)
    lax.fori_loop(1, 4, forward, 0)
    tokens.step(2, 0)
    tokens.step(2, 1)
    cots.start(1)
    lax.fori_loop(4, 8, forward, 0)
    tokens.step(3, 0)
    tokens.step(3, 1)
    cots.step(1, 0)
    lax.fori_loop(0, 4, cross, 0)
    cots.step(1, 1)
    lax.fori_loop(4, 8, cross, 0)

    def arrive(k, _):
        source = (s + 8 - k) % 8
        for d in (core_peer, core_peer + y_peer - dp):
            there = block(d, source)
            remote(there, there, core_send.at[k], block_recv.at[d, source], (core_peer, s)).wait_recv()
        return 0

    lax.fori_loop(0, 8, arrive, 0)
    stores = [pltpu.make_async_copy(w_in_v, w_in, store.at[0])]
    stores[0].start()

    def segments_in(k, _):
        source = (s + 8 - k) % 8
        remote(seg, seg_all.at[source], seg_send.at[k], seg_recv.at[source], (dp, x_peer)).wait_recv()
        return 0

    lax.fori_loop(1, 8, segments_in, 0)
    lane = lax.broadcasted_iota(jnp.int32, (1, 128), 1)
    for q in range(n_own):
        pieces = [
            jnp.where(lane < 64, seg_all[2 * m, q : q + 1], pltpu.roll(seg_all[2 * m + 1, q : q + 1], 64, axis=1))
            for m in range(4)
        ]
        row = jnp.concatenate(pieces, axis=1)
        seg_row[q] = row
        seg_col[q] = jnp.transpose(jnp.broadcast_to(row, (128, length)))[:, :1]

    def project(q):
        at = slice(q * length, (q + 1) * length)
        half = chan // 2

        @pl.loop(0, 2)
        def gates(n):
            cols = pl.ds(pl.multiple_of(n * half, half), half)
            z_v[at, cols] = jnp.dot(tok_v[q], w_in_v[:, cols], preferred_element_type=f32)

        @pl.loop(0, 2)
        def values(n):
            cols = pl.ds(pl.multiple_of(n * half, half), half)
            from_cols = pl.ds(pl.multiple_of(chan + n * half, half), half)
            x_raw[at, cols] = jnp.dot(tok_v[q], w_in_v[:, from_cols], preferred_element_type=f32).astype(bf16)

        last = jnp.dot(tok_v[q], w_in_v[:, 2 * chan :], preferred_element_type=f32).astype(bf16)
        bc_raw[at] = last[:, : 2 * NST]
        dt_raw[at] = last[:, 2 * NST :]

    for q in range(n_own):
        tokens.arrive_x(q)
        stores.append(pltpu.make_async_copy(tok_v.at[q], n_all.at[q], store.at[1 + q]))
        stores[-1].start()
        project(q)
        cots.step(2, q)

    for q in range(n_own):
        at = pl.ds(q * length, length)
        forward_prepare(
            h_own, bc_raw.at[at], dt_raw.at[at], seg_col[q], seg_row[q], wbc, heads,
            dt_mat, cum_mat, cum_rows, inner_prod, bias,
        )

        @pl.loop(0, chan // 128)
        def pairs(pair):
            cols = pl.ds(pl.multiple_of(pair * 128, 128), 128)
            forward_pair(
                pair, x_raw.at[at, cols], seg_col[q], wx.at[:, cols], y_v.at[at, cols], inner.at[at, cols],
                dt_mat, cum_mat, cum_rows, inner_prod, bias,
            )

            if q == 0:

                @pl.when(pair == 0)
                def hook_0_0():
                    cots.step(3, 0)

            if q == 0:

                @pl.when(pair == 2)
                def hook_0_2():
                    cots.step(3, 1)

    out_cross = remote(out_part(y_peer), out_part(y_peer), out_send.at[2], out_recv.at[y_peer], (core_peer, s))
    out_cross.wait_recv()
    out_cross.start()
    for d in (core_peer, core_peer + y_peer - dp):
        remote(out_part(d), out_part(d), out_send.at[0], out_recv.at[d], (core_peer, s)).wait_recv()
    stores.append(pltpu.make_async_copy(w_out_v, w_out, store.at[3]))
    stores[-1].start()
    gain = jnp.concatenate(
        [gate_gain[:, pl.ds(pl.multiple_of((d * 8 + s) * 128, 128), 128)] for d in range(chan // 128)], axis=1
    )
    lane_wide = lax.broadcasted_iota(jnp.int32, (TILE, 128), 1)

    def sum_copy(q, k):
        return remote(
            sums.at[q, s], sums.at[q, s], sum_send.at[q, k], sum_recv.at[q, s], (dp, (s + k) % 8)
        )

    def gate(q):
        for k in range(1, 8):
            source = (s + 8 - k) % 8
            remote(
                sums.at[q, source], sums.at[q, source], sum_send.at[q, k], sum_recv.at[q, source], (dp, x_peer)
            ).wait_recv()
        total = sums[q, 0]
        for source in range(1, 8):
            total = total + sums[q, source]
        total = jnp.concatenate([total, jnp.zeros((120, length), f32)], axis=0)
        sum_cols[...] = jnp.transpose(total)

        @pl.loop(0, length // TILE)
        def gate_rows(n):
            at = pl.ds(pl.multiple_of(q * length + n * TILE, TILE), TILE)
            both = sum_cols[pl.ds(pl.multiple_of(n * TILE, TILE), TILE)]
            r = lax.rsqrt(both[:, 0:1] / DI + 1e-05)
            fall = (r * r * r) * (both[:, 1:2] / DI)
            zz = z_v[at]
            sig = jax.nn.sigmoid(zz)
            act = zz * sig
            yy = y_v[at].astype(f32)
            g = yy * act
            gr = g * r
            back = dg[at]
            d_g = r * (back * gain) - fall * g
            gated[at] = (gr * gain).astype(bf16)
            d_y[at] = (d_g * act).astype(bf16)
            d_z[at] = (d_g * yy * (sig * (1.0 + zz * (1.0 - sig)))).astype(bf16)
            gain_back[0:1] += jnp.sum(back * gr, axis=0, keepdims=True)

    gain_back[...] = jnp.zeros(gain_back.shape, f32)
    for q in range(n_own):
        if q == 1:
            gate(0)
        cots.arrive_x(q)
        stores.append(pltpu.make_async_copy(cot_v.at[q], c_all.at[q], store.at[4 + q]))
        stores[-1].start()
        half = chan // 2

        @pl.loop(0, 2)
        def back(n):
            cols = pl.ds(pl.multiple_of(n * half, half), half)
            dg[q * length : (q + 1) * length, cols] = lax.dot_general(
                cot_v[q], w_out_v[cols], (((1,), (1,)), ((), ())), preferred_element_type=f32
            )

        @pl.loop(0, length // TILE)
        def reduce_rows(n):
            at = pl.ds(pl.multiple_of(q * length + n * TILE, TILE), TILE)
            zz = z_v[at]
            g = y_v[at].astype(f32) * (zz * jax.nn.sigmoid(zz))
            first = jnp.sum(g * g, axis=1, keepdims=True)
            second = jnp.sum(dg[at] * gain * g, axis=1, keepdims=True)
            sum_cols[pl.ds(pl.multiple_of(n * TILE, TILE), TILE)] = jnp.where(
                lane_wide == 0, first, jnp.where(lane_wide == 1, second, 0.0)
            )

        sums[q, s] = jnp.transpose(sum_cols[...])[:8]
        for k in range(1, 8):
            sum_copy(q, k).start()

    gate(1)

    for q in range(n_own):
        tokens.settle(q)
        cots.settle(q)
        for k in range(1, 8):
            sum_copy(q, k).wait_send()

    def settle(k, _):
        shard = (s + 8 - k) % 8
        there = block(dp, shard)
        remote(there, there, y_send.at[k], block_recv.at[dp, shard], (y_peer, s)).wait_send()
        remote(there, there, core_send.at[k], block_recv.at[dp, shard], (core_peer, s)).wait_send()
        remote(there, there, cross_send.at[k], block_recv.at[dp, shard], (core_peer, s)).wait_send()
        return 0

    lax.fori_loop(0, 8, settle, 0)

    def settle_push(k, _):
        source = (s + 8 - k) % 8
        remote(seg, seg_all.at[source], seg_send.at[k], seg_recv.at[source], (dp, x_peer)).wait_send()
        wide_copy(source, k).wait_send()
        tail_copy(source, k).wait_send()
        return 0

    lax.fori_loop(1, 8, settle_push, 0)
    out_y.wait_send()
    out_core.wait_send()
    out_cross.wait_send()
    for copy in stores:
        copy.wait()


def run_ahead(hidden, cot, in_w, out_w, seg, conv_t, conv_b, norm_gain, gate_gain, dt_bias, a_log, d_skip):
    f32, bf16 = jnp.float32, jnp.bfloat16
    n_own, span, width = hidden.shape
    in_rows, rows = in_w.shape[0], out_w.shape[0]
    chan, length = 4 * rows, 8 * span
    tokens, h_own = n_own * length, chan // HDIM
    columns = 2 * chan + 2 * NST + 128
    sem, vmem = pltpu.SemaphoreType.DMA, pltpu.VMEM
    anywhere, inside = pl.BlockSpec(memory_space=pl.ANY), pl.BlockSpec(memory_space=vmem)
    scalars = pl.BlockSpec(memory_space=pltpu.SMEM)
    shape = jax.ShapeDtypeStruct
    return pl.pallas_call(
        ahead_kernel,
        in_specs=[inside] * 9 + [scalars] * 3,
        out_specs=[anywhere] * 4 + [inside] * 13,
        out_shape=[
            shape((n_own, length, width), bf16),
            shape((n_own, length, width), bf16),
            shape((32 * in_rows, columns), bf16),
            shape((chan, width), bf16),
            shape((tokens, chan), bf16),
            shape((tokens, 2 * NST), bf16),
            shape((tokens, 128), bf16),
            shape((tokens, chan), f32),
            shape((tokens, chan), bf16),
            shape((tokens, chan), bf16),
            shape((tokens, chan), bf16),
            shape((n_own, length, 1), f32),
            shape((n_own, 1, length), f32),
            shape((8, chan), f32),
            shape((8, 2 * NST), f32),
            shape((8, 128), f32),
            shape((8, chan), f32),
        ],
        scratch_shapes=[
            vmem((8, 128), f32),
            vmem((in_rows, 2 * NST + 128), bf16),
            vmem((n_own, length, width), bf16),
            vmem((n_own, length, width), bf16),
            vmem((width, columns), bf16),
            vmem((chan, width), bf16),
            vmem((tokens, chan), f32),
            vmem((tokens, chan), bf16),
            vmem((tokens, chan), f32),
            vmem((8, 8, 128), f32),
            vmem((length, 128), f32),
            vmem((length, 128), f32),
            vmem((h_own, 1, length), f32),
            vmem((length, length), f32),
            vmem((length, length), f32),
            vmem((length, 128), f32),
            vmem((n_own, 8, 8, length), f32),
            sem((3, 4, 2)), sem((8, 2)), sem((3, 4, 2)), sem((8, 2)),
            sem((8,)), sem((8,)), sem((8,)), sem((8,)),
            sem((8,)), sem((8,)), sem((8,)), sem((4, 8)), sem((3,)), sem((4,)), sem((8,)), sem((8,)),
            sem((6,)), sem((2, 8)), sem((2, 8)),
        ],
        compiler_params=pltpu.CompilerParams(collective_id=0, has_side_effects=True, vmem_limit_bytes=56 << 20),
        name="ahead",
    )(hidden, cot, in_w, out_w, seg, conv_t, conv_b, norm_gain, gate_gain, dt_bias, a_log, d_skip)


def backward_prepare(h_own, bc_ref, dt_ref, seg_col, seg_row, wbc, heads, dt_mat, cum_mat, cum_rows, inner_prod, bias,
                     d_inner, d_cum, d_dt):
    length = bc_ref.shape[0]
    keep = keep_masks(seg_col)
    head_mats(dt_ref[...], heads[...], h_own, dt_mat, cum_mat, cum_rows)
    bc = convolve_bc(bc_ref, wbc, keep)
    inner_prod[...] = lax.dot_general(bc[0], bc[1], (((1,), (1,)), ((), ())), preferred_element_type=jnp.float32)
    mask_rows(bias, seg_col, seg_row, True)
    d_inner[...] = jnp.zeros((length, length), jnp.float32)
    d_cum[...] = jnp.zeros((length, 128), jnp.float32)
    d_dt[...] = jnp.zeros((length, 128), jnp.float32)


def backward_pair(pair, x_ref, seg_col, wx_ref, dy_ref, inner_ref, dx_ref, gx_ref, dt_mat, cum_mat, cum_rows,
                  inner_prod, bias, d_inner, d_cum, d_dt):
    f32, bf16 = jnp.float32, jnp.bfloat16
    length = x_ref.shape[0]
    keep = keep_masks(seg_col)
    x_in = x_ref[...].astype(f32)
    taps = wx_ref[0:CONV]
    total, gate, xc = conv_silu(x_in, taps, wx_ref[CONV : CONV + 1], keep)
    dt_wide = pair_lanes(dt_mat[...], pair)
    moved = (xc * dt_wide).astype(bf16)
    skip = wx_ref[CONV + 1 : CONV + 2]
    dy = dy_ref[...]
    first = lax.broadcasted_iota(jnp.int32, (TILE, 128), 1) < HDIM
    cum = [column_of(cum_mat[...], 2 * pair + half) for half in range(2)]
    pieces = []
    for block in range(length // TILE):
        rows, later = slice(block * TILE, (block + 1) * TILE), slice(block * TILE, length)
        halves = []
        for half in range(2):
            decay = jnp.exp2(cum_rows[2 * pair + half, :, later] - cum[half][rows] + bias[rows, later])
            scores = (inner_prod[rows, later] * decay).astype(bf16)
            halves.append(jnp.dot(scores, dy[later], preferred_element_type=f32))
            mine = jnp.where(first if half == 0 else ~first, moved[rows].astype(f32), 0.0).astype(bf16)
            d_scores = lax.dot_general(mine, dy[later], (((1,), (1,)), ((), ())), preferred_element_type=f32)
            d_inner[rows, later] += d_scores * decay
        pieces.append(jnp.where(first, halves[0], halves[1]))
    d_moved = jnp.concatenate(pieces, axis=0)
    dy_f = dy.astype(f32)
    change = dy_f * inner_ref[...] - moved.astype(f32) * d_moved
    direct = d_moved * xc
    lane = lax.broadcasted_iota(jnp.int32, (length, 128), 1)
    low = lane < HDIM
    for half in range(2):
        mine = low if half == 0 else ~low
        spot = lane == 2 * pair + half
        d_cum[...] += jnp.where(spot, jnp.sum(jnp.where(mine, change, 0.0), axis=1, keepdims=True), 0.0)
        d_dt[...] += jnp.where(spot, jnp.sum(jnp.where(mine, direct, 0.0), axis=1, keepdims=True), 0.0)
    d_xc = d_moved * dt_wide + skip * dy_f
    d_x, tap_rows, d_offset = conv_back(d_xc, total, gate, x_in, taps, keep)
    dx_ref[...] = d_x.astype(bf16)
    d_skip = jnp.sum(dy_f * xc, axis=0, keepdims=True)
    gx_ref[...] += jnp.concatenate(tap_rows + [d_offset, d_skip, jnp.zeros((2, 128), f32)], axis=0)


def backward_finish(h_own, bc_ref, dt_ref, seg_col, wbc, heads, d_inner, d_cum, d_dt, dbc_ref, ddt_ref, gbc_ref, gh_ref):
    f32, bf16 = jnp.float32, jnp.bfloat16
    length = bc_ref.shape[0]
    keep = keep_masks(seg_col)
    bc = convolve_bc(bc_ref, wbc, keep)
    d_in = d_inner[...].astype(bf16)
    for part in range(2):
        lanes = slice(part * NST, (part + 1) * NST)
        side = 1 - part
        d_value = lax.dot_general(d_in, bc[side], (((side,), (0,)), ((), ())), preferred_element_type=f32)
        bc_in = bc_ref[:, lanes].astype(f32)
        taps = wbc[0:CONV, lanes]
        total, gate, _ = conv_silu(bc_in, taps, wbc[CONV : CONV + 1, lanes], keep)
        d_bc, tap_rows, offset = conv_back(d_value, total, gate, bc_in, taps, keep)
        dbc_ref[:, lanes] = d_bc.astype(bf16)
        gbc_ref[:, lanes] += jnp.concatenate(tap_rows + [offset, jnp.zeros((3, NST), f32)], axis=0)
    shifted, dt = step_sizes_of(dt_ref[...], heads[...], h_own, 8, 2)
    rates = -jnp.exp(heads[1:2])
    across = jnp.transpose(d_cum[...])
    d_log_t = lane_sums(across[:h_own], True)
    d_log = jnp.transpose(jnp.concatenate([d_log_t, jnp.zeros((128 - h_own, length), f32)], axis=0))
    d_raw = (d_log * rates + d_dt[...]) * jax.nn.sigmoid(shifted)
    rank = lax.axis_index("seq")
    row = lax.broadcasted_iota(jnp.int32, (128, 128), 0)
    head = ((row // 2) * 8 + rank) * 2 + row % 2
    pick = ((lax.broadcasted_iota(jnp.int32, (128, 128), 1) == head) & (row < h_own)).astype(bf16)
    ddt_ref[...] = jnp.dot(d_raw.astype(bf16), pick, preferred_element_type=f32).astype(bf16)
    gh_ref[...] += jnp.concatenate(
        [
            jnp.sum(d_raw, axis=0, keepdims=True),
            jnp.sum(d_log * dt, axis=0, keepdims=True) * rates,
            jnp.zeros((6, 128), f32),
        ],
        axis=0,
    )


class TokenReduce:
    def __init__(self, part, from_x, from_near, from_far, x_sems, near_sems, far_sems, where, span):
        self.part, self.from_x, self.from_near, self.from_far = part, from_x, from_near, from_far
        self.x_sems, self.near_sems, self.far_sems, self.span = x_sems, near_sems, far_sems, span
        self.dp, self.s, self.z, self.x, self.x_peer, _, _ = where
        self.near = self.s + 2 - 4 * (self.z % 2)
        self.far = self.s + 4 - 8 * (self.z // 2)

    def rows(self, shard, q):
        return self.part.at[q, pl.ds(pl.multiple_of(shard * self.span, self.span), self.span)]

    def x_copy(self, shard_z, q):
        return remote(
            self.rows(shard_z * 2 + 1 - self.x, q), self.from_x.at[shard_z, q],
            self.x_sems.at[0, shard_z, q], self.x_sems.at[1, shard_z, q], (self.dp, self.x_peer),
        )

    def near_copy(self, high, q):
        shard = (high * 2 + 1 - self.z % 2) * 2 + self.x
        return remote(
            self.rows(shard, q), self.from_near.at[high, q],
            self.near_sems.at[0, high, q], self.near_sems.at[1, high, q], (self.dp, self.near),
        )

    def far_copy(self, q):
        shard = ((1 - self.z // 2) * 2 + self.z % 2) * 2 + self.x
        return remote(
            self.rows(shard, q), self.from_far.at[q], self.far_sems.at[0, q], self.far_sems.at[1, q],
            (self.dp, self.far),
        )

    def start(self, q):
        for turn in range(4):
            self.x_copy(self.turn(turn), q).start()

    def turn(self, turn):
        return (1 - self.z // 2 + turn % 2) % 2 * 2 + (1 - self.z % 2 + turn // 2) % 2

    def add(self, shard, q, other):
        rows = self.rows(shard, q)
        rows[...] = (rows[...].astype(jnp.float32) + other[...].astype(jnp.float32)).astype(jnp.bfloat16)

    def step_near(self, q):
        for turn in range(2):
            high = (1 - self.z // 2 + turn) % 2
            shard_z = high * 2 + 1 - self.z % 2
            self.x_copy(shard_z, q).wait_recv()
            self.add(shard_z * 2 + self.x, q, self.from_x.at[shard_z, q])
            self.near_copy(high, q).start()

    def step_keep(self, q):
        for turn in range(2):
            high = (1 - self.z // 2 + turn) % 2
            shard_z = high * 2 + self.z % 2
            self.x_copy(shard_z, q).wait_recv()
            self.add(shard_z * 2 + self.x, q, self.from_x.at[shard_z, q])

    def step_far(self, q):
        high = 1 - self.z // 2
        self.near_copy(high, q).wait_recv()
        self.add((high * 2 + self.z % 2) * 2 + self.x, q, self.from_near.at[high, q])
        self.far_copy(q).start()

    def total(self, q):
        high = self.z // 2
        self.near_copy(high, q).wait_recv()
        self.far_copy(q).wait_recv()
        f32 = jnp.float32
        return (
            self.rows(self.s, q)[...].astype(f32)
            + self.from_near[high, q].astype(f32)
            + self.from_far[q].astype(f32)
        )

    def settle(self):
        for q in range(2):
            for shard_z in range(4):
                self.x_copy(shard_z, q).wait_send()
            for high in range(2):
                self.near_copy(high, q).wait_send()
            self.far_copy(q).wait_send()


def finish_kernel(gated, w_out, d_z, d_y, x_raw, inner, w_in, cot_all, normed_all,
                  bc_raw, dt_raw, seg_col, seg_row, wx, wbc, heads, gain_back, hidden, cot, gain,
                  result, d_hidden, plane_in, grad_out, small_all, gain_sum,
                  gated_v, w_out_v, dp_v, w_in_v, tok_v, inner_v, dy_v,
                  dt_mat, cum_mat, cum_rows, inner_prod, bias, d_inner, d_cum, d_dt,
                  part_r, rx, rn, rf, part_d, dx, dn, df,
                  core_out, core_in, keep, y_in,
                  out_core_in, out_y, out_y_in, small_v, small_in, gain_v, gain_in,
                  load, rxs, rns, rfs, dxs, dns, dfs, core_sems, y_sems, plane_sems, out_sems, out_y_sems,
                  small_sems, small_plane, gain_sems, gain_plane):
    f32, bf16 = jnp.float32, jnp.bfloat16
    where = place()
    dp, s, z, x, x_peer, y_peer, core_peer = where
    y, core = dp // 2, dp % 2
    n_own, span, width = hidden.shape
    length = 8 * span
    chan = w_out.shape[0]
    rows = chan // 4
    in_rows = plane_in.shape[1]
    columns = keep.shape[3]
    tail = columns - 2 * chan
    peers = [(dp, (s + k) % 8) for k in range(1, 8)] + [(y_peer, s), (core_peer, s)]
    h_own = chan // HDIM

    def scan_loads(q):
        at = pl.ds(q * length, length)
        return [
            pltpu.make_async_copy(inner.at[at], inner_v, load.at[3]),
            pltpu.make_async_copy(d_y.at[at], dy_v, load.at[4]),
        ]

    loads = [
        pltpu.make_async_copy(gated, gated_v, load.at[0]),
        pltpu.make_async_copy(w_out, w_out_v, load.at[1]),
        pltpu.make_async_copy(cot_all, tok_v, load.at[7]),
        pltpu.make_async_copy(w_in, w_in_v, load.at[6]),
        pltpu.make_async_copy(d_z, dp_v.at[:, pl.ds(0, chan)], load.at[5]),
        pltpu.make_async_copy(x_raw, dp_v.at[:, pl.ds(chan, chan)], load.at[2]),
    ]
    first_scan = scan_loads(0)
    for copy in loads[:3] + first_scan + loads[3:]:
        copy.start()
    greet(peers)
    small_v[0] = jnp.zeros(small_v.shape[1:], f32)

    def small_copy(stage, device):
        return remote(small_v.at[stage], small_in.at[stage], small_sems.at[0, stage], small_sems.at[1, stage], device)

    reduce_r = TokenReduce(part_r, rx, rn, rf, rxs, rns, rfs, where, span)
    reduce_d = TokenReduce(part_d, dx, dn, df, dxs, dns, dfs, where, span)
    loads[0].wait()
    loads[1].wait()
    step = 512

    def branch(q):
        @pl.loop(0, width // 256)
        def forward(n):
            cols = pl.ds(pl.multiple_of(n * 256, 256), 256)
            part_r[q, :, cols] = jnp.dot(
                gated_v[q * length : (q + 1) * length], w_out_v[:, cols], preferred_element_type=f32
            ).astype(bf16)

    def first_rows(turn):
        shard_z = reduce_r.turn(turn)
        at = pl.ds(pl.multiple_of(shard_z * 2 * span, 2 * span), 2 * span)
        for half in range(2):
            cols = slice(half * width // 2, (half + 1) * width // 2)
            part_r[0, at, cols] = jnp.dot(gated_v[at], w_out_v[:, cols], preferred_element_type=f32).astype(bf16)
        return shard_z

    first = first_rows(0)
    greeted(peers)
    reduce_r.x_copy(first, 0).start()

    @pl.loop(1, 4)
    def other_rows(turn):
        reduce_r.x_copy(first_rows(turn), 0).start()

    def out_term(d, n):
        lanes = pl.ds(pl.multiple_of(d * rows, rows), rows)
        return lax.dot_general(
            gated_v[:, lanes], tok_v[:, n * step : (n + 1) * step], (((0,), (0,)), ((), ())),
            preferred_element_type=f32,
        )

    def out_core_copy(yy):
        return remote(w_out_v.at[pl.ds(yy * rows, rows)], out_core_in.at[yy], out_sems.at[0, yy], out_sems.at[1, yy], (core_peer, s))

    def out_gradient():
        loads[2].wait()
        for yy in range(2):
            for n in range(width // step):
                w_out_v[yy * rows : (yy + 1) * rows, n * step : (n + 1) * step] = out_term(yy * 2 + 1 - core, n).astype(bf16)
            out_core_copy(yy).start()
        for n in range(width // step):
            out_y[:, n * step : (n + 1) * step] = out_term((1 - y) * 2 + core, n).astype(bf16)
        for n in range(width // step):
            grad_out[:, n * step : (n + 1) * step] = out_term(y * 2 + core, n)
        norm_load.start()

    norm_load = pltpu.make_async_copy(normed_all, tok_v, load.at[8])
    out_y_copy = remote(out_y, out_y_in, out_y_sems.at[0], out_y_sems.at[1], (y_peer, s))
    for q in range(2):
        at = pl.ds(q * length, length)
        scan_in = first_scan if q == 0 else scan_loads(1)
        if q == 1:
            for copy in scan_in:
                copy.start()
        backward_prepare(
            h_own, bc_raw.at[at], dt_raw.at[at], seg_col[q], seg_row[q], wbc, heads,
            dt_mat, cum_mat, cum_rows, inner_prod, bias, d_inner, d_cum, d_dt,
        )
        for copy in scan_in:
            copy.wait()
        if q == 0:
            loads[5].wait()

        @pl.loop(0, chan // 128)
        def pairs(pair):
            cols = pl.ds(pl.multiple_of(pair * 128, 128), 128)
            x_cols = pl.ds(pl.multiple_of(chan + pair * 128, 128), 128)
            backward_pair(
                pair, dp_v.at[at, x_cols], seg_col[q], wx.at[:, cols], dy_v.at[:, cols], inner_v.at[:, cols],
                dp_v.at[at, x_cols], small_v.at[0, :, cols], dt_mat, cum_mat, cum_rows,
                inner_prod, bias, d_inner, d_cum, d_dt,
            )
            if q == 0:

                @pl.when(pair == 3)
                def near_result():
                    reduce_r.step_near(0)
            else:

                @pl.when(pair == 0)
                def far_result():
                    reduce_r.step_far(0)

                @pl.when(pair == 3)
                def near_back():
                    reduce_d.step_near(0)

        backward_finish(
            h_own, bc_raw.at[at], dt_raw.at[at], seg_col[q], wbc, heads, d_inner, d_cum, d_dt,
            dp_v.at[at, pl.ds(2 * chan, 2 * NST)], dp_v.at[at, pl.ds(2 * chan + 2 * NST, 128)],
            small_v.at[0, :, pl.ds(chan, 2 * NST)], small_v.at[0, :, pl.ds(chan + 2 * NST, 128)],
        )
        if q == 0:
            loads[3].wait()
            loads[4].wait()

        @pl.loop(0, width // 256)
        def backward(n):
            cols = pl.ds(pl.multiple_of(n * 256, 256), 256)
            part_d[q, :, cols] = lax.dot_general(
                dp_v[q * length : (q + 1) * length], w_in_v[cols], (((1,), (1,)), ((), ())),
                preferred_element_type=f32,
            ).astype(bf16)

        reduce_d.start(q)
        if q == 0:
            branch(1)
            reduce_r.step_keep(0)

    reduce_r.start(1)
    small_v[0, CONV + 2 : CONV + 3, :chan] = gain_back[0:1]
    small_core = small_copy(0, (core_peer, s))
    small_core.start()

    def small_push(k):
        return remote(
            small_all.at[s], small_all.at[s], small_plane.at[0, k], small_plane.at[1, s], (dp, (s + k) % 8)
        )

    out_gradient()

    def in_term(d, m, lo, size):
        lanes = pl.ds(pl.multiple_of(d * 8 * in_rows + m * 2 * in_rows, 2 * in_rows), 2 * in_rows)
        return lax.dot_general(
            tok_v[:, lanes], dp_v[:, lo : lo + size], (((0,), (0,)), ((), ())), preferred_element_type=f32
        )

    pieces = ((0, chan, chan), (chan, chan, chan), (2 * chan, tail, 2 * NST + 128))

    def core_copy(t, yy):
        return remote(
            core_out.at[t % 2, yy], core_in.at[t, yy], core_sems.at[0, t, yy], core_sems.at[1, t, yy], (core_peer, s)
        )

    def y_copy(t):
        return remote(keep.at[t, 1 - y], y_in.at[t], y_sems.at[0, t], y_sems.at[1, t], (y_peer, s))

    def target_of(t):
        return (z + 1 + t) % 4

    def in_compute(t):
        for yy in range(2):
            if t >= 2:
                core_copy(t - 2, yy).wait_send()
            for lo, size, span_in in pieces:
                core_out[t % 2, yy, :, lo : lo + size] = in_term(yy * 2 + 1 - core, target_of(t), lo, span_in)[
                    :, :size
                ].astype(bf16)
            core_copy(t, yy).start()
        for yy in range(2):
            for lo, size, span_in in pieces:
                keep[t, yy, :, lo : lo + size] = in_term(yy * 2 + core, target_of(t), lo, span_in)[:, :size].astype(bf16)

    def in_core(t):
        for yy in range(2):
            core_copy(t, yy).wait_recv()
            keep[t, yy] = (keep[t, yy].astype(f32) + core_in[t, yy].astype(f32)).astype(bf16)
        y_copy(t).start()

    def half_rows(half):
        return pl.ds(pl.multiple_of(half * in_rows, in_rows), in_rows)

    def plane_copy(t, half):
        return remote(
            keep.at[t, y, half_rows(half)], plane_in.at[s],
            plane_sems.at[0, t, half], plane_sems.at[1, s // 2, s % 2], (dp, 2 * target_of(t) + half),
        )

    def plane_halves(t):
        return (0, 1) if t < 3 else (1 - x,)

    def in_plane(t):
        y_copy(t).wait_recv()
        keep[t, y] = (keep[t, y].astype(f32) + y_in[t].astype(f32)).astype(bf16)
        for half in plane_halves(t):
            plane_copy(t, half).start()
        if t == 3:
            plane_in[s] = keep[t, y, half_rows(x)]

    reduce_d.step_keep(0)
    reduce_d.step_far(0)
    norm_load.wait()
    in_compute(0)
    out_core_copy(1 - y).wait_recv()
    out_y[...] = (out_y[...].astype(f32) + out_core_in[1 - y].astype(f32)).astype(bf16)
    out_y_copy.start()
    in_core(0)
    small_core.wait_recv()
    small_v[1] = small_v[0] + small_in[0]
    small_y = small_copy(1, (y_peer, s))
    small_y.start()
    reduce_d.step_near(1)
    in_compute(1)
    in_core(1)
    in_compute(2)
    in_core(2)
    small_y.wait_recv()
    small_all[s] = small_v[1] + small_in[1]
    for k in range(1, 8):
        small_push(k).start()
    in_plane(0)
    reduce_d.step_keep(1)
    reduce_d.step_far(1)
    in_compute(3)
    in_core(3)
    in_plane(1)
    result[0] = (hidden[0].astype(f32) + reduce_r.total(0)).astype(bf16)
    reduce_r.step_near(1)
    in_plane(2)
    out_y_copy.wait_recv()
    out_core_copy(y).wait_recv()
    grad_out[...] = grad_out[...] + out_core_in[y].astype(f32) + out_y_in[...].astype(f32)
    gain_row = gain[...]
    gain_part = None
    for q in range(2):
        d_normed = reduce_d.total(q)
        h = hidden[q].astype(f32)
        inv = lax.rsqrt(jnp.mean(h * h, axis=-1, keepdims=True) + 1e-05)
        scaled = d_normed * gain_row
        along = jnp.mean(scaled * h, axis=-1, keepdims=True)
        d_hidden[q] = (cot[q].astype(f32) + inv * scaled - (inv * inv * inv) * along * h).astype(bf16)
        term = jnp.sum(d_normed * h * inv, axis=0, keepdims=True)
        gain_part = term if q == 0 else gain_part + term
    folded = width // 8
    gain_v[0] = jnp.concatenate([gain_part[:, k * folded : (k + 1) * folded] for k in range(8)], axis=0)

    def gain_copy(stage, device):
        return remote(gain_v.at[stage], gain_in.at[stage], gain_sems.at[0, stage], gain_sems.at[1, stage], device)

    gain_core = gain_copy(0, (core_peer, s))
    gain_core.start()
    in_plane(3)
    reduce_r.step_keep(1)
    reduce_r.step_far(1)
    gain_core.wait_recv()
    gain_v[1] = gain_v[0] + gain_in[0]
    gain_y = gain_copy(1, (y_peer, s))
    gain_y.start()
    for k in range(1, 8):
        source = (s + 8 - k) % 8
        there = plane_in.at[source]
        remote(there, there, plane_sems.at[0, 0, 0], plane_sems.at[1, source // 2, source % 2], (dp, x_peer)).wait_recv()
    gain_y.wait_recv()
    gain_v[2 + s] = gain_v[1] + gain_in[1]

    def gain_push(k):
        return remote(gain_v.at[2 + s], gain_v.at[2 + s], gain_plane.at[0, k], gain_plane.at[1, s], (dp, (s + k) % 8))

    for k in range(1, 8):
        gain_push(k).start()
    result[1] = (hidden[1].astype(f32) + reduce_r.total(1)).astype(bf16)
    reduce_r.settle()
    reduce_d.settle()
    small_core.wait_send()
    small_y.wait_send()
    out_y_copy.wait_send()
    for yy in range(2):
        out_core_copy(yy).wait_send()
    for m in range(4):
        for yy in range(2 if m >= 2 else 0):
            core_copy(m, yy).wait_send()
        y_copy(m).wait_send()
        for half in plane_halves(m):
            plane_copy(m, half).wait_send()

    for k in range(1, 8):
        source = (s + 8 - k) % 8
        remote(
            small_all.at[source], small_all.at[source], small_plane.at[0, k], small_plane.at[1, source], (dp, x_peer)
        ).wait_recv()
        small_push(k).wait_send()
        remote(
            gain_v.at[2 + source], gain_v.at[2 + source], gain_plane.at[0, k], gain_plane.at[1, source], (dp, x_peer)
        ).wait_recv()
        gain_push(k).wait_send()
    gain_core.wait_send()
    gain_y.wait_send()
    gain_total = gain_v[2]
    for source in range(1, 8):
        gain_total = gain_total + gain_v[2 + source]
    gain_sum[...] = gain_total


def run_finish(gated, w_out, d_z, d_y, x_raw, inner, w_in, cot_all, normed_all,
               bc_raw, dt_raw, seg_col, seg_row, wx, wbc, heads, gain_back, hidden, cot, gain, in_rows):
    f32, bf16 = jnp.float32, jnp.bfloat16
    n_own, span, width = hidden.shape
    tokens, chan = gated.shape
    length, rows = 8 * span, chan // 4
    columns = 2 * chan + 2 * NST + HEADS
    small = (8, chan + 2 * NST + 128)
    vmem = pltpu.VMEM
    anywhere, inside = pl.BlockSpec(memory_space=pl.ANY), pl.BlockSpec(memory_space=vmem)
    sem = pltpu.SemaphoreType.DMA
    tokens_like = [
        vmem((n_own, length, width), bf16), vmem((4, n_own, span, width), bf16),
        vmem((2, n_own, span, width), bf16), vmem((n_own, span, width), bf16),
    ]
    return pl.pallas_call(
        finish_kernel,
        in_specs=[anywhere] * 9 + [inside] * 11,
        out_specs=[inside] * 6,
        out_shape=[
            jax.ShapeDtypeStruct(hidden.shape, bf16),
            jax.ShapeDtypeStruct(hidden.shape, bf16),
            jax.ShapeDtypeStruct((8, in_rows, columns), bf16),
            jax.ShapeDtypeStruct((rows, width), f32),
            jax.ShapeDtypeStruct((8,) + small, f32),
            jax.ShapeDtypeStruct((8, width // 8), f32),
        ],
        scratch_shapes=[
            vmem((tokens, chan), bf16), vmem((chan, width), bf16),
            vmem((tokens, 2 * chan + 2 * NST + 128), bf16), vmem((width, 2 * chan + 2 * NST + 128), bf16),
            vmem((tokens, width), bf16),
            vmem((length, chan), f32), vmem((length, chan), bf16),
            vmem((length, 128), f32), vmem((length, 128), f32), vmem((chan // HDIM, 1, length), f32),
            vmem((length, length), f32), vmem((length, length), f32), vmem((length, length), f32),
            vmem((length, 128), f32), vmem((length, 128), f32),
        ]
        + tokens_like + tokens_like
        + [
            vmem((2, 2, 2 * in_rows, columns), bf16), vmem((4, 2, 2 * in_rows, columns), bf16),
            vmem((4, 2, 2 * in_rows, columns), bf16), vmem((4, 2 * in_rows, columns), bf16),
            vmem((2, rows, width), bf16),
            vmem((rows, width), bf16), vmem((rows, width), bf16),
            vmem((2,) + small, f32), vmem((2,) + small, f32),
            vmem((10, 8, width // 8), f32), vmem((2, 8, width // 8), f32),
            sem((9,)), sem((2, 4, 2)), sem((2, 2, 2)), sem((2, 2)), sem((2, 4, 2)), sem((2, 2, 2)), sem((2, 2)),
            sem((2, 4, 2)), sem((2, 4)), sem((2, 4, 2)), sem((2, 2)), sem((2,)),
            sem((2, 2)), sem((2, 8)), sem((2, 2)), sem((2, 8)),
        ],
        compiler_params=pltpu.CompilerParams(
            collective_id=1, has_side_effects=True, vmem_limit_bytes=63 << 20
        ),
        name="finish",
    )(
        gated, w_out, d_z, d_y, x_raw, inner, w_in, cot_all, normed_all,
        bc_raw, dt_raw, seg_col, seg_row, wx, wbc, heads, gain_back, hidden, cot, gain,
    )


def spots(lane_head, count, source):
    row = lax.broadcasted_iota(jnp.int32, (count, HEADS), 0)
    own = row // lane_head
    head = ((own // 2) * 8 + source) * 2 + own % 2
    fits = own < 8
    return ((lax.broadcasted_iota(jnp.int32, (count, HEADS), 1) == head) & fits).astype(jnp.float32)


def assemble_kernel(result_in, d_hidden_in, plane_in, grad_out_in, small_all, gain_sum,
                    result, d_hidden, grad_in, conv_w, conv_b, dt_bias, a_log, d_skip, norm_gain, gate_gain, grad_out):
    f32 = jnp.float32
    rows = grad_out.shape[0]
    chan = 4 * rows
    result[...] = result_in[...]
    d_hidden[...] = d_hidden_in[...]
    grad_out[...] = grad_out_in[...]
    tail_sum, bc_sum, head_sum, skip_sum = 0.0, 0.0, 0.0, 0.0
    for source in range(8):
        for piece in range(WIDE):
            at = (piece * 8 + source) * rows
            grad_in[:, at : at + rows] = plane_in[source, :, piece * rows : (piece + 1) * rows].astype(f32)
        tail_sum = tail_sum + plane_in[source, :, 2 * chan :].astype(f32)
        for d in range(4):
            at, own = (d * 8 + source) * rows, slice(d * rows, (d + 1) * rows)
            conv_w[:, at : at + rows] = small_all[source, :CONV, own]
            conv_b[pl.ds(at, rows)] = small_all[source, CONV, own]
            gate_gain[pl.ds(at, rows)] = small_all[source, CONV + 2, own]
        bc_sum = bc_sum + small_all[source, :, chan : chan + 2 * NST]
        head_sum = head_sum + jnp.dot(
            small_all[source, :, chan + 2 * NST :], spots(1, 128, source),
            precision=lax.Precision.HIGHEST, preferred_element_type=f32,
        )
        skip_sum = skip_sum + jnp.dot(
            small_all[source, :, :chan], spots(HDIM, chan, source),
            precision=lax.Precision.HIGHEST, preferred_element_type=f32,
        )
    grad_in[:, 2 * DI :] = tail_sum
    conv_w[:, DI:] = bc_sum[:CONV]
    conv_b[pl.ds(DI, 2 * NST)] = bc_sum[CONV]
    dt_bias[...] = head_sum[0]
    a_log[...] = head_sum[1]
    d_skip[...] = skip_sum[CONV + 1]
    folded = gain_sum.shape[1]
    for k in range(8):
        norm_gain[pl.ds(k * folded, folded)] = gain_sum[k]


def run_assemble(result, d_hidden, plane_in, grad_out, small_all, gain_sum):
    f32 = jnp.float32
    width = result.shape[2]
    in_rows = plane_in.shape[1]
    shape = jax.ShapeDtypeStruct
    channels = DI + 2 * NST
    return pl.pallas_call(
        assemble_kernel,
        in_specs=[pl.BlockSpec(memory_space=pltpu.VMEM)] * 6,
        out_specs=[pl.BlockSpec(memory_space=pltpu.VMEM)] * 11,
        out_shape=[
            shape(result.shape, result.dtype),
            shape(d_hidden.shape, d_hidden.dtype),
            shape((in_rows, 2 * DI + 2 * NST + HEADS), f32),
            shape((CONV, channels), f32),
            shape((channels,), f32),
            shape((HEADS,), f32),
            shape((HEADS,), f32),
            shape((HEADS,), f32),
            shape((width,), f32),
            shape((DI,), f32),
            shape(grad_out.shape, f32),
        ],
        compiler_params=pltpu.CompilerParams(vmem_limit_bytes=62 << 20),
        name="assemble",
    )(result, d_hidden, plane_in, grad_out, small_all, gain_sum)


def head_plan(
    hidden,
    segments,
    in_weight,
    conv_weight,
    conv_bias,
    dt_bias,
    a_log,
    d_skip,
    norm_gain,
    gate_gain,
    out_weight,
    cotangent,
):
    f32, bf16 = jnp.float32, jnp.bfloat16
    n_dp, n_seq = lax.axis_size("dp"), lax.axis_size("seq")
    seq_rank = lax.axis_index("seq")
    n_own, shard_len, width = hidden.shape
    length = shard_len * n_seq
    rows = out_weight.shape[0]
    in_rows = in_weight.shape[0]
    chan = rows * n_dp
    h_own = chan // HDIM
    (n_all, cot_all, w_in, w_out, x_raw, bc_raw, dt_raw, inner, gated, d_y, d_z, seg_col, seg_row, wx, wbc, head_vals,
     gain_back) = run_ahead(
        hidden, cotangent, in_weight, out_weight, segments, conv_weight.T, conv_bias,
        norm_gain[None], gate_gain[None], dt_bias, a_log, d_skip,
    )
    normed_all = n_all.reshape(n_own * length, width)
    cot_all = cot_all.reshape(n_own * length, width)
    result, d_hidden, plane_in, grad_out, small_all, gain_sum = run_finish(
        gated, w_out, d_z, d_y, x_raw, inner, w_in, cot_all, normed_all,
        bc_raw, dt_raw, seg_col, seg_row, wx, wbc, head_vals, gain_back, hidden, cotangent, norm_gain[None], in_rows,
    )
    outs = list(run_assemble(result, d_hidden, plane_in, grad_out, small_all, gain_sum))
    outs[3] = outs[3].T
    return tuple(outs)


def solution(mesh):
    whole_heads = mesh.shape["dp"] == 4 and mesh.shape["seq"] == 8
    shards = head_plan if whole_heads else general_plan
    placed = (
        P("dp", "seq", None),
        P("dp", "seq"),
        P(("dp", "seq"), None),
        P(),
        P(),
        P(),
        P(),
        P(),
        P(),
        P(),
        P(("dp", "seq"), None),
        P("dp", "seq", None),
    )
    return jax.shard_map(
        shards,
        mesh=mesh,
        in_specs=placed,
        out_specs=(
            P("dp", "seq", None),
            P("dp", "seq", None),
            P(("dp", "seq"), None),
            P(),
            P(),
            P(),
            P(),
            P(),
            P(),
            P(),
            P(("dp", "seq"), None),
        ),
        check_vma=False,
    )
```

```python
import functools

import jax
import jax.numpy as jnp
from jax import lax
from jax.experimental import pallas as pl
from jax.experimental.pallas import tpu as pltpu
from jax.sharding import PartitionSpec as P

HEADS = 64
HDIM = 64
NST = 128
GROUP = 256
CONV = 4
DI = 4096


def pre_norm(hidden_f, gain_vec):
    return (
        hidden_f
        * lax.rsqrt(jnp.mean(hidden_f * hidden_f, axis=-1, keepdims=True) + 1e-05)
        * gain_vec
    )


def gate_norm(y_values, gate_values, gain_vec):
    product = y_values * jax.nn.silu(gate_values)
    return (
        product * lax.rsqrt(jnp.mean(product * product, axis=-1, keepdims=True) + 1e-05) * gain_vec
    )


def conv_reset(signal, kernel, offset, seg_ids):
    tap_count = kernel.shape[1]
    summed = offset[None, :] + kernel[None, :, tap_count - 1] * signal
    for lag_steps in range(1, tap_count):
        shifted = jnp.pad(signal, ((lag_steps, 0), (0, 0)))[:-lag_steps]
        earlier = jnp.pad(seg_ids, (lag_steps, 0), constant_values=-1)[:-lag_steps]
        matches = (earlier == seg_ids).astype(jnp.float32)
        summed = summed + kernel[None, :, tap_count - 1 - lag_steps] * shifted * matches[:, None]
    return summed


def state_scan(values, deltas, rates, b_mat, c_mat, seg_ids):
    length, head_count, head_width = values.shape
    block_count = length // GROUP
    log_decay = deltas * rates[None, :]
    pieces = (
        values.reshape(block_count, GROUP, head_count, head_width),
        deltas.reshape(block_count, GROUP, head_count),
        log_decay.reshape(block_count, GROUP, head_count),
        b_mat.reshape(block_count, GROUP, b_mat.shape[-1]),
        c_mat.reshape(block_count, GROUP, c_mat.shape[-1]),
        seg_ids.reshape(block_count, GROUP),
    )
    position = lax.broadcasted_iota(jnp.int32, (GROUP, GROUP), 0)
    source = lax.broadcasted_iota(jnp.int32, (GROUP, GROUP), 1)

    def advance(carry, piece):
        memory, ending = carry
        block_vals, block_dt, block_log, b_block, c_block, seg_block = piece
        cumulative = jnp.cumsum(block_log, axis=0).T
        causal = (source <= position) & (seg_block[:, None] == seg_block[None, :])
        spread = cumulative[:, :, None] - cumulative[:, None, :]
        decays = jnp.where(causal[None], jnp.exp(jnp.where(causal[None], spread, 0.0)), 0.0)
        inner_prod = jnp.dot(c_block, b_block.T, precision=lax.Precision.HIGHEST)
        scores = inner_prod[None] * decays * block_dt.T[:, None, :]
        output = jnp.einsum("hij,jhp->ihp", scores, block_vals, precision=lax.Precision.HIGHEST)
        follows = (seg_block == ending).astype(jnp.float32)
        carried = jnp.einsum("in,hpn->ihp", c_block, memory, precision=lax.Precision.HIGHEST)
        output = output + (jnp.exp(cumulative).T * follows[:, None])[:, :, None] * carried
        last_seg = seg_block[-1]
        weights = (
            jnp.exp(cumulative[:, -1:] - cumulative)
            * (seg_block == last_seg).astype(jnp.float32)[None, :]
            * block_dt.T
        )
        keep_on = jnp.exp(cumulative[:, -1]) * (last_seg == ending).astype(jnp.float32)
        memory = memory * keep_on[:, None, None] + jnp.einsum(
            "hj,jhp,jn->hpn", weights, block_vals, b_block, precision=lax.Precision.HIGHEST
        )
        return ((memory, last_seg), output)

    initial = (
        jnp.zeros((head_count, head_width, b_mat.shape[-1]), jnp.float32),
        jnp.array(-1, jnp.int32),
    )
    unused, outputs = lax.scan(jax.checkpoint(advance), initial, pieces)
    return outputs.reshape(length, head_count, head_width)


def mixer(
    x_values,
    step_raw,
    bc_values,
    seg_ids,
    kernel_x,
    offset_x,
    kernel_bc,
    offset_bc,
    dt_shift,
    decay_log,
    skip_gain,
):
    x_conv = jax.nn.silu(conv_reset(x_values, kernel_x, offset_x, seg_ids))
    bc_conv = jax.nn.silu(conv_reset(bc_values, kernel_bc, offset_bc, seg_ids))
    step_sizes = jax.nn.softplus(step_raw + dt_shift[None, :])
    rates = -jnp.exp(decay_log)
    length = x_values.shape[0]
    head_count = step_raw.shape[1]
    shaped = x_conv.reshape(length, head_count, HDIM)
    mixed = (
        state_scan(shaped, step_sizes, rates, bc_conv[:, :NST], bc_conv[:, NST:], seg_ids)
        + skip_gain[None, :, None] * shaped
    )
    return mixed.reshape(length, head_count * HDIM)


def general_plan(
    hidden,
    segments,
    in_weight,
    conv_weight,
    conv_bias,
    dt_bias,
    a_log,
    d_skip,
    norm_gain,
    gate_gain,
    out_weight,
    cotangent,
):
    full_in, full_out = (
        lax.all_gather(in_weight, ("dp", "seq"), axis=0, tiled=True),
        lax.all_gather(out_weight, ("dp", "seq"), axis=0, tiled=True),
    )
    hidden_f = hidden.astype(jnp.float32)
    normed_f, pull_pre = jax.vjp(pre_norm, hidden_f, norm_gain)
    normed = normed_f.astype(jnp.bfloat16)
    project = jnp.einsum("mtd,df->mtf", normed, full_in, preferred_element_type=jnp.float32)
    gate_part = project[:, :, :DI]
    x_part = project[:, :, DI : 2 * DI].astype(jnp.bfloat16)
    bc_part = project[:, :, 2 * DI : 2 * DI + 2 * NST].astype(jnp.bfloat16)
    step_part = project[:, :, 2 * DI + 2 * NST :].astype(jnp.bfloat16)
    x_heads, step_heads = (
        lax.all_to_all(x_part, "seq", split_axis=2, concat_axis=1, tiled=True),
        lax.all_to_all(step_part, "seq", split_axis=2, concat_axis=1, tiled=True),
    )
    bc_full = lax.all_gather(bc_part, "seq", axis=1, tiled=True)
    seg_full = lax.all_gather(segments, "seq", axis=1, tiled=True)
    seq_rank = lax.axis_index("seq")
    head_local = step_heads.shape[2]
    chan_local = x_heads.shape[2]
    kernel_x = lax.dynamic_slice_in_dim(conv_weight, seq_rank * chan_local, chan_local, 0)
    offset_x = lax.dynamic_slice_in_dim(conv_bias, seq_rank * chan_local, chan_local, 0)
    shift_local = lax.dynamic_slice_in_dim(dt_bias, seq_rank * head_local, head_local, 0)
    decay_local = lax.dynamic_slice_in_dim(a_log, seq_rank * head_local, head_local, 0)
    skip_local = lax.dynamic_slice_in_dim(d_skip, seq_rank * head_local, head_local, 0)
    local_params = (
        kernel_x,
        offset_x,
        conv_weight[DI:],
        conv_bias[DI:],
        shift_local,
        decay_local,
        skip_local,
    )

    def head_mixer(x_values, step_raw, bc_values, params_in):

        def single_seq(x_one, step_one, bc_one, seg_one):
            return mixer(x_one, step_one, bc_one, seg_one, *params_in)

        return jax.vmap(single_seq)(x_values, step_raw, bc_values, seg_full)

    mixed, pull_mix = jax.vjp(
        head_mixer,
        x_heads.astype(jnp.float32),
        step_heads.astype(jnp.float32),
        bc_full.astype(jnp.float32),
        local_params,
    )
    y_tokens = lax.all_to_all(
        mixed.astype(jnp.bfloat16), "seq", split_axis=1, concat_axis=2, tiled=True
    )
    gated_f, pull_gate = jax.vjp(gate_norm, y_tokens.astype(jnp.float32), gate_part, gate_gain)
    gated = gated_f.astype(jnp.bfloat16)
    branch_out = jnp.einsum("mtf,fd->mtd", gated, full_out, preferred_element_type=jnp.float32)
    result = (hidden_f + branch_out).astype(jnp.bfloat16)
    d_gated = jnp.einsum("mtd,fd->mtf", cotangent, full_out, preferred_element_type=jnp.float32)
    d_mixed, d_gate_part, d_gate_gain = pull_gate(d_gated)
    d_heads = lax.all_to_all(
        d_mixed.astype(jnp.bfloat16), "seq", split_axis=2, concat_axis=1, tiled=True
    )
    d_x_heads, d_step_heads, d_bc_full, d_params = pull_mix(d_heads.astype(jnp.float32))
    d_x_part, d_step_part = (
        lax.all_to_all(
            d_x_heads.astype(jnp.bfloat16), "seq", split_axis=1, concat_axis=2, tiled=True
        ),
        lax.all_to_all(
            d_step_heads.astype(jnp.bfloat16), "seq", split_axis=1, concat_axis=2, tiled=True
        ),
    )
    d_bc_part = lax.psum_scatter(
        d_bc_full.astype(jnp.bfloat16), "seq", scatter_dimension=1, tiled=True
    )
    d_project = jnp.concatenate(
        [d_gate_part.astype(jnp.bfloat16), d_x_part, d_bc_part, d_step_part], axis=2
    )
    d_normed = jnp.einsum("mtf,df->mtd", d_project, full_in, preferred_element_type=jnp.float32)
    d_hidden_f, d_norm_gain = pull_pre(d_normed)
    d_hidden = (cotangent.astype(jnp.float32) + d_hidden_f).astype(jnp.bfloat16)
    in_rows = in_weight.shape[0]
    out_rows = out_weight.shape[0]
    column_ranges = ((0, DI), (DI, d_project.shape[2]))
    in_pieces = [jnp.zeros((in_rows, upper - lower), jnp.float32) for lower, upper in column_ranges]
    grad_out = jnp.zeros(out_weight.shape, jnp.float32)
    for batch_index in range(hidden.shape[0]):
        for range_index in range(len(column_ranges)):
            lower, upper = column_ranges[range_index]

            def in_term(
                start,
                count,
                normed_one=normed[batch_index],
                d_one=d_project[batch_index, :, lower:upper],
            ):
                return lax.dot_general(
                    normed_one, d_one, (((0,), (0,)), ((), ())), preferred_element_type=jnp.float32
                )

            in_pieces[range_index] = in_pieces[range_index] + lax.psum_scatter(
                in_term(jnp.int32(0), in_rows * lax.axis_size(("dp", "seq"))),
                ("dp", "seq"),
                scatter_dimension=0,
                tiled=True,
            )

        def out_term(start, count, gated_one=gated[batch_index], cot_one=cotangent[batch_index]):
            return lax.dot_general(
                gated_one, cot_one, (((0,), (0,)), ((), ())), preferred_element_type=jnp.float32
            )

        grad_out = grad_out + lax.psum_scatter(
            out_term(jnp.int32(0), out_rows * lax.axis_size(("dp", "seq"))),
            ("dp", "seq"),
            scatter_dimension=0,
            tiled=True,
        )
    grad_in = jnp.concatenate(in_pieces, axis=1)
    d_kernel_x, d_offset_x, d_kernel_bc, d_offset_bc, d_shift, d_decay, d_skip_part = d_params
    tap_count = conv_weight.shape[1]
    grad_conv_w = jnp.concatenate(
        [
            lax.dynamic_update_slice_in_dim(
                jnp.zeros((DI, tap_count), jnp.float32), d_kernel_x, seq_rank * chan_local, 0
            ),
            d_kernel_bc,
        ],
        axis=0,
    )
    grad_conv_b = jnp.concatenate(
        [
            lax.dynamic_update_slice_in_dim(
                jnp.zeros((DI,), jnp.float32), d_offset_x, seq_rank * chan_local, 0
            ),
            d_offset_bc,
        ],
        axis=0,
    )
    grad_shift = lax.dynamic_update_slice_in_dim(
        jnp.zeros((HEADS,), jnp.float32), d_shift, seq_rank * head_local, 0
    )
    grad_decay = lax.dynamic_update_slice_in_dim(
        jnp.zeros((HEADS,), jnp.float32), d_decay, seq_rank * head_local, 0
    )
    grad_skip = lax.dynamic_update_slice_in_dim(
        jnp.zeros((HEADS,), jnp.float32), d_skip_part, seq_rank * head_local, 0
    )
    totals = lax.psum(
        (grad_conv_w, grad_conv_b, grad_shift, grad_decay, grad_skip, d_norm_gain, d_gate_gain),
        ("dp", "seq"),
    )
    return (
        result,
        d_hidden,
        grad_in,
        totals[0],
        totals[1],
        totals[2],
        totals[3],
        totals[4],
        totals[5],
        totals[6],
        grad_out,
    )


LOG2E = 1.4426950408889634
TILE = 128
FAR = -1e30


def shift_rows(v, lag):
    return v if lag == 0 else pltpu.roll(v, lag % v.shape[0], axis=0)


def conv_silu(sig, taps, offset, keep):
    total = offset + taps[CONV - 1 : CONV] * sig
    for lag in range(1, CONV):
        total = total + taps[CONV - 1 - lag : CONV - lag] * (shift_rows(sig, lag) * keep[lag])
    gate = jax.nn.sigmoid(total)
    return total, gate, total * gate


def conv_back(d_out, total, gate, sig, taps, keep):
    d_total = d_out * (gate * (1.0 + total * (1.0 - gate)))
    d_sig = taps[CONV - 1 : CONV] * d_total
    tap_rows = [jnp.sum(d_total * sig, axis=0, keepdims=True)]
    for lag in range(1, CONV):
        kept = d_total * keep[lag]
        d_sig = d_sig + taps[CONV - 1 - lag : CONV - lag] * shift_rows(kept, -lag)
        tap_rows.append(jnp.sum(kept * shift_rows(sig, lag), axis=0, keepdims=True))
    return d_sig, tap_rows[::-1], jnp.sum(d_total, axis=0, keepdims=True)


def keep_masks(seg_col):
    length = seg_col.shape[0]
    row = lax.broadcasted_iota(jnp.int32, (length, 1), 0)
    masks = [None]
    for lag in range(1, CONV):
        same = (pltpu.roll(seg_col, lag, axis=0) == seg_col) & (row >= lag)
        masks.append(same.astype(jnp.float32))
    return masks


def lane_sums(v, reverse):
    length = v.shape[1]
    lane = lax.broadcasted_iota(jnp.int32, v.shape, 1)
    step = 1
    while step < length:
        if reverse:
            v = v + jnp.where(lane < length - step, pltpu.roll(v, length - step, axis=1), 0.0)
        else:
            v = v + jnp.where(lane >= step, pltpu.roll(v, step, axis=1), 0.0)
        step *= 2
    return v


def step_sizes_of(dt_all, head_rows, h_own, n_seq, heads_row):
    rank = lax.axis_index("seq")
    all_heads = dt_all.shape[1]
    lane = lax.broadcasted_iota(jnp.int32, (all_heads, 128), 1)
    row = lax.broadcasted_iota(jnp.int32, (all_heads, 128), 0)
    head = ((lane // heads_row) * n_seq + rank) * heads_row + lane % heads_row
    pick = ((row == head) & (lane < h_own)).astype(jnp.bfloat16)
    raw = jnp.dot(dt_all, pick, preferred_element_type=jnp.float32)
    shifted = raw + head_rows[0:1]
    dt = jnp.maximum(shifted, 0.0) + jnp.log1p(jnp.exp(-jnp.abs(shifted)))
    return shifted, dt


MESH = pl.DeviceIdType.MESH
WIDE = 8


def place():
    dp, s = lax.axis_index("dp"), lax.axis_index("seq")
    z, x = s // 2, s % 2
    y, core = dp // 2, dp % 2
    return dp, s, z, x, s + 1 - 2 * x, dp + 2 - 4 * y, dp + 1 - 2 * core


def greet(peers):
    barrier = pltpu.get_barrier_semaphore()
    for device in peers:
        pl.semaphore_signal(barrier, inc=1, device_id=device, device_id_type=MESH)


def greeted(peers):
    pl.semaphore_wait(pltpu.get_barrier_semaphore(), len(peers))


def remote(src, dst, send, recv, device):
    return pltpu.make_async_remote_copy(
        src_ref=src, dst_ref=dst, send_sem=send, recv_sem=recv, device_id=device, device_id_type=MESH
    )


class TokenGather:
    def __init__(self, full, send, recv, where):
        self.full, self.send, self.recv = full, send, recv
        self.dp, self.s, self.z, self.x, self.x_peer, _, _ = where
        self.span = full.shape[1] // 8

    def part(self, shard, q):
        return self.full.at[q, pl.ds(pl.multiple_of(shard * self.span, self.span), self.span)]

    def copy(self, shard_z, way, q):
        shard = shard_z * 2 + self.x
        target = (self.s + 2, self.s - 2, self.x_peer)[way]
        part = self.part(shard, q)
        return remote(part, part, self.send.at[way, shard_z, q], self.recv.at[shard, q], (self.dp, target))

    def arrived(self, shard, q):
        part = self.part(shard, q)
        remote(part, part, self.send.at[0, 0, q], self.recv.at[shard, q], (self.dp, self.x_peer)).wait_recv()

    def start(self, q):
        @pl.when(self.z < 3)
        def up():
            self.copy(self.z, 0, q).start()

        @pl.when(self.z > 0)
        def down():
            self.copy(self.z, 1, q).start()

        self.copy(self.z, 2, q).start()

    def step(self, hop, q):
        @pl.when(self.z >= hop)
        def from_below():
            shard_z = self.z - hop
            self.arrived(shard_z * 2 + self.x, q)

            @pl.when(self.z < 3)
            def up():
                self.copy(shard_z, 0, q).start()

            self.copy(shard_z, 2, q).start()

        @pl.when(self.z + hop <= 3)
        def from_above():
            shard_z = self.z + hop
            self.arrived(shard_z * 2 + self.x, q)

            @pl.when(self.z > 0)
            def down():
                self.copy(shard_z, 1, q).start()

            self.copy(shard_z, 2, q).start()

    def arrive_x(self, q):
        for shard_z in range(4):
            self.arrived(shard_z * 2 + 1 - self.x, q)

    def settle(self, q):
        for shard_z in range(4):
            self.copy(shard_z, 2, q).wait_send()

            @pl.when((self.z < 3) & (self.z >= shard_z))
            def up():
                self.copy(shard_z, 0, q).wait_send()

            @pl.when((self.z > 0) & (self.z <= shard_z))
            def down():
                self.copy(shard_z, 1, q).wait_send()


def column_of(mat, index):
    return pltpu.roll(mat, (128 - index) % 128, axis=1)[:, :1]


def pair_lanes(mat, pair):
    lane = lax.broadcasted_iota(jnp.int32, (mat.shape[0], 128), 1)
    return jnp.where(lane < HDIM, column_of(mat, 2 * pair), column_of(mat, 2 * pair + 1))


def load_params(rank, conv_t, conv_b, dt_bias, a_log, d_skip, wx, wbc, heads):
    lane = lax.broadcasted_iota(jnp.int32, (1, 128), 1)
    bias_row, log_row = jnp.zeros((1, 128), jnp.float32), jnp.zeros((1, 128), jnp.float32)
    wx[...] = jnp.zeros(wx.shape, jnp.float32)
    wbc[...] = jnp.zeros(wbc.shape, jnp.float32)
    heads[...] = jnp.zeros(heads.shape, jnp.float32)
    for d in range(wx.shape[1] // 128):
        cols, own = pl.ds(pl.multiple_of((d * 8 + rank) * 128, 128), 128), slice(d * 128, (d + 1) * 128)
        head = (d * 8 + rank) * 2
        wx[0:CONV, own] = conv_t[:, cols]
        wx[CONV : CONV + 1, own] = conv_b[cols].reshape(1, 128)
        wx[CONV + 1 : CONV + 2, own] = jnp.where(lane < HDIM, d_skip[head], d_skip[head + 1])
        for half in range(2):
            bias_row = jnp.where(lane == 2 * d + half, dt_bias[head + half], bias_row)
            log_row = jnp.where(lane == 2 * d + half, a_log[head + half], log_row)
    wbc[0:CONV] = conv_t[:, DI:]
    wbc[CONV : CONV + 1] = conv_b[pl.ds(DI, 2 * NST)].reshape(1, 2 * NST)
    heads[0:1] = bias_row
    heads[1:2] = log_row


def head_mats(dt_all, heads, h_own, dt_mat, cum_mat, cum_rows):
    shifted, dt = step_sizes_of(dt_all, heads, h_own, 8, 2)
    rates = -jnp.exp(heads[1:2])
    across = jnp.transpose(dt * (rates * LOG2E))
    cum_t = lane_sums(across[:h_own], False)
    pad = jnp.zeros((128 - h_own, cum_t.shape[1]), jnp.float32)
    dt_mat[...] = dt
    cum_mat[...] = jnp.transpose(jnp.concatenate([cum_t, pad], axis=0))
    for k in range(h_own):
        cum_rows[k] = cum_t[k : k + 1, :]


def mask_rows(bias, seg_col, seg_row, source_first):
    length = bias.shape[0]
    for block in range(length // TILE):
        rows = slice(block * TILE, (block + 1) * TILE)
        down = lax.broadcasted_iota(jnp.int32, (TILE, length), 0) + block * TILE
        over = lax.broadcasted_iota(jnp.int32, (TILE, length), 1)
        past = down <= over if source_first else over <= down
        bias[rows] = jnp.where(past & (seg_col[rows] == seg_row), 0.0, FAR)


def convolve_bc(bc_ref, wbc, keep):
    out = []
    for part in range(2):
        lanes = slice(part * NST, (part + 1) * NST)
        _, _, values = conv_silu(
            bc_ref[:, lanes].astype(jnp.float32), wbc[0:CONV, lanes], wbc[CONV : CONV + 1, lanes], keep
        )
        out.append(values.astype(jnp.bfloat16))
    return out


def forward_prepare(h_own, bc_ref, dt_ref, seg_col, seg_row, wbc, heads, dt_mat, cum_mat, cum_rows, inner_prod, bias):
    length = bc_ref.shape[0]
    keep = keep_masks(seg_col)
    head_mats(dt_ref[...], heads[...], h_own, dt_mat, cum_mat, cum_rows)
    bc = convolve_bc(bc_ref, wbc, keep)
    inner_prod[...] = lax.dot_general(bc[1], bc[0], (((1,), (1,)), ((), ())), preferred_element_type=jnp.float32)
    mask_rows(bias, seg_col, seg_row, False)


def forward_pair(pair, x_ref, seg_col, wx_ref, y_ref, inner_ref, dt_mat, cum_mat, cum_rows, inner_prod, bias):
    length = x_ref.shape[0]
    keep = keep_masks(seg_col)
    _, _, xc = conv_silu(x_ref[...].astype(jnp.float32), wx_ref[0:CONV], wx_ref[CONV : CONV + 1], keep)
    moved = (xc * pair_lanes(dt_mat[...], pair)).astype(jnp.bfloat16)
    skip = wx_ref[CONV + 1 : CONV + 2]
    first = lax.broadcasted_iota(jnp.int32, (TILE, 128), 1) < HDIM
    cum = [column_of(cum_mat[...], 2 * pair + half) for half in range(2)]
    for block in range(length // TILE):
        rows, wide = slice(block * TILE, (block + 1) * TILE), (block + 1) * TILE
        halves = []
        for half in range(2):
            decay = jnp.exp2(cum[half][rows] - cum_rows[2 * pair + half, :, :wide] + bias[rows, :wide])
            scores = (inner_prod[rows, :wide] * decay).astype(jnp.bfloat16)
            halves.append(jnp.dot(scores, moved[:wide], preferred_element_type=jnp.float32))
        inner = jnp.where(first, halves[0], halves[1])
        inner_ref[rows] = inner
        y_ref[rows] = (inner + skip * xc[rows]).astype(jnp.bfloat16)


def ahead_kernel(hidden, cot, in_w, out_w, seg_in, conv_t, conv_b, norm_gain, gate_gain, dt_bias, a_log, d_skip,
                 n_all, c_all, w_in, w_out, x_out, bc_raw, dt_raw, inner_out, gated_out, d_y_out, d_z_out, seg_col, seg_row,
                 wx, wbc, heads, gain_back,
                 seg, in_tail, tok_v, cot_v, w_in_v, w_out_v, z_v, y_v, dg, seg_all, dt_mat, cum_mat, cum_rows, inner_prod, bias,
                 sum_cols, sums, x_raw, inner, gated, d_y, d_z,
                 n_send, n_recv, c_send, c_recv, wide_send, tail_send, wide_recv, tail_recv,
                 y_send, core_send, cross_send, block_recv, out_send, out_recv, seg_send, seg_recv, store,
                 sum_send, sum_recv):
    f32, bf16 = jnp.float32, jnp.bfloat16
    where = place()
    dp, s, z, x, x_peer, y_peer, core_peer = where
    peers = [(dp, (s + k) % 8) for k in range(1, 8)] + [(y_peer, s), (core_peer, s)]
    greet(peers)
    in_rows, rows = in_w.shape[0], out_w.shape[0]
    chan = w_out.shape[0]
    h_own = chan // HDIM
    tail = in_tail.shape[1]
    n_own, length, width = n_all.shape
    in_tail[...] = jnp.zeros(in_tail.shape, bf16)
    in_tail[:, : in_w.shape[1] - 2 * DI] = in_w[:, 2 * DI :]
    seg[...] = jnp.zeros(seg.shape, f32)
    seg[:n_own, : seg_in.shape[1]] = seg_in[...].astype(f32)

    def block(d, shard, lo=0, size=None):
        size = w_in_v.shape[1] if size is None else size
        at = pl.multiple_of((d * 8 + shard) * in_rows, in_rows)
        return w_in_v.at[pl.ds(at, in_rows), pl.ds(lo, size)]

    def wide_src(piece, target):
        at = pl.multiple_of((piece * 8 + target) * rows, rows)
        return in_w.at[:, pl.ds(at, rows)]

    def push(k, _):
        target = (s + k) % 8
        remote(seg, seg_all.at[s], seg_send.at[k], seg_recv.at[s], (dp, target)).start()
        for piece in range(WIDE):
            remote(
                wide_src(piece, target), block(dp, s, piece * rows, rows), wide_send.at[k], wide_recv.at[s],
                (dp, target),
            ).start()
        remote(in_tail, block(dp, s, 2 * chan, tail), tail_send.at[k], tail_recv.at[s], (dp, target)).start()
        return 0

    span = hidden.shape[1]
    own_tokens = pl.ds(pl.multiple_of(s * span, span), span)
    for q in range(n_own):
        h = hidden[q].astype(f32)
        inv = lax.rsqrt(jnp.mean(h * h, axis=-1, keepdims=True) + 1e-05)
        tok_v[q, own_tokens] = (h * inv * norm_gain[...]).astype(bf16)
    tokens = TokenGather(tok_v, n_send, n_recv, where)
    cots = TokenGather(cot_v, c_send, c_recv, where)
    seg_all[s] = seg[...]
    own_rows = pl.ds(pl.multiple_of((dp * 8 + s) * in_rows, in_rows), in_rows)
    for piece in range(WIDE):
        at = pl.multiple_of((piece * 8 + s) * rows, rows)
        w_in_v[own_rows, piece * rows : (piece + 1) * rows] = in_w[:, pl.ds(at, rows)]
    w_in_v[own_rows, 2 * chan :] = in_tail[...]

    def out_part(d):
        return w_out_v.at[pl.ds(pl.multiple_of(d * rows, rows), rows)]

    w_out_v[pl.ds(pl.multiple_of(dp * rows, rows), rows)] = out_w[...]
    out_y = remote(out_part(dp), out_part(dp), out_send.at[0], out_recv.at[dp], (y_peer, s))
    out_core = remote(out_part(dp), out_part(dp), out_send.at[1], out_recv.at[dp], (core_peer, s))
    for q in range(n_own):
        cot_v[q, own_tokens] = cot[q]
    greeted(peers)
    tokens.start(0)
    tokens.start(1)
    out_y.start()
    out_core.start()
    lax.fori_loop(1, 8, push, 0)

    def spread(shard, k):
        there = block(dp, shard)
        remote(there, there, y_send.at[k], block_recv.at[dp, shard], (y_peer, s)).start()
        remote(there, there, core_send.at[k], block_recv.at[dp, shard], (core_peer, s)).start()

    spread(s, 0)
    load_params(s, conv_t, conv_b, dt_bias, a_log, d_skip, wx, wbc, heads)

    def wide_copy(source, k):
        there = block(dp, source, 0, 2 * chan)
        return remote(there, there, wide_send.at[k], wide_recv.at[source], (dp, x_peer))

    def tail_copy(source, k):
        there = block(dp, source, 2 * chan, tail)
        return remote(there, there, tail_send.at[k], tail_recv.at[source], (dp, x_peer))

    def forward(k, _):
        source = (s + 8 - k) % 8
        wide_copy(source, k).wait_recv()
        tail_copy(source, k).wait_recv()
        spread(source, k)
        return 0

    def cross(k, _):
        source = (s + 8 - k) % 8
        there = block(y_peer, source)
        copy = remote(there, there, cross_send.at[k], block_recv.at[y_peer, source], (core_peer, s))
        copy.wait_recv()
        copy.start()
        return 0

    tokens.step(1, 0)
    tokens.step(1, 1)
    cots.start(0)
    lax.fori_loop(1, 4, forward, 0)
    tokens.step(2, 0)
    tokens.step(2, 1)
    cots.start(1)
    lax.fori_loop(4, 8, forward, 0)
    tokens.step(3, 0)
    tokens.step(3, 1)
    cots.step(1, 0)
    lax.fori_loop(0, 4, cross, 0)
    cots.step(1, 1)
    lax.fori_loop(4, 8, cross, 0)

    def arrive(k, _):
        source = (s + 8 - k) % 8
        for d in (core_peer, core_peer + y_peer - dp):
            there = block(d, source)
            remote(there, there, core_send.at[k], block_recv.at[d, source], (core_peer, s)).wait_recv()
        return 0

    lax.fori_loop(0, 8, arrive, 0)
    stores = [pltpu.make_async_copy(w_in_v, w_in, store.at[0])]
    stores[0].start()

    def keep_for_later(q, *pairs):
        at = pl.ds(q * length, length)
        for held, there in pairs:
            stores.append(pltpu.make_async_copy(held.at[at], there.at[at], store.at[5 + len(stores)]))
            stores[-1].start()

    def segments_in(k, _):
        source = (s + 8 - k) % 8
        remote(seg, seg_all.at[source], seg_send.at[k], seg_recv.at[source], (dp, x_peer)).wait_recv()
        return 0

    lax.fori_loop(1, 8, segments_in, 0)
    lane = lax.broadcasted_iota(jnp.int32, (1, 128), 1)
    for q in range(n_own):
        pieces = [
            jnp.where(lane < 64, seg_all[2 * m, q : q + 1], pltpu.roll(seg_all[2 * m + 1, q : q + 1], 64, axis=1))
            for m in range(4)
        ]
        row = jnp.concatenate(pieces, axis=1)
        seg_row[q] = row
        seg_col[q] = jnp.transpose(jnp.broadcast_to(row, (128, length)))[:, :1]

    def project(q):
        at = slice(q * length, (q + 1) * length)
        half = chan // 2

        @pl.loop(0, 2)
        def gates(n):
            cols = pl.ds(pl.multiple_of(n * half, half), half)
            z_v[at, cols] = jnp.dot(tok_v[q], w_in_v[:, cols], preferred_element_type=f32)

        @pl.loop(0, 2)
        def values(n):
            cols = pl.ds(pl.multiple_of(n * half, half), half)
            from_cols = pl.ds(pl.multiple_of(chan + n * half, half), half)
            x_raw[at, cols] = jnp.dot(tok_v[q], w_in_v[:, from_cols], preferred_element_type=f32).astype(bf16)

        last = jnp.dot(tok_v[q], w_in_v[:, 2 * chan :], preferred_element_type=f32).astype(bf16)
        bc_raw[at] = last[:, : 2 * NST]
        dt_raw[at] = last[:, 2 * NST :]

    for q in range(n_own):
        tokens.arrive_x(q)
        stores.append(pltpu.make_async_copy(tok_v.at[q], n_all.at[q], store.at[1 + q]))
        stores[-1].start()
        project(q)
        keep_for_later(q, (x_raw, x_out))
        cots.step(2, q)

    for q in range(n_own):
        at = pl.ds(q * length, length)
        forward_prepare(
            h_own, bc_raw.at[at], dt_raw.at[at], seg_col[q], seg_row[q], wbc, heads,
            dt_mat, cum_mat, cum_rows, inner_prod, bias,
        )

        @pl.loop(0, chan // 128)
        def pairs(pair):
            cols = pl.ds(pl.multiple_of(pair * 128, 128), 128)
            forward_pair(
                pair, x_raw.at[at, cols], seg_col[q], wx.at[:, cols], y_v.at[at, cols], inner.at[at, cols],
                dt_mat, cum_mat, cum_rows, inner_prod, bias,
            )

            if q == 0:

                @pl.when(pair == 0)
                def hook_0_0():
                    cots.step(3, 0)

            if q == 0:

                @pl.when(pair == 2)
                def hook_0_2():
                    cots.step(3, 1)

    for q in range(n_own):
        keep_for_later(q, (inner, inner_out))
    out_cross = remote(out_part(y_peer), out_part(y_peer), out_send.at[2], out_recv.at[y_peer], (core_peer, s))
    out_cross.wait_recv()
    out_cross.start()
    for d in (core_peer, core_peer + y_peer - dp):
        remote(out_part(d), out_part(d), out_send.at[0], out_recv.at[d], (core_peer, s)).wait_recv()
    stores.append(pltpu.make_async_copy(w_out_v, w_out, store.at[3]))
    stores[-1].start()
    gain = jnp.concatenate(
        [gate_gain[:, pl.ds(pl.multiple_of((d * 8 + s) * 128, 128), 128)] for d in range(chan // 128)], axis=1
    )
    lane_wide = lax.broadcasted_iota(jnp.int32, (TILE, 128), 1)

    def sum_copy(q, k):
        return remote(
            sums.at[q, s], sums.at[q, s], sum_send.at[q, k], sum_recv.at[q, s], (dp, (s + k) % 8)
        )

    def gate(q):
        for k in range(1, 8):
            source = (s + 8 - k) % 8
            remote(
                sums.at[q, source], sums.at[q, source], sum_send.at[q, k], sum_recv.at[q, source], (dp, x_peer)
            ).wait_recv()
        total = sums[q, 0]
        for source in range(1, 8):
            total = total + sums[q, source]
        total = jnp.concatenate([total, jnp.zeros((120, length), f32)], axis=0)
        sum_cols[...] = jnp.transpose(total)

        @pl.loop(0, length // TILE)
        def gate_rows(n):
            at = pl.ds(pl.multiple_of(q * length + n * TILE, TILE), TILE)
            both = sum_cols[pl.ds(pl.multiple_of(n * TILE, TILE), TILE)]
            r = lax.rsqrt(both[:, 0:1] / DI + 1e-05)
            fall = (r * r * r) * (both[:, 1:2] / DI)
            zz = z_v[at]
            sig = jax.nn.sigmoid(zz)
            act = zz * sig
            yy = y_v[at].astype(f32)
            g = yy * act
            gr = g * r
            back = dg[at]
            d_g = r * (back * gain) - fall * g
            gated[at] = (gr * gain).astype(bf16)
            d_y[at] = (d_g * act).astype(bf16)
            d_z[at] = (d_g * yy * (sig * (1.0 + zz * (1.0 - sig)))).astype(bf16)
            gain_back[0:1] += jnp.sum(back * gr, axis=0, keepdims=True)

    gain_back[...] = jnp.zeros(gain_back.shape, f32)
    for q in range(n_own):
        if q == 1:
            gate(0)
            keep_for_later(0, (gated, gated_out), (d_y, d_y_out), (d_z, d_z_out))
        cots.arrive_x(q)
        stores.append(pltpu.make_async_copy(cot_v.at[q], c_all.at[q], store.at[4 + q]))
        stores[-1].start()
        half = chan // 2

        @pl.loop(0, 2)
        def back(n):
            cols = pl.ds(pl.multiple_of(n * half, half), half)
            dg[q * length : (q + 1) * length, cols] = lax.dot_general(
                cot_v[q], w_out_v[cols], (((1,), (1,)), ((), ())), preferred_element_type=f32
            )

        @pl.loop(0, length // TILE)
        def reduce_rows(n):
            at = pl.ds(pl.multiple_of(q * length + n * TILE, TILE), TILE)
            zz = z_v[at]
            g = y_v[at].astype(f32) * (zz * jax.nn.sigmoid(zz))
            first = jnp.sum(g * g, axis=1, keepdims=True)
            second = jnp.sum(dg[at] * gain * g, axis=1, keepdims=True)
            sum_cols[pl.ds(pl.multiple_of(n * TILE, TILE), TILE)] = jnp.where(
                lane_wide == 0, first, jnp.where(lane_wide == 1, second, 0.0)
            )

        sums[q, s] = jnp.transpose(sum_cols[...])[:8]
        for k in range(1, 8):
            sum_copy(q, k).start()

    gate(1)
    keep_for_later(1, (gated, gated_out), (d_y, d_y_out), (d_z, d_z_out))

    for q in range(n_own):
        tokens.settle(q)
        cots.settle(q)
        for k in range(1, 8):
            sum_copy(q, k).wait_send()

    def settle(k, _):
        shard = (s + 8 - k) % 8
        there = block(dp, shard)
        remote(there, there, y_send.at[k], block_recv.at[dp, shard], (y_peer, s)).wait_send()
        remote(there, there, core_send.at[k], block_recv.at[dp, shard], (core_peer, s)).wait_send()
        remote(there, there, cross_send.at[k], block_recv.at[dp, shard], (core_peer, s)).wait_send()
        return 0

    lax.fori_loop(0, 8, settle, 0)

    def settle_push(k, _):
        source = (s + 8 - k) % 8
        remote(seg, seg_all.at[source], seg_send.at[k], seg_recv.at[source], (dp, x_peer)).wait_send()
        wide_copy(source, k).wait_send()
        tail_copy(source, k).wait_send()
        return 0

    lax.fori_loop(1, 8, settle_push, 0)
    out_y.wait_send()
    out_core.wait_send()
    out_cross.wait_send()
    for copy in stores:
        copy.wait()


def run_ahead(hidden, cot, in_w, out_w, seg, conv_t, conv_b, norm_gain, gate_gain, dt_bias, a_log, d_skip):
    f32, bf16 = jnp.float32, jnp.bfloat16
    n_own, span, width = hidden.shape
    in_rows, rows = in_w.shape[0], out_w.shape[0]
    chan, length = 4 * rows, 8 * span
    tokens, h_own = n_own * length, chan // HDIM
    columns = 2 * chan + 2 * NST + 128
    sem, vmem = pltpu.SemaphoreType.DMA, pltpu.VMEM
    anywhere, inside = pl.BlockSpec(memory_space=pl.ANY), pl.BlockSpec(memory_space=vmem)
    scalars = pl.BlockSpec(memory_space=pltpu.SMEM)
    shape = jax.ShapeDtypeStruct
    return pl.pallas_call(
        ahead_kernel,
        in_specs=[inside] * 9 + [scalars] * 3,
        out_specs=[anywhere] * 5 + [inside] * 2 + [anywhere] * 4 + [inside] * 6,
        out_shape=[
            shape((n_own, length, width), bf16),
            shape((n_own, length, width), bf16),
            shape((32 * in_rows, columns), bf16),
            shape((chan, width), bf16),
            shape((tokens, chan), bf16),
            shape((tokens, 2 * NST), bf16),
            shape((tokens, 128), bf16),
            shape((tokens, chan), f32),
            shape((tokens, chan), bf16),
            shape((tokens, chan), bf16),
            shape((tokens, chan), bf16),
            shape((n_own, length, 1), f32),
            shape((n_own, 1, length), f32),
            shape((8, chan), f32),
            shape((8, 2 * NST), f32),
            shape((8, 128), f32),
            shape((8, chan), f32),
        ],
        scratch_shapes=[
            vmem((8, 128), f32),
            vmem((in_rows, 2 * NST + 128), bf16),
            vmem((n_own, length, width), bf16),
            vmem((n_own, length, width), bf16),
            vmem((width, columns), bf16),
            vmem((chan, width), bf16),
            vmem((tokens, chan), f32),
            vmem((tokens, chan), bf16),
            vmem((tokens, chan), f32),
            vmem((8, 8, 128), f32),
            vmem((length, 128), f32),
            vmem((length, 128), f32),
            vmem((h_own, 1, length), f32),
            vmem((length, length), f32),
            vmem((length, length), f32),
            vmem((length, 128), f32),
            vmem((n_own, 8, 8, length), f32),
            vmem((tokens, chan), bf16),
            vmem((tokens, chan), f32),
            vmem((tokens, chan), bf16),
            vmem((tokens, chan), bf16),
            vmem((tokens, chan), bf16),
            sem((3, 4, 2)), sem((8, 2)), sem((3, 4, 2)), sem((8, 2)),
            sem((8,)), sem((8,)), sem((8,)), sem((8,)),
            sem((8,)), sem((8,)), sem((8,)), sem((4, 8)), sem((3,)), sem((4,)), sem((8,)), sem((8,)),
            sem((24,)), sem((2, 8)), sem((2, 8)),
        ],
        compiler_params=pltpu.CompilerParams(collective_id=0, has_side_effects=True, vmem_limit_bytes=56 << 20),
        name="ahead",
    )(hidden, cot, in_w, out_w, seg, conv_t, conv_b, norm_gain, gate_gain, dt_bias, a_log, d_skip)


def backward_prepare(h_own, bc_ref, dt_ref, seg_col, seg_row, wbc, heads, dt_mat, cum_mat, cum_rows, inner_prod, bias,
                     d_inner, d_cum, d_dt):
    length = bc_ref.shape[0]
    keep = keep_masks(seg_col)
    head_mats(dt_ref[...], heads[...], h_own, dt_mat, cum_mat, cum_rows)
    bc = convolve_bc(bc_ref, wbc, keep)
    inner_prod[...] = lax.dot_general(bc[0], bc[1], (((1,), (1,)), ((), ())), preferred_element_type=jnp.float32)
    mask_rows(bias, seg_col, seg_row, True)
    d_inner[...] = jnp.zeros((length, length), jnp.float32)
    d_cum[...] = jnp.zeros((length, 128), jnp.float32)
    d_dt[...] = jnp.zeros((length, 128), jnp.float32)


def backward_pair(pair, x_ref, seg_col, wx_ref, dy_ref, inner_ref, dx_ref, gx_ref, dt_mat, cum_mat, cum_rows,
                  inner_prod, bias, d_inner, d_cum, d_dt):
    f32, bf16 = jnp.float32, jnp.bfloat16
    length = x_ref.shape[0]
    keep = keep_masks(seg_col)
    x_in = x_ref[...].astype(f32)
    taps = wx_ref[0:CONV]
    total, gate, xc = conv_silu(x_in, taps, wx_ref[CONV : CONV + 1], keep)
    dt_wide = pair_lanes(dt_mat[...], pair)
    moved = (xc * dt_wide).astype(bf16)
    skip = wx_ref[CONV + 1 : CONV + 2]
    dy = dy_ref[...]
    first = lax.broadcasted_iota(jnp.int32, (TILE, 128), 1) < HDIM
    cum = [column_of(cum_mat[...], 2 * pair + half) for half in range(2)]
    pieces = []
    for block in range(length // TILE):
        rows, later = slice(block * TILE, (block + 1) * TILE), slice(block * TILE, length)
        halves = []
        for half in range(2):
            decay = jnp.exp2(cum_rows[2 * pair + half, :, later] - cum[half][rows] + bias[rows, later])
            scores = (inner_prod[rows, later] * decay).astype(bf16)
            halves.append(jnp.dot(scores, dy[later], preferred_element_type=f32))
            mine = jnp.where(first if half == 0 else ~first, moved[rows].astype(f32), 0.0).astype(bf16)
            d_scores = lax.dot_general(mine, dy[later], (((1,), (1,)), ((), ())), preferred_element_type=f32)
            d_inner[rows, later] += d_scores * decay
        pieces.append(jnp.where(first, halves[0], halves[1]))
    d_moved = jnp.concatenate(pieces, axis=0)
    dy_f = dy.astype(f32)
    change = dy_f * inner_ref[...] - moved.astype(f32) * d_moved
    direct = d_moved * xc
    lane = lax.broadcasted_iota(jnp.int32, (length, 128), 1)
    low = lane < HDIM
    for half in range(2):
        mine = low if half == 0 else ~low
        spot = lane == 2 * pair + half
        d_cum[...] += jnp.where(spot, jnp.sum(jnp.where(mine, change, 0.0), axis=1, keepdims=True), 0.0)
        d_dt[...] += jnp.where(spot, jnp.sum(jnp.where(mine, direct, 0.0), axis=1, keepdims=True), 0.0)
    d_xc = d_moved * dt_wide + skip * dy_f
    d_x, tap_rows, d_offset = conv_back(d_xc, total, gate, x_in, taps, keep)
    dx_ref[...] = d_x.astype(bf16)
    d_skip = jnp.sum(dy_f * xc, axis=0, keepdims=True)
    gx_ref[...] += jnp.concatenate(tap_rows + [d_offset, d_skip, jnp.zeros((2, 128), f32)], axis=0)


def backward_finish(h_own, bc_ref, dt_ref, seg_col, wbc, heads, d_inner, d_cum, d_dt, dbc_ref, ddt_ref, gbc_ref, gh_ref):
    f32, bf16 = jnp.float32, jnp.bfloat16
    length = bc_ref.shape[0]
    keep = keep_masks(seg_col)
    bc = convolve_bc(bc_ref, wbc, keep)
    d_in = d_inner[...].astype(bf16)
    for part in range(2):
        lanes = slice(part * NST, (part + 1) * NST)
        side = 1 - part
        d_value = lax.dot_general(d_in, bc[side], (((side,), (0,)), ((), ())), preferred_element_type=f32)
        bc_in = bc_ref[:, lanes].astype(f32)
        taps = wbc[0:CONV, lanes]
        total, gate, _ = conv_silu(bc_in, taps, wbc[CONV : CONV + 1, lanes], keep)
        d_bc, tap_rows, offset = conv_back(d_value, total, gate, bc_in, taps, keep)
        dbc_ref[:, lanes] = d_bc.astype(bf16)
        gbc_ref[:, lanes] += jnp.concatenate(tap_rows + [offset, jnp.zeros((3, NST), f32)], axis=0)
    shifted, dt = step_sizes_of(dt_ref[...], heads[...], h_own, 8, 2)
    rates = -jnp.exp(heads[1:2])
    across = jnp.transpose(d_cum[...])
    d_log_t = lane_sums(across[:h_own], True)
    d_log = jnp.transpose(jnp.concatenate([d_log_t, jnp.zeros((128 - h_own, length), f32)], axis=0))
    d_raw = (d_log * rates + d_dt[...]) * jax.nn.sigmoid(shifted)
    rank = lax.axis_index("seq")
    row = lax.broadcasted_iota(jnp.int32, (128, 128), 0)
    head = ((row // 2) * 8 + rank) * 2 + row % 2
    pick = ((lax.broadcasted_iota(jnp.int32, (128, 128), 1) == head) & (row < h_own)).astype(bf16)
    ddt_ref[...] = jnp.dot(d_raw.astype(bf16), pick, preferred_element_type=f32).astype(bf16)
    gh_ref[...] += jnp.concatenate(
        [
            jnp.sum(d_raw, axis=0, keepdims=True),
            jnp.sum(d_log * dt, axis=0, keepdims=True) * rates,
            jnp.zeros((6, 128), f32),
        ],
        axis=0,
    )


class TokenReduce:
    def __init__(self, part, from_x, from_near, from_far, x_sems, near_sems, far_sems, where, span):
        self.part, self.from_x, self.from_near, self.from_far = part, from_x, from_near, from_far
        self.x_sems, self.near_sems, self.far_sems, self.span = x_sems, near_sems, far_sems, span
        self.dp, self.s, self.z, self.x, self.x_peer, _, _ = where
        self.near = self.s + 2 - 4 * (self.z % 2)
        self.far = self.s + 4 - 8 * (self.z // 2)

    def rows(self, shard, q):
        return self.part.at[q, pl.ds(pl.multiple_of(shard * self.span, self.span), self.span)]

    def x_copy(self, shard_z, q):
        return remote(
            self.rows(shard_z * 2 + 1 - self.x, q), self.from_x.at[shard_z, q],
            self.x_sems.at[0, shard_z, q], self.x_sems.at[1, shard_z, q], (self.dp, self.x_peer),
        )

    def near_copy(self, high, q):
        shard = (high * 2 + 1 - self.z % 2) * 2 + self.x
        return remote(
            self.rows(shard, q), self.from_near.at[high, q],
            self.near_sems.at[0, high, q], self.near_sems.at[1, high, q], (self.dp, self.near),
        )

    def far_copy(self, q):
        shard = ((1 - self.z // 2) * 2 + self.z % 2) * 2 + self.x
        return remote(
            self.rows(shard, q), self.from_far.at[q], self.far_sems.at[0, q], self.far_sems.at[1, q],
            (self.dp, self.far),
        )

    def start(self, q):
        for turn in range(4):
            self.x_copy(self.turn(turn), q).start()

    def turn(self, turn):
        return (1 - self.z // 2 + turn % 2) % 2 * 2 + (1 - self.z % 2 + turn // 2) % 2

    def add(self, shard, q, other):
        rows = self.rows(shard, q)
        rows[...] = (rows[...].astype(jnp.float32) + other[...].astype(jnp.float32)).astype(jnp.bfloat16)

    def step_near(self, q):
        for turn in range(2):
            high = (1 - self.z // 2 + turn) % 2
            shard_z = high * 2 + 1 - self.z % 2
            self.x_copy(shard_z, q).wait_recv()
            self.add(shard_z * 2 + self.x, q, self.from_x.at[shard_z, q])
            self.near_copy(high, q).start()

    def step_keep(self, q):
        for turn in range(2):
            high = (1 - self.z // 2 + turn) % 2
            shard_z = high * 2 + self.z % 2
            self.x_copy(shard_z, q).wait_recv()
            self.add(shard_z * 2 + self.x, q, self.from_x.at[shard_z, q])

    def step_far(self, q):
        high = 1 - self.z // 2
        self.near_copy(high, q).wait_recv()
        self.add((high * 2 + self.z % 2) * 2 + self.x, q, self.from_near.at[high, q])
        self.far_copy(q).start()

    def total(self, q):
        high = self.z // 2
        self.near_copy(high, q).wait_recv()
        self.far_copy(q).wait_recv()
        f32 = jnp.float32
        return (
            self.rows(self.s, q)[...].astype(f32)
            + self.from_near[high, q].astype(f32)
            + self.from_far[q].astype(f32)
        )

    def settle(self):
        for q in range(2):
            for shard_z in range(4):
                self.x_copy(shard_z, q).wait_send()
            for high in range(2):
                self.near_copy(high, q).wait_send()
            self.far_copy(q).wait_send()


def finish_kernel(gated, w_out, d_z, d_y, x_raw, inner, w_in, cot_all, normed_all,
                  bc_raw, dt_raw, seg_col, seg_row, wx, wbc, heads, gain_back, hidden, cot, gain,
                  result, d_hidden, plane_in, grad_out, small_all, gain_sum,
                  gated_v, w_out_v, dp_v, w_in_v, tok_v, inner_v, dy_v,
                  dt_mat, cum_mat, cum_rows, inner_prod, bias, d_inner, d_cum, d_dt,
                  part_r, rx, rn, rf, part_d, dx, dn, df,
                  core_out, core_in, keep, y_in,
                  out_core_in, out_y, out_y_in, small_v, small_in, gain_v, gain_in,
                  load, rxs, rns, rfs, dxs, dns, dfs, core_sems, y_sems, plane_sems, out_sems, out_y_sems,
                  small_sems, small_plane, gain_sems, gain_plane):
    f32, bf16 = jnp.float32, jnp.bfloat16
    where = place()
    dp, s, z, x, x_peer, y_peer, core_peer = where
    y, core = dp // 2, dp % 2
    n_own, span, width = hidden.shape
    length = 8 * span
    chan = w_out.shape[0]
    rows = chan // 4
    in_rows = plane_in.shape[1]
    columns = keep.shape[3]
    tail = columns - 2 * chan
    peers = [(dp, (s + k) % 8) for k in range(1, 8)] + [(y_peer, s), (core_peer, s)]
    h_own = chan // HDIM

    def scan_loads(q):
        at = pl.ds(q * length, length)
        return [
            pltpu.make_async_copy(inner.at[at], inner_v, load.at[3]),
            pltpu.make_async_copy(d_y.at[at], dy_v, load.at[4]),
        ]

    loads = [
        pltpu.make_async_copy(gated, gated_v, load.at[0]),
        pltpu.make_async_copy(w_out, w_out_v, load.at[1]),
        pltpu.make_async_copy(cot_all, tok_v, load.at[7]),
        pltpu.make_async_copy(w_in, w_in_v, load.at[6]),
        pltpu.make_async_copy(d_z, dp_v.at[:, pl.ds(0, chan)], load.at[5]),
        pltpu.make_async_copy(x_raw, dp_v.at[:, pl.ds(chan, chan)], load.at[2]),
    ]
    first_scan = scan_loads(0)
    for copy in loads[:3] + first_scan + loads[3:]:
        copy.start()
    greet(peers)
    small_v[0] = jnp.zeros(small_v.shape[1:], f32)

    def small_copy(stage, device):
        return remote(small_v.at[stage], small_in.at[stage], small_sems.at[0, stage], small_sems.at[1, stage], device)

    reduce_r = TokenReduce(part_r, rx, rn, rf, rxs, rns, rfs, where, span)
    reduce_d = TokenReduce(part_d, dx, dn, df, dxs, dns, dfs, where, span)
    loads[0].wait()
    loads[1].wait()
    step = 512

    def branch(q):
        @pl.loop(0, width // 256)
        def forward(n):
            cols = pl.ds(pl.multiple_of(n * 256, 256), 256)
            part_r[q, :, cols] = jnp.dot(
                gated_v[q * length : (q + 1) * length], w_out_v[:, cols], preferred_element_type=f32
            ).astype(bf16)

    def first_rows(turn):
        shard_z = reduce_r.turn(turn)
        at = pl.ds(pl.multiple_of(shard_z * 2 * span, 2 * span), 2 * span)
        for half in range(2):
            cols = slice(half * width // 2, (half + 1) * width // 2)
            part_r[0, at, cols] = jnp.dot(gated_v[at], w_out_v[:, cols], preferred_element_type=f32).astype(bf16)
        return shard_z

    first = first_rows(0)
    greeted(peers)
    reduce_r.x_copy(first, 0).start()

    @pl.loop(1, 4)
    def other_rows(turn):
        reduce_r.x_copy(first_rows(turn), 0).start()

    def out_term(d, n):
        lanes = pl.ds(pl.multiple_of(d * rows, rows), rows)
        return lax.dot_general(
            gated_v[:, lanes], tok_v[:, n * step : (n + 1) * step], (((0,), (0,)), ((), ())),
            preferred_element_type=f32,
        )

    def out_core_copy(yy):
        return remote(w_out_v.at[pl.ds(yy * rows, rows)], out_core_in.at[yy], out_sems.at[0, yy], out_sems.at[1, yy], (core_peer, s))

    def out_gradient():
        loads[2].wait()
        for yy in range(2):
            for n in range(width // step):
                w_out_v[yy * rows : (yy + 1) * rows, n * step : (n + 1) * step] = out_term(yy * 2 + 1 - core, n).astype(bf16)
            out_core_copy(yy).start()
        for n in range(width // step):
            out_y[:, n * step : (n + 1) * step] = out_term((1 - y) * 2 + core, n).astype(bf16)
        for n in range(width // step):
            grad_out[:, n * step : (n + 1) * step] = out_term(y * 2 + core, n)
        norm_load.start()

    norm_load = pltpu.make_async_copy(normed_all, tok_v, load.at[8])
    out_y_copy = remote(out_y, out_y_in, out_y_sems.at[0], out_y_sems.at[1], (y_peer, s))
    for q in range(2):
        at = pl.ds(q * length, length)
        scan_in = first_scan if q == 0 else scan_loads(1)
        if q == 1:
            for copy in scan_in:
                copy.start()
        backward_prepare(
            h_own, bc_raw.at[at], dt_raw.at[at], seg_col[q], seg_row[q], wbc, heads,
            dt_mat, cum_mat, cum_rows, inner_prod, bias, d_inner, d_cum, d_dt,
        )
        for copy in scan_in:
            copy.wait()
        if q == 0:
            loads[5].wait()

        @pl.loop(0, chan // 128)
        def pairs(pair):
            cols = pl.ds(pl.multiple_of(pair * 128, 128), 128)
            x_cols = pl.ds(pl.multiple_of(chan + pair * 128, 128), 128)
            backward_pair(
                pair, dp_v.at[at, x_cols], seg_col[q], wx.at[:, cols], dy_v.at[:, cols], inner_v.at[:, cols],
                dp_v.at[at, x_cols], small_v.at[0, :, cols], dt_mat, cum_mat, cum_rows,
                inner_prod, bias, d_inner, d_cum, d_dt,
            )
            if q == 0:

                @pl.when(pair == 3)
                def near_result():
                    reduce_r.step_near(0)
            else:

                @pl.when(pair == 0)
                def far_result():
                    reduce_r.step_far(0)

                @pl.when(pair == 3)
                def near_back():
                    reduce_d.step_near(0)

        backward_finish(
            h_own, bc_raw.at[at], dt_raw.at[at], seg_col[q], wbc, heads, d_inner, d_cum, d_dt,
            dp_v.at[at, pl.ds(2 * chan, 2 * NST)], dp_v.at[at, pl.ds(2 * chan + 2 * NST, 128)],
            small_v.at[0, :, pl.ds(chan, 2 * NST)], small_v.at[0, :, pl.ds(chan + 2 * NST, 128)],
        )
        if q == 0:
            loads[3].wait()
            loads[4].wait()

        @pl.loop(0, width // 256)
        def backward(n):
            cols = pl.ds(pl.multiple_of(n * 256, 256), 256)
            part_d[q, :, cols] = lax.dot_general(
                dp_v[q * length : (q + 1) * length], w_in_v[cols], (((1,), (1,)), ((), ())),
                preferred_element_type=f32,
            ).astype(bf16)

        reduce_d.start(q)
        if q == 0:
            branch(1)
            reduce_r.step_keep(0)

    reduce_r.start(1)
    small_v[0, CONV + 2 : CONV + 3, :chan] = gain_back[0:1]
    small_core = small_copy(0, (core_peer, s))
    small_core.start()

    def small_push(k):
        return remote(
            small_all.at[s], small_all.at[s], small_plane.at[0, k], small_plane.at[1, s], (dp, (s + k) % 8)
        )

    out_gradient()

    def in_term(d, m, lo, size):
        lanes = pl.ds(pl.multiple_of(d * 8 * in_rows + m * 2 * in_rows, 2 * in_rows), 2 * in_rows)
        return lax.dot_general(
            tok_v[:, lanes], dp_v[:, lo : lo + size], (((0,), (0,)), ((), ())), preferred_element_type=f32
        )

    pieces = ((0, chan, chan), (chan, chan, chan), (2 * chan, tail, 2 * NST + 128))

    def core_copy(t, yy):
        return remote(
            core_out.at[t % 2, yy], core_in.at[t, yy], core_sems.at[0, t, yy], core_sems.at[1, t, yy], (core_peer, s)
        )

    def y_copy(t):
        return remote(keep.at[t, 1 - y], y_in.at[t], y_sems.at[0, t], y_sems.at[1, t], (y_peer, s))

    def target_of(t):
        return (z + 1 + t) % 4

    def in_compute(t):
        for yy in range(2):
            if t >= 2:
                core_copy(t - 2, yy).wait_send()
            for lo, size, span_in in pieces:
                core_out[t % 2, yy, :, lo : lo + size] = in_term(yy * 2 + 1 - core, target_of(t), lo, span_in)[
                    :, :size
                ].astype(bf16)
            core_copy(t, yy).start()
        for yy in range(2):
            for lo, size, span_in in pieces:
                keep[t, yy, :, lo : lo + size] = in_term(yy * 2 + core, target_of(t), lo, span_in)[:, :size].astype(bf16)

    def in_core(t):
        for yy in range(2):
            core_copy(t, yy).wait_recv()
            keep[t, yy] = (keep[t, yy].astype(f32) + core_in[t, yy].astype(f32)).astype(bf16)
        y_copy(t).start()

    def half_rows(half):
        return pl.ds(pl.multiple_of(half * in_rows, in_rows), in_rows)

    def plane_copy(t, half):
        return remote(
            keep.at[t, y, half_rows(half)], plane_in.at[s],
            plane_sems.at[0, t, half], plane_sems.at[1, s // 2, s % 2], (dp, 2 * target_of(t) + half),
        )

    def plane_halves(t):
        return (0, 1) if t < 3 else (1 - x,)

    def in_plane(t):
        y_copy(t).wait_recv()
        keep[t, y] = (keep[t, y].astype(f32) + y_in[t].astype(f32)).astype(bf16)
        for half in plane_halves(t):
            plane_copy(t, half).start()
        if t == 3:
            plane_in[s] = keep[t, y, half_rows(x)]

    reduce_d.step_keep(0)
    reduce_d.step_far(0)
    norm_load.wait()
    in_compute(0)
    out_core_copy(1 - y).wait_recv()
    out_y[...] = (out_y[...].astype(f32) + out_core_in[1 - y].astype(f32)).astype(bf16)
    out_y_copy.start()
    in_core(0)
    small_core.wait_recv()
    small_v[1] = small_v[0] + small_in[0]
    small_y = small_copy(1, (y_peer, s))
    small_y.start()
    reduce_d.step_near(1)
    in_compute(1)
    in_core(1)
    in_compute(2)
    in_core(2)
    small_y.wait_recv()
    small_all[s] = small_v[1] + small_in[1]
    for k in range(1, 8):
        small_push(k).start()
    in_plane(0)
    reduce_d.step_keep(1)
    reduce_d.step_far(1)
    in_compute(3)
    in_core(3)
    in_plane(1)
    result[0] = (hidden[0].astype(f32) + reduce_r.total(0)).astype(bf16)
    reduce_r.step_near(1)
    in_plane(2)
    out_y_copy.wait_recv()
    out_core_copy(y).wait_recv()
    grad_out[...] = grad_out[...] + out_core_in[y].astype(f32) + out_y_in[...].astype(f32)
    gain_row = gain[...]
    gain_part = None
    for q in range(2):
        d_normed = reduce_d.total(q)
        h = hidden[q].astype(f32)
        inv = lax.rsqrt(jnp.mean(h * h, axis=-1, keepdims=True) + 1e-05)
        scaled = d_normed * gain_row
        along = jnp.mean(scaled * h, axis=-1, keepdims=True)
        d_hidden[q] = (cot[q].astype(f32) + inv * scaled - (inv * inv * inv) * along * h).astype(bf16)
        term = jnp.sum(d_normed * h * inv, axis=0, keepdims=True)
        gain_part = term if q == 0 else gain_part + term
    folded = width // 8
    gain_v[0] = jnp.concatenate([gain_part[:, k * folded : (k + 1) * folded] for k in range(8)], axis=0)

    def gain_copy(stage, device):
        return remote(gain_v.at[stage], gain_in.at[stage], gain_sems.at[0, stage], gain_sems.at[1, stage], device)

    gain_core = gain_copy(0, (core_peer, s))
    gain_core.start()
    in_plane(3)
    reduce_r.step_keep(1)
    reduce_r.step_far(1)
    gain_core.wait_recv()
    gain_v[1] = gain_v[0] + gain_in[0]
    gain_y = gain_copy(1, (y_peer, s))
    gain_y.start()
    for k in range(1, 8):
        source = (s + 8 - k) % 8
        there = plane_in.at[source]
        remote(there, there, plane_sems.at[0, 0, 0], plane_sems.at[1, source // 2, source % 2], (dp, x_peer)).wait_recv()
    gain_y.wait_recv()
    gain_v[2 + s] = gain_v[1] + gain_in[1]

    def gain_push(k):
        return remote(gain_v.at[2 + s], gain_v.at[2 + s], gain_plane.at[0, k], gain_plane.at[1, s], (dp, (s + k) % 8))

    for k in range(1, 8):
        gain_push(k).start()
    result[1] = (hidden[1].astype(f32) + reduce_r.total(1)).astype(bf16)
    reduce_r.settle()
    reduce_d.settle()
    small_core.wait_send()
    small_y.wait_send()
    out_y_copy.wait_send()
    for yy in range(2):
        out_core_copy(yy).wait_send()
    for m in range(4):
        for yy in range(2 if m >= 2 else 0):
            core_copy(m, yy).wait_send()
        y_copy(m).wait_send()
        for half in plane_halves(m):
            plane_copy(m, half).wait_send()

    for k in range(1, 8):
        source = (s + 8 - k) % 8
        remote(
            small_all.at[source], small_all.at[source], small_plane.at[0, k], small_plane.at[1, source], (dp, x_peer)
        ).wait_recv()
        small_push(k).wait_send()
        remote(
            gain_v.at[2 + source], gain_v.at[2 + source], gain_plane.at[0, k], gain_plane.at[1, source], (dp, x_peer)
        ).wait_recv()
        gain_push(k).wait_send()
    gain_core.wait_send()
    gain_y.wait_send()
    gain_total = gain_v[2]
    for source in range(1, 8):
        gain_total = gain_total + gain_v[2 + source]
    gain_sum[...] = gain_total


def run_finish(gated, w_out, d_z, d_y, x_raw, inner, w_in, cot_all, normed_all,
               bc_raw, dt_raw, seg_col, seg_row, wx, wbc, heads, gain_back, hidden, cot, gain, in_rows):
    f32, bf16 = jnp.float32, jnp.bfloat16
    n_own, span, width = hidden.shape
    tokens, chan = gated.shape
    length, rows = 8 * span, chan // 4
    columns = 2 * chan + 2 * NST + HEADS
    small = (8, chan + 2 * NST + 128)
    vmem = pltpu.VMEM
    anywhere, inside = pl.BlockSpec(memory_space=pl.ANY), pl.BlockSpec(memory_space=vmem)
    sem = pltpu.SemaphoreType.DMA
    tokens_like = [
        vmem((n_own, length, width), bf16), vmem((4, n_own, span, width), bf16),
        vmem((2, n_own, span, width), bf16), vmem((n_own, span, width), bf16),
    ]
    return pl.pallas_call(
        finish_kernel,
        in_specs=[anywhere] * 9 + [inside] * 11,
        out_specs=[inside] * 6,
        out_shape=[
            jax.ShapeDtypeStruct(hidden.shape, bf16),
            jax.ShapeDtypeStruct(hidden.shape, bf16),
            jax.ShapeDtypeStruct((8, in_rows, columns), bf16),
            jax.ShapeDtypeStruct((rows, width), f32),
            jax.ShapeDtypeStruct((8,) + small, f32),
            jax.ShapeDtypeStruct((8, width // 8), f32),
        ],
        scratch_shapes=[
            vmem((tokens, chan), bf16), vmem((chan, width), bf16),
            vmem((tokens, 2 * chan + 2 * NST + 128), bf16), vmem((width, 2 * chan + 2 * NST + 128), bf16),
            vmem((tokens, width), bf16),
            vmem((length, chan), f32), vmem((length, chan), bf16),
            vmem((length, 128), f32), vmem((length, 128), f32), vmem((chan // HDIM, 1, length), f32),
            vmem((length, length), f32), vmem((length, length), f32), vmem((length, length), f32),
            vmem((length, 128), f32), vmem((length, 128), f32),
        ]
        + tokens_like + tokens_like
        + [
            vmem((2, 2, 2 * in_rows, columns), bf16), vmem((4, 2, 2 * in_rows, columns), bf16),
            vmem((4, 2, 2 * in_rows, columns), bf16), vmem((4, 2 * in_rows, columns), bf16),
            vmem((2, rows, width), bf16),
            vmem((rows, width), bf16), vmem((rows, width), bf16),
            vmem((2,) + small, f32), vmem((2,) + small, f32),
            vmem((10, 8, width // 8), f32), vmem((2, 8, width // 8), f32),
            sem((9,)), sem((2, 4, 2)), sem((2, 2, 2)), sem((2, 2)), sem((2, 4, 2)), sem((2, 2, 2)), sem((2, 2)),
            sem((2, 4, 2)), sem((2, 4)), sem((2, 4, 2)), sem((2, 2)), sem((2,)),
            sem((2, 2)), sem((2, 8)), sem((2, 2)), sem((2, 8)),
        ],
        compiler_params=pltpu.CompilerParams(
            collective_id=1, has_side_effects=True, vmem_limit_bytes=63 << 20
        ),
        name="finish",
    )(
        gated, w_out, d_z, d_y, x_raw, inner, w_in, cot_all, normed_all,
        bc_raw, dt_raw, seg_col, seg_row, wx, wbc, heads, gain_back, hidden, cot, gain,
    )


def over_heads(rows, lane_head):
    lane = lax.broadcasted_iota(jnp.int32, (rows.shape[1], HEADS), 1)
    own = lax.broadcasted_iota(jnp.int32, (rows.shape[1], HEADS), 0) // lane_head
    map_own = (own == lane // 16 * 2 + lane % 2).astype(jnp.float32)
    sums = jnp.dot(rows, map_own, precision=lax.Precision.HIGHEST, preferred_element_type=jnp.float32)
    source = lax.broadcasted_iota(jnp.int32, (8, HEADS), 0)
    mine = lax.broadcasted_iota(jnp.int32, (8, HEADS), 1) // 2 % 8 == source
    return jnp.sum(jnp.where(mine, sums, 0.0), axis=0)


def assemble_kernel(result_in, d_hidden_in, plane_in, grad_out_in, small_all, gain_sum,
                    result, d_hidden, grad_in_out, conv_w, conv_b, dt_bias, a_log, d_skip, norm_gain, gate_gain, grad_out,
                    plane_v, result_v, d_hidden_v, grad_out_v, grad_in, load, store):
    f32 = jnp.float32
    rows = grad_out.shape[0]
    chan = 4 * rows
    passed = [(result_in, result_v, result), (d_hidden_in, d_hidden_v, d_hidden), (grad_out_in, grad_out_v, grad_out)]
    plane_load = pltpu.make_async_copy(plane_in, plane_v, load.at[3])
    plane_load.start()
    loads = [pltpu.make_async_copy(a, b, load.at[k]) for k, (a, b, _) in enumerate(passed)]
    stores = [pltpu.make_async_copy(b, c, store.at[k]) for k, (_, b, c) in enumerate(passed)]
    for copy in loads:
        copy.start()
    plane_load.wait()
    for source in range(8):
        for piece in range(WIDE):
            at = (piece * 8 + source) * rows
            grad_in[:, at : at + rows] = plane_v[source, :, piece * rows : (piece + 1) * rows].astype(f32)
    tail_sum = 0.0
    for source in range(8):
        tail_sum = tail_sum + plane_v[source, :, 2 * chan :].astype(f32)
    grad_in[:, 2 * DI :] = tail_sum
    stores.append(pltpu.make_async_copy(grad_in, grad_in_out, store.at[3]))
    stores[-1].start()
    for k in range(3):
        loads[k].wait()
        stores[k].start()
    bc_sum = 0.0
    for source in range(8):
        for d in range(4):
            at, own = (d * 8 + source) * rows, slice(d * rows, (d + 1) * rows)
            conv_w[:, at : at + rows] = small_all[source, :CONV, own]
            conv_b[pl.ds(at, rows)] = small_all[source, CONV, own]
            gate_gain[pl.ds(at, rows)] = small_all[source, CONV + 2, own]
        bc_sum = bc_sum + small_all[source, :, chan : chan + 2 * NST]
    conv_w[:, DI:] = bc_sum[:CONV]
    conv_b[pl.ds(DI, 2 * NST)] = bc_sum[CONV]
    dt_bias[...] = over_heads(small_all[:, 0, chan + 2 * NST :], 1)
    a_log[...] = over_heads(small_all[:, 1, chan + 2 * NST :], 1)
    d_skip[...] = over_heads(small_all[:, CONV + 1, :chan], HDIM)
    folded = gain_sum.shape[1]
    for k in range(8):
        norm_gain[pl.ds(k * folded, folded)] = gain_sum[k]
    for copy in stores:
        copy.wait()


def run_assemble(result, d_hidden, plane_in, grad_out, small_all, gain_sum):
    f32 = jnp.float32
    width = result.shape[2]
    in_rows = plane_in.shape[1]
    shape = jax.ShapeDtypeStruct
    channels = DI + 2 * NST
    anywhere, inside = pl.BlockSpec(memory_space=pl.ANY), pl.BlockSpec(memory_space=pltpu.VMEM)
    return pl.pallas_call(
        assemble_kernel,
        in_specs=[anywhere] * 4 + [inside] * 2,
        out_specs=[anywhere] * 3 + [inside] * 7 + [anywhere],
        out_shape=[
            shape(result.shape, result.dtype),
            shape(d_hidden.shape, d_hidden.dtype),
            shape((in_rows, 2 * DI + 2 * NST + HEADS), f32),
            shape((CONV, channels), f32),
            shape((channels,), f32),
            shape((HEADS,), f32),
            shape((HEADS,), f32),
            shape((HEADS,), f32),
            shape((width,), f32),
            shape((DI,), f32),
            shape(grad_out.shape, f32),
        ],
        scratch_shapes=[
            pltpu.VMEM(plane_in.shape, plane_in.dtype),
            pltpu.VMEM(result.shape, result.dtype),
            pltpu.VMEM(d_hidden.shape, d_hidden.dtype),
            pltpu.VMEM(grad_out.shape, f32),
            pltpu.VMEM((in_rows, 2 * DI + 2 * NST + HEADS), f32),
            pltpu.SemaphoreType.DMA((4,)),
            pltpu.SemaphoreType.DMA((4,)),
        ],
        compiler_params=pltpu.CompilerParams(vmem_limit_bytes=62 << 20),
        name="assemble",
    )(result, d_hidden, plane_in, grad_out, small_all, gain_sum)


def head_plan(
    hidden,
    segments,
    in_weight,
    conv_weight,
    conv_bias,
    dt_bias,
    a_log,
    d_skip,
    norm_gain,
    gate_gain,
    out_weight,
    cotangent,
):
    f32, bf16 = jnp.float32, jnp.bfloat16
    n_dp, n_seq = lax.axis_size("dp"), lax.axis_size("seq")
    seq_rank = lax.axis_index("seq")
    n_own, shard_len, width = hidden.shape
    length = shard_len * n_seq
    rows = out_weight.shape[0]
    in_rows = in_weight.shape[0]
    chan = rows * n_dp
    h_own = chan // HDIM
    (n_all, cot_all, w_in, w_out, x_raw, bc_raw, dt_raw, inner, gated, d_y, d_z, seg_col, seg_row, wx, wbc, head_vals,
     gain_back) = run_ahead(
        hidden, cotangent, in_weight, out_weight, segments, conv_weight.T, conv_bias,
        norm_gain[None], gate_gain[None], dt_bias, a_log, d_skip,
    )
    normed_all = n_all.reshape(n_own * length, width)
    cot_all = cot_all.reshape(n_own * length, width)
    result, d_hidden, plane_in, grad_out, small_all, gain_sum = run_finish(
        gated, w_out, d_z, d_y, x_raw, inner, w_in, cot_all, normed_all,
        bc_raw, dt_raw, seg_col, seg_row, wx, wbc, head_vals, gain_back, hidden, cotangent, norm_gain[None], in_rows,
    )
    outs = list(run_assemble(result, d_hidden, plane_in, grad_out, small_all, gain_sum))
    outs[3] = outs[3].T
    return tuple(outs)


def solution(mesh):
    whole_heads = mesh.shape["dp"] == 4 and mesh.shape["seq"] == 8
    shards = head_plan if whole_heads else general_plan
    placed = (
        P("dp", "seq", None),
        P("dp", "seq"),
        P(("dp", "seq"), None),
        P(),
        P(),
        P(),
        P(),
        P(),
        P(),
        P(),
        P(("dp", "seq"), None),
        P("dp", "seq", None),
    )
    return jax.shard_map(
        shards,
        mesh=mesh,
        in_specs=placed,
        out_specs=(
            P("dp", "seq", None),
            P("dp", "seq", None),
            P(("dp", "seq"), None),
            P(),
            P(),
            P(),
            P(),
            P(),
            P(),
            P(),
            P(("dp", "seq"), None),
        ),
        check_vma=False,
    )
```

```python
import functools

import jax
import jax.numpy as jnp
from jax import lax
from jax.experimental import pallas as pl
from jax.experimental.pallas import tpu as pltpu
from jax.sharding import PartitionSpec as P

HEADS = 64
HDIM = 64
NST = 128
GROUP = 256
CONV = 4
DI = 4096


def pre_norm(hidden_f, gain_vec):
    return (
        hidden_f
        * lax.rsqrt(jnp.mean(hidden_f * hidden_f, axis=-1, keepdims=True) + 1e-05)
        * gain_vec
    )


def gate_norm(y_values, gate_values, gain_vec):
    product = y_values * jax.nn.silu(gate_values)
    return (
        product * lax.rsqrt(jnp.mean(product * product, axis=-1, keepdims=True) + 1e-05) * gain_vec
    )


def conv_reset(signal, kernel, offset, seg_ids):
    tap_count = kernel.shape[1]
    summed = offset[None, :] + kernel[None, :, tap_count - 1] * signal
    for lag_steps in range(1, tap_count):
        shifted = jnp.pad(signal, ((lag_steps, 0), (0, 0)))[:-lag_steps]
        earlier = jnp.pad(seg_ids, (lag_steps, 0), constant_values=-1)[:-lag_steps]
        matches = (earlier == seg_ids).astype(jnp.float32)
        summed = summed + kernel[None, :, tap_count - 1 - lag_steps] * shifted * matches[:, None]
    return summed


def state_scan(values, deltas, rates, b_mat, c_mat, seg_ids):
    length, head_count, head_width = values.shape
    block_count = length // GROUP
    log_decay = deltas * rates[None, :]
    pieces = (
        values.reshape(block_count, GROUP, head_count, head_width),
        deltas.reshape(block_count, GROUP, head_count),
        log_decay.reshape(block_count, GROUP, head_count),
        b_mat.reshape(block_count, GROUP, b_mat.shape[-1]),
        c_mat.reshape(block_count, GROUP, c_mat.shape[-1]),
        seg_ids.reshape(block_count, GROUP),
    )
    position = lax.broadcasted_iota(jnp.int32, (GROUP, GROUP), 0)
    source = lax.broadcasted_iota(jnp.int32, (GROUP, GROUP), 1)

    def advance(carry, piece):
        memory, ending = carry
        block_vals, block_dt, block_log, b_block, c_block, seg_block = piece
        cumulative = jnp.cumsum(block_log, axis=0).T
        causal = (source <= position) & (seg_block[:, None] == seg_block[None, :])
        spread = cumulative[:, :, None] - cumulative[:, None, :]
        decays = jnp.where(causal[None], jnp.exp(jnp.where(causal[None], spread, 0.0)), 0.0)
        inner_prod = jnp.dot(c_block, b_block.T, precision=lax.Precision.HIGHEST)
        scores = inner_prod[None] * decays * block_dt.T[:, None, :]
        output = jnp.einsum("hij,jhp->ihp", scores, block_vals, precision=lax.Precision.HIGHEST)
        follows = (seg_block == ending).astype(jnp.float32)
        carried = jnp.einsum("in,hpn->ihp", c_block, memory, precision=lax.Precision.HIGHEST)
        output = output + (jnp.exp(cumulative).T * follows[:, None])[:, :, None] * carried
        last_seg = seg_block[-1]
        weights = (
            jnp.exp(cumulative[:, -1:] - cumulative)
            * (seg_block == last_seg).astype(jnp.float32)[None, :]
            * block_dt.T
        )
        keep_on = jnp.exp(cumulative[:, -1]) * (last_seg == ending).astype(jnp.float32)
        memory = memory * keep_on[:, None, None] + jnp.einsum(
            "hj,jhp,jn->hpn", weights, block_vals, b_block, precision=lax.Precision.HIGHEST
        )
        return ((memory, last_seg), output)

    initial = (
        jnp.zeros((head_count, head_width, b_mat.shape[-1]), jnp.float32),
        jnp.array(-1, jnp.int32),
    )
    unused, outputs = lax.scan(jax.checkpoint(advance), initial, pieces)
    return outputs.reshape(length, head_count, head_width)


def mixer(
    x_values,
    step_raw,
    bc_values,
    seg_ids,
    kernel_x,
    offset_x,
    kernel_bc,
    offset_bc,
    dt_shift,
    decay_log,
    skip_gain,
):
    x_conv = jax.nn.silu(conv_reset(x_values, kernel_x, offset_x, seg_ids))
    bc_conv = jax.nn.silu(conv_reset(bc_values, kernel_bc, offset_bc, seg_ids))
    step_sizes = jax.nn.softplus(step_raw + dt_shift[None, :])
    rates = -jnp.exp(decay_log)
    length = x_values.shape[0]
    head_count = step_raw.shape[1]
    shaped = x_conv.reshape(length, head_count, HDIM)
    mixed = (
        state_scan(shaped, step_sizes, rates, bc_conv[:, :NST], bc_conv[:, NST:], seg_ids)
        + skip_gain[None, :, None] * shaped
    )
    return mixed.reshape(length, head_count * HDIM)


def general_plan(
    hidden,
    segments,
    in_weight,
    conv_weight,
    conv_bias,
    dt_bias,
    a_log,
    d_skip,
    norm_gain,
    gate_gain,
    out_weight,
    cotangent,
):
    full_in, full_out = (
        lax.all_gather(in_weight, ("dp", "seq"), axis=0, tiled=True),
        lax.all_gather(out_weight, ("dp", "seq"), axis=0, tiled=True),
    )
    hidden_f = hidden.astype(jnp.float32)
    normed_f, pull_pre = jax.vjp(pre_norm, hidden_f, norm_gain)
    normed = normed_f.astype(jnp.bfloat16)
    project = jnp.einsum("mtd,df->mtf", normed, full_in, preferred_element_type=jnp.float32)
    gate_part = project[:, :, :DI]
    x_part = project[:, :, DI : 2 * DI].astype(jnp.bfloat16)
    bc_part = project[:, :, 2 * DI : 2 * DI + 2 * NST].astype(jnp.bfloat16)
    step_part = project[:, :, 2 * DI + 2 * NST :].astype(jnp.bfloat16)
    x_heads, step_heads = (
        lax.all_to_all(x_part, "seq", split_axis=2, concat_axis=1, tiled=True),
        lax.all_to_all(step_part, "seq", split_axis=2, concat_axis=1, tiled=True),
    )
    bc_full = lax.all_gather(bc_part, "seq", axis=1, tiled=True)
    seg_full = lax.all_gather(segments, "seq", axis=1, tiled=True)
    seq_rank = lax.axis_index("seq")
    head_local = step_heads.shape[2]
    chan_local = x_heads.shape[2]
    kernel_x = lax.dynamic_slice_in_dim(conv_weight, seq_rank * chan_local, chan_local, 0)
    offset_x = lax.dynamic_slice_in_dim(conv_bias, seq_rank * chan_local, chan_local, 0)
    shift_local = lax.dynamic_slice_in_dim(dt_bias, seq_rank * head_local, head_local, 0)
    decay_local = lax.dynamic_slice_in_dim(a_log, seq_rank * head_local, head_local, 0)
    skip_local = lax.dynamic_slice_in_dim(d_skip, seq_rank * head_local, head_local, 0)
    local_params = (
        kernel_x,
        offset_x,
        conv_weight[DI:],
        conv_bias[DI:],
        shift_local,
        decay_local,
        skip_local,
    )

    def head_mixer(x_values, step_raw, bc_values, params_in):

        def single_seq(x_one, step_one, bc_one, seg_one):
            return mixer(x_one, step_one, bc_one, seg_one, *params_in)

        return jax.vmap(single_seq)(x_values, step_raw, bc_values, seg_full)

    mixed, pull_mix = jax.vjp(
        head_mixer,
        x_heads.astype(jnp.float32),
        step_heads.astype(jnp.float32),
        bc_full.astype(jnp.float32),
        local_params,
    )
    y_tokens = lax.all_to_all(
        mixed.astype(jnp.bfloat16), "seq", split_axis=1, concat_axis=2, tiled=True
    )
    gated_f, pull_gate = jax.vjp(gate_norm, y_tokens.astype(jnp.float32), gate_part, gate_gain)
    gated = gated_f.astype(jnp.bfloat16)
    branch_out = jnp.einsum("mtf,fd->mtd", gated, full_out, preferred_element_type=jnp.float32)
    result = (hidden_f + branch_out).astype(jnp.bfloat16)
    d_gated = jnp.einsum("mtd,fd->mtf", cotangent, full_out, preferred_element_type=jnp.float32)
    d_mixed, d_gate_part, d_gate_gain = pull_gate(d_gated)
    d_heads = lax.all_to_all(
        d_mixed.astype(jnp.bfloat16), "seq", split_axis=2, concat_axis=1, tiled=True
    )
    d_x_heads, d_step_heads, d_bc_full, d_params = pull_mix(d_heads.astype(jnp.float32))
    d_x_part, d_step_part = (
        lax.all_to_all(
            d_x_heads.astype(jnp.bfloat16), "seq", split_axis=1, concat_axis=2, tiled=True
        ),
        lax.all_to_all(
            d_step_heads.astype(jnp.bfloat16), "seq", split_axis=1, concat_axis=2, tiled=True
        ),
    )
    d_bc_part = lax.psum_scatter(
        d_bc_full.astype(jnp.bfloat16), "seq", scatter_dimension=1, tiled=True
    )
    d_project = jnp.concatenate(
        [d_gate_part.astype(jnp.bfloat16), d_x_part, d_bc_part, d_step_part], axis=2
    )
    d_normed = jnp.einsum("mtf,df->mtd", d_project, full_in, preferred_element_type=jnp.float32)
    d_hidden_f, d_norm_gain = pull_pre(d_normed)
    d_hidden = (cotangent.astype(jnp.float32) + d_hidden_f).astype(jnp.bfloat16)
    in_rows = in_weight.shape[0]
    out_rows = out_weight.shape[0]
    column_ranges = ((0, DI), (DI, d_project.shape[2]))
    in_pieces = [jnp.zeros((in_rows, upper - lower), jnp.float32) for lower, upper in column_ranges]
    grad_out = jnp.zeros(out_weight.shape, jnp.float32)
    for batch_index in range(hidden.shape[0]):
        for range_index in range(len(column_ranges)):
            lower, upper = column_ranges[range_index]

            def in_term(
                start,
                count,
                normed_one=normed[batch_index],
                d_one=d_project[batch_index, :, lower:upper],
            ):
                return lax.dot_general(
                    normed_one, d_one, (((0,), (0,)), ((), ())), preferred_element_type=jnp.float32
                )

            in_pieces[range_index] = in_pieces[range_index] + lax.psum_scatter(
                in_term(jnp.int32(0), in_rows * lax.axis_size(("dp", "seq"))),
                ("dp", "seq"),
                scatter_dimension=0,
                tiled=True,
            )

        def out_term(start, count, gated_one=gated[batch_index], cot_one=cotangent[batch_index]):
            return lax.dot_general(
                gated_one, cot_one, (((0,), (0,)), ((), ())), preferred_element_type=jnp.float32
            )

        grad_out = grad_out + lax.psum_scatter(
            out_term(jnp.int32(0), out_rows * lax.axis_size(("dp", "seq"))),
            ("dp", "seq"),
            scatter_dimension=0,
            tiled=True,
        )
    grad_in = jnp.concatenate(in_pieces, axis=1)
    d_kernel_x, d_offset_x, d_kernel_bc, d_offset_bc, d_shift, d_decay, d_skip_part = d_params
    tap_count = conv_weight.shape[1]
    grad_conv_w = jnp.concatenate(
        [
            lax.dynamic_update_slice_in_dim(
                jnp.zeros((DI, tap_count), jnp.float32), d_kernel_x, seq_rank * chan_local, 0
            ),
            d_kernel_bc,
        ],
        axis=0,
    )
    grad_conv_b = jnp.concatenate(
        [
            lax.dynamic_update_slice_in_dim(
                jnp.zeros((DI,), jnp.float32), d_offset_x, seq_rank * chan_local, 0
            ),
            d_offset_bc,
        ],
        axis=0,
    )
    grad_shift = lax.dynamic_update_slice_in_dim(
        jnp.zeros((HEADS,), jnp.float32), d_shift, seq_rank * head_local, 0
    )
    grad_decay = lax.dynamic_update_slice_in_dim(
        jnp.zeros((HEADS,), jnp.float32), d_decay, seq_rank * head_local, 0
    )
    grad_skip = lax.dynamic_update_slice_in_dim(
        jnp.zeros((HEADS,), jnp.float32), d_skip_part, seq_rank * head_local, 0
    )
    totals = lax.psum(
        (grad_conv_w, grad_conv_b, grad_shift, grad_decay, grad_skip, d_norm_gain, d_gate_gain),
        ("dp", "seq"),
    )
    return (
        result,
        d_hidden,
        grad_in,
        totals[0],
        totals[1],
        totals[2],
        totals[3],
        totals[4],
        totals[5],
        totals[6],
        grad_out,
    )


LOG2E = 1.4426950408889634
TILE = 128
FAR = -1e30


def shift_rows(v, lag):
    return v if lag == 0 else pltpu.roll(v, lag % v.shape[0], axis=0)


def conv_silu(sig, taps, offset, keep):
    total = offset + taps[CONV - 1 : CONV] * sig
    for lag in range(1, CONV):
        total = total + taps[CONV - 1 - lag : CONV - lag] * (shift_rows(sig, lag) * keep[lag])
    gate = jax.nn.sigmoid(total)
    return total, gate, total * gate


def conv_back(d_out, total, gate, sig, taps, keep):
    d_total = d_out * (gate * (1.0 + total * (1.0 - gate)))
    d_sig = taps[CONV - 1 : CONV] * d_total
    tap_rows = [jnp.sum(d_total * sig, axis=0, keepdims=True)]
    for lag in range(1, CONV):
        kept = d_total * keep[lag]
        d_sig = d_sig + taps[CONV - 1 - lag : CONV - lag] * shift_rows(kept, -lag)
        tap_rows.append(jnp.sum(kept * shift_rows(sig, lag), axis=0, keepdims=True))
    return d_sig, tap_rows[::-1], jnp.sum(d_total, axis=0, keepdims=True)


def keep_masks(seg_col):
    length = seg_col.shape[0]
    row = lax.broadcasted_iota(jnp.int32, (length, 1), 0)
    masks = [None]
    for lag in range(1, CONV):
        same = (pltpu.roll(seg_col, lag, axis=0) == seg_col) & (row >= lag)
        masks.append(same.astype(jnp.float32))
    return masks


def lane_sums(v, reverse):
    length = v.shape[1]
    lane = lax.broadcasted_iota(jnp.int32, v.shape, 1)
    step = 1
    while step < length:
        if reverse:
            v = v + jnp.where(lane < length - step, pltpu.roll(v, length - step, axis=1), 0.0)
        else:
            v = v + jnp.where(lane >= step, pltpu.roll(v, step, axis=1), 0.0)
        step *= 2
    return v


def step_sizes_of(dt_all, head_rows, h_own, n_seq, heads_row):
    rank = lax.axis_index("seq")
    all_heads = dt_all.shape[1]
    lane = lax.broadcasted_iota(jnp.int32, (all_heads, 128), 1)
    row = lax.broadcasted_iota(jnp.int32, (all_heads, 128), 0)
    head = ((lane // heads_row) * n_seq + rank) * heads_row + lane % heads_row
    pick = ((row == head) & (lane < h_own)).astype(jnp.bfloat16)
    raw = jnp.dot(dt_all, pick, preferred_element_type=jnp.float32)
    shifted = raw + head_rows[0:1]
    dt = jnp.maximum(shifted, 0.0) + jnp.log1p(jnp.exp(-jnp.abs(shifted)))
    return shifted, dt


MESH = pl.DeviceIdType.MESH
WIDE = 8


def place():
    dp, s = lax.axis_index("dp"), lax.axis_index("seq")
    z, x = s // 2, s % 2
    y, core = dp // 2, dp % 2
    return dp, s, z, x, s + 1 - 2 * x, dp + 2 - 4 * y, dp + 1 - 2 * core


def greet(peers):
    barrier = pltpu.get_barrier_semaphore()
    for device in peers:
        pl.semaphore_signal(barrier, inc=1, device_id=device, device_id_type=MESH)


def greeted(peers):
    pl.semaphore_wait(pltpu.get_barrier_semaphore(), len(peers))


def remote(src, dst, send, recv, device):
    return pltpu.make_async_remote_copy(
        src_ref=src, dst_ref=dst, send_sem=send, recv_sem=recv, device_id=device, device_id_type=MESH
    )


class TokenGather:
    def __init__(self, full, send, recv, where):
        self.full, self.send, self.recv = full, send, recv
        self.dp, self.s, self.z, self.x, self.x_peer, _, _ = where
        self.span = full.shape[1] // 8

    def part(self, shard, q):
        return self.full.at[q, pl.ds(pl.multiple_of(shard * self.span, self.span), self.span)]

    def copy(self, shard_z, way, q):
        shard = shard_z * 2 + self.x
        target = (self.s + 2, self.s - 2, self.x_peer)[way]
        part = self.part(shard, q)
        return remote(part, part, self.send.at[way, shard_z, q], self.recv.at[shard, q], (self.dp, target))

    def arrived(self, shard, q):
        part = self.part(shard, q)
        remote(part, part, self.send.at[0, 0, q], self.recv.at[shard, q], (self.dp, self.x_peer)).wait_recv()

    def start(self, q):
        @pl.when(self.z < 3)
        def up():
            self.copy(self.z, 0, q).start()

        @pl.when(self.z > 0)
        def down():
            self.copy(self.z, 1, q).start()

        self.copy(self.z, 2, q).start()

    def step(self, hop, q):
        @pl.when(self.z >= hop)
        def from_below():
            shard_z = self.z - hop
            self.arrived(shard_z * 2 + self.x, q)

            @pl.when(self.z < 3)
            def up():
                self.copy(shard_z, 0, q).start()

            self.copy(shard_z, 2, q).start()

        @pl.when(self.z + hop <= 3)
        def from_above():
            shard_z = self.z + hop
            self.arrived(shard_z * 2 + self.x, q)

            @pl.when(self.z > 0)
            def down():
                self.copy(shard_z, 1, q).start()

            self.copy(shard_z, 2, q).start()

    def arrive_x(self, q):
        for shard_z in range(4):
            self.arrived(shard_z * 2 + 1 - self.x, q)

    def settle(self, q):
        for shard_z in range(4):
            self.copy(shard_z, 2, q).wait_send()

            @pl.when((self.z < 3) & (self.z >= shard_z))
            def up():
                self.copy(shard_z, 0, q).wait_send()

            @pl.when((self.z > 0) & (self.z <= shard_z))
            def down():
                self.copy(shard_z, 1, q).wait_send()


def column_of(mat, index):
    return pltpu.roll(mat, (128 - index) % 128, axis=1)[:, :1]


def pair_lanes(mat, pair):
    lane = lax.broadcasted_iota(jnp.int32, (mat.shape[0], 128), 1)
    return jnp.where(lane < HDIM, column_of(mat, 2 * pair), column_of(mat, 2 * pair + 1))


def load_params(rank, conv_t, conv_b, dt_bias, a_log, d_skip, wx, wbc, heads):
    lane = lax.broadcasted_iota(jnp.int32, (1, 128), 1)
    bias_row, log_row = jnp.zeros((1, 128), jnp.float32), jnp.zeros((1, 128), jnp.float32)
    wx[...] = jnp.zeros(wx.shape, jnp.float32)
    wbc[...] = jnp.zeros(wbc.shape, jnp.float32)
    heads[...] = jnp.zeros(heads.shape, jnp.float32)
    for d in range(wx.shape[1] // 128):
        cols, own = pl.ds(pl.multiple_of((d * 8 + rank) * 128, 128), 128), slice(d * 128, (d + 1) * 128)
        head = (d * 8 + rank) * 2
        wx[0:CONV, own] = conv_t[:, cols]
        wx[CONV : CONV + 1, own] = conv_b[cols].reshape(1, 128)
        wx[CONV + 1 : CONV + 2, own] = jnp.where(lane < HDIM, d_skip[head], d_skip[head + 1])
        for half in range(2):
            bias_row = jnp.where(lane == 2 * d + half, dt_bias[head + half], bias_row)
            log_row = jnp.where(lane == 2 * d + half, a_log[head + half], log_row)
    wbc[0:CONV] = conv_t[:, DI:]
    wbc[CONV : CONV + 1] = conv_b[pl.ds(DI, 2 * NST)].reshape(1, 2 * NST)
    heads[0:1] = bias_row
    heads[1:2] = log_row


def head_mats(dt_all, heads, h_own, dt_mat, cum_mat, cum_rows):
    shifted, dt = step_sizes_of(dt_all, heads, h_own, 8, 2)
    rates = -jnp.exp(heads[1:2])
    across = jnp.transpose(dt * (rates * LOG2E))
    cum_t = lane_sums(across[:h_own], False)
    pad = jnp.zeros((128 - h_own, cum_t.shape[1]), jnp.float32)
    dt_mat[...] = dt
    cum_mat[...] = jnp.transpose(jnp.concatenate([cum_t, pad], axis=0))
    for k in range(h_own):
        cum_rows[k] = cum_t[k : k + 1, :]


def mask_rows(bias, seg_col, seg_row, source_first):
    length = bias.shape[0]
    for block in range(length // TILE):
        rows = slice(block * TILE, (block + 1) * TILE)
        down = lax.broadcasted_iota(jnp.int32, (TILE, length), 0) + block * TILE
        over = lax.broadcasted_iota(jnp.int32, (TILE, length), 1)
        past = down <= over if source_first else over <= down
        bias[rows] = jnp.where(past & (seg_col[rows] == seg_row), 0.0, FAR)


def convolve_bc(bc_ref, wbc, keep):
    out = []
    for part in range(2):
        lanes = slice(part * NST, (part + 1) * NST)
        _, _, values = conv_silu(
            bc_ref[:, lanes].astype(jnp.float32), wbc[0:CONV, lanes], wbc[CONV : CONV + 1, lanes], keep
        )
        out.append(values.astype(jnp.bfloat16))
    return out


def forward_prepare(h_own, bc_ref, dt_ref, seg_col, seg_row, wbc, heads, dt_mat, cum_mat, cum_rows, inner_prod, bias):
    length = bc_ref.shape[0]
    keep = keep_masks(seg_col)
    head_mats(dt_ref[...], heads[...], h_own, dt_mat, cum_mat, cum_rows)
    bc = convolve_bc(bc_ref, wbc, keep)
    inner_prod[...] = lax.dot_general(bc[1], bc[0], (((1,), (1,)), ((), ())), preferred_element_type=jnp.float32)
    mask_rows(bias, seg_col, seg_row, False)


def forward_pair(pair, x_ref, seg_col, wx_ref, y_ref, inner_ref, dt_mat, cum_mat, cum_rows, inner_prod, bias):
    length = x_ref.shape[0]
    keep = keep_masks(seg_col)
    _, _, xc = conv_silu(x_ref[...].astype(jnp.float32), wx_ref[0:CONV], wx_ref[CONV : CONV + 1], keep)
    moved = (xc * pair_lanes(dt_mat[...], pair)).astype(jnp.bfloat16)
    skip = wx_ref[CONV + 1 : CONV + 2]
    first = lax.broadcasted_iota(jnp.int32, (TILE, 128), 1) < HDIM
    cum = [column_of(cum_mat[...], 2 * pair + half) for half in range(2)]
    for block in range(length // TILE):
        rows, wide = slice(block * TILE, (block + 1) * TILE), (block + 1) * TILE
        halves = []
        for half in range(2):
            decay = jnp.exp2(cum[half][rows] - cum_rows[2 * pair + half, :, :wide] + bias[rows, :wide])
            scores = (inner_prod[rows, :wide] * decay).astype(jnp.bfloat16)
            halves.append(jnp.dot(scores, moved[:wide], preferred_element_type=jnp.float32))
        inner = jnp.where(first, halves[0], halves[1])
        inner_ref[rows] = inner
        y_ref[rows] = (inner + skip * xc[rows]).astype(jnp.bfloat16)


def ahead_kernel(hidden, cot, in_w, out_w, seg_in, conv_t, conv_b, norm_gain, gate_gain, dt_bias, a_log, d_skip,
                 n_all, c_all, w_in, w_out, x_out, bc_raw, dt_raw, inner_out, gated_out, d_y_out, d_z_out, seg_col, seg_row,
                 wx, wbc, heads, gain_back,
                 seg, in_tail, tok_v, cot_v, w_in_v, w_out_v, z_v, y_v, dg, seg_all, dt_mat, cum_mat, cum_rows, inner_prod, bias,
                 sum_cols, sums, x_raw, inner, gated, d_y, d_z,
                 n_send, n_recv, c_send, c_recv, wide_send, tail_send, wide_recv, tail_recv,
                 y_send, core_send, cross_send, block_recv, out_send, out_recv, seg_send, seg_recv, store,
                 sum_send, sum_recv):
    f32, bf16 = jnp.float32, jnp.bfloat16
    where = place()
    dp, s, z, x, x_peer, y_peer, core_peer = where
    peers = [(dp, (s + k) % 8) for k in range(1, 8)] + [(y_peer, s), (core_peer, s)]
    greet(peers)
    in_rows, rows = in_w.shape[0], out_w.shape[0]
    chan = w_out.shape[0]
    h_own = chan // HDIM
    tail = in_tail.shape[1]
    n_own, length, width = n_all.shape
    in_tail[...] = jnp.zeros(in_tail.shape, bf16)
    in_tail[:, : in_w.shape[1] - 2 * DI] = in_w[:, 2 * DI :]
    seg[...] = jnp.zeros(seg.shape, f32)
    seg[:n_own, : seg_in.shape[1]] = seg_in[...].astype(f32)

    def block(d, shard, lo=0, size=None):
        size = w_in_v.shape[1] if size is None else size
        at = pl.multiple_of((d * 8 + shard) * in_rows, in_rows)
        return w_in_v.at[pl.ds(at, in_rows), pl.ds(lo, size)]

    def wide_src(piece, target):
        at = pl.multiple_of((piece * 8 + target) * rows, rows)
        return in_w.at[:, pl.ds(at, rows)]

    def push(k, _):
        target = (s + k) % 8
        remote(seg, seg_all.at[s], seg_send.at[k], seg_recv.at[s], (dp, target)).start()
        for piece in range(WIDE):
            remote(
                wide_src(piece, target), block(dp, s, piece * rows, rows), wide_send.at[k], wide_recv.at[s],
                (dp, target),
            ).start()
        remote(in_tail, block(dp, s, 2 * chan, tail), tail_send.at[k], tail_recv.at[s], (dp, target)).start()
        return 0

    span = hidden.shape[1]
    own_tokens = pl.ds(pl.multiple_of(s * span, span), span)
    for q in range(n_own):
        h = hidden[q].astype(f32)
        inv = lax.rsqrt(jnp.mean(h * h, axis=-1, keepdims=True) + 1e-05)
        tok_v[q, own_tokens] = (h * inv * norm_gain[...]).astype(bf16)
    tokens = TokenGather(tok_v, n_send, n_recv, where)
    cots = TokenGather(cot_v, c_send, c_recv, where)
    seg_all[s] = seg[...]
    own_rows = pl.ds(pl.multiple_of((dp * 8 + s) * in_rows, in_rows), in_rows)
    for piece in range(WIDE):
        at = pl.multiple_of((piece * 8 + s) * rows, rows)
        w_in_v[own_rows, piece * rows : (piece + 1) * rows] = in_w[:, pl.ds(at, rows)]
    w_in_v[own_rows, 2 * chan :] = in_tail[...]

    def out_part(d):
        return w_out_v.at[pl.ds(pl.multiple_of(d * rows, rows), rows)]

    w_out_v[pl.ds(pl.multiple_of(dp * rows, rows), rows)] = out_w[...]
    out_y = remote(out_part(dp), out_part(dp), out_send.at[0], out_recv.at[dp], (y_peer, s))
    out_core = remote(out_part(dp), out_part(dp), out_send.at[1], out_recv.at[dp], (core_peer, s))
    for q in range(n_own):
        cot_v[q, own_tokens] = cot[q]
    greeted(peers)
    tokens.start(0)
    tokens.start(1)
    out_y.start()
    out_core.start()
    lax.fori_loop(1, 8, push, 0)

    def spread(shard, k):
        there = block(dp, shard)
        remote(there, there, y_send.at[k], block_recv.at[dp, shard], (y_peer, s)).start()
        remote(there, there, core_send.at[k], block_recv.at[dp, shard], (core_peer, s)).start()

    spread(s, 0)
    load_params(s, conv_t, conv_b, dt_bias, a_log, d_skip, wx, wbc, heads)

    def wide_copy(source, k):
        there = block(dp, source, 0, 2 * chan)
        return remote(there, there, wide_send.at[k], wide_recv.at[source], (dp, x_peer))

    def tail_copy(source, k):
        there = block(dp, source, 2 * chan, tail)
        return remote(there, there, tail_send.at[k], tail_recv.at[source], (dp, x_peer))

    def forward(k, _):
        source = (s + 8 - k) % 8
        wide_copy(source, k).wait_recv()
        tail_copy(source, k).wait_recv()
        spread(source, k)
        return 0

    def cross(k, _):
        source = (s + 8 - k) % 8
        there = block(y_peer, source)
        copy = remote(there, there, cross_send.at[k], block_recv.at[y_peer, source], (core_peer, s))
        copy.wait_recv()
        copy.start()
        return 0

    tokens.step(1, 0)
    tokens.step(1, 1)
    cots.start(0)
    lax.fori_loop(1, 4, forward, 0)
    tokens.step(2, 0)
    tokens.step(2, 1)
    cots.start(1)
    lax.fori_loop(4, 8, forward, 0)
    tokens.step(3, 0)
    tokens.step(3, 1)
    cots.step(1, 0)
    lax.fori_loop(0, 4, cross, 0)
    cots.step(1, 1)
    lax.fori_loop(4, 8, cross, 0)

    def arrive(k, _):
        source = (s + 8 - k) % 8
        for d in (core_peer, core_peer + y_peer - dp):
            there = block(d, source)
            remote(there, there, core_send.at[k], block_recv.at[d, source], (core_peer, s)).wait_recv()
        return 0

    lax.fori_loop(0, 8, arrive, 0)
    stores = [pltpu.make_async_copy(w_in_v, w_in, store.at[0])]
    stores[0].start()

    def keep_for_later(q, *pairs):
        at = pl.ds(q * length, length)
        for held, there in pairs:
            stores.append(pltpu.make_async_copy(held.at[at], there.at[at], store.at[5 + len(stores)]))
            stores[-1].start()

    def segments_in(k, _):
        source = (s + 8 - k) % 8
        remote(seg, seg_all.at[source], seg_send.at[k], seg_recv.at[source], (dp, x_peer)).wait_recv()
        return 0

    lax.fori_loop(1, 8, segments_in, 0)
    lane = lax.broadcasted_iota(jnp.int32, (1, 128), 1)
    for q in range(n_own):
        pieces = [
            jnp.where(lane < 64, seg_all[2 * m, q : q + 1], pltpu.roll(seg_all[2 * m + 1, q : q + 1], 64, axis=1))
            for m in range(4)
        ]
        row = jnp.concatenate(pieces, axis=1)
        seg_row[q] = row
        seg_col[q] = jnp.transpose(jnp.broadcast_to(row, (128, length)))[:, :1]

    def project(q):
        at = slice(q * length, (q + 1) * length)
        half = chan // 2

        @pl.loop(0, 2)
        def gates(n):
            cols = pl.ds(pl.multiple_of(n * half, half), half)
            z_v[at, cols] = jnp.dot(tok_v[q], w_in_v[:, cols], preferred_element_type=f32)

        @pl.loop(0, 2)
        def values(n):
            cols = pl.ds(pl.multiple_of(n * half, half), half)
            from_cols = pl.ds(pl.multiple_of(chan + n * half, half), half)
            x_raw[at, cols] = jnp.dot(tok_v[q], w_in_v[:, from_cols], preferred_element_type=f32).astype(bf16)

        last = jnp.dot(tok_v[q], w_in_v[:, 2 * chan :], preferred_element_type=f32).astype(bf16)
        bc_raw[at] = last[:, : 2 * NST]
        dt_raw[at] = last[:, 2 * NST :]

    for q in range(n_own):
        tokens.arrive_x(q)
        stores.append(pltpu.make_async_copy(tok_v.at[q], n_all.at[q], store.at[1 + q]))
        stores[-1].start()
        project(q)
        keep_for_later(q, (x_raw, x_out))
        cots.step(2, q)

    for q in range(n_own):
        at = pl.ds(q * length, length)
        forward_prepare(
            h_own, bc_raw.at[at], dt_raw.at[at], seg_col[q], seg_row[q], wbc, heads,
            dt_mat, cum_mat, cum_rows, inner_prod, bias,
        )

        @pl.loop(0, chan // 128)
        def pairs(pair):
            cols = pl.ds(pl.multiple_of(pair * 128, 128), 128)
            forward_pair(
                pair, x_raw.at[at, cols], seg_col[q], wx.at[:, cols], y_v.at[at, cols], inner.at[at, cols],
                dt_mat, cum_mat, cum_rows, inner_prod, bias,
            )

            if q == 0:

                @pl.when(pair == 0)
                def hook_0_0():
                    cots.step(3, 0)

            if q == 0:

                @pl.when(pair == 2)
                def hook_0_2():
                    cots.step(3, 1)

    for q in range(n_own):
        keep_for_later(q, (inner, inner_out))
    out_cross = remote(out_part(y_peer), out_part(y_peer), out_send.at[2], out_recv.at[y_peer], (core_peer, s))
    out_cross.wait_recv()
    out_cross.start()
    for d in (core_peer, core_peer + y_peer - dp):
        remote(out_part(d), out_part(d), out_send.at[0], out_recv.at[d], (core_peer, s)).wait_recv()
    stores.append(pltpu.make_async_copy(w_out_v, w_out, store.at[3]))
    stores[-1].start()
    gain = jnp.concatenate(
        [gate_gain[:, pl.ds(pl.multiple_of((d * 8 + s) * 128, 128), 128)] for d in range(chan // 128)], axis=1
    )
    lane_wide = lax.broadcasted_iota(jnp.int32, (TILE, 128), 1)

    def sum_copy(q, k):
        return remote(
            sums.at[q, s], sums.at[q, s], sum_send.at[q, k], sum_recv.at[q, s], (dp, (s + k) % 8)
        )

    def gate(q):
        for k in range(1, 8):
            source = (s + 8 - k) % 8
            remote(
                sums.at[q, source], sums.at[q, source], sum_send.at[q, k], sum_recv.at[q, source], (dp, x_peer)
            ).wait_recv()
        total = sums[q, 0]
        for source in range(1, 8):
            total = total + sums[q, source]
        total = jnp.concatenate([total, jnp.zeros((120, length), f32)], axis=0)
        sum_cols[...] = jnp.transpose(total)

        @pl.loop(0, length // TILE)
        def gate_rows(n):
            at = pl.ds(pl.multiple_of(q * length + n * TILE, TILE), TILE)
            both = sum_cols[pl.ds(pl.multiple_of(n * TILE, TILE), TILE)]
            r = lax.rsqrt(both[:, 0:1] / DI + 1e-05)
            fall = (r * r * r) * (both[:, 1:2] / DI)
            zz = z_v[at]
            sig = jax.nn.sigmoid(zz)
            act = zz * sig
            yy = y_v[at].astype(f32)
            g = yy * act
            gr = g * r
            back = dg[at]
            d_g = r * (back * gain) - fall * g
            gated[at] = (gr * gain).astype(bf16)
            d_y[at] = (d_g * act).astype(bf16)
            d_z[at] = (d_g * yy * (sig * (1.0 + zz * (1.0 - sig)))).astype(bf16)
            gain_back[0:1] += jnp.sum(back * gr, axis=0, keepdims=True)

    gain_back[...] = jnp.zeros(gain_back.shape, f32)
    for q in range(n_own):
        if q == 1:
            gate(0)
            keep_for_later(0, (gated, gated_out), (d_y, d_y_out), (d_z, d_z_out))
        cots.arrive_x(q)
        stores.append(pltpu.make_async_copy(cot_v.at[q], c_all.at[q], store.at[4 + q]))
        stores[-1].start()
        half = chan // 2

        @pl.loop(0, 2)
        def back(n):
            cols = pl.ds(pl.multiple_of(n * half, half), half)
            dg[q * length : (q + 1) * length, cols] = lax.dot_general(
                cot_v[q], w_out_v[cols], (((1,), (1,)), ((), ())), preferred_element_type=f32
            )

        @pl.loop(0, length // TILE)
        def reduce_rows(n):
            at = pl.ds(pl.multiple_of(q * length + n * TILE, TILE), TILE)
            zz = z_v[at]
            g = y_v[at].astype(f32) * (zz * jax.nn.sigmoid(zz))
            first = jnp.sum(g * g, axis=1, keepdims=True)
            second = jnp.sum(dg[at] * gain * g, axis=1, keepdims=True)
            sum_cols[pl.ds(pl.multiple_of(n * TILE, TILE), TILE)] = jnp.where(
                lane_wide == 0, first, jnp.where(lane_wide == 1, second, 0.0)
            )

        sums[q, s] = jnp.transpose(sum_cols[...])[:8]
        for k in range(1, 8):
            sum_copy(q, k).start()

    gate(1)
    keep_for_later(1, (gated, gated_out), (d_y, d_y_out), (d_z, d_z_out))

    for q in range(n_own):
        tokens.settle(q)
        cots.settle(q)
        for k in range(1, 8):
            sum_copy(q, k).wait_send()

    def settle(k, _):
        shard = (s + 8 - k) % 8
        there = block(dp, shard)
        remote(there, there, y_send.at[k], block_recv.at[dp, shard], (y_peer, s)).wait_send()
        remote(there, there, core_send.at[k], block_recv.at[dp, shard], (core_peer, s)).wait_send()
        remote(there, there, cross_send.at[k], block_recv.at[dp, shard], (core_peer, s)).wait_send()
        return 0

    lax.fori_loop(0, 8, settle, 0)

    def settle_push(k, _):
        source = (s + 8 - k) % 8
        remote(seg, seg_all.at[source], seg_send.at[k], seg_recv.at[source], (dp, x_peer)).wait_send()
        wide_copy(source, k).wait_send()
        tail_copy(source, k).wait_send()
        return 0

    lax.fori_loop(1, 8, settle_push, 0)
    out_y.wait_send()
    out_core.wait_send()
    out_cross.wait_send()
    for copy in stores:
        copy.wait()


def run_ahead(hidden, cot, in_w, out_w, seg, conv_t, conv_b, norm_gain, gate_gain, dt_bias, a_log, d_skip):
    f32, bf16 = jnp.float32, jnp.bfloat16
    n_own, span, width = hidden.shape
    in_rows, rows = in_w.shape[0], out_w.shape[0]
    chan, length = 4 * rows, 8 * span
    tokens, h_own = n_own * length, chan // HDIM
    columns = 2 * chan + 2 * NST + 128
    sem, vmem = pltpu.SemaphoreType.DMA, pltpu.VMEM
    anywhere, inside = pl.BlockSpec(memory_space=pl.ANY), pl.BlockSpec(memory_space=vmem)
    scalars = pl.BlockSpec(memory_space=pltpu.SMEM)
    shape = jax.ShapeDtypeStruct
    return pl.pallas_call(
        ahead_kernel,
        in_specs=[inside] * 9 + [scalars] * 3,
        out_specs=[anywhere] * 5 + [inside] * 2 + [anywhere] * 4 + [inside] * 6,
        out_shape=[
            shape((n_own, length, width), bf16),
            shape((n_own, length, width), bf16),
            shape((32 * in_rows, columns), bf16),
            shape((chan, width), bf16),
            shape((tokens, chan), bf16),
            shape((tokens, 2 * NST), bf16),
            shape((tokens, 128), bf16),
            shape((tokens, chan), f32),
            shape((tokens, chan), bf16),
            shape((tokens, chan), bf16),
            shape((tokens, chan), bf16),
            shape((n_own, length, 1), f32),
            shape((n_own, 1, length), f32),
            shape((8, chan), f32),
            shape((8, 2 * NST), f32),
            shape((8, 128), f32),
            shape((8, chan), f32),
        ],
        scratch_shapes=[
            vmem((8, 128), f32),
            vmem((in_rows, 2 * NST + 128), bf16),
            vmem((n_own, length, width), bf16),
            vmem((n_own, length, width), bf16),
            vmem((width, columns), bf16),
            vmem((chan, width), bf16),
            vmem((tokens, chan), f32),
            vmem((tokens, chan), bf16),
            vmem((tokens, chan), f32),
            vmem((8, 8, 128), f32),
            vmem((length, 128), f32),
            vmem((length, 128), f32),
            vmem((h_own, 1, length), f32),
            vmem((length, length), f32),
            vmem((length, length), f32),
            vmem((length, 128), f32),
            vmem((n_own, 8, 8, length), f32),
            vmem((tokens, chan), bf16),
            vmem((tokens, chan), f32),
            vmem((tokens, chan), bf16),
            vmem((tokens, chan), bf16),
            vmem((tokens, chan), bf16),
            sem((3, 4, 2)), sem((8, 2)), sem((3, 4, 2)), sem((8, 2)),
            sem((8,)), sem((8,)), sem((8,)), sem((8,)),
            sem((8,)), sem((8,)), sem((8,)), sem((4, 8)), sem((3,)), sem((4,)), sem((8,)), sem((8,)),
            sem((24,)), sem((2, 8)), sem((2, 8)),
        ],
        compiler_params=pltpu.CompilerParams(collective_id=0, has_side_effects=True, vmem_limit_bytes=56 << 20),
        name="ahead",
    )(hidden, cot, in_w, out_w, seg, conv_t, conv_b, norm_gain, gate_gain, dt_bias, a_log, d_skip)


def backward_prepare(h_own, bc_ref, dt_ref, seg_col, seg_row, wbc, heads, dt_mat, cum_mat, cum_rows, inner_prod, bias,
                     d_inner, d_cum, d_dt):
    length = bc_ref.shape[0]
    keep = keep_masks(seg_col)
    head_mats(dt_ref[...], heads[...], h_own, dt_mat, cum_mat, cum_rows)
    bc = convolve_bc(bc_ref, wbc, keep)
    inner_prod[...] = lax.dot_general(bc[0], bc[1], (((1,), (1,)), ((), ())), preferred_element_type=jnp.float32)
    mask_rows(bias, seg_col, seg_row, True)
    d_inner[...] = jnp.zeros((length, length), jnp.float32)
    d_cum[...] = jnp.zeros((length, 128), jnp.float32)
    d_dt[...] = jnp.zeros((length, 128), jnp.float32)


def backward_pair(pair, x_ref, seg_col, wx_ref, dy_ref, inner_ref, dx_ref, gx_ref, dt_mat, cum_mat, cum_rows,
                  inner_prod, bias, d_inner, d_cum, d_dt):
    f32, bf16 = jnp.float32, jnp.bfloat16
    length = x_ref.shape[0]
    keep = keep_masks(seg_col)
    x_in = x_ref[...].astype(f32)
    taps = wx_ref[0:CONV]
    total, gate, xc = conv_silu(x_in, taps, wx_ref[CONV : CONV + 1], keep)
    dt_wide = pair_lanes(dt_mat[...], pair)
    moved = (xc * dt_wide).astype(bf16)
    skip = wx_ref[CONV + 1 : CONV + 2]
    dy = dy_ref[...]
    first = lax.broadcasted_iota(jnp.int32, (TILE, 128), 1) < HDIM
    cum = [column_of(cum_mat[...], 2 * pair + half) for half in range(2)]
    pieces = []
    for block in range(length // TILE):
        rows, later = slice(block * TILE, (block + 1) * TILE), slice(block * TILE, length)
        halves = []
        for half in range(2):
            decay = jnp.exp2(cum_rows[2 * pair + half, :, later] - cum[half][rows] + bias[rows, later])
            scores = (inner_prod[rows, later] * decay).astype(bf16)
            halves.append(jnp.dot(scores, dy[later], preferred_element_type=f32))
            mine = jnp.where(first if half == 0 else ~first, moved[rows].astype(f32), 0.0).astype(bf16)
            d_scores = lax.dot_general(mine, dy[later], (((1,), (1,)), ((), ())), preferred_element_type=f32)
            d_inner[rows, later] += d_scores * decay
        pieces.append(jnp.where(first, halves[0], halves[1]))
    d_moved = jnp.concatenate(pieces, axis=0)
    dy_f = dy.astype(f32)
    change = dy_f * inner_ref[...] - moved.astype(f32) * d_moved
    direct = d_moved * xc
    lane = lax.broadcasted_iota(jnp.int32, (length, 128), 1)
    low = lane < HDIM
    for half in range(2):
        mine = low if half == 0 else ~low
        spot = lane == 2 * pair + half
        d_cum[...] += jnp.where(spot, jnp.sum(jnp.where(mine, change, 0.0), axis=1, keepdims=True), 0.0)
        d_dt[...] += jnp.where(spot, jnp.sum(jnp.where(mine, direct, 0.0), axis=1, keepdims=True), 0.0)
    d_xc = d_moved * dt_wide + skip * dy_f
    d_x, tap_rows, d_offset = conv_back(d_xc, total, gate, x_in, taps, keep)
    dx_ref[...] = d_x.astype(bf16)
    d_skip = jnp.sum(dy_f * xc, axis=0, keepdims=True)
    gx_ref[...] += jnp.concatenate(tap_rows + [d_offset, d_skip, jnp.zeros((2, 128), f32)], axis=0)


def backward_finish(h_own, bc_ref, dt_ref, seg_col, wbc, heads, d_inner, d_cum, d_dt, dbc_ref, ddt_ref, gbc_ref, gh_ref):
    f32, bf16 = jnp.float32, jnp.bfloat16
    length = bc_ref.shape[0]
    keep = keep_masks(seg_col)
    bc = convolve_bc(bc_ref, wbc, keep)
    d_in = d_inner[...].astype(bf16)
    for part in range(2):
        lanes = slice(part * NST, (part + 1) * NST)
        side = 1 - part
        d_value = lax.dot_general(d_in, bc[side], (((side,), (0,)), ((), ())), preferred_element_type=f32)
        bc_in = bc_ref[:, lanes].astype(f32)
        taps = wbc[0:CONV, lanes]
        total, gate, _ = conv_silu(bc_in, taps, wbc[CONV : CONV + 1, lanes], keep)
        d_bc, tap_rows, offset = conv_back(d_value, total, gate, bc_in, taps, keep)
        dbc_ref[:, lanes] = d_bc.astype(bf16)
        gbc_ref[:, lanes] += jnp.concatenate(tap_rows + [offset, jnp.zeros((3, NST), f32)], axis=0)
    shifted, dt = step_sizes_of(dt_ref[...], heads[...], h_own, 8, 2)
    rates = -jnp.exp(heads[1:2])
    across = jnp.transpose(d_cum[...])
    d_log_t = lane_sums(across[:h_own], True)
    d_log = jnp.transpose(jnp.concatenate([d_log_t, jnp.zeros((128 - h_own, length), f32)], axis=0))
    d_raw = (d_log * rates + d_dt[...]) * jax.nn.sigmoid(shifted)
    rank = lax.axis_index("seq")
    row = lax.broadcasted_iota(jnp.int32, (128, 128), 0)
    head = ((row // 2) * 8 + rank) * 2 + row % 2
    pick = ((lax.broadcasted_iota(jnp.int32, (128, 128), 1) == head) & (row < h_own)).astype(bf16)
    ddt_ref[...] = jnp.dot(d_raw.astype(bf16), pick, preferred_element_type=f32).astype(bf16)
    gh_ref[...] += jnp.concatenate(
        [
            jnp.sum(d_raw, axis=0, keepdims=True),
            jnp.sum(d_log * dt, axis=0, keepdims=True) * rates,
            jnp.zeros((6, 128), f32),
        ],
        axis=0,
    )


class TokenReduce:
    def __init__(self, part, from_x, from_near, from_far, x_sems, near_sems, far_sems, where, span):
        self.part, self.from_x, self.from_near, self.from_far = part, from_x, from_near, from_far
        self.x_sems, self.near_sems, self.far_sems, self.span = x_sems, near_sems, far_sems, span
        self.dp, self.s, self.z, self.x, self.x_peer, _, _ = where
        self.near = self.s + 2 - 4 * (self.z % 2)
        self.far = self.s + 4 - 8 * (self.z // 2)

    def rows(self, shard, q):
        return self.part.at[q, pl.ds(pl.multiple_of(shard * self.span, self.span), self.span)]

    def x_copy(self, shard_z, q):
        return remote(
            self.rows(shard_z * 2 + 1 - self.x, q), self.from_x.at[shard_z, q],
            self.x_sems.at[0, shard_z, q], self.x_sems.at[1, shard_z, q], (self.dp, self.x_peer),
        )

    def near_copy(self, high, q):
        shard = (high * 2 + 1 - self.z % 2) * 2 + self.x
        return remote(
            self.rows(shard, q), self.from_near.at[high, q],
            self.near_sems.at[0, high, q], self.near_sems.at[1, high, q], (self.dp, self.near),
        )

    def far_copy(self, q):
        shard = ((1 - self.z // 2) * 2 + self.z % 2) * 2 + self.x
        return remote(
            self.rows(shard, q), self.from_far.at[q], self.far_sems.at[0, q], self.far_sems.at[1, q],
            (self.dp, self.far),
        )

    def start(self, q):
        for turn in range(4):
            self.x_copy(self.turn(turn), q).start()

    def turn(self, turn):
        return (1 - self.z // 2 + turn % 2) % 2 * 2 + (1 - self.z % 2 + turn // 2) % 2

    def add(self, shard, q, other):
        rows = self.rows(shard, q)
        rows[...] = (rows[...].astype(jnp.float32) + other[...].astype(jnp.float32)).astype(jnp.bfloat16)

    def step_near(self, q):
        for turn in range(2):
            high = (1 - self.z // 2 + turn) % 2
            shard_z = high * 2 + 1 - self.z % 2
            self.x_copy(shard_z, q).wait_recv()
            self.add(shard_z * 2 + self.x, q, self.from_x.at[shard_z, q])
            self.near_copy(high, q).start()

    def step_keep(self, q):
        for turn in range(2):
            high = (1 - self.z // 2 + turn) % 2
            shard_z = high * 2 + self.z % 2
            self.x_copy(shard_z, q).wait_recv()
            self.add(shard_z * 2 + self.x, q, self.from_x.at[shard_z, q])

    def step_far(self, q):
        high = 1 - self.z // 2
        self.near_copy(high, q).wait_recv()
        self.add((high * 2 + self.z % 2) * 2 + self.x, q, self.from_near.at[high, q])
        self.far_copy(q).start()

    def total(self, q):
        high = self.z // 2
        self.near_copy(high, q).wait_recv()
        self.far_copy(q).wait_recv()
        f32 = jnp.float32
        return (
            self.rows(self.s, q)[...].astype(f32)
            + self.from_near[high, q].astype(f32)
            + self.from_far[q].astype(f32)
        )

    def settle(self):
        for q in range(2):
            for shard_z in range(4):
                self.x_copy(shard_z, q).wait_send()
            for high in range(2):
                self.near_copy(high, q).wait_send()
            self.far_copy(q).wait_send()


def finish_kernel(gated, w_out, d_z, d_y, x_raw, inner, w_in, cot_all, normed_all,
                  bc_in, dt_in, seg_col, seg_row, wx, wbc, heads, gain_back, hidden_in, cot_in, gain,
                  result, d_hidden, plane_in, grad_out, small_all, gain_sum,
                  gated_v, w_out_v, dp_v, w_in_v, tok_v, inner_v, dy_v,
                  dt_mat, cum_mat, cum_rows, inner_prod, bias, d_inner, d_cum, d_dt,
                  part_r, rx, rn, rf, part_d, dx, dn, df,
                  core_out, core_in, keep, y_in,
                  out_core_in, out_y, out_y_in, small_v, small_in, gain_v, gain_in,
                  bc_raw, dt_raw, hidden, cot,
                  load, rxs, rns, rfs, dxs, dns, dfs, core_sems, y_sems, plane_sems, out_sems, out_y_sems,
                  small_sems, small_plane, gain_sems, gain_plane):
    f32, bf16 = jnp.float32, jnp.bfloat16
    where = place()
    dp, s, z, x, x_peer, y_peer, core_peer = where
    y, core = dp // 2, dp % 2
    n_own, span, width = hidden.shape
    length = 8 * span
    chan = w_out.shape[0]
    rows = chan // 4
    in_rows = plane_in.shape[1]
    columns = keep.shape[3]
    tail = columns - 2 * chan
    peers = [(dp, (s + k) % 8) for k in range(1, 8)] + [(y_peer, s), (core_peer, s)]
    h_own = chan // HDIM

    def scan_loads(q):
        at = pl.ds(q * length, length)
        return [
            pltpu.make_async_copy(inner.at[at], inner_v, load.at[3]),
            pltpu.make_async_copy(d_y.at[at], dy_v, load.at[4]),
        ]

    loads = [
        pltpu.make_async_copy(gated, gated_v, load.at[0]),
        pltpu.make_async_copy(w_out, w_out_v, load.at[1]),
        pltpu.make_async_copy(cot_all, tok_v, load.at[7]),
        pltpu.make_async_copy(w_in, w_in_v, load.at[6]),
        pltpu.make_async_copy(d_z, dp_v.at[:, pl.ds(0, chan)], load.at[5]),
        pltpu.make_async_copy(x_raw, dp_v.at[:, pl.ds(chan, chan)], load.at[2]),
    ]
    first_scan = scan_loads(0)
    pair_loads = [
        pltpu.make_async_copy(bc_in, bc_raw, load.at[9]),
        pltpu.make_async_copy(dt_in, dt_raw, load.at[10]),
    ]
    own_loads = [
        pltpu.make_async_copy(hidden_in, hidden, load.at[11]),
        pltpu.make_async_copy(cot_in, cot, load.at[12]),
    ]
    for copy in loads[:2] + pair_loads + loads[2:3] + first_scan + loads[3:] + own_loads:
        copy.start()
    greet(peers)
    small_v[0] = jnp.zeros(small_v.shape[1:], f32)

    def small_copy(stage, device):
        return remote(small_v.at[stage], small_in.at[stage], small_sems.at[0, stage], small_sems.at[1, stage], device)

    reduce_r = TokenReduce(part_r, rx, rn, rf, rxs, rns, rfs, where, span)
    reduce_d = TokenReduce(part_d, dx, dn, df, dxs, dns, dfs, where, span)
    loads[0].wait()
    loads[1].wait()
    step = 512

    def branch(q):
        @pl.loop(0, width // 256)
        def forward(n):
            cols = pl.ds(pl.multiple_of(n * 256, 256), 256)
            part_r[q, :, cols] = jnp.dot(
                gated_v[q * length : (q + 1) * length], w_out_v[:, cols], preferred_element_type=f32
            ).astype(bf16)

    def first_rows(turn):
        shard_z = reduce_r.turn(turn)
        at = pl.ds(pl.multiple_of(shard_z * 2 * span, 2 * span), 2 * span)
        for half in range(2):
            cols = slice(half * width // 2, (half + 1) * width // 2)
            part_r[0, at, cols] = jnp.dot(gated_v[at], w_out_v[:, cols], preferred_element_type=f32).astype(bf16)
        return shard_z

    first = first_rows(0)
    greeted(peers)
    reduce_r.x_copy(first, 0).start()

    @pl.loop(1, 4)
    def other_rows(turn):
        reduce_r.x_copy(first_rows(turn), 0).start()

    def out_term(d, n):
        lanes = pl.ds(pl.multiple_of(d * rows, rows), rows)
        return lax.dot_general(
            gated_v[:, lanes], tok_v[:, n * step : (n + 1) * step], (((0,), (0,)), ((), ())),
            preferred_element_type=f32,
        )

    def out_core_copy(yy):
        return remote(w_out_v.at[pl.ds(yy * rows, rows)], out_core_in.at[yy], out_sems.at[0, yy], out_sems.at[1, yy], (core_peer, s))

    def out_gradient():
        loads[2].wait()
        for yy in range(2):
            for n in range(width // step):
                w_out_v[yy * rows : (yy + 1) * rows, n * step : (n + 1) * step] = out_term(yy * 2 + 1 - core, n).astype(bf16)
            out_core_copy(yy).start()
        for n in range(width // step):
            out_y[:, n * step : (n + 1) * step] = out_term((1 - y) * 2 + core, n).astype(bf16)
        for n in range(width // step):
            grad_out[:, n * step : (n + 1) * step] = out_term(y * 2 + core, n)
        norm_load.start()

    norm_load = pltpu.make_async_copy(normed_all, tok_v, load.at[8])
    out_y_copy = remote(out_y, out_y_in, out_y_sems.at[0], out_y_sems.at[1], (y_peer, s))
    for q in range(2):
        at = pl.ds(q * length, length)
        scan_in = first_scan if q == 0 else scan_loads(1)
        if q == 1:
            for copy in scan_in:
                copy.start()
        if q == 0:
            for copy in pair_loads:
                copy.wait()
        backward_prepare(
            h_own, bc_raw.at[at], dt_raw.at[at], seg_col[q], seg_row[q], wbc, heads,
            dt_mat, cum_mat, cum_rows, inner_prod, bias, d_inner, d_cum, d_dt,
        )
        for copy in scan_in:
            copy.wait()
        if q == 0:
            loads[5].wait()

        @pl.loop(0, chan // 128)
        def pairs(pair):
            cols = pl.ds(pl.multiple_of(pair * 128, 128), 128)
            x_cols = pl.ds(pl.multiple_of(chan + pair * 128, 128), 128)
            backward_pair(
                pair, dp_v.at[at, x_cols], seg_col[q], wx.at[:, cols], dy_v.at[:, cols], inner_v.at[:, cols],
                dp_v.at[at, x_cols], small_v.at[0, :, cols], dt_mat, cum_mat, cum_rows,
                inner_prod, bias, d_inner, d_cum, d_dt,
            )
            if q == 0:

                @pl.when(pair == 3)
                def near_result():
                    reduce_r.step_near(0)
            else:

                @pl.when(pair == 0)
                def far_result():
                    reduce_r.step_far(0)

                @pl.when(pair == 3)
                def near_back():
                    reduce_d.step_near(0)

        backward_finish(
            h_own, bc_raw.at[at], dt_raw.at[at], seg_col[q], wbc, heads, d_inner, d_cum, d_dt,
            dp_v.at[at, pl.ds(2 * chan, 2 * NST)], dp_v.at[at, pl.ds(2 * chan + 2 * NST, 128)],
            small_v.at[0, :, pl.ds(chan, 2 * NST)], small_v.at[0, :, pl.ds(chan + 2 * NST, 128)],
        )
        if q == 0:
            loads[3].wait()
            loads[4].wait()

        @pl.loop(0, width // 256)
        def backward(n):
            cols = pl.ds(pl.multiple_of(n * 256, 256), 256)
            part_d[q, :, cols] = lax.dot_general(
                dp_v[q * length : (q + 1) * length], w_in_v[cols], (((1,), (1,)), ((), ())),
                preferred_element_type=f32,
            ).astype(bf16)

        reduce_d.start(q)
        if q == 0:
            branch(1)
            reduce_r.step_keep(0)

    reduce_r.start(1)
    small_v[0, CONV + 2 : CONV + 3, :chan] = gain_back[0:1]
    small_core = small_copy(0, (core_peer, s))
    small_core.start()

    def small_push(k):
        return remote(
            small_all.at[s], small_all.at[s], small_plane.at[0, k], small_plane.at[1, s], (dp, (s + k) % 8)
        )

    out_gradient()

    def in_term(d, m, lo, size):
        lanes = pl.ds(pl.multiple_of(d * 8 * in_rows + m * 2 * in_rows, 2 * in_rows), 2 * in_rows)
        return lax.dot_general(
            tok_v[:, lanes], dp_v[:, lo : lo + size], (((0,), (0,)), ((), ())), preferred_element_type=f32
        )

    pieces = ((0, chan, chan), (chan, chan, chan), (2 * chan, tail, 2 * NST + 128))

    def core_copy(t, yy):
        return remote(
            core_out.at[t % 2, yy], core_in.at[t, yy], core_sems.at[0, t, yy], core_sems.at[1, t, yy], (core_peer, s)
        )

    def y_copy(t):
        return remote(keep.at[t, 1 - y], y_in.at[t], y_sems.at[0, t], y_sems.at[1, t], (y_peer, s))

    def target_of(t):
        return (z + 1 + t) % 4

    def in_compute(t):
        for yy in range(2):
            if t >= 2:
                core_copy(t - 2, yy).wait_send()
            for lo, size, span_in in pieces:
                core_out[t % 2, yy, :, lo : lo + size] = in_term(yy * 2 + 1 - core, target_of(t), lo, span_in)[
                    :, :size
                ].astype(bf16)
            core_copy(t, yy).start()
        for yy in range(2):
            for lo, size, span_in in pieces:
                keep[t, yy, :, lo : lo + size] = in_term(yy * 2 + core, target_of(t), lo, span_in)[:, :size].astype(bf16)

    def in_core(t):
        for yy in range(2):
            core_copy(t, yy).wait_recv()
            keep[t, yy] = (keep[t, yy].astype(f32) + core_in[t, yy].astype(f32)).astype(bf16)
        y_copy(t).start()

    def half_rows(half):
        return pl.ds(pl.multiple_of(half * in_rows, in_rows), in_rows)

    def plane_copy(t, half):
        return remote(
            keep.at[t, y, half_rows(half)], plane_in.at[s],
            plane_sems.at[0, t, half], plane_sems.at[1, s // 2, s % 2], (dp, 2 * target_of(t) + half),
        )

    def plane_halves(t):
        return (0, 1) if t < 3 else (1 - x,)

    def in_plane(t):
        y_copy(t).wait_recv()
        keep[t, y] = (keep[t, y].astype(f32) + y_in[t].astype(f32)).astype(bf16)
        for half in plane_halves(t):
            plane_copy(t, half).start()
        if t == 3:
            plane_in[s] = keep[t, y, half_rows(x)]

    reduce_d.step_keep(0)
    reduce_d.step_far(0)
    norm_load.wait()
    in_compute(0)
    out_core_copy(1 - y).wait_recv()
    out_y[...] = (out_y[...].astype(f32) + out_core_in[1 - y].astype(f32)).astype(bf16)
    out_y_copy.start()
    in_core(0)
    small_core.wait_recv()
    small_v[1] = small_v[0] + small_in[0]
    small_y = small_copy(1, (y_peer, s))
    small_y.start()
    reduce_d.step_near(1)
    in_compute(1)
    in_core(1)
    in_compute(2)
    in_core(2)
    small_y.wait_recv()
    small_all[s] = small_v[1] + small_in[1]
    for k in range(1, 8):
        small_push(k).start()
    in_plane(0)
    reduce_d.step_keep(1)
    reduce_d.step_far(1)
    in_compute(3)
    in_core(3)
    in_plane(1)
    for copy in own_loads:
        copy.wait()
    result[0] = (hidden[0].astype(f32) + reduce_r.total(0)).astype(bf16)
    reduce_r.step_near(1)
    in_plane(2)
    out_y_copy.wait_recv()
    out_core_copy(y).wait_recv()
    grad_out[...] = grad_out[...] + out_core_in[y].astype(f32) + out_y_in[...].astype(f32)
    gain_row = gain[...]
    gain_part = None
    for q in range(2):
        d_normed = reduce_d.total(q)
        h = hidden[q].astype(f32)
        inv = lax.rsqrt(jnp.mean(h * h, axis=-1, keepdims=True) + 1e-05)
        scaled = d_normed * gain_row
        along = jnp.mean(scaled * h, axis=-1, keepdims=True)
        d_hidden[q] = (cot[q].astype(f32) + inv * scaled - (inv * inv * inv) * along * h).astype(bf16)
        term = jnp.sum(d_normed * h * inv, axis=0, keepdims=True)
        gain_part = term if q == 0 else gain_part + term
    folded = width // 8
    gain_v[0] = jnp.concatenate([gain_part[:, k * folded : (k + 1) * folded] for k in range(8)], axis=0)

    def gain_copy(stage, device):
        return remote(gain_v.at[stage], gain_in.at[stage], gain_sems.at[0, stage], gain_sems.at[1, stage], device)

    gain_core = gain_copy(0, (core_peer, s))
    gain_core.start()
    in_plane(3)
    reduce_r.step_keep(1)
    reduce_r.step_far(1)
    gain_core.wait_recv()
    gain_v[1] = gain_v[0] + gain_in[0]
    gain_y = gain_copy(1, (y_peer, s))
    gain_y.start()
    for k in range(1, 8):
        source = (s + 8 - k) % 8
        there = plane_in.at[source]
        remote(there, there, plane_sems.at[0, 0, 0], plane_sems.at[1, source // 2, source % 2], (dp, x_peer)).wait_recv()
    gain_y.wait_recv()
    gain_v[2 + s] = gain_v[1] + gain_in[1]

    def gain_push(k):
        return remote(gain_v.at[2 + s], gain_v.at[2 + s], gain_plane.at[0, k], gain_plane.at[1, s], (dp, (s + k) % 8))

    for k in range(1, 8):
        gain_push(k).start()
    result[1] = (hidden[1].astype(f32) + reduce_r.total(1)).astype(bf16)
    reduce_r.settle()
    reduce_d.settle()
    small_core.wait_send()
    small_y.wait_send()
    out_y_copy.wait_send()
    for yy in range(2):
        out_core_copy(yy).wait_send()
    for m in range(4):
        for yy in range(2 if m >= 2 else 0):
            core_copy(m, yy).wait_send()
        y_copy(m).wait_send()
        for half in plane_halves(m):
            plane_copy(m, half).wait_send()

    for k in range(1, 8):
        source = (s + 8 - k) % 8
        remote(
            small_all.at[source], small_all.at[source], small_plane.at[0, k], small_plane.at[1, source], (dp, x_peer)
        ).wait_recv()
        small_push(k).wait_send()
        remote(
            gain_v.at[2 + source], gain_v.at[2 + source], gain_plane.at[0, k], gain_plane.at[1, source], (dp, x_peer)
        ).wait_recv()
        gain_push(k).wait_send()
    gain_core.wait_send()
    gain_y.wait_send()
    gain_total = gain_v[2]
    for source in range(1, 8):
        gain_total = gain_total + gain_v[2 + source]
    gain_sum[...] = gain_total


def run_finish(gated, w_out, d_z, d_y, x_raw, inner, w_in, cot_all, normed_all,
               bc_raw, dt_raw, seg_col, seg_row, wx, wbc, heads, gain_back, hidden, cot, gain, in_rows):
    f32, bf16 = jnp.float32, jnp.bfloat16
    n_own, span, width = hidden.shape
    tokens, chan = gated.shape
    length, rows = 8 * span, chan // 4
    columns = 2 * chan + 2 * NST + HEADS
    small = (8, chan + 2 * NST + 128)
    vmem = pltpu.VMEM
    anywhere, inside = pl.BlockSpec(memory_space=pl.ANY), pl.BlockSpec(memory_space=vmem)
    sem = pltpu.SemaphoreType.DMA
    tokens_like = [
        vmem((n_own, length, width), bf16), vmem((4, n_own, span, width), bf16),
        vmem((2, n_own, span, width), bf16), vmem((n_own, span, width), bf16),
    ]
    return pl.pallas_call(
        finish_kernel,
        in_specs=[anywhere] * 11 + [inside] * 6 + [anywhere] * 2 + [inside],
        out_specs=[inside] * 6,
        out_shape=[
            jax.ShapeDtypeStruct(hidden.shape, bf16),
            jax.ShapeDtypeStruct(hidden.shape, bf16),
            jax.ShapeDtypeStruct((8, in_rows, columns), bf16),
            jax.ShapeDtypeStruct((rows, width), f32),
            jax.ShapeDtypeStruct((8,) + small, f32),
            jax.ShapeDtypeStruct((8, width // 8), f32),
        ],
        scratch_shapes=[
            vmem((tokens, chan), bf16), vmem((chan, width), bf16),
            vmem((tokens, 2 * chan + 2 * NST + 128), bf16), vmem((width, 2 * chan + 2 * NST + 128), bf16),
            vmem((tokens, width), bf16),
            vmem((length, chan), f32), vmem((length, chan), bf16),
            vmem((length, 128), f32), vmem((length, 128), f32), vmem((chan // HDIM, 1, length), f32),
            vmem((length, length), f32), vmem((length, length), f32), vmem((length, length), f32),
            vmem((length, 128), f32), vmem((length, 128), f32),
        ]
        + tokens_like + tokens_like
        + [
            vmem((2, 2, 2 * in_rows, columns), bf16), vmem((4, 2, 2 * in_rows, columns), bf16),
            vmem((4, 2, 2 * in_rows, columns), bf16), vmem((4, 2 * in_rows, columns), bf16),
            vmem((2, rows, width), bf16),
            vmem((rows, width), bf16), vmem((rows, width), bf16),
            vmem((2,) + small, f32), vmem((2,) + small, f32),
            vmem((10, 8, width // 8), f32), vmem((2, 8, width // 8), f32),
            vmem((tokens, 2 * NST), bf16), vmem((tokens, 128), bf16), vmem(hidden.shape, bf16), vmem(hidden.shape, bf16),
            sem((13,)), sem((2, 4, 2)), sem((2, 2, 2)), sem((2, 2)), sem((2, 4, 2)), sem((2, 2, 2)), sem((2, 2)),
            sem((2, 4, 2)), sem((2, 4)), sem((2, 4, 2)), sem((2, 2)), sem((2,)),
            sem((2, 2)), sem((2, 8)), sem((2, 2)), sem((2, 8)),
        ],
        compiler_params=pltpu.CompilerParams(
            collective_id=1, has_side_effects=True, vmem_limit_bytes=63 << 20
        ),
        name="finish",
    )(
        gated, w_out, d_z, d_y, x_raw, inner, w_in, cot_all, normed_all,
        bc_raw, dt_raw, seg_col, seg_row, wx, wbc, heads, gain_back, hidden, cot, gain,
    )


def over_heads(rows, lane_head):
    lane = lax.broadcasted_iota(jnp.int32, (rows.shape[1], HEADS), 1)
    own = lax.broadcasted_iota(jnp.int32, (rows.shape[1], HEADS), 0) // lane_head
    map_own = (own == lane // 16 * 2 + lane % 2).astype(jnp.float32)
    sums = jnp.dot(rows, map_own, precision=lax.Precision.HIGHEST, preferred_element_type=jnp.float32)
    source = lax.broadcasted_iota(jnp.int32, (8, HEADS), 0)
    mine = lax.broadcasted_iota(jnp.int32, (8, HEADS), 1) // 2 % 8 == source
    return jnp.sum(jnp.where(mine, sums, 0.0), axis=0)


def assemble_kernel(result_in, d_hidden_in, plane_in, grad_out_in, small_all, gain_sum,
                    result, d_hidden, grad_in_out, conv_w, conv_b, dt_bias, a_log, d_skip, norm_gain, gate_gain, grad_out,
                    plane_v, result_v, d_hidden_v, grad_out_v, grad_in, load, store):
    f32 = jnp.float32
    rows = grad_out.shape[0]
    chan = 4 * rows
    passed = [(result_in, result_v, result), (d_hidden_in, d_hidden_v, d_hidden), (grad_out_in, grad_out_v, grad_out)]
    plane_load = pltpu.make_async_copy(plane_in, plane_v, load.at[3])
    plane_load.start()
    loads = [pltpu.make_async_copy(a, b, load.at[k]) for k, (a, b, _) in enumerate(passed)]
    stores = [pltpu.make_async_copy(b, c, store.at[k]) for k, (_, b, c) in enumerate(passed)]
    for copy in loads:
        copy.start()
    plane_load.wait()
    for source in range(8):
        for piece in range(WIDE):
            at = (piece * 8 + source) * rows
            grad_in[:, at : at + rows] = plane_v[source, :, piece * rows : (piece + 1) * rows].astype(f32)
    tail_sum = 0.0
    for source in range(8):
        tail_sum = tail_sum + plane_v[source, :, 2 * chan :].astype(f32)
    grad_in[:, 2 * DI :] = tail_sum
    stores.append(pltpu.make_async_copy(grad_in, grad_in_out, store.at[3]))
    stores[-1].start()
    for k in range(3):
        loads[k].wait()
        stores[k].start()
    bc_sum = 0.0
    for source in range(8):
        for d in range(4):
            at, own = (d * 8 + source) * rows, slice(d * rows, (d + 1) * rows)
            conv_w[:, at : at + rows] = small_all[source, :CONV, own]
            conv_b[pl.ds(at, rows)] = small_all[source, CONV, own]
            gate_gain[pl.ds(at, rows)] = small_all[source, CONV + 2, own]
        bc_sum = bc_sum + small_all[source, :, chan : chan + 2 * NST]
    conv_w[:, DI:] = bc_sum[:CONV]
    conv_b[pl.ds(DI, 2 * NST)] = bc_sum[CONV]
    dt_bias[...] = over_heads(small_all[:, 0, chan + 2 * NST :], 1)
    a_log[...] = over_heads(small_all[:, 1, chan + 2 * NST :], 1)
    d_skip[...] = over_heads(small_all[:, CONV + 1, :chan], HDIM)
    folded = gain_sum.shape[1]
    for k in range(8):
        norm_gain[pl.ds(k * folded, folded)] = gain_sum[k]
    for copy in stores:
        copy.wait()


def run_assemble(result, d_hidden, plane_in, grad_out, small_all, gain_sum):
    f32 = jnp.float32
    width = result.shape[2]
    in_rows = plane_in.shape[1]
    shape = jax.ShapeDtypeStruct
    channels = DI + 2 * NST
    anywhere, inside = pl.BlockSpec(memory_space=pl.ANY), pl.BlockSpec(memory_space=pltpu.VMEM)
    return pl.pallas_call(
        assemble_kernel,
        in_specs=[anywhere] * 4 + [inside] * 2,
        out_specs=[anywhere] * 3 + [inside] * 7 + [anywhere],
        out_shape=[
            shape(result.shape, result.dtype),
            shape(d_hidden.shape, d_hidden.dtype),
            shape((in_rows, 2 * DI + 2 * NST + HEADS), f32),
            shape((CONV, channels), f32),
            shape((channels,), f32),
            shape((HEADS,), f32),
            shape((HEADS,), f32),
            shape((HEADS,), f32),
            shape((width,), f32),
            shape((DI,), f32),
            shape(grad_out.shape, f32),
        ],
        scratch_shapes=[
            pltpu.VMEM(plane_in.shape, plane_in.dtype),
            pltpu.VMEM(result.shape, result.dtype),
            pltpu.VMEM(d_hidden.shape, d_hidden.dtype),
            pltpu.VMEM(grad_out.shape, f32),
            pltpu.VMEM((in_rows, 2 * DI + 2 * NST + HEADS), f32),
            pltpu.SemaphoreType.DMA((4,)),
            pltpu.SemaphoreType.DMA((4,)),
        ],
        compiler_params=pltpu.CompilerParams(vmem_limit_bytes=62 << 20),
        name="assemble",
    )(result, d_hidden, plane_in, grad_out, small_all, gain_sum)


def head_plan(
    hidden,
    segments,
    in_weight,
    conv_weight,
    conv_bias,
    dt_bias,
    a_log,
    d_skip,
    norm_gain,
    gate_gain,
    out_weight,
    cotangent,
):
    f32, bf16 = jnp.float32, jnp.bfloat16
    n_dp, n_seq = lax.axis_size("dp"), lax.axis_size("seq")
    seq_rank = lax.axis_index("seq")
    n_own, shard_len, width = hidden.shape
    length = shard_len * n_seq
    rows = out_weight.shape[0]
    in_rows = in_weight.shape[0]
    chan = rows * n_dp
    h_own = chan // HDIM
    (n_all, cot_all, w_in, w_out, x_raw, bc_raw, dt_raw, inner, gated, d_y, d_z, seg_col, seg_row, wx, wbc, head_vals,
     gain_back) = run_ahead(
        hidden, cotangent, in_weight, out_weight, segments, conv_weight.T, conv_bias,
        norm_gain[None], gate_gain[None], dt_bias, a_log, d_skip,
    )
    normed_all = n_all.reshape(n_own * length, width)
    cot_all = cot_all.reshape(n_own * length, width)
    result, d_hidden, plane_in, grad_out, small_all, gain_sum = run_finish(
        gated, w_out, d_z, d_y, x_raw, inner, w_in, cot_all, normed_all,
        bc_raw, dt_raw, seg_col, seg_row, wx, wbc, head_vals, gain_back, hidden, cotangent, norm_gain[None], in_rows,
    )
    outs = list(run_assemble(result, d_hidden, plane_in, grad_out, small_all, gain_sum))
    outs[3] = outs[3].T
    return tuple(outs)


def solution(mesh):
    whole_heads = mesh.shape["dp"] == 4 and mesh.shape["seq"] == 8
    shards = head_plan if whole_heads else general_plan
    placed = (
        P("dp", "seq", None),
        P("dp", "seq"),
        P(("dp", "seq"), None),
        P(),
        P(),
        P(),
        P(),
        P(),
        P(),
        P(),
        P(("dp", "seq"), None),
        P("dp", "seq", None),
    )
    return jax.shard_map(
        shards,
        mesh=mesh,
        in_specs=placed,
        out_specs=(
            P("dp", "seq", None),
            P("dp", "seq", None),
            P(("dp", "seq"), None),
            P(),
            P(),
            P(),
            P(),
            P(),
            P(),
            P(),
            P(("dp", "seq"), None),
        ),
        check_vma=False,
    )
```
